32 devices in a mesh: gx: 4 (over y, core), gy: 4 (over z), gz: 2 (over x).
Axes of the slice: x: 2, y: 2, z: 4, core: 2. Of those that a mesh axis runs over, the one named last changes fastest.
Arguments:
- les_state: float32 [5, 32, 32, 256], P(None, 'gx', 'gy', 'gz'), may hold values from -0.4 to 0.4
- acoustic_state: float32 [4, 32, 32, 256], P(None, 'gx', 'gy', 'gz'), may hold values from -0.04 to 0.04
- mean_flow: float32 [3, 32, 32, 256], P(None, 'gx', 'gy', 'gz'), may hold values from -0.5 to 0.5
- projection: float32 [8, 8], replicated, may hold values from -0.3 to 1.3, as said below
- target_owner: int32 [4, 4, 32], P('gx', 'gy', 'gz'), may hold values from 0 to 3, as said below
- target_slot: int32 [4, 4, 32], P('gx', 'gy', 'gz'), may hold values from 0 to 15
Outputs:
- les_next: float32 [5, 32, 32, 256], P(None, 'gx', 'gy', 'gz')
- source_nodes: float32 [3, 32, 32, 256], P(None, 'gx', 'gy', 'gz')
- acoustic_next: float32 [4, 32, 32, 256], P(None, 'gx', 'gy', 'gz')
The draws below stay inside these ranges and needn't reach their ends.
Inputs may be any that keep to these rules, and one draw needn't show every extreme that they name: `target_owner`: the blocks of the device with index i along gx name as owners exactly the 4 consecutive indices from (i * (4 - 3)) // 4 on, each for exactly 4 blocks. `projection`: diagonal entries lie in 0.7 to 1.3, the others in -0.3 to 0.3.
All inputs are finite; a program needn't handle non-finite values.
Results may differ from the reference program's by a relative error of at most 0.00011.
Values sent between devices are 32-bit elements; how exact they have to be, the bound alone decides.
No kernel may reach another device: no remote copies, remote signals or barrier semaphores. Data moves between devices by JAX's collectives and lax.ppermute only.
A program may use at most 64 MiB of HBM per device.

```python
import jax
import jax.numpy as jnp
import numpy as np
from jax import lax

CX = 8
CY = 8
CZ = 128
EX = 1
EY = 1
EZ = 16
NX = 32
NY = 32
NZ = 256
NAX = 32
NAY = 32
NAZ = 256
N_GX = 4
N_GY = 4
N_GZ = 2


def draw_projection(key, part):
    diagonal_key, spread_key = jax.random.split(key)
    diagonal = jax.random.uniform(diagonal_key, (8,), jnp.float32, 0.8, 1.2)
    spread = jax.random.uniform(spread_key, (8, 8), jnp.float32, -0.25, 0.25)
    identity = jnp.eye(8, dtype=jnp.float32)
    return spread * (1.0 - identity) + identity * diagonal[:, None]


def draw_target_owner(key, part):
    count_x = NX // CX
    count_y = NY // CY
    count_z = NZ // CZ
    blocks_x = CX // 8
    blocks_y = CY // 8
    blocks_z = CZ // 8
    block_total = blocks_x * blocks_y * blocks_z
    window = min(4, count_x)
    capacity = block_total // window
    device_keys = jax.random.split(jax.random.fold_in(key, 17), count_x * count_y * count_z)
    ranks = jax.vmap(lambda device_key: jax.random.permutation(device_key, block_total))(device_keys)
    ranks = ranks.reshape(count_x, count_y, count_z, block_total).astype(jnp.int32)
    device_x = jnp.arange(count_x, dtype=jnp.int32)[:, None, None, None]
    start_owner = device_x * (count_x - window + 1) // count_x
    owners = start_owner + ranks // capacity
    owners = owners.reshape(count_x, count_y, count_z, blocks_x, blocks_y, blocks_z).transpose(0, 3, 1, 4, 2, 5)
    return owners.reshape(count_x * blocks_x, count_y * blocks_y, count_z * blocks_z).astype(jnp.int32)


def set_ends(entries, own_key, least, top_value):
    shape = entries.shape
    place = [jax.random.randint(jax.random.fold_in(own_key, axis), (), 0, shape[axis]) for axis in range(len(shape))]
    entries = entries.at[tuple(place)].set(least)
    longest = shape.index(max(shape))
    place[longest] = (place[longest] + 1) % shape[longest]
    return entries.at[tuple(place)].set(top_value)


def level_of(own_key, shape, cuts, low, largest):
    def one(axis_at, parts):
        draws = jax.random.uniform(jax.random.fold_in(jax.random.fold_in(own_key, 6), axis_at), (parts,), jnp.float32, low / len(cuts), largest / len(cuts))
        return jnp.repeat(jnp.exp(draws), shape[axis_at] // parts).reshape((-1,) + (1,) * (len(shape) - axis_at - 1))

    factor_of = one(*cuts[0])
    for cut in cuts[1:]:
        factor_of = factor_of * one(*cut)
    return factor_of


def scatter_about(own_key, dims, deviation, bound, pieces=(), kind=jnp.bfloat16):
    drawn = deviation * jax.random.normal(own_key, dims, jnp.float32)
    if pieces:
        drawn = drawn * level_of(own_key, dims, pieces, -0.22, 0.18)
    return jnp.clip(drawn, -bound, bound).astype(kind)


def setup_inputs(seed: int = 0) -> dict:
    streams_of = jax.random.split(jax.random.key(seed), 7)
    les_state = jnp.clip(jax.random.uniform(streams_of[0], (5, NX, NY, NZ), jnp.float32, -0.4, 0.4) * level_of(streams_of[0], (5, NX, NY, NZ), ((1, 4), (2, 4), (3, 2)), -0.4, 0.0), -0.4, 0.4)
    acoustic_state = scatter_about(streams_of[1], (4, NAX, NAY, NAZ), 0.01, 0.04, ((1, 4), (2, 4), (3, 2)), jnp.float32)
    mean_flow = jnp.clip(jax.random.uniform(streams_of[2], (3, NAX, NAY, NAZ), jnp.float32, -0.5, 0.5) * level_of(streams_of[2], (3, NAX, NAY, NAZ), ((1, 4), (2, 4), (3, 2)), -0.4, 0.0), -0.5, 0.5)
    projection = draw_projection(jax.random.fold_in(streams_of[6], 71), 0)
    target_owner = draw_target_owner(jax.random.fold_in(streams_of[6], 71), 0)
    target_slot = set_ends(jax.random.randint(streams_of[5], (NX // 8, NY // 8, NZ // 8), 0, EX * EY * EZ), jax.random.fold_in(streams_of[5], 1), 0, (EX * EY * EZ) - 1).astype(jnp.int32)
    return dict(les_state=les_state, acoustic_state=acoustic_state, mean_flow=mean_flow, projection=projection, target_owner=target_owner, target_slot=target_slot)


lobatto_points = np.array([-1.0, -0.8717401485096066, -0.5917001814331423, -0.2092992179024789, 0.2092992179024789, 0.5917001814331423, 0.8717401485096066, 1.0])
flux_half = 0.08
viscous_ratio = 0.08
gamma_less = 0.4
acoustic_step = 0.01
upwind_speed = 1.5
face_lift = 28.0


def derivative_matrix():
    products = np.array([np.prod([lobatto_points[row_index] - lobatto_points[partner_index] for partner_index in range(8) if partner_index != row_index]) for row_index in range(8)])
    matrix = np.zeros((8, 8))
    for row_index in range(8):
        for col_index in range(8):
            if col_index != row_index:
                matrix[row_index, col_index] = products[row_index] / (products[col_index] * (lobatto_points[row_index] - lobatto_points[col_index]))
        matrix[row_index, row_index] = -np.sum(matrix[row_index])
    return matrix


def inner_slice(padded, axis_dim, offset):
    selector = [slice(None)]
    for dim_index in range(3):
        extent = padded.shape[dim_index + 1]
        if dim_index == axis_dim:
            selector.append(slice(1 + offset, extent - 1 + offset))
        else:
            selector.append(slice(1, extent - 1))
    return padded[tuple(selector)]


def full_state(padded):
    free_stream = jnp.array([1.0, 0.0, 0.0, 0.0, 2.5], jnp.float32)[:, None, None, None]
    return padded + free_stream


def les_rate(padded):
    state_full = full_state(padded)
    density = state_full[0]
    momentum = state_full[1:4]
    energy = state_full[4]
    velocity = momentum / density
    pressure = gamma_less * (energy - 0.5 * jnp.sum(momentum * velocity, axis=0))
    center = inner_slice(padded, 0, 0)
    change = jnp.zeros_like(center)
    for axis_dim in range(3):
        axis_speed = velocity[axis_dim]
        flux_rows = [momentum[axis_dim]]
        for component in range(3):
            term = momentum[component] * axis_speed
            if component == axis_dim:
                term = term + pressure
            flux_rows.append(term)
        flux_rows.append((energy + pressure) * axis_speed)
        fluxes = jnp.stack(flux_rows)
        change = change - flux_half * (inner_slice(fluxes, axis_dim, 1) - inner_slice(fluxes, axis_dim, -1))
        change = change + viscous_ratio * (inner_slice(padded, axis_dim, 1) + inner_slice(padded, axis_dim, -1) - 2.0 * center)
    return change


def lamb_vector(padded):
    state_full = full_state(padded)
    velocity = state_full[1:4] / state_full[0]

    def slope(component, axis_dim):
        return 0.5 * (inner_slice(velocity, axis_dim, 1)[component] - inner_slice(velocity, axis_dim, -1)[component])

    vort_x = slope(2, 1) - slope(1, 2)
    vort_y = slope(0, 2) - slope(2, 0)
    vort_z = slope(1, 0) - slope(0, 1)
    speed = inner_slice(velocity, 0, 0)
    return jnp.stack([vort_y * speed[2] - vort_z * speed[1], vort_z * speed[0] - vort_x * speed[2], vort_x * speed[1] - vort_y * speed[0]])


def project_blocks(lamb_field, projection):
    component_count, size_x, size_y, size_z = lamb_field.shape
    blocks = lamb_field.reshape(component_count, size_x // 8, 8, size_y // 8, 8, size_z // 8, 8).transpose(1, 3, 5, 0, 2, 4, 6)
    highest = lax.Precision.HIGHEST
    blocks = jnp.einsum('ia,xyzcabe->xyzcibe', projection, blocks, precision=highest)
    blocks = jnp.einsum('jb,xyzcibe->xyzcije', projection, blocks, precision=highest)
    blocks = jnp.einsum('ke,xyzcije->xyzcijk', projection, blocks, precision=highest)
    return blocks.reshape(size_x // 8, size_y // 8, size_z // 8, component_count * 512)


def flux_along(state_now, mean_speed, axis_dim):
    pressure = state_now[0]
    axis_speed = mean_speed[axis_dim]
    flux_rows = [axis_speed * pressure + state_now[1 + axis_dim]]
    for component in range(3):
        term = axis_speed * state_now[1 + component]
        if component == axis_dim:
            term = term + pressure
        flux_rows.append(term)
    return jnp.stack(flux_rows)


def element_derivative(field_data, axis_dim):
    deriv_table = jnp.asarray(derivative_matrix(), jnp.float32)
    moved_field = jnp.moveaxis(field_data, axis_dim + 1, -1)
    lead_shape = moved_field.shape[:-1]
    extent = moved_field.shape[-1]
    grouped = moved_field.reshape(lead_shape + (extent // 8, 8))
    result_data = jnp.einsum('...k,jk->...j', grouped, deriv_table, precision=lax.Precision.HIGHEST)
    return jnp.moveaxis(result_data.reshape(lead_shape + (extent,)), -1, axis_dim + 1)


def acoustic_rate(padded, mean_speed, source):
    center = inner_slice(padded, 0, 0)
    total_rate = jnp.zeros_like(center)
    for axis_dim in range(3):
        extent = center.shape[axis_dim + 1]
        position = jnp.arange(extent) % 8
        shape_list = [1, 1, 1, 1]
        shape_list[axis_dim + 1] = extent
        right_face = (position == 7).astype(jnp.float32).reshape(shape_list)
        left_face = (position == 0).astype(jnp.float32).reshape(shape_list)
        upper_jump = inner_slice(padded, axis_dim, 1) - center
        lower_jump = inner_slice(padded, axis_dim, -1) - center
        total_rate = total_rate - element_derivative(flux_along(center, mean_speed, axis_dim), axis_dim)
        total_rate = total_rate - right_face * face_lift * (0.5 * flux_along(upper_jump, mean_speed, axis_dim) - 0.5 * upwind_speed * upper_jump)
        total_rate = total_rate + left_face * face_lift * (0.5 * flux_along(lower_jump, mean_speed, axis_dim) + 0.5 * upwind_speed * lower_jump)
    return total_rate + jnp.concatenate([jnp.zeros_like(source[:1]), source], axis=0)


def reference(les_state, acoustic_state, mean_flow, projection, target_owner, target_slot):
    pad_width = ((0, 0), (1, 1), (1, 1), (1, 1))
    first_padded = jnp.pad(les_state, pad_width)
    first_rate = les_rate(first_padded)
    lamb_field = lamb_vector(first_padded)
    section_state = les_state + first_rate
    second_rate = les_rate(jnp.pad(section_state, pad_width))
    les_next = les_state + 0.5 * (first_rate + second_rate)
    coeffs = project_blocks(lamb_field, projection)
    grid_y = (jnp.arange(target_owner.shape[1]) // (CY // 8)).astype(jnp.int32)[None, :, None]
    grid_z = (jnp.arange(target_owner.shape[2]) // (CZ // 8)).astype(jnp.int32)[None, None, :]
    count_x = EX * N_GX
    count_y = EY * N_GY
    count_z = EZ * N_GZ
    element_x = target_owner * EX + target_slot // (EY * EZ)
    element_y = grid_y * EY + (target_slot // EZ) % EY
    element_z = grid_z * EZ + target_slot % EZ
    element_ids = ((element_x * count_y + element_y) * count_z + element_z).reshape(-1).astype(jnp.int32)
    element_sums = jax.ops.segment_sum(coeffs.reshape(-1, 1536), element_ids, num_segments=count_x * count_y * count_z)
    source_nodes = element_sums.reshape(count_x, count_y, count_z, 3, 8, 8, 8).transpose(3, 0, 4, 1, 5, 2, 6).reshape(3, count_x * 8, count_y * 8, count_z * 8)
    first_acoustic = acoustic_rate(jnp.pad(acoustic_state, pad_width), mean_flow, source_nodes)
    middle_state = acoustic_state + acoustic_step * first_acoustic
    second_acoustic = acoustic_rate(jnp.pad(middle_state, pad_width), mean_flow, source_nodes)
    acoustic_next = acoustic_state + 0.5 * acoustic_step * (first_acoustic + second_acoustic)
    return les_next, source_nodes, acoustic_next
```

```python
import functools

import jax
import jax.numpy as jnp
import numpy as np
from jax import lax
from jax.experimental import pallas as pl
from jax.experimental.pallas import tpu as pltpu
from jax.sharding import PartitionSpec as P

lobatto_points = np.array(
    [
        -1.0,
        -0.8717401485096066,
        -0.5917001814331423,
        -0.2092992179024789,
        0.2092992179024789,
        0.5917001814331423,
        0.8717401485096066,
        1.0,
    ]
)
flux_half = 0.08
gamma_less = 0.4
acoustic_step = 0.01
upwind_speed = 1.5
face_lift = 28.0
free_stream = (1.0, 0.0, 0.0, 0.0, 2.5)
axes = ("gx", "gy", "gz")
window = 4
f32 = jnp.float32


def derivative_matrix():
    points = lobatto_points
    products = [np.prod([points[i] - points[j] for j in range(8) if j != i]) for i in range(8)]
    matrix = np.zeros((8, 8))
    for i in range(8):
        for j in range(8):
            if j != i:
                matrix[i, j] = products[i] / (products[j] * (points[i] - points[j]))
        matrix[i, i] = -np.sum(matrix[i])
    return matrix


def sublane(shape):
    return lax.broadcasted_iota(jnp.int32, shape, len(shape) - 2)


def lane(shape):
    return lax.broadcasted_iota(jnp.int32, shape, len(shape) - 1)


def shifted(field, axis, step, outer):
    if axis == 0:
        if step == 1:
            return jnp.concatenate([field[1:], outer[None]], axis=0)
        return jnp.concatenate([outer[None], field[:-1]], axis=0)
    count = field.shape[axis]
    moved = pltpu.roll(field, count - 1 if step == 1 else 1, axis)
    edge = count - 1 if step == 1 else 0
    if axis == 1:
        return jnp.where(sublane(field.shape) == edge, outer[:, None, :], moved)
    columns = jnp.stack([outer[:, x : x + 1] for x in range(8)], axis=0)
    return jnp.where(lane(field.shape) == edge, columns, moved)


def fluid(state):
    density, mx, my, mz, energy = [s + r for s, r in zip(state, free_stream)]
    inverse = 1.0 / density
    momentum = (mx, my, mz)
    velocity = [m * inverse for m in momentum]
    pressure = gamma_less * (
        energy - 0.5 * (mx * velocity[0] + my * velocity[1] + mz * velocity[2])
    )
    return momentum, velocity, pressure, energy + pressure


def split_flux(state, parts, axis, sign):
    momentum, velocity, pressure, enthalpy = parts
    speed = velocity[axis]
    flux = [momentum[axis]]
    for c in range(3):
        term = momentum[c] * speed
        flux.append(term + pressure if c == axis else term)
    flux.append(enthalpy * speed)
    if sign > 0:
        return [flux_half * (s + f) for s, f in zip(state, flux)]
    return [flux_half * (s - f) for s, f in zip(state, flux)]


def les_rate(state, halos):
    parts = fluid(state)
    total = [-6.0 * flux_half * s for s in state]
    for axis in range(3):
        before, after = halos[axis]
        ahead = split_flux(state, parts, axis, -1)
        behind = split_flux(state, parts, axis, 1)
        ahead_outer = split_flux(after, fluid(after), axis, -1)
        behind_outer = split_flux(before, fluid(before), axis, 1)
        for c in range(5):
            total[c] = total[c] + (
                shifted(ahead[c], axis, 1, ahead_outer[c])
                + shifted(behind[c], axis, -1, behind_outer[c])
            )
    return total


def wave_flux(state, mean, axis):
    speed = mean[axis]
    pressure = state[0]
    rows = [speed * pressure + state[1 + axis]]
    for c in range(3):
        term = speed * state[1 + c]
        rows.append(term + pressure if c == axis else term)
    return rows


def dot3(left, right):
    high = left.astype(jnp.bfloat16)
    low = (left - high.astype(f32)).astype(jnp.bfloat16)
    dot = functools.partial(jnp.dot, preferred_element_type=f32)
    return dot(high, right[0]) + (dot(low, right[0]) + dot(high, right[1]))


def halves(matrix):
    high = matrix.astype(jnp.bfloat16)
    return high, (matrix - high.astype(f32)).astype(jnp.bfloat16)


def acoustic_rate(state, mean, halos, deriv, along_z):
    shape = state[0].shape
    table = derivative_matrix()
    flux = wave_flux(state, mean, 0)
    before, after = halos[0]
    low_mean, high_mean = [m[0] for m in mean], [m[7] for m in mean]
    low_jump = [b - s[0] for b, s in zip(before, state)]
    high_jump = [a - s[7] for a, s in zip(after, state)]
    low_flux = wave_flux(low_jump, low_mean, 0)
    high_flux = wave_flux(high_jump, high_mean, 0)
    half, lift = 0.5 * face_lift, 0.5 * face_lift * upwind_speed
    total = []
    for c in range(4):
        planes = []
        for i in range(8):
            plane = -float(table[i, 0]) * flux[c][0]
            for a in range(1, 8):
                if abs(table[i, a]) > 1e-12:
                    plane = plane - float(table[i, a]) * flux[c][a]
            if i == 0:
                plane = plane + (half * low_flux[c] + lift * low_jump[c])
            if i == 7:
                plane = plane - (half * high_flux[c] - lift * high_jump[c])
            planes.append(plane)
        total.append(jnp.stack(planes, axis=0))
    flux = wave_flux(state, mean, 1)
    before, after = halos[1]
    row = sublane(shape)
    sign = jnp.where(row == 0, half, jnp.where(row == 7, -half, 0.0))
    jump = [
        jnp.where(row == 0, b[:, None, :], jnp.where(row == 7, a[:, None, :], s)) - s
        for s, b, a in zip(state, before, after)
    ]
    jump_flux = wave_flux(jump, mean, 1)
    for c in range(4):
        change = lift * jump[c] + sign * jump_flux[c]
        for b in range(8):
            change = change - deriv[:, b : b + 1][None] * flux[c][:, b : b + 1, :]
        total[c] = total[c] + change
    flux = wave_flux(state, mean, 2)
    before, after = halos[2]
    column = lane(shape)
    place = lax.rem(column, 8)
    sign = jnp.where(place == 0, half, jnp.where(place == 7, -half, 0.0))
    jump = [
        jnp.where(
            place == 0,
            shifted(s, 2, -1, b),
            jnp.where(place == 7, shifted(s, 2, 1, a), s),
        )
        - s
        for s, b, a in zip(state, before, after)
    ]
    jump_flux = wave_flux(jump, mean, 2)
    for c in range(4):
        slope = dot3(flux[c].reshape(64, 128), along_z).reshape(shape)
        total[c] = total[c] + (lift * jump[c] + sign * jump_flux[c] - slope)
    return total


def tile_rows(matrix, transposed):
    spread = (lax.rem(lane((8, 128)), 8) == sublane((8, 128))).astype(f32)
    contract = ((1,), (0,)) if transposed else ((0,), (0,))
    return lax.dot_general(
        matrix, spread, (contract, ((), ())),
        precision=lax.Precision.HIGHEST, preferred_element_type=f32,
    )


def block_diagonal(tile):
    rows = [jnp.where(lane((8, 128)) // 8 == n, tile, 0.0) for n in range(16)]
    return halves(jnp.concatenate(rows, axis=0))


def pairings(count):
    sets = []
    for first in (0, 1):
        pairs = [(i, i + 1) for i in range(first, count - 1, 2)]
        if pairs:
            sets.append([p for i, j in pairs for p in ((i, j), (j, i))])
    return sets


def pack_z(fields, at):
    packed = jnp.zeros((8, 128), f32)
    column = lane((8, 128))
    for c, field in enumerate(fields):
        for x in range(8):
            packed = jnp.where(column == c * 8 + x, field[x][:, at : at + 1], packed)
    return packed


def store_faces(fields, out_refs, counts):
    at = 0
    for axis in range(3):
        even = lax.rem(lax.axis_index(axes[axis]), 2) == 0
        sets = len(pairings(counts[axis]))
        if axis == 2:
            low, high = pack_z(fields, 0), pack_z(fields, 127)
            for s in range(sets):
                out_refs[at + s][...] = jnp.where(even == (s == 0), high, low)
        else:
            for c, field in enumerate(fields):
                low = field[0] if axis == 0 else field[:, 0, :]
                high = field[7] if axis == 0 else field[:, 7, :]
                for s in range(sets):
                    out_refs[at + s][c] = jnp.where(even == (s == 0), high, low)
        at += sets


def load_faces(in_refs, counts, first, last):
    halos = []
    at = 0
    for axis in range(3):
        even = lax.rem(lax.axis_index(axes[axis]), 2) == 0
        sets = len(pairings(counts[axis]))
        got = []
        for s in range(sets):
            if axis == 2:
                packed = in_refs[at + s][...]
                got.append(
                    [
                        pltpu.roll(packed, (128 - 8 * c) % 128, 1) if c else packed
                        for c in range(first, last)
                    ]
                )
            else:
                got.append([in_refs[at + s][c] for c in range(first, last)])
        while len(got) < 2:
            got.append([jnp.zeros((8, 128), f32)] * (last - first))
        before = [jnp.where(even, b, a) for a, b in zip(*got)]
        after = [jnp.where(even, a, b) for a, b in zip(*got)]
        halos.append((before, after))
        at += sets
    return halos


def face_shapes(counts, width):
    shapes = []
    for axis in range(3):
        shape = (8, 128) if axis == 2 else (width, 8, 128)
        shapes += [jax.ShapeDtypeStruct(shape, f32)] * len(pairings(counts[axis]))
    return shapes


def exchange(faces, counts):
    result = []
    at = 0
    for axis in range(3):
        for pairs in pairings(counts[axis]):
            result.append(lax.ppermute(faces[at], axes[axis], pairs))
            at += 1
    return result


def read_all(ref):
    return [ref[c] for c in range(ref.shape[0])]


def faces_kernel(counts, les_ref, wave_ref, *out_refs):
    store_faces(read_all(les_ref) + read_all(wave_ref), out_refs, counts)


def rotations(count):
    reach = window if count >= window else count
    found = []
    for d in list(range(reach)) + list(range(1 - reach, 0)):
        if d % count not in found:
            found.append(d % count)
    return found


def lamb_kernel(counts, n_faces, owner_ref, slot_ref, proj_smem, proj_ref, les_ref, *refs):
    face_refs, out_refs, (counter,) = refs[:n_faces], refs[n_faces:-1], refs[-1:]
    halos = load_faces(face_refs, counts, 0, 4)

    def speeds(state):
        inverse = 1.0 / (state[0] + 1.0)
        return [state[c] * inverse for c in (1, 2, 3)]

    velocity = speeds([les_ref[c] for c in range(4)])

    def slope(c, axis):
        before, after = halos[axis]
        return 0.5 * (
            shifted(velocity[c], axis, 1, outer[axis][1][c])
            - shifted(velocity[c], axis, -1, outer[axis][0][c])
        )

    outer = [(speeds(before), speeds(after)) for before, after in halos]
    vort = [slope(2, 1) - slope(1, 2), slope(0, 2) - slope(2, 0), slope(1, 0) - slope(0, 1)]
    lamb = [
        vort[1] * velocity[2] - vort[2] * velocity[1],
        vort[2] * velocity[0] - vort[0] * velocity[2],
        vort[0] * velocity[1] - vort[1] * velocity[0],
    ]
    proj = proj_ref[...]
    blocks = []
    for field in lamb:
        along_y = proj[:, 0:1][None] * field[:, 0:1, :]
        for b in range(1, 8):
            along_y = along_y + proj[:, b : b + 1][None] * field[:, b : b + 1, :]
        for i in range(8):
            plane = proj_smem[i, 0] * along_y[0]
            for a in range(1, 8):
                plane = plane + proj_smem[i, a] * along_y[a]
            blocks.append(plane)

    turns = rotations(counts[0])
    groups = 4 * ((len(turns) + 3) // 4)
    own = lax.axis_index("gx")
    n_blocks = owner_ref.shape[-1]
    for g in range(groups):
        counter[g] = 0
    places = []
    for n in range(n_blocks):
        turn = lax.rem(owner_ref[0, 0, n] - own + counts[0], counts[0])
        group = turn if len(turns) == counts[0] else jnp.where(
            turn < window, turn, turn - (counts[0] - len(turns))
        )
        taken = counter[group]
        counter[group] = taken + 1
        places.append(group * window + taken)

    tile = tile_rows(proj, False)
    block_of_lane = lane((8, 128)) // 8
    quarter = lane((8, 128)) // 32
    for s in range(groups // 4):
        products = []
        for t in range(4):
            rows = [
                jnp.where(block_of_lane == lax.rem(place + 4 * t, 16) , tile, 0.0)
                if groups == 4
                else jnp.where(
                    (block_of_lane == lax.rem(place + 4 * t, 16)) & (place // 16 == s), tile, 0.0
                )
                for place in places
            ]
            matrix = halves(jnp.concatenate(rows, axis=0))
            data = jnp.concatenate([blocks[4 * q + t] for q in range(6)], axis=0)
            products.append(dot3(data, matrix))
        labels = jnp.full((8, 128), -1.0, f32)
        for n, place in enumerate(places):
            labels = jnp.where(
                block_of_lane == place - 16 * s, slot_ref[0, 0, n].astype(f32), labels
            )
        for r in range(4):
            if 4 * s + r >= len(turns):
                continue
            out = out_refs[4 * s + r]
            for q in range(6):
                packed = products[0][8 * q : 8 * q + 8]
                for t in range(1, 4):
                    packed = jnp.where(
                        quarter == (r + t) % 4, products[t][8 * q : 8 * q + 8], packed
                    )
                out[q] = packed
            marks = labels
            for t in range(1, 4):
                marks = jnp.where(
                    quarter == (r + t) % 4, pltpu.roll(labels, 32 * t, 1), marks
                )
            out[6] = marks


def first_kernel(
    counts, n_faces, deriv_ref, high_ref, low_ref, les_ref, wave_ref, mean_ref, *refs
):
    face_refs, (section_ref, rate_ref) = refs[:n_faces], refs[n_faces:]
    state = read_all(les_ref)
    rate = les_rate(state, load_faces(face_refs, counts, 0, 5))
    for c in range(5):
        section_ref[c] = state[c] + rate[c]
    rate = acoustic_rate(
        read_all(wave_ref), read_all(mean_ref), load_faces(face_refs, counts, 5, 9),
        deriv_ref[...], (high_ref[...], low_ref[...]),
    )
    for c in range(4):
        rate_ref[c] = rate[c]


def source_kernel(counts, n_pieces, wave_ref, rate_ref, section_ref, *refs):
    pieces, (source_ref, middle_ref), face_refs = (
        refs[:n_pieces], refs[n_pieces : n_pieces + 2], refs[n_pieces + 2 :],
    )
    quarter = lane((8, 128)) // 32
    slot_of_row = sublane((128, 128)) // 8
    same_node = lax.rem(sublane((128, 128)), 8) == lax.rem(lane((128, 128)), 8)
    sums = [None] * 24
    for s in range((n_pieces + 3) // 4):
        count = min(4, n_pieces - 4 * s)

        def gathered(q, t):
            value = jnp.full((8, 128), -1.0 if q == 6 else 0.0, f32)
            for r in range(count):
                value = jnp.where(quarter == (r + t) % 4, pieces[4 * s + r][q], value)
            return value

        for t in range(4):
            marks = gathered(6, t)[0:1].astype(jnp.int32)
            chosen = ((slot_of_row == marks) & same_node).astype(f32).astype(jnp.bfloat16)
            data = jnp.concatenate([gathered(q, t) for q in range(6)], axis=0)
            high = data.astype(jnp.bfloat16)
            low = (data - high.astype(f32)).astype(jnp.bfloat16)
            dims = (((1,), (1,)), ((), ()))
            moved = lax.dot_general(high, chosen, dims, preferred_element_type=f32)
            moved = moved + lax.dot_general(low, chosen, dims, preferred_element_type=f32)
            for q in range(6):
                part = moved[8 * q : 8 * q + 8]
                k = 4 * q + t
                sums[k] = part if sums[k] is None else sums[k] + part
    source = [jnp.stack(sums[8 * c : 8 * c + 8], axis=0) for c in range(3)]
    middle = []
    for c in range(4):
        rate = rate_ref[c]
        if c:
            source_ref[c - 1] = source[c - 1]
            rate = rate + source[c - 1]
        middle.append(wave_ref[c] + acoustic_step * rate)
        middle_ref[c] = middle[c]
    store_faces(read_all(section_ref) + middle, face_refs, counts)


def last_kernel(
    counts, n_faces, deriv_ref, high_ref, low_ref, les_ref, section_ref, wave_ref, middle_ref,
    mean_ref, source_ref, *refs,
):
    face_refs, (les_out, wave_out) = refs[:n_faces], refs[n_faces:]
    section = read_all(section_ref)
    rate = les_rate(section, load_faces(face_refs, counts, 0, 5))
    for c in range(5):
        les_out[c] = 0.5 * ((les_ref[c] + section[c]) + rate[c])
    middle = read_all(middle_ref)
    rate = acoustic_rate(
        middle, read_all(mean_ref), load_faces(face_refs, counts, 5, 9),
        deriv_ref[...], (high_ref[...], low_ref[...]),
    )
    for c in range(4):
        total = rate[c] + source_ref[c - 1] if c else rate[c]
        wave_out[c] = 0.5 * ((wave_ref[c] + middle[c]) + acoustic_step * total)


VMEM = pl.BlockSpec(memory_space=pltpu.VMEM)
SMEM = pl.BlockSpec(memory_space=pltpu.SMEM)


def call(kernel, in_specs, out_shapes, name, cost, scratch=()):
    return pl.pallas_call(
        kernel,
        in_specs=in_specs,
        out_specs=[VMEM] * len(out_shapes),
        out_shape=out_shapes,
        scratch_shapes=list(scratch),
        name=name,
        cost_estimate=pl.CostEstimate(flops=cost, bytes_accessed=800000, transcendentals=0),
        compiler_params=pltpu.CompilerParams(vmem_limit_bytes=24 * 1024 * 1024),
    )


def local(counts, les, wave, mean, projection, owner, slot):
    shape = les.shape[1:]
    faces = face_shapes(counts, 9)
    n_faces = len(faces)
    like = lambda n: jax.ShapeDtypeStruct((n,) + shape, f32)

    table = derivative_matrix()
    deriv = jnp.asarray(table, f32)
    along_z = np.kron(np.eye(16), table.T).astype(np.float32)
    high = along_z.astype(jnp.bfloat16)
    low = (along_z - high.astype(np.float32)).astype(jnp.bfloat16)
    tables = (deriv, jnp.asarray(high), jnp.asarray(low))

    sent = call(functools.partial(faces_kernel, counts), [VMEM] * 2, faces, "faces", 100000)(les, wave)
    got = exchange(sent, counts)

    turns = rotations(counts[0])
    pieces = call(
        functools.partial(lamb_kernel, counts, n_faces),
        [SMEM] * 3 + [VMEM] * (2 + n_faces),
        [jax.ShapeDtypeStruct((7, 8, 128), f32)] * len(turns),
        "lamb_blocks",
        10000000,
        [pltpu.SMEM((8,), jnp.int32)],
    )(owner, slot, projection, projection, les, *got)
    moved = [
        lax.ppermute(piece, "gx", [(i, (i + turn) % counts[0]) for i in range(counts[0])])
        if turn
        else piece
        for turn, piece in zip(turns, pieces)
    ]
    section, rate = call(
        functools.partial(first_kernel, counts, n_faces),
        [VMEM] * (6 + n_faces),
        [like(5), like(4)],
        "first_rates",
        40000000,
    )(*tables, les, wave, mean, *got)

    source, middle, *sent = call(
        functools.partial(source_kernel, counts, len(turns)),
        [VMEM] * (3 + len(turns)),
        [like(3), like(4)] + faces,
        "source_and_faces",
        10000000,
    )(wave, rate, section, *moved)
    got = exchange(sent, counts)
    les_next, wave_next = call(
        functools.partial(last_kernel, counts, n_faces),
        [VMEM] * (9 + n_faces),
        [like(5), like(4)],
        "second_rates",
        40000000,
    )(*tables, les, section, wave, middle, mean, source, *got)
    return les_next, source, wave_next


def solution(mesh):
    counts = tuple(mesh.shape[axis] for axis in axes)
    field = P(None, *axes)
    return jax.shard_map(
        functools.partial(local, counts),
        mesh=mesh,
        in_specs=(field, field, field, P(), P(*axes), P(*axes)),
        out_specs=(field, field, field),
        check_vma=False,
    )
```

```python
import functools

import jax
import jax.numpy as jnp
import numpy as np
from jax import lax
from jax.experimental import pallas as pl
from jax.experimental.pallas import tpu as pltpu
from jax.sharding import PartitionSpec as P

lobatto_points = np.array(
    [
        -1.0,
        -0.8717401485096066,
        -0.5917001814331423,
        -0.2092992179024789,
        0.2092992179024789,
        0.5917001814331423,
        0.8717401485096066,
        1.0,
    ]
)
flux_half = 0.08
gamma_less = 0.4
acoustic_step = 0.01
upwind_speed = 1.5
face_lift = 28.0
free_stream = (1.0, 0.0, 0.0, 0.0, 2.5)
axes = ("gx", "gy", "gz")
window = 4
f32 = jnp.float32


def derivative_matrix():
    points = lobatto_points
    products = [np.prod([points[i] - points[j] for j in range(8) if j != i]) for i in range(8)]
    matrix = np.zeros((8, 8))
    for i in range(8):
        for j in range(8):
            if j != i:
                matrix[i, j] = products[i] / (products[j] * (points[i] - points[j]))
        matrix[i, i] = -np.sum(matrix[i])
    return matrix


def sublane(shape):
    return lax.broadcasted_iota(jnp.int32, shape, len(shape) - 2)


def lane(shape):
    return lax.broadcasted_iota(jnp.int32, shape, len(shape) - 1)


def shifted(field, axis, step, outer):
    if axis == 0:
        if step == 1:
            return jnp.concatenate([field[1:], outer[None]], axis=0)
        return jnp.concatenate([outer[None], field[:-1]], axis=0)
    count = field.shape[axis]
    moved = pltpu.roll(field, count - 1 if step == 1 else 1, axis)
    edge = count - 1 if step == 1 else 0
    if axis == 1:
        return jnp.where(sublane(field.shape) == edge, outer[:, None, :], moved)
    columns = jnp.stack([outer[:, x : x + 1] for x in range(8)], axis=0)
    return jnp.where(lane(field.shape) == edge, columns, moved)


def fluid(state):
    density, mx, my, mz, energy = [s + r for s, r in zip(state, free_stream)]
    inverse = 1.0 / density
    momentum = (mx, my, mz)
    velocity = [m * inverse for m in momentum]
    pressure = gamma_less * (
        energy - 0.5 * (mx * velocity[0] + my * velocity[1] + mz * velocity[2])
    )
    return momentum, velocity, pressure, energy + pressure


def split_flux(state, parts, axis, sign):
    momentum, velocity, pressure, enthalpy = parts
    speed = velocity[axis]
    flux = [momentum[axis]]
    for c in range(3):
        term = momentum[c] * speed
        flux.append(term + pressure if c == axis else term)
    flux.append(enthalpy * speed)
    if sign > 0:
        return [flux_half * (s + f) for s, f in zip(state, flux)]
    return [flux_half * (s - f) for s, f in zip(state, flux)]


def les_rate(state, halos):
    parts = fluid(state)
    total = [-6.0 * flux_half * s for s in state]
    for axis in range(3):
        before, after = halos[axis]
        ahead = split_flux(state, parts, axis, -1)
        behind = split_flux(state, parts, axis, 1)
        ahead_outer = split_flux(after, fluid(after), axis, -1)
        behind_outer = split_flux(before, fluid(before), axis, 1)
        for c in range(5):
            total[c] = total[c] + (
                shifted(ahead[c], axis, 1, ahead_outer[c])
                + shifted(behind[c], axis, -1, behind_outer[c])
            )
    return total


def wave_flux(state, mean, axis):
    speed = mean[axis]
    pressure = state[0]
    rows = [speed * pressure + state[1 + axis]]
    for c in range(3):
        term = speed * state[1 + c]
        rows.append(term + pressure if c == axis else term)
    return rows


def dot3(left, right):
    high = left.astype(jnp.bfloat16)
    low = (left - high.astype(f32)).astype(jnp.bfloat16)
    dot = functools.partial(jnp.dot, preferred_element_type=f32)
    return dot(high, right[0]) + (dot(low, right[0]) + dot(high, right[1]))


def halves(matrix):
    high = matrix.astype(jnp.bfloat16)
    return high, (matrix - high.astype(f32)).astype(jnp.bfloat16)


def acoustic_rate(state, mean, halos, deriv, along_z):
    shape = state[0].shape
    table = derivative_matrix()
    flux = wave_flux(state, mean, 0)
    before, after = halos[0]
    low_mean, high_mean = [m[0] for m in mean], [m[7] for m in mean]
    low_jump = [b - s[0] for b, s in zip(before, state)]
    high_jump = [a - s[7] for a, s in zip(after, state)]
    low_flux = wave_flux(low_jump, low_mean, 0)
    high_flux = wave_flux(high_jump, high_mean, 0)
    half, lift = 0.5 * face_lift, 0.5 * face_lift * upwind_speed
    total = []
    for c in range(4):
        planes = []
        for i in range(8):
            plane = -float(table[i, 0]) * flux[c][0]
            for a in range(1, 8):
                if abs(table[i, a]) > 1e-12:
                    plane = plane - float(table[i, a]) * flux[c][a]
            if i == 0:
                plane = plane + (half * low_flux[c] + lift * low_jump[c])
            if i == 7:
                plane = plane - (half * high_flux[c] - lift * high_jump[c])
            planes.append(plane)
        total.append(jnp.stack(planes, axis=0))
    flux = wave_flux(state, mean, 1)
    before, after = halos[1]
    row = sublane(shape)
    sign = jnp.where(row == 0, half, jnp.where(row == 7, -half, 0.0))
    jump = [
        jnp.where(row == 0, b[:, None, :], jnp.where(row == 7, a[:, None, :], s)) - s
        for s, b, a in zip(state, before, after)
    ]
    jump_flux = wave_flux(jump, mean, 1)
    for c in range(4):
        change = lift * jump[c] + sign * jump_flux[c]
        for b in range(8):
            change = change - deriv[:, b : b + 1][None] * flux[c][:, b : b + 1, :]
        total[c] = total[c] + change
    flux = wave_flux(state, mean, 2)
    before, after = halos[2]
    column = lane(shape)
    place = lax.rem(column, 8)
    sign = jnp.where(place == 0, half, jnp.where(place == 7, -half, 0.0))
    jump = [
        jnp.where(
            place == 0,
            shifted(s, 2, -1, b),
            jnp.where(place == 7, shifted(s, 2, 1, a), s),
        )
        - s
        for s, b, a in zip(state, before, after)
    ]
    jump_flux = wave_flux(jump, mean, 2)
    for c in range(4):
        slope = dot3(flux[c].reshape(64, 128), along_z).reshape(shape)
        total[c] = total[c] + (lift * jump[c] + sign * jump_flux[c] - slope)
    return total


def tile_rows(matrix, transposed):
    spread = (lax.rem(lane((8, 128)), 8) == sublane((8, 128))).astype(f32)
    contract = ((1,), (0,)) if transposed else ((0,), (0,))
    return lax.dot_general(
        matrix, spread, (contract, ((), ())),
        precision=lax.Precision.HIGHEST, preferred_element_type=f32,
    )


def block_diagonal(tile):
    rows = [jnp.where(lane((8, 128)) // 8 == n, tile, 0.0) for n in range(16)]
    return halves(jnp.concatenate(rows, axis=0))


def pairings(count):
    sets = []
    for first in (0, 1):
        pairs = [(i, i + 1) for i in range(first, count - 1, 2)]
        if pairs:
            sets.append([p for i, j in pairs for p in ((i, j), (j, i))])
    return sets


def pack_z(fields, at):
    packed = jnp.zeros((8, 128), f32)
    column = lane((8, 128))
    for c, field in enumerate(fields):
        for x in range(8):
            packed = jnp.where(column == c * 8 + x, field[x][:, at : at + 1], packed)
    return packed


def store_faces(fields, out_refs, counts):
    at = 0
    for axis in range(3):
        even = lax.rem(lax.axis_index(axes[axis]), 2) == 0
        sets = len(pairings(counts[axis]))
        if axis == 2:
            low, high = pack_z(fields, 0), pack_z(fields, 127)
            for s in range(sets):
                out_refs[at + s][...] = jnp.where(even == (s == 0), high, low)
        else:
            for c, field in enumerate(fields):
                low = field[0] if axis == 0 else field[:, 0, :]
                high = field[7] if axis == 0 else field[:, 7, :]
                for s in range(sets):
                    out_refs[at + s][c] = jnp.where(even == (s == 0), high, low)
        at += sets


def load_faces(in_refs, counts, first, last):
    halos = []
    at = 0
    for axis in range(3):
        even = lax.rem(lax.axis_index(axes[axis]), 2) == 0
        sets = len(pairings(counts[axis]))
        got = []
        for s in range(sets):
            if axis == 2:
                packed = in_refs[at + s][...]
                got.append(
                    [
                        pltpu.roll(packed, (128 - 8 * c) % 128, 1) if c else packed
                        for c in range(first, last)
                    ]
                )
            else:
                got.append([in_refs[at + s][c] for c in range(first, last)])
        while len(got) < 2:
            got.append([jnp.zeros((8, 128), f32)] * (last - first))
        before = [jnp.where(even, b, a) for a, b in zip(*got)]
        after = [jnp.where(even, a, b) for a, b in zip(*got)]
        halos.append((before, after))
        at += sets
    return halos


def face_shapes(counts, width):
    shapes = []
    for axis in range(3):
        shape = (8, 128) if axis == 2 else (width, 8, 128)
        shapes += [jax.ShapeDtypeStruct(shape, f32)] * len(pairings(counts[axis]))
    return shapes


def exchange(faces, counts):
    result = []
    at = 0
    for axis in range(3):
        for pairs in pairings(counts[axis]):
            result.append(lax.ppermute(faces[at], axes[axis], pairs))
            at += 1
    return result


def read_all(ref):
    return [ref[c] for c in range(ref.shape[0])]


def faces_kernel(counts, les_hbm, wave_hbm, *refs):
    out_refs, (les_ref, wave_ref, sems) = refs[:-3], refs[-3:]
    copies = [
        pltpu.make_async_copy(les_hbm, les_ref, sems.at[0]),
        pltpu.make_async_copy(wave_hbm, wave_ref, sems.at[1]),
    ]
    for copy in copies:
        copy.start()
    for copy in copies:
        copy.wait()
    store_faces(read_all(les_ref) + read_all(wave_ref), out_refs, counts)


def rotations(count):
    reach = window if count >= window else count
    found = []
    for d in list(range(reach)) + list(range(1 - reach, 0)):
        if d % count not in found:
            found.append(d % count)
    return found


def lamb_kernel(counts, n_faces, owner_ref, slot_ref, proj_smem, proj_ref, les_ref, *refs):
    face_refs, out_refs, (counter,) = refs[:n_faces], refs[n_faces:-1], refs[-1:]
    halos = load_faces(face_refs, counts, 0, 4)

    def speeds(state):
        inverse = 1.0 / (state[0] + 1.0)
        return [state[c] * inverse for c in (1, 2, 3)]

    velocity = speeds([les_ref[c] for c in range(4)])

    def slope(c, axis):
        before, after = halos[axis]
        return 0.5 * (
            shifted(velocity[c], axis, 1, outer[axis][1][c])
            - shifted(velocity[c], axis, -1, outer[axis][0][c])
        )

    outer = [(speeds(before), speeds(after)) for before, after in halos]
    vort = [slope(2, 1) - slope(1, 2), slope(0, 2) - slope(2, 0), slope(1, 0) - slope(0, 1)]
    lamb = [
        vort[1] * velocity[2] - vort[2] * velocity[1],
        vort[2] * velocity[0] - vort[0] * velocity[2],
        vort[0] * velocity[1] - vort[1] * velocity[0],
    ]
    proj = proj_ref[...]
    blocks = []
    for field in lamb:
        along_y = proj[:, 0:1][None] * field[:, 0:1, :]
        for b in range(1, 8):
            along_y = along_y + proj[:, b : b + 1][None] * field[:, b : b + 1, :]
        for i in range(8):
            plane = proj_smem[i, 0] * along_y[0]
            for a in range(1, 8):
                plane = plane + proj_smem[i, a] * along_y[a]
            blocks.append(plane)

    turns = rotations(counts[0])
    groups = 4 * ((len(turns) + 3) // 4)
    own = lax.axis_index("gx")
    n_blocks = owner_ref.shape[-1]
    for g in range(groups):
        counter[g] = 0
    places = []
    for n in range(n_blocks):
        turn = lax.rem(owner_ref[0, 0, n] - own + counts[0], counts[0])
        group = turn if len(turns) == counts[0] else jnp.where(
            turn < window, turn, turn - (counts[0] - len(turns))
        )
        taken = counter[group]
        counter[group] = taken + 1
        places.append(group * window + taken)

    tile = tile_rows(proj, False)
    block_of_lane = lane((8, 128)) // 8
    quarter = lane((8, 128)) // 32
    for s in range(groups // 4):
        products = []
        for t in range(4):
            rows = [
                jnp.where(block_of_lane == lax.rem(place + 4 * t, 16) , tile, 0.0)
                if groups == 4
                else jnp.where(
                    (block_of_lane == lax.rem(place + 4 * t, 16)) & (place // 16 == s), tile, 0.0
                )
                for place in places
            ]
            matrix = halves(jnp.concatenate(rows, axis=0))
            data = jnp.concatenate([blocks[4 * q + t] for q in range(6)], axis=0)
            products.append(dot3(data, matrix))
        labels = jnp.full((8, 128), -1.0, f32)
        for n, place in enumerate(places):
            labels = jnp.where(
                block_of_lane == place - 16 * s, slot_ref[0, 0, n].astype(f32), labels
            )
        for r in range(4):
            if 4 * s + r >= len(turns):
                continue
            if len(turns) == counts[0]:
                out = out_refs[0].at[lax.rem(own + turns[r], counts[0])]
            else:
                out = out_refs[4 * s + r]
            for q in range(6):
                packed = products[0][8 * q : 8 * q + 8]
                for t in range(1, 4):
                    packed = jnp.where(
                        quarter == (r + t) % 4, products[t][8 * q : 8 * q + 8], packed
                    )
                out[q] = packed
            marks = labels
            for t in range(1, 4):
                marks = jnp.where(
                    quarter == (r + t) % 4, pltpu.roll(labels, 32 * t, 1), marks
                )
            out[6] = marks


def first_kernel(
    counts, n_faces, deriv_ref, high_ref, low_ref, les_ref, wave_ref, mean_ref, *refs
):
    face_refs, (section_ref, rate_ref) = refs[:n_faces], refs[n_faces:]
    state = read_all(les_ref)
    rate = les_rate(state, load_faces(face_refs, counts, 0, 5))
    for c in range(5):
        section_ref[c] = state[c] + rate[c]
    rate = acoustic_rate(
        read_all(wave_ref), read_all(mean_ref), load_faces(face_refs, counts, 5, 9),
        deriv_ref[...], (high_ref[...], low_ref[...]),
    )
    for c in range(4):
        rate_ref[c] = rate[c]


def source_kernel(counts, wave_ref, rate_ref, section_ref, *refs):
    turns = rotations(counts[0])
    n_pieces = len(turns)
    if n_pieces == counts[0]:
        own = lax.axis_index("gx")
        pieces = [refs[0].at[lax.rem(own - turn + counts[0], counts[0])] for turn in turns]
        refs = refs[1:]
    else:
        pieces, refs = refs[:n_pieces], refs[n_pieces:]
    (source_ref, middle_ref, carry_ref), face_refs = refs[:3], refs[3:]
    quarter = lane((8, 128)) // 32
    slot_of_row = sublane((128, 128)) // 8
    same_node = lax.rem(sublane((128, 128)), 8) == lax.rem(lane((128, 128)), 8)
    sums = [None] * 24
    for s in range((n_pieces + 3) // 4):
        count = min(4, n_pieces - 4 * s)

        def gathered(q, t):
            value = jnp.full((8, 128), -1.0 if q == 6 else 0.0, f32)
            for r in range(count):
                value = jnp.where(quarter == (r + t) % 4, pieces[4 * s + r][q], value)
            return value

        for t in range(4):
            marks = gathered(6, t)[0:1].astype(jnp.int32)
            chosen = ((slot_of_row == marks) & same_node).astype(f32).astype(jnp.bfloat16)
            data = jnp.concatenate([gathered(q, t) for q in range(6)], axis=0)
            high = data.astype(jnp.bfloat16)
            low = (data - high.astype(f32)).astype(jnp.bfloat16)
            dims = (((1,), (1,)), ((), ()))
            moved = lax.dot_general(high, chosen, dims, preferred_element_type=f32)
            moved = moved + lax.dot_general(low, chosen, dims, preferred_element_type=f32)
            for q in range(6):
                part = moved[8 * q : 8 * q + 8]
                k = 4 * q + t
                sums[k] = part if sums[k] is None else sums[k] + part
    source = [jnp.stack(sums[8 * c : 8 * c + 8], axis=0) for c in range(3)]
    middle = []
    for c in range(4):
        rate = rate_ref[c]
        if c:
            source_ref[c - 1] = source[c - 1]
            rate = rate + source[c - 1]
        middle.append(wave_ref[c] + acoustic_step * rate)
        middle_ref[c] = middle[c]
        carry = wave_ref[c] + middle[c]
        carry_ref[c] = carry + acoustic_step * source[c - 1] if c else carry
    store_faces(read_all(section_ref) + middle, face_refs, counts)


def last_kernel(
    counts, n_faces, deriv_ref, high_ref, low_ref, les_ref, section_ref, middle_ref, carry_ref,
    mean_ref, *refs,
):
    face_refs, (les_out, wave_out) = refs[:n_faces], refs[n_faces:]
    section = read_all(section_ref)
    rate = les_rate(section, load_faces(face_refs, counts, 0, 5))
    for c in range(5):
        les_out[c] = 0.5 * ((les_ref[c] + section[c]) + rate[c])
    middle = read_all(middle_ref)
    rate = acoustic_rate(
        middle, read_all(mean_ref), load_faces(face_refs, counts, 5, 9),
        deriv_ref[...], (high_ref[...], low_ref[...]),
    )
    for c in range(4):
        wave_out[c] = 0.5 * (carry_ref[c] + acoustic_step * rate[c])


VMEM = pl.BlockSpec(memory_space=pltpu.VMEM)
SMEM = pl.BlockSpec(memory_space=pltpu.SMEM)


def call(kernel, in_specs, out_shapes, name, cost, scratch=(), room=24):
    return pl.pallas_call(
        kernel,
        in_specs=in_specs,
        out_specs=[VMEM] * len(out_shapes),
        out_shape=out_shapes,
        scratch_shapes=list(scratch),
        name=name,
        cost_estimate=pl.CostEstimate(flops=cost, bytes_accessed=800000, transcendentals=0),
        compiler_params=pltpu.CompilerParams(vmem_limit_bytes=room * 1024 * 1024),
    )


def local(counts, les, wave, mean, projection, owner, slot):
    shape = les.shape[1:]
    faces = face_shapes(counts, 9)
    n_faces = len(faces)
    like = lambda n: jax.ShapeDtypeStruct((n,) + shape, f32)

    table = derivative_matrix()
    deriv = jnp.asarray(table, f32)
    along_z = np.kron(np.eye(16), table.T).astype(np.float32)
    high = along_z.astype(jnp.bfloat16)
    low = (along_z - high.astype(np.float32)).astype(jnp.bfloat16)
    tables = (deriv, jnp.asarray(high), jnp.asarray(low))

    sent = call(
        functools.partial(faces_kernel, counts),
        [pl.BlockSpec(memory_space=pl.ANY)] * 2,
        faces,
        "faces",
        100000,
        [pltpu.VMEM(les.shape, f32), pltpu.VMEM(wave.shape, f32), pltpu.SemaphoreType.DMA((2,))],
        56,
    )(les, wave)
    got = exchange(sent, counts)

    turns = rotations(counts[0])
    together = len(turns) == counts[0]
    piece = (7, 8, 128)
    pieces = call(
        functools.partial(lamb_kernel, counts, n_faces),
        [SMEM] * 3 + [VMEM] * (2 + n_faces),
        [jax.ShapeDtypeStruct((counts[0],) + piece, f32)]
        if together
        else [jax.ShapeDtypeStruct(piece, f32)] * len(turns),
        "lamb_blocks",
        10000000,
        [pltpu.SMEM((8,), jnp.int32)],
    )(owner, slot, projection, projection, les, *got)
    if together:
        moved = [lax.all_to_all(pieces[0], "gx", 0, 0, tiled=True)]
    else:
        moved = [
            lax.ppermute(piece, "gx", [(i, (i + turn) % counts[0]) for i in range(counts[0])])
            if turn
            else piece
            for turn, piece in zip(turns, pieces)
        ]
    section, rate = call(
        functools.partial(first_kernel, counts, n_faces),
        [VMEM] * (6 + n_faces),
        [like(5), like(4)],
        "first_rates",
        40000000,
    )(*tables, les, wave, mean, *got)

    source, middle, carry, *sent = call(
        functools.partial(source_kernel, counts),
        [VMEM] * (3 + len(moved)),
        [like(3), like(4), like(4)] + faces,
        "source_and_faces",
        10000000,
    )(wave, rate, section, *moved)
    got = exchange(sent, counts)
    les_next, wave_next = call(
        functools.partial(last_kernel, counts, n_faces),
        [VMEM] * (8 + n_faces),
        [like(5), like(4)],
        "second_rates",
        40000000,
    )(*tables, les, section, middle, carry, mean, *got)
    return les_next, source, wave_next


def solution(mesh):
    counts = tuple(mesh.shape[axis] for axis in axes)
    field = P(None, *axes)
    return jax.shard_map(
        functools.partial(local, counts),
        mesh=mesh,
        in_specs=(field, field, field, P(), P(*axes), P(*axes)),
        out_specs=(field, field, field),
        check_vma=False,
    )
```

```python
import functools

import jax
import jax.numpy as jnp
import numpy as np
from jax import lax
from jax.experimental import pallas as pl
from jax.experimental.pallas import tpu as pltpu
from jax.sharding import PartitionSpec as P

lobatto_points = np.array(
    [
        -1.0,
        -0.8717401485096066,
        -0.5917001814331423,
        -0.2092992179024789,
        0.2092992179024789,
        0.5917001814331423,
        0.8717401485096066,
        1.0,
    ]
)
flux_half = 0.08
gamma_less = 0.4
acoustic_step = 0.01
upwind_speed = 1.5
face_lift = 28.0
free_stream = (1.0, 0.0, 0.0, 0.0, 2.5)
axes = ("gx", "gy", "gz")
window = 4
f32 = jnp.float32


def derivative_matrix():
    points = lobatto_points
    products = [np.prod([points[i] - points[j] for j in range(8) if j != i]) for i in range(8)]
    matrix = np.zeros((8, 8))
    for i in range(8):
        for j in range(8):
            if j != i:
                matrix[i, j] = products[i] / (products[j] * (points[i] - points[j]))
        matrix[i, i] = -np.sum(matrix[i])
    return matrix


def sublane(shape):
    return lax.broadcasted_iota(jnp.int32, shape, len(shape) - 2)


def lane(shape):
    return lax.broadcasted_iota(jnp.int32, shape, len(shape) - 1)


def shifted(field, axis, step, outer):
    if axis == 0:
        if step == 1:
            return jnp.concatenate([field[1:], outer[None]], axis=0)
        return jnp.concatenate([outer[None], field[:-1]], axis=0)
    count = field.shape[axis]
    moved = pltpu.roll(field, count - 1 if step == 1 else 1, axis)
    edge = count - 1 if step == 1 else 0
    if axis == 1:
        return jnp.where(sublane(field.shape) == edge, outer[:, None, :], moved)
    columns = jnp.stack([outer[:, x : x + 1] for x in range(8)], axis=0)
    return jnp.where(lane(field.shape) == edge, columns, moved)


def fluid(state):
    density, mx, my, mz, energy = [s + r for s, r in zip(state, free_stream)]
    inverse = 1.0 / density
    momentum = (mx, my, mz)
    velocity = [m * inverse for m in momentum]
    pressure = gamma_less * (
        energy - 0.5 * (mx * velocity[0] + my * velocity[1] + mz * velocity[2])
    )
    return momentum, velocity, pressure, energy + pressure


def split_flux(state, parts, axis, sign):
    momentum, velocity, pressure, enthalpy = parts
    speed = velocity[axis]
    flux = [momentum[axis]]
    for c in range(3):
        term = momentum[c] * speed
        flux.append(term + pressure if c == axis else term)
    flux.append(enthalpy * speed)
    if sign > 0:
        return [flux_half * (s + f) for s, f in zip(state, flux)]
    return [flux_half * (s - f) for s, f in zip(state, flux)]


def les_rate(state, halos):
    parts = fluid(state)
    total = [-6.0 * flux_half * s for s in state]
    for axis in range(3):
        before, after = halos[axis]
        ahead = split_flux(state, parts, axis, -1)
        behind = split_flux(state, parts, axis, 1)
        ahead_outer = split_flux(after, fluid(after), axis, -1)
        behind_outer = split_flux(before, fluid(before), axis, 1)
        for c in range(5):
            total[c] = total[c] + (
                shifted(ahead[c], axis, 1, ahead_outer[c])
                + shifted(behind[c], axis, -1, behind_outer[c])
            )
    return total


def wave_flux(state, mean, axis):
    speed = mean[axis]
    pressure = state[0]
    rows = [speed * pressure + state[1 + axis]]
    for c in range(3):
        term = speed * state[1 + c]
        rows.append(term + pressure if c == axis else term)
    return rows


def dot3(left, right):
    high = left.astype(jnp.bfloat16)
    low = (left - high.astype(f32)).astype(jnp.bfloat16)
    dot = functools.partial(jnp.dot, preferred_element_type=f32)
    return dot(high, right[0]) + (dot(low, right[0]) + dot(high, right[1]))


def halves(matrix):
    high = matrix.astype(jnp.bfloat16)
    return high, (matrix - high.astype(f32)).astype(jnp.bfloat16)


def acoustic_rate(state, mean, halos, deriv, along_z):
    shape = state[0].shape
    table = derivative_matrix()
    flux = wave_flux(state, mean, 0)
    before, after = halos[0]
    low_mean, high_mean = [m[0] for m in mean], [m[7] for m in mean]
    low_jump = [b - s[0] for b, s in zip(before, state)]
    high_jump = [a - s[7] for a, s in zip(after, state)]
    low_flux = wave_flux(low_jump, low_mean, 0)
    high_flux = wave_flux(high_jump, high_mean, 0)
    half, lift = 0.5 * face_lift, 0.5 * face_lift * upwind_speed
    total = []
    for c in range(4):
        planes = []
        for i in range(8):
            plane = -float(table[i, 0]) * flux[c][0]
            for a in range(1, 8):
                if abs(table[i, a]) > 1e-12:
                    plane = plane - float(table[i, a]) * flux[c][a]
            if i == 0:
                plane = plane + (half * low_flux[c] + lift * low_jump[c])
            if i == 7:
                plane = plane - (half * high_flux[c] - lift * high_jump[c])
            planes.append(plane)
        total.append(jnp.stack(planes, axis=0))
    flux = wave_flux(state, mean, 1)
    before, after = halos[1]
    row = sublane(shape)
    sign = jnp.where(row == 0, half, jnp.where(row == 7, -half, 0.0))
    jump = [
        jnp.where(row == 0, b[:, None, :], jnp.where(row == 7, a[:, None, :], s)) - s
        for s, b, a in zip(state, before, after)
    ]
    jump_flux = wave_flux(jump, mean, 1)
    for c in range(4):
        change = lift * jump[c] + sign * jump_flux[c]
        for b in range(8):
            change = change - deriv[:, b : b + 1][None] * flux[c][:, b : b + 1, :]
        total[c] = total[c] + change
    flux = wave_flux(state, mean, 2)
    before, after = halos[2]
    column = lane(shape)
    place = lax.rem(column, 8)
    sign = jnp.where(place == 0, half, jnp.where(place == 7, -half, 0.0))
    jump = [
        jnp.where(
            place == 0,
            shifted(s, 2, -1, b),
            jnp.where(place == 7, shifted(s, 2, 1, a), s),
        )
        - s
        for s, b, a in zip(state, before, after)
    ]
    jump_flux = wave_flux(jump, mean, 2)
    for c in range(4):
        slope = dot3(flux[c].reshape(64, 128), along_z).reshape(shape)
        total[c] = total[c] + (lift * jump[c] + sign * jump_flux[c] - slope)
    return total


def tile_rows(matrix, transposed):
    spread = (lax.rem(lane((8, 128)), 8) == sublane((8, 128))).astype(f32)
    contract = ((1,), (0,)) if transposed else ((0,), (0,))
    return lax.dot_general(
        matrix, spread, (contract, ((), ())),
        precision=lax.Precision.HIGHEST, preferred_element_type=f32,
    )


def block_diagonal(tile):
    rows = [jnp.where(lane((8, 128)) // 8 == n, tile, 0.0) for n in range(16)]
    return halves(jnp.concatenate(rows, axis=0))


def pairings(count):
    sets = []
    for first in (0, 1):
        pairs = [(i, i + 1) for i in range(first, count - 1, 2)]
        if pairs:
            joined = [p for i, j in pairs for p in ((i, j), (j, i))]
            alone = set(range(count)) - {i for i, _ in joined}
            sets.append(joined + [(i, i) for i in sorted(alone)])
    return sets


def pack_z(fields, at):
    packed = jnp.zeros((8, 128), f32)
    column = lane((8, 128))
    for c, field in enumerate(fields):
        for x in range(8):
            packed = jnp.where(column == c * 8 + x, field[x][:, at : at + 1], packed)
    return packed


def store_faces(fields, out_refs, counts, which=(0, 1, 2)):
    at = 0
    for axis in which:
        even = lax.rem(lax.axis_index(axes[axis]), 2) == 0
        sets = len(pairings(counts[axis]))
        if axis == 2:
            low, high = pack_z(fields, 0), pack_z(fields, 127)
            for s in range(sets):
                out_refs[at + s][...] = jnp.where(even == (s == 0), high, low)
        else:
            for c, field in enumerate(fields):
                low = field[0] if axis == 0 else field[:, 0, :]
                high = field[7] if axis == 0 else field[:, 7, :]
                for s in range(sets):
                    out_refs[at + s][c] = jnp.where(even == (s == 0), high, low)
        at += sets


def load_faces(in_refs, counts, first, last):
    halos = []
    at = 0
    for axis in range(3):
        even = lax.rem(lax.axis_index(axes[axis]), 2) == 0
        sets = len(pairings(counts[axis]))
        got = []
        for s in range(sets):
            if axis == 2:
                packed = in_refs[at + s][...]
                got.append(
                    [
                        pltpu.roll(packed, (128 - 8 * c) % 128, 1) if c else packed
                        for c in range(first, last)
                    ]
                )
            else:
                got.append([in_refs[at + s][c] for c in range(first, last)])
        while len(got) < 2:
            got.append([jnp.zeros((8, 128), f32)] * (last - first))
        place = lax.axis_index(axes[axis])
        before = [
            jnp.where(place == 0, 0.0, jnp.where(even, b, a)) for a, b in zip(*got)
        ]
        after = [
            jnp.where(place == counts[axis] - 1, 0.0, jnp.where(even, a, b))
            for a, b in zip(*got)
        ]
        halos.append((before, after))
        at += sets
    return halos


def face_shapes(counts, width):
    shapes = []
    for axis in range(3):
        shape = (8, 128) if axis == 2 else (width, 8, 128)
        shapes += [jax.ShapeDtypeStruct(shape, f32)] * len(pairings(counts[axis]))
    return shapes


def exchange(faces, counts):
    result = []
    at = 0
    for axis in range(3):
        for pairs in pairings(counts[axis]):
            result.append(lax.ppermute(faces[at], axes[axis], pairs))
            at += 1
    return result


def read_all(ref):
    return [ref[c] for c in range(ref.shape[0])]


def x_faces_kernel(counts, les_hbm, wave_hbm, *refs):
    out_refs, sems = refs[:-1], refs[-1]
    odd = lax.rem(lax.axis_index("gx"), 2)
    copies = []
    for s, out in enumerate(out_refs):
        plane = 7 * (1 - odd) if s == 0 else 7 * odd
        for k, (first, source) in enumerate(((0, les_hbm), (5, wave_hbm))):
            copies.append(
                pltpu.make_async_copy(
                    source.at[:, plane], out.at[first : first + source.shape[0]], sems.at[s, k]
                )
            )
    for copy in copies:
        copy.start()
    for copy in copies:
        copy.wait()


def faces_kernel(counts, les_ref, wave_ref, *out_refs):
    store_faces(read_all(les_ref) + read_all(wave_ref), out_refs, counts, (1, 2))


def rotations(count):
    reach = window if count >= window else count
    found = []
    for d in list(range(reach)) + list(range(1 - reach, 0)):
        if d % count not in found:
            found.append(d % count)
    return found


def lamb_kernel(counts, n_faces, owner_ref, slot_ref, proj_smem, proj_ref, les_ref, *refs):
    face_refs, out_refs, (counter,) = refs[:n_faces], refs[n_faces:-1], refs[-1:]
    halos = load_faces(face_refs, counts, 0, 4)

    def speeds(state):
        inverse = 1.0 / (state[0] + 1.0)
        return [state[c] * inverse for c in (1, 2, 3)]

    velocity = speeds([les_ref[c] for c in range(4)])

    def slope(c, axis):
        before, after = halos[axis]
        return 0.5 * (
            shifted(velocity[c], axis, 1, outer[axis][1][c])
            - shifted(velocity[c], axis, -1, outer[axis][0][c])
        )

    outer = [(speeds(before), speeds(after)) for before, after in halos]
    vort = [slope(2, 1) - slope(1, 2), slope(0, 2) - slope(2, 0), slope(1, 0) - slope(0, 1)]
    lamb = [
        vort[1] * velocity[2] - vort[2] * velocity[1],
        vort[2] * velocity[0] - vort[0] * velocity[2],
        vort[0] * velocity[1] - vort[1] * velocity[0],
    ]
    proj = proj_ref[...]
    blocks = []
    for field in lamb:
        along_y = proj[:, 0:1][None] * field[:, 0:1, :]
        for b in range(1, 8):
            along_y = along_y + proj[:, b : b + 1][None] * field[:, b : b + 1, :]
        for i in range(8):
            plane = proj_smem[i, 0] * along_y[0]
            for a in range(1, 8):
                plane = plane + proj_smem[i, a] * along_y[a]
            blocks.append(plane)

    turns = rotations(counts[0])
    groups = 4 * ((len(turns) + 3) // 4)
    own = lax.axis_index("gx")
    n_blocks = owner_ref.shape[-1]
    for g in range(groups):
        counter[g] = 0
    places = []
    for n in range(n_blocks):
        turn = lax.rem(owner_ref[0, 0, n] - own + counts[0], counts[0])
        group = turn if len(turns) == counts[0] else jnp.where(
            turn < window, turn, turn - (counts[0] - len(turns))
        )
        taken = counter[group]
        counter[group] = taken + 1
        places.append(group * window + taken)

    tile = tile_rows(proj, False)
    block_of_lane = lane((8, 128)) // 8
    quarter = lane((8, 128)) // 32
    for s in range(groups // 4):
        products = []
        for t in range(4):
            rows = [
                jnp.where(block_of_lane == lax.rem(place + 4 * t, 16) , tile, 0.0)
                if groups == 4
                else jnp.where(
                    (block_of_lane == lax.rem(place + 4 * t, 16)) & (place // 16 == s), tile, 0.0
                )
                for place in places
            ]
            matrix = halves(jnp.concatenate(rows, axis=0))
            data = jnp.concatenate([blocks[4 * q + t] for q in range(6)], axis=0)
            products.append(dot3(data, matrix))
        labels = jnp.full((8, 128), -1.0, f32)
        for n, place in enumerate(places):
            labels = jnp.where(
                block_of_lane == place - 16 * s, slot_ref[0, 0, n].astype(f32), labels
            )
        for r in range(4):
            if 4 * s + r >= len(turns):
                continue
            out = out_refs[4 * s + r]
            for q in range(6):
                packed = products[0][8 * q : 8 * q + 8]
                for t in range(1, 4):
                    packed = jnp.where(
                        quarter == (r + t) % 4, products[t][8 * q : 8 * q + 8], packed
                    )
                out[q] = packed
            marks = labels
            for t in range(1, 4):
                marks = jnp.where(
                    quarter == (r + t) % 4, pltpu.roll(labels, 32 * t, 1), marks
                )
            out[6] = marks


def first_kernel(
    counts, n_faces, deriv_ref, high_ref, low_ref, les_ref, wave_ref, mean_ref, *refs
):
    face_refs, (section_ref, rate_ref) = refs[:n_faces], refs[n_faces:]
    state = read_all(les_ref)
    rate = les_rate(state, load_faces(face_refs, counts, 0, 5))
    for c in range(5):
        section_ref[c] = state[c] + rate[c]
    rate = acoustic_rate(
        read_all(wave_ref), read_all(mean_ref), load_faces(face_refs, counts, 5, 9),
        deriv_ref[...], (high_ref[...], low_ref[...]),
    )
    for c in range(4):
        rate_ref[c] = rate[c]


def source_kernel(counts, wave_ref, rate_ref, section_ref, *refs):
    n_pieces = len(rotations(counts[0]))
    pieces, refs = refs[:n_pieces], refs[n_pieces:]
    (source_ref, middle_ref, carry_ref), face_refs = refs[:3], refs[3:]
    quarter = lane((8, 128)) // 32
    slot_of_row = sublane((128, 128)) // 8
    same_node = lax.rem(sublane((128, 128)), 8) == lax.rem(lane((128, 128)), 8)
    sums = [None] * 24
    for s in range((n_pieces + 3) // 4):
        count = min(4, n_pieces - 4 * s)

        def gathered(q, t):
            value = jnp.full((8, 128), -1.0 if q == 6 else 0.0, f32)
            for r in range(count):
                value = jnp.where(quarter == (r + t) % 4, pieces[4 * s + r][q], value)
            return value

        for t in range(4):
            marks = gathered(6, t)[0:1].astype(jnp.int32)
            chosen = ((slot_of_row == marks) & same_node).astype(f32).astype(jnp.bfloat16)
            data = jnp.concatenate([gathered(q, t) for q in range(6)], axis=0)
            high = data.astype(jnp.bfloat16)
            low = (data - high.astype(f32)).astype(jnp.bfloat16)
            dims = (((1,), (1,)), ((), ()))
            moved = lax.dot_general(high, chosen, dims, preferred_element_type=f32)
            moved = moved + lax.dot_general(low, chosen, dims, preferred_element_type=f32)
            for q in range(6):
                part = moved[8 * q : 8 * q + 8]
                k = 4 * q + t
                sums[k] = part if sums[k] is None else sums[k] + part
    source = [jnp.stack(sums[8 * c : 8 * c + 8], axis=0) for c in range(3)]
    middle = []
    for c in range(4):
        rate = rate_ref[c]
        if c:
            source_ref[c - 1] = source[c - 1]
            rate = rate + source[c - 1]
        middle.append(wave_ref[c] + acoustic_step * rate)
        middle_ref[c] = middle[c]
        carry = wave_ref[c] + middle[c]
        carry_ref[c] = carry + acoustic_step * source[c - 1] if c else carry
    store_faces(read_all(section_ref) + middle, face_refs, counts)


def last_kernel(
    counts, n_faces, deriv_ref, high_ref, low_ref, les_ref, section_ref, middle_ref, carry_ref,
    mean_ref, *refs,
):
    face_refs, (les_out, wave_out) = refs[:n_faces], refs[n_faces:]
    section = read_all(section_ref)
    rate = les_rate(section, load_faces(face_refs, counts, 0, 5))
    for c in range(5):
        les_out[c] = 0.5 * ((les_ref[c] + section[c]) + rate[c])
    middle = read_all(middle_ref)
    rate = acoustic_rate(
        middle, read_all(mean_ref), load_faces(face_refs, counts, 5, 9),
        deriv_ref[...], (high_ref[...], low_ref[...]),
    )
    for c in range(4):
        wave_out[c] = 0.5 * (carry_ref[c] + acoustic_step * rate[c])


VMEM = pl.BlockSpec(memory_space=pltpu.VMEM)
SMEM = pl.BlockSpec(memory_space=pltpu.SMEM)


def call(kernel, in_specs, out_shapes, name, cost, scratch=(), room=24):
    return pl.pallas_call(
        kernel,
        in_specs=in_specs,
        out_specs=[VMEM] * len(out_shapes),
        out_shape=out_shapes,
        scratch_shapes=list(scratch),
        name=name,
        cost_estimate=pl.CostEstimate(flops=cost, bytes_accessed=800000, transcendentals=0),
        compiler_params=pltpu.CompilerParams(vmem_limit_bytes=room * 1024 * 1024),
    )


def local(counts, les, wave, mean, projection, owner, slot):
    shape = les.shape[1:]
    faces = face_shapes(counts, 9)
    n_faces = len(faces)
    like = lambda n: jax.ShapeDtypeStruct((n,) + shape, f32)

    table = derivative_matrix()
    deriv = jnp.asarray(table, f32)
    along_z = np.kron(np.eye(16), table.T).astype(np.float32)
    high = along_z.astype(jnp.bfloat16)
    low = (along_z - high.astype(np.float32)).astype(jnp.bfloat16)
    tables = (deriv, jnp.asarray(high), jnp.asarray(low))

    x_sets = len(pairings(counts[0]))
    sent = call(
        functools.partial(x_faces_kernel, counts),
        [pl.BlockSpec(memory_space=pl.ANY)] * 2,
        faces[:x_sets],
        "x_faces",
        10000,
        [pltpu.SemaphoreType.DMA((x_sets, 2))],
        56,
    )(les, wave)
    sent += call(
        functools.partial(faces_kernel, counts), [VMEM] * 2, faces[x_sets:], "faces", 100000
    )(les, wave)
    got = exchange(sent, counts)

    turns = rotations(counts[0])
    pieces = call(
        functools.partial(lamb_kernel, counts, n_faces),
        [SMEM] * 3 + [VMEM] * (2 + n_faces),
        [jax.ShapeDtypeStruct((7, 8, 128), f32)] * len(turns),
        "lamb_blocks",
        10000000,
        [pltpu.SMEM((8,), jnp.int32)],
    )(owner, slot, projection, projection, les, *got)
    moved = [
        lax.ppermute(piece, "gx", [(i, (i + turn) % counts[0]) for i in range(counts[0])])
        if turn
        else piece
        for turn, piece in zip(turns, pieces)
    ]
    section, rate = call(
        functools.partial(first_kernel, counts, n_faces),
        [VMEM] * (6 + n_faces),
        [like(5), like(4)],
        "first_rates",
        40000000,
    )(*tables, les, wave, mean, *got)

    source, middle, carry, *sent = call(
        functools.partial(source_kernel, counts),
        [VMEM] * (3 + len(moved)),
        [like(3), like(4), like(4)] + faces,
        "source_and_faces",
        10000000,
    )(wave, rate, section, *moved)
    got = exchange(sent, counts)
    les_next, wave_next = call(
        functools.partial(last_kernel, counts, n_faces),
        [VMEM] * (8 + n_faces),
        [like(5), like(4)],
        "second_rates",
        40000000,
    )(*tables, les, section, middle, carry, mean, *got)
    return les_next, source, wave_next


def solution(mesh):
    counts = tuple(mesh.shape[axis] for axis in axes)
    field = P(None, *axes)
    return jax.shard_map(
        functools.partial(local, counts),
        mesh=mesh,
        in_specs=(field, field, field, P(), P(*axes), P(*axes)),
        out_specs=(field, field, field),
        check_vma=False,
    )
```

```python
import functools

import jax
import jax.numpy as jnp
import numpy as np
from jax import lax
from jax.experimental import pallas as pl
from jax.experimental.pallas import tpu as pltpu
from jax.sharding import PartitionSpec as P

lobatto_points = np.array(
    [
        -1.0,
        -0.8717401485096066,
        -0.5917001814331423,
        -0.2092992179024789,
        0.2092992179024789,
        0.5917001814331423,
        0.8717401485096066,
        1.0,
    ]
)
flux_half = 0.08
gamma_less = 0.4
acoustic_step = 0.01
upwind_speed = 1.5
face_lift = 28.0
free_stream = (1.0, 0.0, 0.0, 0.0, 2.5)
axes = ("gx", "gy", "gz")
window = 4
f32 = jnp.float32


def derivative_matrix():
    points = lobatto_points
    products = [np.prod([points[i] - points[j] for j in range(8) if j != i]) for i in range(8)]
    matrix = np.zeros((8, 8))
    for i in range(8):
        for j in range(8):
            if j != i:
                matrix[i, j] = products[i] / (products[j] * (points[i] - points[j]))
        matrix[i, i] = -np.sum(matrix[i])
    return matrix


def sublane(shape):
    return lax.broadcasted_iota(jnp.int32, shape, len(shape) - 2)


def lane(shape):
    return lax.broadcasted_iota(jnp.int32, shape, len(shape) - 1)


def shifted(field, axis, step, outer):
    if axis == 0:
        if step == 1:
            return jnp.concatenate([field[1:], outer[None]], axis=0)
        return jnp.concatenate([outer[None], field[:-1]], axis=0)
    count = field.shape[axis]
    moved = pltpu.roll(field, count - 1 if step == 1 else 1, axis)
    edge = count - 1 if step == 1 else 0
    if axis == 1:
        return jnp.where(sublane(field.shape) == edge, outer[:, None, :], moved)
    columns = jnp.stack([outer[:, x : x + 1] for x in range(8)], axis=0)
    return jnp.where(lane(field.shape) == edge, columns, moved)


def fluid(state):
    density, mx, my, mz, energy = [s + r for s, r in zip(state, free_stream)]
    inverse = 1.0 / density
    momentum = (mx, my, mz)
    velocity = [m * inverse for m in momentum]
    pressure = gamma_less * (
        energy - 0.5 * (mx * velocity[0] + my * velocity[1] + mz * velocity[2])
    )
    return momentum, velocity, pressure, energy + pressure


def split_flux(state, parts, axis, sign):
    momentum, velocity, pressure, enthalpy = parts
    speed = velocity[axis]
    flux = [momentum[axis]]
    for c in range(3):
        term = momentum[c] * speed
        flux.append(term + pressure if c == axis else term)
    flux.append(enthalpy * speed)
    if sign > 0:
        return [flux_half * (s + f) for s, f in zip(state, flux)]
    return [flux_half * (s - f) for s, f in zip(state, flux)]


def les_rate(state, halos):
    parts = fluid(state)
    total = [-6.0 * flux_half * s for s in state]
    nothing = jnp.zeros((8, 128), f32)
    for axis in range(3):
        ahead = split_flux(state, parts, axis, -1)
        behind = split_flux(state, parts, axis, 1)
        ahead_outer = behind_outer = [nothing] * 5
        if halos is not None:
            before, after = halos[axis]
            ahead_outer = split_flux(after, fluid(after), axis, -1)
            behind_outer = split_flux(before, fluid(before), axis, 1)
        for c in range(5):
            total[c] = total[c] + (
                shifted(ahead[c], axis, 1, ahead_outer[c])
                + shifted(behind[c], axis, -1, behind_outer[c])
            )
    return total


def les_outer(halos):
    return [
        (
            split_flux(before, fluid(before), axis, 1),
            split_flux(after, fluid(after), axis, -1),
        )
        for axis, (before, after) in enumerate(halos)
    ]


def with_layers(field, layers):
    (x0, x1), (y0, y1), (z0, z1) = layers
    row, column = sublane((8, 128)), lane((8, 128))
    planes = []
    for x in range(8):
        plane = field[x]
        if x == 0:
            plane = plane + x0
        if x == 7:
            plane = plane + x1
        plane = plane + jnp.where(
            row == 0, y0[x : x + 1], jnp.where(row == 7, y1[x : x + 1], 0.0)
        )
        plane = plane + jnp.where(
            column == 0, z0[:, x : x + 1], jnp.where(column == 127, z1[:, x : x + 1], 0.0)
        )
        planes.append(plane)
    return planes


def wave_flux(state, mean, axis):
    speed = mean[axis]
    pressure = state[0]
    rows = [speed * pressure + state[1 + axis]]
    for c in range(3):
        term = speed * state[1 + c]
        rows.append(term + pressure if c == axis else term)
    return rows


def dot3(left, right):
    high = left.astype(jnp.bfloat16)
    low = (left - high.astype(f32)).astype(jnp.bfloat16)
    dot = functools.partial(jnp.dot, preferred_element_type=f32)
    return dot(high, right[0]) + (dot(low, right[0]) + dot(high, right[1]))


def halves(matrix):
    high = matrix.astype(jnp.bfloat16)
    return high, (matrix - high.astype(f32)).astype(jnp.bfloat16)


def acoustic_rate(state, mean, halos, deriv, along_z):
    shape = state[0].shape
    table = derivative_matrix()
    flux = wave_flux(state, mean, 0)
    if halos is None:
        halos = [([jnp.zeros((8, 128), f32)] * 4,) * 2] * 3
    before, after = halos[0]
    low_mean, high_mean = [m[0] for m in mean], [m[7] for m in mean]
    low_jump = [b - s[0] for b, s in zip(before, state)]
    high_jump = [a - s[7] for a, s in zip(after, state)]
    low_flux = wave_flux(low_jump, low_mean, 0)
    high_flux = wave_flux(high_jump, high_mean, 0)
    half, lift = 0.5 * face_lift, 0.5 * face_lift * upwind_speed
    total = []
    for c in range(4):
        planes = []
        for i in range(8):
            plane = -float(table[i, 0]) * flux[c][0]
            for a in range(1, 8):
                if abs(table[i, a]) > 1e-12:
                    plane = plane - float(table[i, a]) * flux[c][a]
            if i == 0:
                plane = plane + (half * low_flux[c] + lift * low_jump[c])
            if i == 7:
                plane = plane - (half * high_flux[c] - lift * high_jump[c])
            planes.append(plane)
        total.append(jnp.stack(planes, axis=0))
    flux = wave_flux(state, mean, 1)
    before, after = halos[1]
    row = sublane(shape)
    sign = jnp.where(row == 0, half, jnp.where(row == 7, -half, 0.0))
    jump = [
        jnp.where(row == 0, b[:, None, :], jnp.where(row == 7, a[:, None, :], s)) - s
        for s, b, a in zip(state, before, after)
    ]
    jump_flux = wave_flux(jump, mean, 1)
    for c in range(4):
        change = lift * jump[c] + sign * jump_flux[c]
        for b in range(8):
            change = change - deriv[:, b : b + 1][None] * flux[c][:, b : b + 1, :]
        total[c] = total[c] + change
    flux = wave_flux(state, mean, 2)
    before, after = halos[2]
    column = lane(shape)
    place = lax.rem(column, 8)
    sign = jnp.where(place == 0, half, jnp.where(place == 7, -half, 0.0))
    jump = [
        jnp.where(
            place == 0,
            shifted(s, 2, -1, b),
            jnp.where(place == 7, shifted(s, 2, 1, a), s),
        )
        - s
        for s, b, a in zip(state, before, after)
    ]
    jump_flux = wave_flux(jump, mean, 2)
    for c in range(4):
        slope = dot3(flux[c].reshape(64, 128), along_z).reshape(shape)
        total[c] = total[c] + (lift * jump[c] + sign * jump_flux[c] - slope)
    return total


def acoustic_outer(mean, halos):
    half, lift = 0.5 * face_lift, 0.5 * face_lift * upwind_speed
    layers = []
    column = lane((8, 128))
    for axis, (before, after) in enumerate(halos):
        if axis == 0:
            low, high = [m[0] for m in mean], [m[7] for m in mean]
        elif axis == 1:
            low, high = [m[:, 0, :] for m in mean], [m[:, 7, :] for m in mean]
        else:
            low, high = [], []
            for m in mean:
                first = last = jnp.zeros((8, 128), f32)
                for x in range(8):
                    first = jnp.where(column == x, m[x][:, 0:1], first)
                    last = jnp.where(column == x, m[x][:, 127:128], last)
                low.append(first)
                high.append(last)
        low_flux = wave_flux(before, low, axis)
        high_flux = wave_flux(after, high, axis)
        layers.append(
            (
                [half * f + lift * b for f, b in zip(low_flux, before)],
                [lift * a - half * f for f, a in zip(high_flux, after)],
            )
        )
    return layers


def tile_rows(matrix, transposed):
    spread = (lax.rem(lane((8, 128)), 8) == sublane((8, 128))).astype(f32)
    contract = ((1,), (0,)) if transposed else ((0,), (0,))
    return lax.dot_general(
        matrix, spread, (contract, ((), ())),
        precision=lax.Precision.HIGHEST, preferred_element_type=f32,
    )


def block_diagonal(tile):
    rows = [jnp.where(lane((8, 128)) // 8 == n, tile, 0.0) for n in range(16)]
    return halves(jnp.concatenate(rows, axis=0))


def pairings(count):
    sets = []
    for first in (0, 1):
        pairs = [(i, i + 1) for i in range(first, count - 1, 2)]
        if pairs:
            joined = [p for i, j in pairs for p in ((i, j), (j, i))]
            alone = set(range(count)) - {i for i, _ in joined}
            sets.append(joined + [(i, i) for i in sorted(alone)])
    return sets


def pack_z(fields, at):
    packed = jnp.zeros((8, 128), f32)
    column = lane((8, 128))
    for c, field in enumerate(fields):
        for x in range(8):
            packed = jnp.where(column == c * 8 + x, field[x][:, at : at + 1], packed)
    return packed


def store_faces(fields, out_refs, counts, which=(0, 1, 2)):
    at = 0
    for axis in which:
        even = lax.rem(lax.axis_index(axes[axis]), 2) == 0
        sets = len(pairings(counts[axis]))
        if axis == 2:
            low, high = pack_z(fields, 0), pack_z(fields, 127)
            for s in range(sets):
                out_refs[at + s][...] = jnp.where(even == (s == 0), high, low)
        else:
            for c, field in enumerate(fields):
                low = field[0] if axis == 0 else field[:, 0, :]
                high = field[7] if axis == 0 else field[:, 7, :]
                for s in range(sets):
                    out_refs[at + s][c] = jnp.where(even == (s == 0), high, low)
        at += sets


def load_faces(in_refs, counts, first, last):
    halos = []
    at = 0
    for axis in range(3):
        even = lax.rem(lax.axis_index(axes[axis]), 2) == 0
        sets = len(pairings(counts[axis]))
        got = []
        for s in range(sets):
            if axis == 2:
                packed = in_refs[at + s][...]
                got.append(
                    [
                        pltpu.roll(packed, (128 - 8 * c) % 128, 1) if c else packed
                        for c in range(first, last)
                    ]
                )
            else:
                got.append([in_refs[at + s][c] for c in range(first, last)])
        while len(got) < 2:
            got.append([jnp.zeros((8, 128), f32)] * (last - first))
        place = lax.axis_index(axes[axis])
        before = [
            jnp.where(place == 0, 0.0, jnp.where(even, b, a)) for a, b in zip(*got)
        ]
        after = [
            jnp.where(place == counts[axis] - 1, 0.0, jnp.where(even, a, b))
            for a, b in zip(*got)
        ]
        halos.append((before, after))
        at += sets
    return halos


def face_shapes(counts, width):
    shapes = []
    for axis in range(3):
        shape = (8, 128) if axis == 2 else (width, 8, 128)
        shapes += [jax.ShapeDtypeStruct(shape, f32)] * len(pairings(counts[axis]))
    return shapes


def exchange(faces, counts):
    where = [(axis, s) for axis in range(3) for s in range(len(pairings(counts[axis])))]
    result = [None] * len(where)
    order = [(0, 1), (1, 1), (2, 1), (2, 0), (1, 0), (0, 0)]
    for axis, s in order:
        if (axis, s) in where:
            at = where.index((axis, s))
            result[at] = lax.ppermute(faces[at], axes[axis], pairings(counts[axis])[s])
    return result


def read_all(ref):
    return [ref[c] for c in range(ref.shape[0])]


def x_faces_kernel(counts, les_hbm, wave_hbm, *refs):
    out_refs, sems = refs[:-1], refs[-1]
    odd = lax.rem(lax.axis_index("gx"), 2)
    copies = []
    for s, out in enumerate(out_refs):
        plane = 7 * (1 - odd) if s == 0 else 7 * odd
        for k, (first, source) in enumerate(((0, les_hbm), (5, wave_hbm))):
            copies.append(
                pltpu.make_async_copy(
                    source.at[:, plane], out.at[first : first + source.shape[0]], sems.at[s, k]
                )
            )
    for copy in copies:
        copy.start()
    for copy in copies:
        copy.wait()


def faces_kernel(counts, les_ref, wave_ref, *out_refs):
    store_faces(read_all(les_ref) + read_all(wave_ref), out_refs, counts, (1, 2))


def partners(count):
    if count == window:
        return [[(i, i ^ mask) for i in range(count)] for mask in range(count)]
    turns = sorted({d % count for d in range(1 - window, window)})
    return [[(i, (i + turn) % count) for i in range(count)] for turn in turns]


def plan_kernel(counts, owner_ref, slot_ref, proj_ref, high_ref, low_ref, marks_ref, counter):
    count = counts[0]
    n_sets = len(partners(count))
    groups = 4 * ((n_sets + 3) // 4)
    own = lax.axis_index("gx")
    for g in range(groups):
        counter[g] = 0
    places = []
    for n in range(owner_ref.shape[-1]):
        if count == window:
            group = lax.bitwise_xor(owner_ref[0, 0, n], own)
        else:
            turn = lax.rem(owner_ref[0, 0, n] - own + count, count)
            group = turn if n_sets == count else jnp.where(
                turn < window, turn, turn - (count - n_sets)
            )
        taken = counter[group]
        counter[group] = taken + 1
        places.append(group * window + taken)
    tile = tile_rows(proj_ref[...], False)
    tile_high = tile.astype(jnp.bfloat16).astype(f32)
    tile_low = tile - tile_high
    block_of_lane = lane((8, 128)) // 8
    quarter = lane((8, 128)) // 32
    for s in range(groups // 4):
        labels = jnp.full((8, 128), -1.0, f32)
        for n, place in enumerate(places):
            labels = jnp.where(
                block_of_lane == place - 16 * s, slot_ref[0, 0, n].astype(f32), labels
            )
        for t in range(4):
            chosen = []
            for place in places:
                here = block_of_lane == lax.rem(place + 4 * t, 16)
                chosen.append(here if groups == 4 else here & (place // 16 == s))
            for ref, part in ((high_ref, tile_high), (low_ref, tile_low)):
                rows = [jnp.where(here, part, 0.0) for here in chosen]
                ref[4 * s + t] = jnp.concatenate(rows, axis=0).astype(jnp.bfloat16)
        for r in range(min(4, n_sets - 4 * s)):
            marks = labels
            for t in range(1, 4):
                marks = jnp.where(quarter == (r + t) % 4, pltpu.roll(labels, 32 * t, 1), marks)
            marks_ref[4 * s + r] = marks


def lamb_kernel(counts, n_faces, proj_smem, proj_ref, high_ref, low_ref, marks_ref, les_ref, *refs):
    face_refs, out_refs = refs[:n_faces], refs[n_faces:]
    halos = load_faces(face_refs, counts, 0, 4)

    def speeds(state):
        inverse = 1.0 / (state[0] + 1.0)
        return [state[c] * inverse for c in (1, 2, 3)]

    velocity = speeds([les_ref[c] for c in range(4)])
    outer = [(speeds(before), speeds(after)) for before, after in halos]

    def slope(c, axis):
        return 0.5 * (
            shifted(velocity[c], axis, 1, outer[axis][1][c])
            - shifted(velocity[c], axis, -1, outer[axis][0][c])
        )

    vort = [slope(2, 1) - slope(1, 2), slope(0, 2) - slope(2, 0), slope(1, 0) - slope(0, 1)]
    lamb = [
        vort[1] * velocity[2] - vort[2] * velocity[1],
        vort[2] * velocity[0] - vort[0] * velocity[2],
        vort[0] * velocity[1] - vort[1] * velocity[0],
    ]
    proj = proj_ref[...]
    blocks = []
    for field in lamb:
        along_y = proj[:, 0:1][None] * field[:, 0:1, :]
        for b in range(1, 8):
            along_y = along_y + proj[:, b : b + 1][None] * field[:, b : b + 1, :]
        for i in range(8):
            plane = proj_smem[i, 0] * along_y[0]
            for a in range(1, 8):
                plane = plane + proj_smem[i, a] * along_y[a]
            blocks.append(plane)

    quarter = lane((8, 128)) // 32
    data = [
        jnp.concatenate([blocks[4 * q + t] for q in range(6)], axis=0) for t in range(4)
    ]
    for s in range((len(out_refs) + 3) // 4):
        products = [
            dot3(data[t], (high_ref[4 * s + t], low_ref[4 * s + t])) for t in range(4)
        ]
        for r in range(min(4, len(out_refs) - 4 * s)):
            out = out_refs[4 * s + r]
            for q in range(6):
                packed = products[0][8 * q : 8 * q + 8]
                for t in range(1, 4):
                    packed = jnp.where(
                        quarter == (r + t) % 4, products[t][8 * q : 8 * q + 8], packed
                    )
                out[q] = packed
            out[6] = marks_ref[4 * s + r]


def first_kernel(
    counts, n_faces, deriv_ref, high_ref, low_ref, les_ref, wave_ref, mean_ref, *refs
):
    face_refs, (section_ref, rate_ref) = refs[:n_faces], refs[n_faces:]
    state = read_all(les_ref)
    rate = les_rate(state, load_faces(face_refs, counts, 0, 5))
    for c in range(5):
        section_ref[c] = state[c] + rate[c]
    rate = acoustic_rate(
        read_all(wave_ref), read_all(mean_ref), load_faces(face_refs, counts, 5, 9),
        deriv_ref[...], (high_ref[...], low_ref[...]),
    )
    for c in range(4):
        rate_ref[c] = rate[c]


def source_kernel(counts, wave_ref, rate_ref, section_ref, *refs):
    n_pieces = len(partners(counts[0]))
    pieces, refs = refs[:n_pieces], refs[n_pieces:]
    (source_ref, middle_ref, carry_ref), face_refs = refs[:3], refs[3:]
    quarter = lane((8, 128)) // 32
    slot_of_row = sublane((128, 128)) // 8
    same_node = lax.rem(sublane((128, 128)), 8) == lax.rem(lane((128, 128)), 8)
    sums = [None] * 24
    for s in range((n_pieces + 3) // 4):
        count = min(4, n_pieces - 4 * s)

        def gathered(q, t):
            value = jnp.full((8, 128), -1.0 if q == 6 else 0.0, f32)
            for r in range(count):
                value = jnp.where(quarter == (r + t) % 4, pieces[4 * s + r][q], value)
            return value

        for t in range(4):
            marks = gathered(6, t)[0:1].astype(jnp.int32)
            chosen = ((slot_of_row == marks) & same_node).astype(f32).astype(jnp.bfloat16)
            data = jnp.concatenate([gathered(q, t) for q in range(6)], axis=0)
            high = data.astype(jnp.bfloat16)
            low = (data - high.astype(f32)).astype(jnp.bfloat16)
            dims = (((1,), (1,)), ((), ()))
            moved = lax.dot_general(high, chosen, dims, preferred_element_type=f32)
            moved = moved + lax.dot_general(low, chosen, dims, preferred_element_type=f32)
            for q in range(6):
                part = moved[8 * q : 8 * q + 8]
                k = 4 * q + t
                sums[k] = part if sums[k] is None else sums[k] + part
    source = [jnp.stack(sums[8 * c : 8 * c + 8], axis=0) for c in range(3)]
    middle = []
    for c in range(4):
        rate = rate_ref[c]
        if c:
            source_ref[c - 1] = source[c - 1]
            rate = rate + source[c - 1]
        middle.append(wave_ref[c] + acoustic_step * rate)
        middle_ref[c] = middle[c]
        carry = wave_ref[c] + middle[c]
        carry_ref[c] = carry + acoustic_step * source[c - 1] if c else carry
    store_faces(read_all(section_ref) + middle, face_refs, counts)


def inner_kernel(
    deriv_ref, high_ref, low_ref, les_ref, section_ref, middle_ref, carry_ref, mean_ref,
    les_base_ref, wave_base_ref,
):
    section = read_all(section_ref)
    rate = les_rate(section, None)
    for c in range(5):
        les_base_ref[c] = 0.5 * ((les_ref[c] + section[c]) + rate[c])
    rate = acoustic_rate(
        read_all(middle_ref), read_all(mean_ref), None,
        deriv_ref[...], (high_ref[...], low_ref[...]),
    )
    for c in range(4):
        wave_base_ref[c] = 0.5 * (carry_ref[c] + acoustic_step * rate[c])


def last_kernel(counts, n_faces, source_ref, les_base_ref, wave_base_ref, mean_ref, *refs):
    face_refs, (les_out, source_out, wave_out, les_ref, wave_ref, sems) = (
        refs[:n_faces], refs[n_faces:],
    )
    copies = [
        pltpu.make_async_copy(source_ref, source_out, sems.at[0]),
        pltpu.make_async_copy(les_ref, les_out, sems.at[1]),
        pltpu.make_async_copy(wave_ref, wave_out, sems.at[2]),
    ]
    copies[0].start()
    layers = les_outer(load_faces(face_refs, counts, 0, 5))
    for c in range(5):
        part = [(0.5 * low[c], 0.5 * high[c]) for low, high in layers]
        for x, plane in enumerate(with_layers(les_base_ref[c], part)):
            les_ref[c, x] = plane
    copies[1].start()
    layers = acoustic_outer(read_all(mean_ref), load_faces(face_refs, counts, 5, 9))
    step = 0.5 * acoustic_step
    for c in range(4):
        part = [(step * low[c], step * high[c]) for low, high in layers]
        for x, plane in enumerate(with_layers(wave_base_ref[c], part)):
            wave_ref[c, x] = plane
    copies[2].start()
    for copy in copies:
        copy.wait()


VMEM = pl.BlockSpec(memory_space=pltpu.VMEM)
SMEM = pl.BlockSpec(memory_space=pltpu.SMEM)


ANY = pl.BlockSpec(memory_space=pl.ANY)


def call(kernel, in_specs, out_shapes, name, cost, scratch=(), room=24, out_spec=VMEM):
    return pl.pallas_call(
        kernel,
        in_specs=in_specs,
        out_specs=[out_spec] * len(out_shapes),
        out_shape=out_shapes,
        scratch_shapes=list(scratch),
        name=name,
        cost_estimate=pl.CostEstimate(flops=cost, bytes_accessed=800000, transcendentals=0),
        compiler_params=pltpu.CompilerParams(vmem_limit_bytes=room * 1024 * 1024),
    )


def local(counts, les, wave, mean, projection, owner, slot):
    shape = les.shape[1:]
    faces = face_shapes(counts, 9)
    n_faces = len(faces)
    like = lambda n: jax.ShapeDtypeStruct((n,) + shape, f32)

    table = derivative_matrix()
    deriv = jnp.asarray(table, f32)
    along_z = np.kron(np.eye(16), table.T).astype(np.float32)
    high = along_z.astype(jnp.bfloat16)
    low = (along_z - high.astype(np.float32)).astype(jnp.bfloat16)
    tables = (deriv, jnp.asarray(high), jnp.asarray(low))

    x_sets = len(pairings(counts[0]))
    sent = call(
        functools.partial(x_faces_kernel, counts),
        [ANY] * 2,
        faces[:x_sets],
        "x_faces",
        10000,
        [pltpu.SemaphoreType.DMA((x_sets, 2))],
        56,
    )(les, wave)
    sent += call(
        functools.partial(faces_kernel, counts), [VMEM] * 2, faces[x_sets:], "faces", 100000
    )(les, wave)
    got = exchange(sent, counts)

    sets = partners(counts[0])
    n_plans = 4 * ((len(sets) + 3) // 4)
    plan = call(
        functools.partial(plan_kernel, counts),
        [SMEM] * 2 + [VMEM],
        [jax.ShapeDtypeStruct((n_plans, 128, 128), jnp.bfloat16)] * 2
        + [jax.ShapeDtypeStruct((len(sets), 8, 128), f32)],
        "plan",
        4000000,
        [pltpu.SMEM((8,), jnp.int32)],
    )(owner, slot, projection)
    pieces = call(
        functools.partial(lamb_kernel, counts, n_faces),
        [SMEM] + [VMEM] * (5 + n_faces),
        [jax.ShapeDtypeStruct((7, 8, 128), f32)] * len(sets),
        "lamb_blocks",
        10000000,
    )(projection, projection, *plan, les, *got)
    moved = [None] * len(sets)
    for k in reversed(range(len(sets))):
        still = all(i == j for i, j in sets[k])
        moved[k] = pieces[k] if still else lax.ppermute(pieces[k], "gx", sets[k])
    section, rate = call(
        functools.partial(first_kernel, counts, n_faces),
        [VMEM] * (6 + n_faces),
        [like(5), like(4)],
        "first_rates",
        40000000,
    )(*tables, les, wave, mean, *got)

    source, middle, carry, *sent = call(
        functools.partial(source_kernel, counts),
        [VMEM] * (3 + len(moved)),
        [like(3), like(4), like(4)] + faces,
        "source_and_faces",
        10000000,
    )(wave, rate, section, *moved)
    got = exchange(sent, counts)
    les_base, wave_base = call(
        inner_kernel,
        [VMEM] * 8,
        [like(5), like(4)],
        "second_rates_inner",
        40000000,
    )(*tables, les, section, middle, carry, mean)
    return tuple(
        call(
            functools.partial(last_kernel, counts, n_faces),
            [VMEM] * (4 + n_faces),
            [like(5), like(3), like(4)],
            "second_rates_outer",
            4000000,
            [
                pltpu.VMEM(les.shape, f32),
                pltpu.VMEM(wave.shape, f32),
                pltpu.SemaphoreType.DMA((3,)),
            ],
            out_spec=ANY,
        )(source, les_base, wave_base, mean, *got)
    )


def solution(mesh):
    counts = tuple(mesh.shape[axis] for axis in axes)
    field = P(None, *axes)
    return jax.shard_map(
        functools.partial(local, counts),
        mesh=mesh,
        in_specs=(field, field, field, P(), P(*axes), P(*axes)),
        out_specs=(field, field, field),
        check_vma=False,
    )
```

```python
import functools

import jax
import jax.numpy as jnp
import numpy as np
from jax import lax
from jax.experimental import pallas as pl
from jax.experimental.pallas import tpu as pltpu
from jax.sharding import PartitionSpec as P

lobatto_points = np.array(
    [
        -1.0,
        -0.8717401485096066,
        -0.5917001814331423,
        -0.2092992179024789,
        0.2092992179024789,
        0.5917001814331423,
        0.8717401485096066,
        1.0,
    ]
)
flux_half = 0.08
gamma_less = 0.4
acoustic_step = 0.01
upwind_speed = 1.5
face_lift = 28.0
free_stream = (1.0, 0.0, 0.0, 0.0, 2.5)
axes = ("gx", "gy", "gz")
window = 4
f32 = jnp.float32


def derivative_matrix():
    points = lobatto_points
    products = [np.prod([points[i] - points[j] for j in range(8) if j != i]) for i in range(8)]
    matrix = np.zeros((8, 8))
    for i in range(8):
        for j in range(8):
            if j != i:
                matrix[i, j] = products[i] / (products[j] * (points[i] - points[j]))
        matrix[i, i] = -np.sum(matrix[i])
    return matrix


def sublane(shape):
    return lax.broadcasted_iota(jnp.int32, shape, len(shape) - 2)


def lane(shape):
    return lax.broadcasted_iota(jnp.int32, shape, len(shape) - 1)


def shifted(field, axis, step, outer):
    if axis == 0:
        if step == 1:
            return jnp.concatenate([field[1:], outer[None]], axis=0)
        return jnp.concatenate([outer[None], field[:-1]], axis=0)
    count = field.shape[axis]
    moved = pltpu.roll(field, count - 1 if step == 1 else 1, axis)
    edge = count - 1 if step == 1 else 0
    if axis == 1:
        return jnp.where(sublane(field.shape) == edge, outer[:, None, :], moved)
    columns = jnp.stack([outer[:, x : x + 1] for x in range(8)], axis=0)
    return jnp.where(lane(field.shape) == edge, columns, moved)


def fluid(state):
    density, mx, my, mz, energy = [s + r for s, r in zip(state, free_stream)]
    inverse = 1.0 / density
    momentum = (mx, my, mz)
    velocity = [m * inverse for m in momentum]
    pressure = gamma_less * (
        energy - 0.5 * (mx * velocity[0] + my * velocity[1] + mz * velocity[2])
    )
    return momentum, velocity, pressure, energy + pressure


def split_flux(state, parts, axis, sign):
    momentum, velocity, pressure, enthalpy = parts
    speed = velocity[axis]
    flux = [momentum[axis]]
    for c in range(3):
        term = momentum[c] * speed
        flux.append(term + pressure if c == axis else term)
    flux.append(enthalpy * speed)
    if sign > 0:
        return [flux_half * (s + f) for s, f in zip(state, flux)]
    return [flux_half * (s - f) for s, f in zip(state, flux)]


def les_rate(state, halos):
    parts = fluid(state)
    total = [-6.0 * flux_half * s for s in state]
    nothing = jnp.zeros((8, 128), f32)
    for axis in range(3):
        ahead = split_flux(state, parts, axis, -1)
        behind = split_flux(state, parts, axis, 1)
        ahead_outer = behind_outer = [nothing] * 5
        if halos is not None:
            before, after = halos[axis]
            ahead_outer = split_flux(after, fluid(after), axis, -1)
            behind_outer = split_flux(before, fluid(before), axis, 1)
        for c in range(5):
            total[c] = total[c] + (
                shifted(ahead[c], axis, 1, ahead_outer[c])
                + shifted(behind[c], axis, -1, behind_outer[c])
            )
    return total


def les_outer(halos):
    return [
        (
            split_flux(before, fluid(before), axis, 1),
            split_flux(after, fluid(after), axis, -1),
        )
        for axis, (before, after) in enumerate(halos)
    ]


def with_layers(field, layers):
    (x0, x1), (y0, y1), (z0, z1) = layers
    row, column = sublane((8, 128)), lane((8, 128))
    planes = []
    for x in range(8):
        plane = field[x]
        if x == 0:
            plane = plane + x0
        if x == 7:
            plane = plane + x1
        plane = plane + jnp.where(
            row == 0, y0[x : x + 1], jnp.where(row == 7, y1[x : x + 1], 0.0)
        )
        plane = plane + jnp.where(
            column == 0, z0[:, x : x + 1], jnp.where(column == 127, z1[:, x : x + 1], 0.0)
        )
        planes.append(plane)
    return planes


def wave_flux(state, mean, axis):
    speed = mean[axis]
    pressure = state[0]
    rows = [speed * pressure + state[1 + axis]]
    for c in range(3):
        term = speed * state[1 + c]
        rows.append(term + pressure if c == axis else term)
    return rows


def dot3(left, right):
    high = left.astype(jnp.bfloat16)
    low = (left - high.astype(f32)).astype(jnp.bfloat16)
    dot = functools.partial(jnp.dot, preferred_element_type=f32)
    return dot(high, right[0]) + (dot(low, right[0]) + dot(high, right[1]))


def halves(matrix):
    high = matrix.astype(jnp.bfloat16)
    return high, (matrix - high.astype(f32)).astype(jnp.bfloat16)


def acoustic_rate(state, mean, halos, deriv, along_z):
    shape = state[0].shape
    table = derivative_matrix()
    flux = wave_flux(state, mean, 0)
    if halos is None:
        halos = [([jnp.zeros((8, 128), f32)] * 4,) * 2] * 3
    before, after = halos[0]
    low_mean, high_mean = [m[0] for m in mean], [m[7] for m in mean]
    low_jump = [b - s[0] for b, s in zip(before, state)]
    high_jump = [a - s[7] for a, s in zip(after, state)]
    low_flux = wave_flux(low_jump, low_mean, 0)
    high_flux = wave_flux(high_jump, high_mean, 0)
    half, lift = 0.5 * face_lift, 0.5 * face_lift * upwind_speed
    total = []
    for c in range(4):
        planes = []
        for i in range(8):
            plane = -float(table[i, 0]) * flux[c][0]
            for a in range(1, 8):
                if abs(table[i, a]) > 1e-12:
                    plane = plane - float(table[i, a]) * flux[c][a]
            if i == 0:
                plane = plane + (half * low_flux[c] + lift * low_jump[c])
            if i == 7:
                plane = plane - (half * high_flux[c] - lift * high_jump[c])
            planes.append(plane)
        total.append(jnp.stack(planes, axis=0))
    flux = wave_flux(state, mean, 1)
    before, after = halos[1]
    row = sublane(shape)
    sign = jnp.where(row == 0, half, jnp.where(row == 7, -half, 0.0))
    jump = [
        jnp.where(row == 0, b[:, None, :], jnp.where(row == 7, a[:, None, :], s)) - s
        for s, b, a in zip(state, before, after)
    ]
    jump_flux = wave_flux(jump, mean, 1)
    for c in range(4):
        change = lift * jump[c] + sign * jump_flux[c]
        for b in range(8):
            change = change - deriv[:, b : b + 1][None] * flux[c][:, b : b + 1, :]
        total[c] = total[c] + change
    flux = wave_flux(state, mean, 2)
    before, after = halos[2]
    column = lane(shape)
    place = lax.rem(column, 8)
    sign = jnp.where(place == 0, half, jnp.where(place == 7, -half, 0.0))
    jump = [
        jnp.where(
            place == 0,
            shifted(s, 2, -1, b),
            jnp.where(place == 7, shifted(s, 2, 1, a), s),
        )
        - s
        for s, b, a in zip(state, before, after)
    ]
    jump_flux = wave_flux(jump, mean, 2)
    for c in range(4):
        slope = dot3(flux[c].reshape(64, 128), along_z).reshape(shape)
        total[c] = total[c] + (lift * jump[c] + sign * jump_flux[c] - slope)
    return total


def acoustic_outer(mean, halos):
    half, lift = 0.5 * face_lift, 0.5 * face_lift * upwind_speed
    layers = []
    column = lane((8, 128))
    for axis, (before, after) in enumerate(halos):
        if axis == 0:
            low, high = [m[0] for m in mean], [m[7] for m in mean]
        elif axis == 1:
            low, high = [m[:, 0, :] for m in mean], [m[:, 7, :] for m in mean]
        else:
            low, high = [], []
            for m in mean:
                first = last = jnp.zeros((8, 128), f32)
                for x in range(8):
                    first = jnp.where(column == x, m[x][:, 0:1], first)
                    last = jnp.where(column == x, m[x][:, 127:128], last)
                low.append(first)
                high.append(last)
        low_flux = wave_flux(before, low, axis)
        high_flux = wave_flux(after, high, axis)
        layers.append(
            (
                [half * f + lift * b for f, b in zip(low_flux, before)],
                [lift * a - half * f for f, a in zip(high_flux, after)],
            )
        )
    return layers


def tile_rows(matrix, transposed):
    spread = (lax.rem(lane((8, 128)), 8) == sublane((8, 128))).astype(f32)
    contract = ((1,), (0,)) if transposed else ((0,), (0,))
    return lax.dot_general(
        matrix, spread, (contract, ((), ())),
        precision=lax.Precision.HIGHEST, preferred_element_type=f32,
    )


def block_diagonal(tile):
    rows = [jnp.where(lane((8, 128)) // 8 == n, tile, 0.0) for n in range(16)]
    return halves(jnp.concatenate(rows, axis=0))


def pairings(count):
    sets = []
    for first in (0, 1):
        pairs = [(i, i + 1) for i in range(first, count - 1, 2)]
        if pairs:
            joined = [p for i, j in pairs for p in ((i, j), (j, i))]
            alone = set(range(count)) - {i for i, _ in joined}
            sets.append(joined + [(i, i) for i in sorted(alone)])
    return sets


def pack_z(fields, at):
    packed = jnp.zeros((8, 128), f32)
    column = lane((8, 128))
    for c, field in enumerate(fields):
        for x in range(8):
            packed = jnp.where(column == c * 8 + x, field[x][:, at : at + 1], packed)
    return packed


def store_faces(fields, out_refs, counts, which=(0, 1, 2)):
    at = 0
    for axis in which:
        even = lax.rem(lax.axis_index(axes[axis]), 2) == 0
        sets = len(pairings(counts[axis]))
        if axis == 2:
            out_refs[at][0] = pack_z(fields, 0)
            out_refs[at][1] = pack_z(fields, 127)
        else:
            for c, field in enumerate(fields):
                low = field[0] if axis == 0 else field[:, 0, :]
                high = field[7] if axis == 0 else field[:, 7, :]
                for s in range(sets):
                    out_refs[at + s][c] = jnp.where(even == (s == 0), high, low)
        at += sets


def sending_order(counts):
    where = [(axis, s) for axis in (0, 1) for s in range(len(pairings(counts[axis])))]
    where.append((2, 0))
    return [where.index(p) for p in ((2, 0), (0, 1), (1, 1), (1, 0), (0, 0)) if p in where]


def load_faces(sent_refs, counts, first, last):
    in_refs = [None] * len(sent_refs)
    for ref, at in zip(sent_refs, sending_order(counts)):
        in_refs[at] = ref
    halos = []
    at = 0
    for axis in range(3):
        place = lax.axis_index(axes[axis])
        ends = counts[axis] - 1
        if axis == 2:
            got = []
            for index, side in ((jnp.maximum(place - 1, 0), 1), (jnp.minimum(place + 1, ends), 0)):
                packed = in_refs[at][index, side]
                got.append(
                    [
                        pltpu.roll(packed, (128 - 8 * c) % 128, 1) if c else packed
                        for c in range(first, last)
                    ]
                )
            before = [jnp.where(place == 0, 0.0, b) for b in got[0]]
            after = [jnp.where(place == ends, 0.0, a) for a in got[1]]
            halos.append((before, after))
            continue
        even = lax.rem(place, 2) == 0
        sets = len(pairings(counts[axis]))
        got = [[in_refs[at + s][c] for c in range(first, last)] for s in range(sets)]
        while len(got) < 2:
            got.append([jnp.zeros((8, 128), f32)] * (last - first))
        before = [jnp.where(place == 0, 0.0, jnp.where(even, b, a)) for a, b in zip(*got)]
        after = [jnp.where(place == ends, 0.0, jnp.where(even, a, b)) for a, b in zip(*got)]
        halos.append((before, after))
        at += sets
    return halos


def face_shapes(counts, width):
    shapes = []
    for axis in (0, 1):
        shapes += [jax.ShapeDtypeStruct((width, 8, 128), f32)] * len(pairings(counts[axis]))
    return shapes + [jax.ShapeDtypeStruct((2, 8, 128), f32)]


def exchange(faces, counts):
    routes = [(axes[axis], pairs) for axis in (0, 1) for pairs in pairings(counts[axis])]
    result = []
    for at in sending_order(counts):
        if at == len(routes):
            result.append(lax.all_gather(faces[at], axes[2]))
        else:
            result.append(lax.ppermute(faces[at], *routes[at]))
    return result


def read_all(ref):
    return [ref[c] for c in range(ref.shape[0])]


def x_faces_kernel(counts, les_hbm, wave_hbm, *refs):
    out_refs, sems = refs[:-1], refs[-1]
    odd = lax.rem(lax.axis_index("gx"), 2)
    copies = []
    for s, out in enumerate(out_refs):
        plane = 7 * (1 - odd) if s == 0 else 7 * odd
        for k, (first, source) in enumerate(((0, les_hbm), (5, wave_hbm))):
            copies.append(
                pltpu.make_async_copy(
                    source.at[:, plane], out.at[first : first + source.shape[0]], sems.at[s, k]
                )
            )
    for copy in copies:
        copy.start()
    for copy in copies:
        copy.wait()


def faces_kernel(counts, les_ref, wave_ref, *out_refs):
    store_faces(read_all(les_ref) + read_all(wave_ref), out_refs, counts, (1, 2))


def partners(count):
    if count == window:
        return [[(i, i ^ mask) for i in range(count)] for mask in range(count)]
    turns = sorted({d % count for d in range(1 - window, window)})
    return [[(i, (i + turn) % count) for i in range(count)] for turn in turns]


def plan_kernel(counts, owner_ref, slot_ref, proj_ref, high_ref, low_ref, marks_ref, counter):
    count = counts[0]
    n_sets = len(partners(count))
    groups = 4 * ((n_sets + 3) // 4)
    own = lax.axis_index("gx")
    for g in range(groups):
        counter[g] = 0
    places = []
    for n in range(owner_ref.shape[-1]):
        if count == window:
            group = lax.bitwise_xor(owner_ref[0, 0, n], own)
        else:
            turn = lax.rem(owner_ref[0, 0, n] - own + count, count)
            group = turn if n_sets == count else jnp.where(
                turn < window, turn, turn - (count - n_sets)
            )
        taken = counter[group]
        counter[group] = taken + 1
        places.append(group * window + taken)
    tile = tile_rows(proj_ref[...], False)
    tile_high = tile.astype(jnp.bfloat16).astype(f32)
    tile_low = tile - tile_high
    block_of_lane = lane((8, 128)) // 8
    quarter = lane((8, 128)) // 32
    for s in range(groups // 4):
        labels = jnp.full((8, 128), -1.0, f32)
        for n, place in enumerate(places):
            labels = jnp.where(
                block_of_lane == place - 16 * s, slot_ref[0, 0, n].astype(f32), labels
            )
        for t in range(4):
            chosen = []
            for place in places:
                here = block_of_lane == lax.rem(place + 4 * t, 16)
                chosen.append(here if groups == 4 else here & (place // 16 == s))
            for ref, part in ((high_ref, tile_high), (low_ref, tile_low)):
                rows = [jnp.where(here, part, 0.0) for here in chosen]
                ref[4 * s + t] = jnp.concatenate(rows, axis=0).astype(jnp.bfloat16)
        for r in range(min(4, n_sets - 4 * s)):
            marks = labels
            for t in range(1, 4):
                marks = jnp.where(quarter == (r + t) % 4, pltpu.roll(labels, 32 * t, 1), marks)
            marks_ref[4 * s + r] = marks


def lamb_kernel(counts, n_faces, proj_smem, proj_ref, high_ref, low_ref, marks_ref, les_ref, *refs):
    face_refs, out_refs = refs[:n_faces], refs[n_faces:]
    halos = load_faces(face_refs, counts, 0, 4)

    def speeds(state):
        inverse = 1.0 / (state[0] + 1.0)
        return [state[c] * inverse for c in (1, 2, 3)]

    velocity = speeds([les_ref[c] for c in range(4)])
    outer = [(speeds(before), speeds(after)) for before, after in halos]

    def slope(c, axis):
        return 0.5 * (
            shifted(velocity[c], axis, 1, outer[axis][1][c])
            - shifted(velocity[c], axis, -1, outer[axis][0][c])
        )

    vort = [slope(2, 1) - slope(1, 2), slope(0, 2) - slope(2, 0), slope(1, 0) - slope(0, 1)]
    lamb = [
        vort[1] * velocity[2] - vort[2] * velocity[1],
        vort[2] * velocity[0] - vort[0] * velocity[2],
        vort[0] * velocity[1] - vort[1] * velocity[0],
    ]
    proj = proj_ref[...]
    blocks = []
    for field in lamb:
        along_y = proj[:, 0:1][None] * field[:, 0:1, :]
        for b in range(1, 8):
            along_y = along_y + proj[:, b : b + 1][None] * field[:, b : b + 1, :]
        for i in range(8):
            plane = proj_smem[i, 0] * along_y[0]
            for a in range(1, 8):
                plane = plane + proj_smem[i, a] * along_y[a]
            blocks.append(plane)

    quarter = lane((8, 128)) // 32
    data = [
        jnp.concatenate([blocks[4 * q + t] for q in range(6)], axis=0) for t in range(4)
    ]
    for s in range((len(out_refs) + 3) // 4):
        products = [
            dot3(data[t], (high_ref[4 * s + t], low_ref[4 * s + t])) for t in range(4)
        ]
        for r in range(min(4, len(out_refs) - 4 * s)):
            out = out_refs[4 * s + r]
            for q in range(6):
                packed = products[0][8 * q : 8 * q + 8]
                for t in range(1, 4):
                    packed = jnp.where(
                        quarter == (r + t) % 4, products[t][8 * q : 8 * q + 8], packed
                    )
                out[q] = packed
            out[6] = marks_ref[4 * s + r]


def first_kernel(
    counts, n_faces, deriv_ref, high_ref, low_ref, les_ref, wave_ref, mean_ref, *refs
):
    face_refs, (section_ref, rate_ref) = refs[:n_faces], refs[n_faces:]
    state = read_all(les_ref)
    rate = les_rate(state, load_faces(face_refs, counts, 0, 5))
    for c in range(5):
        section_ref[c] = state[c] + rate[c]
    rate = acoustic_rate(
        read_all(wave_ref), read_all(mean_ref), load_faces(face_refs, counts, 5, 9),
        deriv_ref[...], (high_ref[...], low_ref[...]),
    )
    for c in range(4):
        rate_ref[c] = rate[c]


def source_kernel(counts, wave_ref, rate_ref, section_ref, *refs):
    n_pieces = len(partners(counts[0]))
    pieces, refs = refs[:n_pieces][::-1], refs[n_pieces:]
    (source_ref, middle_ref, carry_ref), face_refs = refs[:3], refs[3:]
    quarter = lane((8, 128)) // 32
    slot_of_row = sublane((128, 128)) // 8
    same_node = lax.rem(sublane((128, 128)), 8) == lax.rem(lane((128, 128)), 8)
    sums = [None] * 24
    for s in range((n_pieces + 3) // 4):
        count = min(4, n_pieces - 4 * s)

        def gathered(q, t):
            value = jnp.full((8, 128), -1.0 if q == 6 else 0.0, f32)
            for r in range(count):
                value = jnp.where(quarter == (r + t) % 4, pieces[4 * s + r][q], value)
            return value

        for t in range(4):
            marks = gathered(6, t)[0:1].astype(jnp.int32)
            chosen = ((slot_of_row == marks) & same_node).astype(f32).astype(jnp.bfloat16)
            data = jnp.concatenate([gathered(q, t) for q in range(6)], axis=0)
            high = data.astype(jnp.bfloat16)
            low = (data - high.astype(f32)).astype(jnp.bfloat16)
            dims = (((1,), (1,)), ((), ()))
            moved = lax.dot_general(high, chosen, dims, preferred_element_type=f32)
            moved = moved + lax.dot_general(low, chosen, dims, preferred_element_type=f32)
            for q in range(6):
                part = moved[8 * q : 8 * q + 8]
                k = 4 * q + t
                sums[k] = part if sums[k] is None else sums[k] + part
    source = [jnp.stack(sums[8 * c : 8 * c + 8], axis=0) for c in range(3)]
    middle = []
    for c in range(4):
        rate = rate_ref[c]
        if c:
            source_ref[c - 1] = source[c - 1]
            rate = rate + source[c - 1]
        middle.append(wave_ref[c] + acoustic_step * rate)
        middle_ref[c] = middle[c]
        carry = wave_ref[c] + middle[c]
        carry_ref[c] = carry + acoustic_step * source[c - 1] if c else carry
    store_faces(read_all(section_ref) + middle, face_refs, counts)


def inner_kernel(
    deriv_ref, high_ref, low_ref, les_ref, section_ref, middle_ref, carry_ref, mean_ref,
    les_base_ref, wave_base_ref,
):
    section = read_all(section_ref)
    rate = les_rate(section, None)
    for c in range(5):
        les_base_ref[c] = 0.5 * ((les_ref[c] + section[c]) + rate[c])
    rate = acoustic_rate(
        read_all(middle_ref), read_all(mean_ref), None,
        deriv_ref[...], (high_ref[...], low_ref[...]),
    )
    for c in range(4):
        wave_base_ref[c] = 0.5 * (carry_ref[c] + acoustic_step * rate[c])


def last_kernel(counts, n_faces, source_ref, les_base_ref, wave_base_ref, mean_ref, *refs):
    face_refs, (les_out, source_out, wave_out, les_ref, wave_ref, sems) = (
        refs[:n_faces], refs[n_faces:],
    )
    copies = [
        pltpu.make_async_copy(source_ref, source_out, sems.at[0]),
        pltpu.make_async_copy(les_ref, les_out, sems.at[1]),
        pltpu.make_async_copy(wave_ref, wave_out, sems.at[2]),
    ]
    copies[0].start()
    layers = les_outer(load_faces(face_refs, counts, 0, 5))
    for c in range(5):
        part = [(0.5 * low[c], 0.5 * high[c]) for low, high in layers]
        for x, plane in enumerate(with_layers(les_base_ref[c], part)):
            les_ref[c, x] = plane
    copies[1].start()
    layers = acoustic_outer(read_all(mean_ref), load_faces(face_refs, counts, 5, 9))
    step = 0.5 * acoustic_step
    for c in range(4):
        part = [(step * low[c], step * high[c]) for low, high in layers]
        for x, plane in enumerate(with_layers(wave_base_ref[c], part)):
            wave_ref[c, x] = plane
    copies[2].start()
    for copy in copies:
        copy.wait()


VMEM = pl.BlockSpec(memory_space=pltpu.VMEM)
SMEM = pl.BlockSpec(memory_space=pltpu.SMEM)


ANY = pl.BlockSpec(memory_space=pl.ANY)


def call(kernel, in_specs, out_shapes, name, cost, scratch=(), room=24, out_spec=VMEM):
    return pl.pallas_call(
        kernel,
        in_specs=in_specs,
        out_specs=[out_spec] * len(out_shapes),
        out_shape=out_shapes,
        scratch_shapes=list(scratch),
        name=name,
        cost_estimate=pl.CostEstimate(flops=cost, bytes_accessed=800000, transcendentals=0),
        compiler_params=pltpu.CompilerParams(vmem_limit_bytes=room * 1024 * 1024),
    )


def local(counts, les, wave, mean, projection, owner, slot):
    shape = les.shape[1:]
    faces = face_shapes(counts, 9)
    n_faces = len(faces)
    like = lambda n: jax.ShapeDtypeStruct((n,) + shape, f32)

    table = derivative_matrix()
    deriv = jnp.asarray(table, f32)
    along_z = np.kron(np.eye(16), table.T).astype(np.float32)
    high = along_z.astype(jnp.bfloat16)
    low = (along_z - high.astype(np.float32)).astype(jnp.bfloat16)
    tables = (deriv, jnp.asarray(high), jnp.asarray(low))

    x_sets = len(pairings(counts[0]))
    sent = call(
        functools.partial(x_faces_kernel, counts),
        [ANY] * 2,
        faces[:x_sets],
        "x_faces",
        10000,
        [pltpu.SemaphoreType.DMA((x_sets, 2))],
        56,
    )(les, wave)
    sent += call(
        functools.partial(faces_kernel, counts), [VMEM] * 2, faces[x_sets:], "faces", 100000
    )(les, wave)
    got = exchange(sent, counts)

    sets = partners(counts[0])
    n_plans = 4 * ((len(sets) + 3) // 4)
    plan = call(
        functools.partial(plan_kernel, counts),
        [SMEM] * 2 + [VMEM],
        [jax.ShapeDtypeStruct((n_plans, 128, 128), jnp.bfloat16)] * 2
        + [jax.ShapeDtypeStruct((len(sets), 8, 128), f32)],
        "plan",
        4000000,
        [pltpu.SMEM((8,), jnp.int32)],
    )(owner, slot, projection)
    pieces = call(
        functools.partial(lamb_kernel, counts, n_faces),
        [SMEM] + [VMEM] * (5 + n_faces),
        [jax.ShapeDtypeStruct((7, 8, 128), f32)] * len(sets),
        "lamb_blocks",
        10000000,
    )(projection, projection, *plan, les, *got)
    moved = [None] * len(sets)
    for k in reversed(range(len(sets))):
        still = all(i == j for i, j in sets[k])
        moved[k] = pieces[k] if still else lax.ppermute(pieces[k], "gx", sets[k])
    section, rate = call(
        functools.partial(first_kernel, counts, n_faces),
        [VMEM] * (6 + n_faces),
        [like(5), like(4)],
        "first_rates",
        40000000,
    )(*tables, les, wave, mean, *got)

    source, middle, carry, *sent = call(
        functools.partial(source_kernel, counts),
        [VMEM] * (3 + len(moved)),
        [like(3), like(4), like(4)] + faces,
        "source_and_faces",
        10000000,
    )(wave, rate, section, *moved[::-1])
    got = exchange(sent, counts)
    les_base, wave_base = call(
        inner_kernel,
        [VMEM] * 8,
        [like(5), like(4)],
        "second_rates_inner",
        40000000,
    )(*tables, les, section, middle, carry, mean)
    return tuple(
        call(
            functools.partial(last_kernel, counts, n_faces),
            [VMEM] * (4 + n_faces),
            [like(5), like(3), like(4)],
            "second_rates_outer",
            4000000,
            [
                pltpu.VMEM(les.shape, f32),
                pltpu.VMEM(wave.shape, f32),
                pltpu.SemaphoreType.DMA((3,)),
            ],
            out_spec=ANY,
        )(source, les_base, wave_base, mean, *got)
    )


def solution(mesh):
    counts = tuple(mesh.shape[axis] for axis in axes)
    field = P(None, *axes)
    return jax.shard_map(
        functools.partial(local, counts),
        mesh=mesh,
        in_specs=(field, field, field, P(), P(*axes), P(*axes)),
        out_specs=(field, field, field),
        check_vma=False,
    )
```

```python
import functools

import jax
import jax.numpy as jnp
import numpy as np
from jax import lax
from jax.experimental import pallas as pl
from jax.experimental.pallas import tpu as pltpu
from jax.sharding import PartitionSpec as P

lobatto_points = np.array(
    [
        -1.0,
        -0.8717401485096066,
        -0.5917001814331423,
        -0.2092992179024789,
        0.2092992179024789,
        0.5917001814331423,
        0.8717401485096066,
        1.0,
    ]
)
flux_half = 0.08
gamma_less = 0.4
acoustic_step = 0.01
upwind_speed = 1.5
face_lift = 28.0
free_stream = (1.0, 0.0, 0.0, 0.0, 2.5)
axes = ("gx", "gy", "gz")
window = 4
f32 = jnp.float32


def derivative_matrix():
    points = lobatto_points
    products = [np.prod([points[i] - points[j] for j in range(8) if j != i]) for i in range(8)]
    matrix = np.zeros((8, 8))
    for i in range(8):
        for j in range(8):
            if j != i:
                matrix[i, j] = products[i] / (products[j] * (points[i] - points[j]))
        matrix[i, i] = -np.sum(matrix[i])
    return matrix


def sublane(shape):
    return lax.broadcasted_iota(jnp.int32, shape, len(shape) - 2)


def lane(shape):
    return lax.broadcasted_iota(jnp.int32, shape, len(shape) - 1)


def shifted(field, axis, step, outer):
    if axis == 0:
        if step == 1:
            return jnp.concatenate([field[1:], outer[None]], axis=0)
        return jnp.concatenate([outer[None], field[:-1]], axis=0)
    count = field.shape[axis]
    moved = pltpu.roll(field, count - 1 if step == 1 else 1, axis)
    edge = count - 1 if step == 1 else 0
    if axis == 1:
        return jnp.where(sublane(field.shape) == edge, outer[:, None, :], moved)
    columns = jnp.stack([outer[:, x : x + 1] for x in range(8)], axis=0)
    return jnp.where(lane(field.shape) == edge, columns, moved)


def fluid(state):
    density, mx, my, mz, energy = [s + r for s, r in zip(state, free_stream)]
    inverse = 1.0 / density
    momentum = (mx, my, mz)
    velocity = [m * inverse for m in momentum]
    pressure = gamma_less * (
        energy - 0.5 * (mx * velocity[0] + my * velocity[1] + mz * velocity[2])
    )
    return momentum, velocity, pressure, energy + pressure


def split_flux(state, parts, axis, sign):
    momentum, velocity, pressure, enthalpy = parts
    speed = velocity[axis]
    flux = [momentum[axis]]
    for c in range(3):
        term = momentum[c] * speed
        flux.append(term + pressure if c == axis else term)
    flux.append(enthalpy * speed)
    if sign > 0:
        return [flux_half * (s + f) for s, f in zip(state, flux)]
    return [flux_half * (s - f) for s, f in zip(state, flux)]


def les_rate(state, halos):
    parts = fluid(state)
    total = [-6.0 * flux_half * s for s in state]
    nothing = jnp.zeros((8, 128), f32)
    for axis in range(3):
        ahead = split_flux(state, parts, axis, -1)
        behind = split_flux(state, parts, axis, 1)
        ahead_outer = behind_outer = [nothing] * 5
        if halos is not None:
            before, after = halos[axis]
            ahead_outer = split_flux(after, fluid(after), axis, -1)
            behind_outer = split_flux(before, fluid(before), axis, 1)
        for c in range(5):
            total[c] = total[c] + (
                shifted(ahead[c], axis, 1, ahead_outer[c])
                + shifted(behind[c], axis, -1, behind_outer[c])
            )
    return total


def les_outer(halos):
    return [
        (
            split_flux(before, fluid(before), axis, 1),
            split_flux(after, fluid(after), axis, -1),
        )
        for axis, (before, after) in enumerate(halos)
    ]


def with_layers(field, layers):
    (x0, x1), (y0, y1), (z0, z1) = layers
    row, column = sublane((8, 128)), lane((8, 128))
    planes = []
    for x in range(8):
        plane = field[x]
        if x == 0:
            plane = plane + x0
        if x == 7:
            plane = plane + x1
        plane = plane + jnp.where(
            row == 0, y0[x : x + 1], jnp.where(row == 7, y1[x : x + 1], 0.0)
        )
        plane = plane + jnp.where(
            column == 0, z0[:, x : x + 1], jnp.where(column == 127, z1[:, x : x + 1], 0.0)
        )
        planes.append(plane)
    return planes


def wave_flux(state, mean, axis):
    speed = mean[axis]
    pressure = state[0]
    rows = [speed * pressure + state[1 + axis]]
    for c in range(3):
        term = speed * state[1 + c]
        rows.append(term + pressure if c == axis else term)
    return rows


def dot3(left, right):
    high = left.astype(jnp.bfloat16)
    low = (left - high.astype(f32)).astype(jnp.bfloat16)
    dot = functools.partial(jnp.dot, preferred_element_type=f32)
    return dot(high, right[0]) + (dot(low, right[0]) + dot(high, right[1]))


def halves(matrix):
    high = matrix.astype(jnp.bfloat16)
    return high, (matrix - high.astype(f32)).astype(jnp.bfloat16)


def acoustic_rate(state, mean, halos, deriv, along_z):
    shape = state[0].shape
    table = derivative_matrix()
    flux = wave_flux(state, mean, 0)
    if halos is None:
        halos = [([jnp.zeros((8, 128), f32)] * 4,) * 2] * 3
    before, after = halos[0]
    low_mean, high_mean = [m[0] for m in mean], [m[7] for m in mean]
    low_jump = [b - s[0] for b, s in zip(before, state)]
    high_jump = [a - s[7] for a, s in zip(after, state)]
    low_flux = wave_flux(low_jump, low_mean, 0)
    high_flux = wave_flux(high_jump, high_mean, 0)
    half, lift = 0.5 * face_lift, 0.5 * face_lift * upwind_speed
    total = []
    for c in range(4):
        planes = []
        for i in range(8):
            plane = -float(table[i, 0]) * flux[c][0]
            for a in range(1, 8):
                if abs(table[i, a]) > 1e-12:
                    plane = plane - float(table[i, a]) * flux[c][a]
            if i == 0:
                plane = plane + (half * low_flux[c] + lift * low_jump[c])
            if i == 7:
                plane = plane - (half * high_flux[c] - lift * high_jump[c])
            planes.append(plane)
        total.append(jnp.stack(planes, axis=0))
    flux = wave_flux(state, mean, 1)
    before, after = halos[1]
    row = sublane(shape)
    sign = jnp.where(row == 0, half, jnp.where(row == 7, -half, 0.0))
    jump = [
        jnp.where(row == 0, b[:, None, :], jnp.where(row == 7, a[:, None, :], s)) - s
        for s, b, a in zip(state, before, after)
    ]
    jump_flux = wave_flux(jump, mean, 1)
    for c in range(4):
        change = lift * jump[c] + sign * jump_flux[c]
        for b in range(8):
            change = change - deriv[:, b : b + 1][None] * flux[c][:, b : b + 1, :]
        total[c] = total[c] + change
    flux = wave_flux(state, mean, 2)
    before, after = halos[2]
    column = lane(shape)
    place = lax.rem(column, 8)
    sign = jnp.where(place == 0, half, jnp.where(place == 7, -half, 0.0))
    jump = [
        jnp.where(
            place == 0,
            shifted(s, 2, -1, b),
            jnp.where(place == 7, shifted(s, 2, 1, a), s),
        )
        - s
        for s, b, a in zip(state, before, after)
    ]
    jump_flux = wave_flux(jump, mean, 2)
    for c in range(4):
        slope = dot3(flux[c].reshape(64, 128), along_z).reshape(shape)
        total[c] = total[c] + (lift * jump[c] + sign * jump_flux[c] - slope)
    return total


def acoustic_outer(mean, halos):
    half, lift = 0.5 * face_lift, 0.5 * face_lift * upwind_speed
    layers = []
    column = lane((8, 128))
    for axis, (before, after) in enumerate(halos):
        if axis == 0:
            low, high = [m[0] for m in mean], [m[7] for m in mean]
        elif axis == 1:
            low, high = [m[:, 0, :] for m in mean], [m[:, 7, :] for m in mean]
        else:
            low, high = [], []
            for m in mean:
                first = last = jnp.zeros((8, 128), f32)
                for x in range(8):
                    first = jnp.where(column == x, m[x][:, 0:1], first)
                    last = jnp.where(column == x, m[x][:, 127:128], last)
                low.append(first)
                high.append(last)
        low_flux = wave_flux(before, low, axis)
        high_flux = wave_flux(after, high, axis)
        layers.append(
            (
                [half * f + lift * b for f, b in zip(low_flux, before)],
                [lift * a - half * f for f, a in zip(high_flux, after)],
            )
        )
    return layers


def tile_rows(matrix, transposed):
    spread = (lax.rem(lane((8, 128)), 8) == sublane((8, 128))).astype(f32)
    contract = ((1,), (0,)) if transposed else ((0,), (0,))
    return lax.dot_general(
        matrix, spread, (contract, ((), ())),
        precision=lax.Precision.HIGHEST, preferred_element_type=f32,
    )


def block_diagonal(tile):
    rows = [jnp.where(lane((8, 128)) // 8 == n, tile, 0.0) for n in range(16)]
    return halves(jnp.concatenate(rows, axis=0))


def pairings(count):
    sets = []
    for first in (0, 1):
        pairs = [(i, i + 1) for i in range(first, count - 1, 2)]
        if pairs:
            alone = sorted(set(range(count)) - {i for pair in pairs for i in pair})
            if len(alone) == 2:
                pairs.append(tuple(alone))
            sets.append([p for i, j in pairs for p in ((i, j), (j, i))])
    return sets


def pack_z(fields, at):
    packed = jnp.zeros((8, 128), f32)
    column = lane((8, 128))
    for c, field in enumerate(fields):
        for x in range(8):
            packed = jnp.where(column == c * 8 + x, field[x][:, at : at + 1], packed)
    return packed


def store_faces(fields, out_refs, counts, which=(0, 1, 2)):
    at = 0
    for axis in which:
        even = lax.rem(lax.axis_index(axes[axis]), 2) == 0
        sets = len(pairings(counts[axis]))
        if axis == 2:
            low, high = pack_z(fields, 0), pack_z(fields, 127)
            for s in range(sets):
                out_refs[at + s][...] = jnp.where(even == (s == 0), high, low)
        else:
            for c, field in enumerate(fields):
                low = field[0] if axis == 0 else field[:, 0, :]
                high = field[7] if axis == 0 else field[:, 7, :]
                for s in range(sets):
                    out_refs[at + s][c] = jnp.where(even == (s == 0), high, low)
        at += sets


def sending_order(counts):
    where = [(axis, s) for axis in range(3) for s in range(len(pairings(counts[axis])))]
    wanted = ((0, 1), (2, 1), (2, 0), (1, 1), (1, 0), (0, 0))
    return [where.index(p) for p in wanted if p in where]


def load_faces(sent_refs, counts, first, last):
    in_refs = [None] * len(sent_refs)
    for ref, at in zip(sent_refs, sending_order(counts)):
        in_refs[at] = ref
    halos = []
    at = 0
    for axis in range(3):
        even = lax.rem(lax.axis_index(axes[axis]), 2) == 0
        sets = len(pairings(counts[axis]))
        got = []
        for s in range(sets):
            if axis == 2:
                packed = in_refs[at + s][...]
                got.append(
                    [
                        pltpu.roll(packed, (128 - 8 * c) % 128, 1) if c else packed
                        for c in range(first, last)
                    ]
                )
            else:
                got.append([in_refs[at + s][c] for c in range(first, last)])
        while len(got) < 2:
            got.append([jnp.zeros((8, 128), f32)] * (last - first))
        place = lax.axis_index(axes[axis])
        before = [
            jnp.where(place == 0, 0.0, jnp.where(even, b, a)) for a, b in zip(*got)
        ]
        after = [
            jnp.where(place == counts[axis] - 1, 0.0, jnp.where(even, a, b))
            for a, b in zip(*got)
        ]
        halos.append((before, after))
        at += sets
    return halos


def face_shapes(counts, width):
    shapes = []
    for axis in range(3):
        shape = (8, 128) if axis == 2 else (width, 8, 128)
        shapes += [jax.ShapeDtypeStruct(shape, f32)] * len(pairings(counts[axis]))
    return shapes


def exchange(faces, counts):
    routes = [(axes[axis], pairs) for axis in range(3) for pairs in pairings(counts[axis])]
    return [lax.ppermute(faces[at], *routes[at]) for at in sending_order(counts)]


def read_all(ref):
    return [ref[c] for c in range(ref.shape[0])]


def x_faces_kernel(counts, les_hbm, wave_hbm, *refs):
    out_refs, sems = refs[:-1], refs[-1]
    odd = lax.rem(lax.axis_index("gx"), 2)
    copies = []
    for s, out in enumerate(out_refs):
        plane = 7 * (1 - odd) if s == 0 else 7 * odd
        for k, (first, source) in enumerate(((0, les_hbm), (5, wave_hbm))):
            copies.append(
                pltpu.make_async_copy(
                    source.at[:, plane], out.at[first : first + source.shape[0]], sems.at[s, k]
                )
            )
    for copy in copies:
        copy.start()
    for copy in copies:
        copy.wait()


def faces_kernel(counts, les_ref, wave_ref, *out_refs):
    store_faces(read_all(les_ref) + read_all(wave_ref), out_refs, counts, (1, 2))


def partners(count):
    if count == window:
        return [[(i, i ^ mask) for i in range(count)] for mask in range(count)]
    turns = sorted({d % count for d in range(1 - window, window)})
    return [[(i, (i + turn) % count) for i in range(count)] for turn in turns]


def plan_kernel(counts, owner_ref, slot_ref, proj_ref, high_ref, low_ref, marks_ref, counter):
    count = counts[0]
    n_sets = len(partners(count))
    groups = 4 * ((n_sets + 3) // 4)
    own = lax.axis_index("gx")
    for g in range(groups):
        counter[g] = 0
    places = []
    for n in range(owner_ref.shape[-1]):
        if count == window:
            group = lax.bitwise_xor(owner_ref[0, 0, n], own)
        else:
            turn = lax.rem(owner_ref[0, 0, n] - own + count, count)
            group = turn if n_sets == count else jnp.where(
                turn < window, turn, turn - (count - n_sets)
            )
        taken = counter[group]
        counter[group] = taken + 1
        places.append(group * window + taken)
    tile = tile_rows(proj_ref[...], False)
    tile_high = tile.astype(jnp.bfloat16).astype(f32)
    tile_low = tile - tile_high
    block_of_lane = lane((8, 128)) // 8
    quarter = lane((8, 128)) // 32
    for s in range(groups // 4):
        labels = jnp.full((8, 128), -1.0, f32)
        for n, place in enumerate(places):
            labels = jnp.where(
                block_of_lane == place - 16 * s, slot_ref[0, 0, n].astype(f32), labels
            )
        for t in range(4):
            chosen = []
            for place in places:
                here = block_of_lane == lax.rem(place + 4 * t, 16)
                chosen.append(here if groups == 4 else here & (place // 16 == s))
            for ref, part in ((high_ref, tile_high), (low_ref, tile_low)):
                rows = [jnp.where(here, part, 0.0) for here in chosen]
                ref[4 * s + t] = jnp.concatenate(rows, axis=0).astype(jnp.bfloat16)
        for r in range(min(4, n_sets - 4 * s)):
            marks = labels
            for t in range(1, 4):
                marks = jnp.where(quarter == (r + t) % 4, pltpu.roll(labels, 32 * t, 1), marks)
            marks_ref[4 * s + r] = marks


def lamb_kernel(counts, n_faces, proj_smem, proj_ref, high_ref, low_ref, marks_ref, les_ref, *refs):
    face_refs, out_refs = refs[:n_faces], refs[n_faces:]
    halos = load_faces(face_refs, counts, 0, 4)

    def speeds(state):
        inverse = 1.0 / (state[0] + 1.0)
        return [state[c] * inverse for c in (1, 2, 3)]

    velocity = speeds([les_ref[c] for c in range(4)])
    outer = [(speeds(before), speeds(after)) for before, after in halos]

    def slope(c, axis):
        return 0.5 * (
            shifted(velocity[c], axis, 1, outer[axis][1][c])
            - shifted(velocity[c], axis, -1, outer[axis][0][c])
        )

    vort = [slope(2, 1) - slope(1, 2), slope(0, 2) - slope(2, 0), slope(1, 0) - slope(0, 1)]
    lamb = [
        vort[1] * velocity[2] - vort[2] * velocity[1],
        vort[2] * velocity[0] - vort[0] * velocity[2],
        vort[0] * velocity[1] - vort[1] * velocity[0],
    ]
    proj = proj_ref[...]
    blocks = []
    for field in lamb:
        along_y = proj[:, 0:1][None] * field[:, 0:1, :]
        for b in range(1, 8):
            along_y = along_y + proj[:, b : b + 1][None] * field[:, b : b + 1, :]
        for i in range(8):
            plane = proj_smem[i, 0] * along_y[0]
            for a in range(1, 8):
                plane = plane + proj_smem[i, a] * along_y[a]
            blocks.append(plane)

    quarter = lane((8, 128)) // 32
    data = [
        jnp.concatenate([blocks[4 * q + t] for q in range(6)], axis=0) for t in range(4)
    ]
    for s in range((len(out_refs) + 3) // 4):
        products = [
            dot3(data[t], (high_ref[4 * s + t], low_ref[4 * s + t])) for t in range(4)
        ]
        for r in range(min(4, len(out_refs) - 4 * s)):
            out = out_refs[4 * s + r]
            for q in range(6):
                packed = products[0][8 * q : 8 * q + 8]
                for t in range(1, 4):
                    packed = jnp.where(
                        quarter == (r + t) % 4, products[t][8 * q : 8 * q + 8], packed
                    )
                out[q] = packed
            out[6] = marks_ref[4 * s + r]


def first_kernel(
    counts, n_faces, deriv_ref, high_ref, low_ref, les_ref, wave_ref, mean_ref, *refs
):
    face_refs, (section_ref, rate_ref) = refs[:n_faces], refs[n_faces:]
    state = read_all(les_ref)
    rate = les_rate(state, load_faces(face_refs, counts, 0, 5))
    for c in range(5):
        section_ref[c] = state[c] + rate[c]
    rate = acoustic_rate(
        read_all(wave_ref), read_all(mean_ref), load_faces(face_refs, counts, 5, 9),
        deriv_ref[...], (high_ref[...], low_ref[...]),
    )
    for c in range(4):
        rate_ref[c] = rate[c]


def source_kernel(counts, wave_ref, rate_ref, section_ref, *refs):
    n_pieces = len(partners(counts[0]))
    pieces, refs = refs[:n_pieces][::-1], refs[n_pieces:]
    (source_ref, middle_ref, carry_ref), face_refs = refs[:3], refs[3:]
    quarter = lane((8, 128)) // 32
    slot_of_row = sublane((128, 128)) // 8
    same_node = lax.rem(sublane((128, 128)), 8) == lax.rem(lane((128, 128)), 8)
    sums = [None] * 24
    for s in range((n_pieces + 3) // 4):
        count = min(4, n_pieces - 4 * s)

        def gathered(q, t):
            value = jnp.full((8, 128), -1.0 if q == 6 else 0.0, f32)
            for r in range(count):
                value = jnp.where(quarter == (r + t) % 4, pieces[4 * s + r][q], value)
            return value

        for t in range(4):
            marks = gathered(6, t)[0:1].astype(jnp.int32)
            chosen = ((slot_of_row == marks) & same_node).astype(f32).astype(jnp.bfloat16)
            data = jnp.concatenate([gathered(q, t) for q in range(6)], axis=0)
            high = data.astype(jnp.bfloat16)
            low = (data - high.astype(f32)).astype(jnp.bfloat16)
            dims = (((1,), (1,)), ((), ()))
            moved = lax.dot_general(high, chosen, dims, preferred_element_type=f32)
            moved = moved + lax.dot_general(low, chosen, dims, preferred_element_type=f32)
            for q in range(6):
                part = moved[8 * q : 8 * q + 8]
                k = 4 * q + t
                sums[k] = part if sums[k] is None else sums[k] + part
    source = [jnp.stack(sums[8 * c : 8 * c + 8], axis=0) for c in range(3)]
    middle = []
    for c in range(4):
        rate = rate_ref[c]
        if c:
            source_ref[c - 1] = source[c - 1]
            rate = rate + source[c - 1]
        middle.append(wave_ref[c] + acoustic_step * rate)
        middle_ref[c] = middle[c]
        carry = wave_ref[c] + middle[c]
        carry_ref[c] = carry + acoustic_step * source[c - 1] if c else carry
    store_faces(read_all(section_ref) + middle, face_refs, counts)


def inner_kernel(
    deriv_ref, high_ref, low_ref, les_ref, section_ref, middle_ref, carry_ref, mean_ref,
    les_base_ref, wave_base_ref,
):
    section = read_all(section_ref)
    rate = les_rate(section, None)
    for c in range(5):
        les_base_ref[c] = 0.5 * ((les_ref[c] + section[c]) + rate[c])
    rate = acoustic_rate(
        read_all(middle_ref), read_all(mean_ref), None,
        deriv_ref[...], (high_ref[...], low_ref[...]),
    )
    for c in range(4):
        wave_base_ref[c] = 0.5 * (carry_ref[c] + acoustic_step * rate[c])


def last_kernel(counts, n_faces, source_ref, les_base_ref, wave_base_ref, mean_ref, *refs):
    face_refs, (les_out, source_out, wave_out, les_ref, wave_ref, sems) = (
        refs[:n_faces], refs[n_faces:],
    )
    copies = [
        pltpu.make_async_copy(source_ref, source_out, sems.at[0]),
        pltpu.make_async_copy(les_ref, les_out, sems.at[1]),
        pltpu.make_async_copy(wave_ref, wave_out, sems.at[2]),
    ]
    copies[0].start()
    layers = les_outer(load_faces(face_refs, counts, 0, 5))
    for c in range(5):
        part = [(0.5 * low[c], 0.5 * high[c]) for low, high in layers]
        for x, plane in enumerate(with_layers(les_base_ref[c], part)):
            les_ref[c, x] = plane
    copies[1].start()
    layers = acoustic_outer(read_all(mean_ref), load_faces(face_refs, counts, 5, 9))
    step = 0.5 * acoustic_step
    for c in range(4):
        part = [(step * low[c], step * high[c]) for low, high in layers]
        for x, plane in enumerate(with_layers(wave_base_ref[c], part)):
            wave_ref[c, x] = plane
    copies[2].start()
    for copy in copies:
        copy.wait()


VMEM = pl.BlockSpec(memory_space=pltpu.VMEM)
SMEM = pl.BlockSpec(memory_space=pltpu.SMEM)


ANY = pl.BlockSpec(memory_space=pl.ANY)


def call(kernel, in_specs, out_shapes, name, cost, scratch=(), room=24, out_spec=VMEM):
    return pl.pallas_call(
        kernel,
        in_specs=in_specs,
        out_specs=[out_spec] * len(out_shapes),
        out_shape=out_shapes,
        scratch_shapes=list(scratch),
        name=name,
        cost_estimate=pl.CostEstimate(flops=cost, bytes_accessed=800000, transcendentals=0),
        compiler_params=pltpu.CompilerParams(vmem_limit_bytes=room * 1024 * 1024),
    )


def local(counts, les, wave, mean, projection, owner, slot):
    shape = les.shape[1:]
    faces = face_shapes(counts, 9)
    n_faces = len(faces)
    like = lambda n: jax.ShapeDtypeStruct((n,) + shape, f32)

    table = derivative_matrix()
    deriv = jnp.asarray(table, f32)
    along_z = np.kron(np.eye(16), table.T).astype(np.float32)
    high = along_z.astype(jnp.bfloat16)
    low = (along_z - high.astype(np.float32)).astype(jnp.bfloat16)
    tables = (deriv, jnp.asarray(high), jnp.asarray(low))

    x_sets = len(pairings(counts[0]))
    sent = call(
        functools.partial(x_faces_kernel, counts),
        [ANY] * 2,
        faces[:x_sets],
        "x_faces",
        10000,
        [pltpu.SemaphoreType.DMA((x_sets, 2))],
        56,
    )(les, wave)
    sent += call(
        functools.partial(faces_kernel, counts), [VMEM] * 2, faces[x_sets:], "faces", 100000
    )(les, wave)
    got = exchange(sent, counts)

    sets = partners(counts[0])
    n_plans = 4 * ((len(sets) + 3) // 4)
    plan = call(
        functools.partial(plan_kernel, counts),
        [SMEM] * 2 + [VMEM],
        [jax.ShapeDtypeStruct((n_plans, 128, 128), jnp.bfloat16)] * 2
        + [jax.ShapeDtypeStruct((len(sets), 8, 128), f32)],
        "plan",
        4000000,
        [pltpu.SMEM((8,), jnp.int32)],
    )(owner, slot, projection)
    pieces = call(
        functools.partial(lamb_kernel, counts, n_faces),
        [SMEM] + [VMEM] * (5 + n_faces),
        [jax.ShapeDtypeStruct((7, 8, 128), f32)] * len(sets),
        "lamb_blocks",
        10000000,
    )(projection, projection, *plan, les, *got)
    moved = [None] * len(sets)
    for k in reversed(range(len(sets))):
        still = all(i == j for i, j in sets[k])
        moved[k] = pieces[k] if still else lax.ppermute(pieces[k], "gx", sets[k])
    section, rate = call(
        functools.partial(first_kernel, counts, n_faces),
        [VMEM] * (6 + n_faces),
        [like(5), like(4)],
        "first_rates",
        40000000,
    )(*tables, les, wave, mean, *got)

    source, middle, carry, *sent = call(
        functools.partial(source_kernel, counts),
        [VMEM] * (3 + len(moved)),
        [like(3), like(4), like(4)] + faces,
        "source_and_faces",
        10000000,
    )(wave, rate, section, *moved[::-1])
    got = exchange(sent, counts)
    les_base, wave_base = call(
        inner_kernel,
        [VMEM] * 8,
        [like(5), like(4)],
        "second_rates_inner",
        40000000,
    )(*tables, les, section, middle, carry, mean)
    return tuple(
        call(
            functools.partial(last_kernel, counts, n_faces),
            [VMEM] * (4 + n_faces),
            [like(5), like(3), like(4)],
            "second_rates_outer",
            4000000,
            [
                pltpu.VMEM(les.shape, f32),
                pltpu.VMEM(wave.shape, f32),
                pltpu.SemaphoreType.DMA((3,)),
            ],
            out_spec=ANY,
        )(source, les_base, wave_base, mean, *got)
    )


def solution(mesh):
    counts = tuple(mesh.shape[axis] for axis in axes)
    field = P(None, *axes)
    return jax.shard_map(
        functools.partial(local, counts),
        mesh=mesh,
        in_specs=(field, field, field, P(), P(*axes), P(*axes)),
        out_specs=(field, field, field),
        check_vma=False,
    )
```

```python
import functools

import jax
import jax.numpy as jnp
import numpy as np
from jax import lax
from jax.experimental import pallas as pl
from jax.experimental.pallas import tpu as pltpu
from jax.sharding import PartitionSpec as P

lobatto_points = np.array(
    [
        -1.0,
        -0.8717401485096066,
        -0.5917001814331423,
        -0.2092992179024789,
        0.2092992179024789,
        0.5917001814331423,
        0.8717401485096066,
        1.0,
    ]
)
flux_half = 0.08
gamma_less = 0.4
acoustic_step = 0.01
upwind_speed = 1.5
face_lift = 28.0
free_stream = (1.0, 0.0, 0.0, 0.0, 2.5)
axes = ("gx", "gy", "gz")
window = 4
f32 = jnp.float32


def derivative_matrix():
    points = lobatto_points
    products = [np.prod([points[i] - points[j] for j in range(8) if j != i]) for i in range(8)]
    matrix = np.zeros((8, 8))
    for i in range(8):
        for j in range(8):
            if j != i:
                matrix[i, j] = products[i] / (products[j] * (points[i] - points[j]))
        matrix[i, i] = -np.sum(matrix[i])
    return matrix


def sublane(shape):
    return lax.broadcasted_iota(jnp.int32, shape, len(shape) - 2)


def lane(shape):
    return lax.broadcasted_iota(jnp.int32, shape, len(shape) - 1)


def shifted(field, axis, step, outer):
    if axis == 0:
        if step == 1:
            return jnp.concatenate([field[1:], outer[None]], axis=0)
        return jnp.concatenate([outer[None], field[:-1]], axis=0)
    count = field.shape[axis]
    moved = pltpu.roll(field, count - 1 if step == 1 else 1, axis)
    edge = count - 1 if step == 1 else 0
    if axis == 1:
        return jnp.where(sublane(field.shape) == edge, outer[:, None, :], moved)
    columns = jnp.stack([outer[:, x : x + 1] for x in range(8)], axis=0)
    return jnp.where(lane(field.shape) == edge, columns, moved)


def fluid(state):
    density, mx, my, mz, energy = [s + r for s, r in zip(state, free_stream)]
    inverse = 1.0 / density
    momentum = (mx, my, mz)
    velocity = [m * inverse for m in momentum]
    pressure = gamma_less * (
        energy - 0.5 * (mx * velocity[0] + my * velocity[1] + mz * velocity[2])
    )
    return momentum, velocity, pressure, energy + pressure


def split_flux(state, parts, axis, sign):
    momentum, velocity, pressure, enthalpy = parts
    speed = velocity[axis]
    flux = [momentum[axis]]
    for c in range(3):
        term = momentum[c] * speed
        flux.append(term + pressure if c == axis else term)
    flux.append(enthalpy * speed)
    if sign > 0:
        return [flux_half * (s + f) for s, f in zip(state, flux)]
    return [flux_half * (s - f) for s, f in zip(state, flux)]


def les_rate(state, halos):
    parts = fluid(state)
    total = [-6.0 * flux_half * s for s in state]
    nothing = jnp.zeros((8, 128), f32)
    for axis in range(3):
        ahead = split_flux(state, parts, axis, -1)
        behind = split_flux(state, parts, axis, 1)
        ahead_outer = behind_outer = [nothing] * 5
        if halos is not None:
            before, after = halos[axis]
            ahead_outer = split_flux(after, fluid(after), axis, -1)
            behind_outer = split_flux(before, fluid(before), axis, 1)
        for c in range(5):
            total[c] = total[c] + (
                shifted(ahead[c], axis, 1, ahead_outer[c])
                + shifted(behind[c], axis, -1, behind_outer[c])
            )
    return total


def les_outer(halos):
    return [
        (
            split_flux(before, fluid(before), axis, 1),
            split_flux(after, fluid(after), axis, -1),
        )
        for axis, (before, after) in enumerate(halos)
    ]


def with_layers(field, layers):
    (x0, x1), (y0, y1), (z0, z1) = layers
    row, column = sublane((8, 128)), lane((8, 128))
    planes = []
    for x in range(8):
        plane = field[x]
        if x == 0:
            plane = plane + x0
        if x == 7:
            plane = plane + x1
        plane = plane + jnp.where(
            row == 0, y0[x : x + 1], jnp.where(row == 7, y1[x : x + 1], 0.0)
        )
        plane = plane + jnp.where(
            column == 0, z0[:, x : x + 1], jnp.where(column == 127, z1[:, x : x + 1], 0.0)
        )
        planes.append(plane)
    return planes


def wave_flux(state, mean, axis):
    speed = mean[axis]
    pressure = state[0]
    rows = [speed * pressure + state[1 + axis]]
    for c in range(3):
        term = speed * state[1 + c]
        rows.append(term + pressure if c == axis else term)
    return rows


def dot3(left, right):
    high = left.astype(jnp.bfloat16)
    low = (left - high.astype(f32)).astype(jnp.bfloat16)
    dot = functools.partial(jnp.dot, preferred_element_type=f32)
    return dot(high, right[0]) + (dot(low, right[0]) + dot(high, right[1]))


def acoustic_rate(state, mean, halos, deriv, along_z):
    shape = state[0].shape
    table = derivative_matrix()
    flux = wave_flux(state, mean, 0)
    if halos is None:
        halos = [([jnp.zeros((8, 128), f32)] * 4,) * 2] * 3
    before, after = halos[0]
    low_mean, high_mean = [m[0] for m in mean], [m[7] for m in mean]
    low_jump = [b - s[0] for b, s in zip(before, state)]
    high_jump = [a - s[7] for a, s in zip(after, state)]
    low_flux = wave_flux(low_jump, low_mean, 0)
    high_flux = wave_flux(high_jump, high_mean, 0)
    half, lift = 0.5 * face_lift, 0.5 * face_lift * upwind_speed
    total = []
    for c in range(4):
        planes = []
        for i in range(8):
            plane = -float(table[i, 0]) * flux[c][0]
            for a in range(1, 8):
                if abs(table[i, a]) > 1e-12:
                    plane = plane - float(table[i, a]) * flux[c][a]
            if i == 0:
                plane = plane + (half * low_flux[c] + lift * low_jump[c])
            if i == 7:
                plane = plane - (half * high_flux[c] - lift * high_jump[c])
            planes.append(plane)
        total.append(jnp.stack(planes, axis=0))
    flux = wave_flux(state, mean, 1)
    before, after = halos[1]
    row = sublane(shape)
    sign = jnp.where(row == 0, half, jnp.where(row == 7, -half, 0.0))
    jump = [
        jnp.where(row == 0, b[:, None, :], jnp.where(row == 7, a[:, None, :], s)) - s
        for s, b, a in zip(state, before, after)
    ]
    jump_flux = wave_flux(jump, mean, 1)
    for c in range(4):
        change = lift * jump[c] + sign * jump_flux[c]
        for b in range(8):
            change = change - deriv[:, b : b + 1][None] * flux[c][:, b : b + 1, :]
        total[c] = total[c] + change
    flux = wave_flux(state, mean, 2)
    before, after = halos[2]
    column = lane(shape)
    place = lax.rem(column, 8)
    sign = jnp.where(place == 0, half, jnp.where(place == 7, -half, 0.0))
    jump = [
        jnp.where(
            place == 0,
            shifted(s, 2, -1, b),
            jnp.where(place == 7, shifted(s, 2, 1, a), s),
        )
        - s
        for s, b, a in zip(state, before, after)
    ]
    jump_flux = wave_flux(jump, mean, 2)
    for c in range(4):
        slope = dot3(flux[c].reshape(64, 128), along_z).reshape(shape)
        total[c] = total[c] + (lift * jump[c] + sign * jump_flux[c] - slope)
    return total


def acoustic_outer(mean, halos):
    half, lift = 0.5 * face_lift, 0.5 * face_lift * upwind_speed
    layers = []
    for axis, (before, after) in enumerate(halos):
        if axis == 0:
            low, high = [m[0] for m in mean], [m[7] for m in mean]
        elif axis == 1:
            low, high = [m[:, 0, :] for m in mean], [m[:, 7, :] for m in mean]
        else:
            low, high = [z_layer(m, 0) for m in mean], [z_layer(m, 127) for m in mean]
        low_flux = wave_flux(before, low, axis)
        high_flux = wave_flux(after, high, axis)
        layers.append(
            (
                [half * f + lift * b for f, b in zip(low_flux, before)],
                [lift * a - half * f for f, a in zip(high_flux, after)],
            )
        )
    return layers


def tile_rows(matrix, transposed):
    spread = (lax.rem(lane((8, 128)), 8) == sublane((8, 128))).astype(f32)
    contract = ((1,), (0,)) if transposed else ((0,), (0,))
    return lax.dot_general(
        matrix, spread, (contract, ((), ())),
        precision=lax.Precision.HIGHEST, preferred_element_type=f32,
    )


def pairings(count):
    sets = []
    for first in (0, 1):
        pairs = [(i, i + 1) for i in range(first, count - 1, 2)]
        if pairs:
            sets.append(pairs)
    return sets


def routes(counts):
    places = [(x, y, z) for x in range(counts[0]) for y in range(counts[1]) for z in range(counts[2])]
    number = {place: n for n, place in enumerate(places)}
    found = []
    for axis in range(3):
        for pairs in pairings(counts[axis]):
            swap = dict(pairs + [(j, i) for i, j in pairs])
            alone = [i for i in range(counts[axis]) if i not in swap]
            spare = 0 if axis else 2
            route = []
            for place in places:
                other = list(place)
                if place[axis] in swap:
                    other[axis] = swap[place[axis]]
                elif axis == 0 and len(alone) == 2:
                    other[axis] = sum(alone) - place[axis]
                elif counts[spare] % 2 == 0:
                    other[spare] = place[spare] ^ 1
                route.append((number[place], number[tuple(other)]))
            found.append(route)
    return found


def z_layer(field, at):
    packed = jnp.zeros((8, 128), f32)
    column = lane((8, 128))
    for x in range(8):
        packed = jnp.where(column == x, field[x][:, at : at + 1], packed)
    return packed


def store_faces(fields, out_refs, counts, which=(0, 1, 2)):
    at = 0
    for axis in which:
        even = lax.rem(lax.axis_index(axes[axis]), 2) == 0
        sets = len(pairings(counts[axis]))
        for c, field in enumerate(fields):
            if axis == 0:
                low, high = field[0], field[7]
            elif axis == 1:
                low, high = field[:, 0, :], field[:, 7, :]
            else:
                low, high = z_layer(field, 0), z_layer(field, 127)
            for s in range(sets):
                out_refs[at + s][c] = jnp.where(even == (s == 0), high, low)
        at += sets


def sending_order(counts):
    where = [(axis, s) for axis in range(3) for s in range(len(pairings(counts[axis])))]
    wanted = ((0, 1), (2, 1), (2, 0), (1, 1), (1, 0), (0, 0))
    return [where.index(p) for p in wanted if p in where]


def load_faces(sent_refs, counts, first, last):
    in_refs = [None] * len(sent_refs)
    for ref, at in zip(sent_refs, sending_order(counts)):
        in_refs[at] = ref
    halos = []
    at = 0
    for axis in range(3):
        even = lax.rem(lax.axis_index(axes[axis]), 2) == 0
        sets = len(pairings(counts[axis]))
        got = [[in_refs[at + s][c] for c in range(first, last)] for s in range(sets)]
        while len(got) < 2:
            got.append([jnp.zeros((8, 128), f32)] * (last - first))
        place = lax.axis_index(axes[axis])
        before = [
            jnp.where(place == 0, 0.0, jnp.where(even, b, a)) for a, b in zip(*got)
        ]
        after = [
            jnp.where(place == counts[axis] - 1, 0.0, jnp.where(even, a, b))
            for a, b in zip(*got)
        ]
        halos.append((before, after))
        at += sets
    return halos


def face_shapes(counts, width):
    total = sum(len(pairings(count)) for count in counts)
    return [jax.ShapeDtypeStruct((width, 8, 128), f32)] * total


def exchange(faces, counts):
    ways = routes(counts)
    return [lax.ppermute(faces[at], axes, ways[at]) for at in sending_order(counts)]


def read_all(ref):
    return [ref[c] for c in range(ref.shape[0])]


def x_faces_kernel(counts, les_hbm, wave_hbm, *refs):
    out_refs, sems = refs[:-1], refs[-1]
    odd = lax.rem(lax.axis_index("gx"), 2)
    copies = []
    for s, out in enumerate(out_refs):
        plane = 7 * (1 - odd) if s == 0 else 7 * odd
        for k, (first, source) in enumerate(((0, les_hbm), (5, wave_hbm))):
            copies.append(
                pltpu.make_async_copy(
                    source.at[:, plane], out.at[first : first + source.shape[0]], sems.at[s, k]
                )
            )
    for copy in copies:
        copy.start()
    for copy in copies:
        copy.wait()


def faces_kernel(counts, les_ref, wave_ref, *out_refs):
    store_faces(read_all(les_ref) + read_all(wave_ref), out_refs, counts, (1, 2))


def partners(count):
    if count == window:
        return [[(i, i ^ mask) for i in range(count)] for mask in range(count)]
    turns = sorted({d % count for d in range(1 - window, window)})
    return [[(i, (i + turn) % count) for i in range(count)] for turn in turns]


def plan_kernel(counts, owner_ref, slot_ref, order_ref, marks_ref, counter):
    count = counts[0]
    n_sets = len(partners(count))
    groups = 4 * ((n_sets + 3) // 4)
    own = lax.axis_index("gx")
    for g in range(groups):
        counter[g] = 0
    places = []
    for n in range(owner_ref.shape[-1]):
        if count == window:
            group = lax.bitwise_xor(owner_ref[0, 0, n], own)
        else:
            turn = lax.rem(owner_ref[0, 0, n] - own + count, count)
            group = turn if n_sets == count else jnp.where(
                turn < window, turn, turn - (count - n_sets)
            )
        taken = counter[group]
        counter[group] = taken + 1
        places.append(group * window + taken)
    column = lane((8, 128))
    quarter = column // 32
    for s in range(groups // 4):
        labels = jnp.full((8, 128), -1.0, f32)
        order = column
        for n, place in enumerate(places):
            here = column // 8 == place - 16 * s
            labels = jnp.where(here, slot_ref[0, 0, n].astype(f32), labels)
            order = jnp.where(here, 8 * n + lax.rem(column, 8), order)
        for t in range(4):
            order_ref[4 * s + t] = pltpu.roll(order, 32 * t, 1) if t else order
        for r in range(min(4, n_sets - 4 * s)):
            marks = labels
            for t in range(1, 4):
                marks = jnp.where(quarter == (r + t) % 4, pltpu.roll(labels, 32 * t, 1), marks)
            marks_ref[4 * s + r] = marks


def lamb_kernel(counts, n_faces, proj_smem, proj_ref, order_ref, marks_ref, les_ref, *refs):
    face_refs, out_refs = refs[:n_faces], refs[n_faces:]
    halos = load_faces(face_refs, counts, 0, 4)

    def speeds(state):
        inverse = 1.0 / (state[0] + 1.0)
        return [state[c] * inverse for c in (1, 2, 3)]

    velocity = speeds([les_ref[c] for c in range(4)])
    outer = [(speeds(before), speeds(after)) for before, after in halos]

    def slope(c, axis):
        return 0.5 * (
            shifted(velocity[c], axis, 1, outer[axis][1][c])
            - shifted(velocity[c], axis, -1, outer[axis][0][c])
        )

    vort = [slope(2, 1) - slope(1, 2), slope(0, 2) - slope(2, 0), slope(1, 0) - slope(0, 1)]
    lamb = [
        vort[1] * velocity[2] - vort[2] * velocity[1],
        vort[2] * velocity[0] - vort[0] * velocity[2],
        vort[0] * velocity[1] - vort[1] * velocity[0],
    ]
    proj = proj_ref[...]
    blocks = []
    for field in lamb:
        along_y = proj[:, 0:1][None] * field[:, 0:1, :]
        for b in range(1, 8):
            along_y = along_y + proj[:, b : b + 1][None] * field[:, b : b + 1, :]
        for i in range(8):
            plane = proj_smem[i, 0] * along_y[0]
            for a in range(1, 8):
                plane = plane + proj_smem[i, a] * along_y[a]
            blocks.append(plane)

    quarter = lane((8, 128)) // 32
    for s in range((len(out_refs) + 3) // 4):
        ordered = [
            jnp.take_along_axis(block, order_ref[4 * s + k % 4], axis=1)
            for k, block in enumerate(blocks)
        ]
        for r in range(min(4, len(out_refs) - 4 * s)):
            out = out_refs[4 * s + r]
            for q in range(6):
                packed = ordered[4 * q]
                for t in range(1, 4):
                    packed = jnp.where(quarter == (r + t) % 4, ordered[4 * q + t], packed)
                out[q] = packed
            out[6] = marks_ref[4 * s + r]


def first_kernel(
    counts, n_faces, deriv_ref, high_ref, low_ref, les_ref, wave_ref, mean_ref, *refs
):
    face_refs, (section_ref, rate_ref) = refs[:n_faces], refs[n_faces:]
    state = read_all(les_ref)
    rate = les_rate(state, load_faces(face_refs, counts, 0, 5))
    for c in range(5):
        section_ref[c] = state[c] + rate[c]
    rate = acoustic_rate(
        read_all(wave_ref), read_all(mean_ref), load_faces(face_refs, counts, 5, 9),
        deriv_ref[...], (high_ref[...], low_ref[...]),
    )
    for c in range(4):
        rate_ref[c] = rate[c]


def source_kernel(counts, proj_ref, wave_ref, rate_ref, section_ref, *refs):
    n_pieces = len(partners(counts[0]))
    pieces, refs = refs[:n_pieces][::-1], refs[n_pieces:]
    (source_ref, middle_ref, carry_ref), face_refs = refs[:3], refs[3:]
    quarter = lane((8, 128)) // 32
    tile = tile_rows(proj_ref[...], True)
    tile_high = tile.astype(jnp.bfloat16).astype(f32)
    tile_low = tile - tile_high
    sums = [None] * 24
    for s in range((n_pieces + 3) // 4):
        count = min(4, n_pieces - 4 * s)

        def gathered(q, t):
            value = jnp.full((8, 128), -1.0 if q == 6 else 0.0, f32)
            for r in range(count):
                value = jnp.where(quarter == (r + t) % 4, pieces[4 * s + r][q], value)
            return value

        for t in range(4):
            marks = gathered(6, t).astype(jnp.int32)
            here = [marks == slot for slot in range(16)]
            chosen_high, chosen_low = [
                jnp.concatenate([jnp.where(h, part, 0.0) for h in here], axis=0).astype(
                    jnp.bfloat16
                )
                for part in (tile_high, tile_low)
            ]
            data = jnp.concatenate([gathered(q, t) for q in range(6)], axis=0)
            high = data.astype(jnp.bfloat16)
            low = (data - high.astype(f32)).astype(jnp.bfloat16)
            dims = (((1,), (1,)), ((), ()))
            dot = functools.partial(
                lax.dot_general, dimension_numbers=dims, preferred_element_type=f32
            )
            moved = dot(high, chosen_high) + (dot(low, chosen_high) + dot(high, chosen_low))
            for q in range(6):
                part = moved[8 * q : 8 * q + 8]
                k = 4 * q + t
                sums[k] = part if sums[k] is None else sums[k] + part
    source = [jnp.stack(sums[8 * c : 8 * c + 8], axis=0) for c in range(3)]
    middle = []
    for c in range(4):
        rate = rate_ref[c]
        if c:
            source_ref[c - 1] = source[c - 1]
            rate = rate + source[c - 1]
        middle.append(wave_ref[c] + acoustic_step * rate)
        middle_ref[c] = middle[c]
        carry = wave_ref[c] + middle[c]
        carry_ref[c] = carry + acoustic_step * source[c - 1] if c else carry
    store_faces(read_all(section_ref) + middle, face_refs, counts)


def inner_kernel(
    deriv_ref, high_ref, low_ref, les_ref, section_ref, middle_ref, carry_ref, mean_ref,
    les_base_ref, wave_base_ref,
):
    section = read_all(section_ref)
    rate = les_rate(section, None)
    for c in range(5):
        les_base_ref[c] = 0.5 * ((les_ref[c] + section[c]) + rate[c])
    rate = acoustic_rate(
        read_all(middle_ref), read_all(mean_ref), None,
        deriv_ref[...], (high_ref[...], low_ref[...]),
    )
    for c in range(4):
        wave_base_ref[c] = 0.5 * (carry_ref[c] + acoustic_step * rate[c])


def last_kernel(counts, n_faces, source_ref, les_base_ref, wave_base_ref, mean_ref, *refs):
    face_refs, (les_out, source_out, wave_out, les_ref, wave_ref, sems) = (
        refs[:n_faces], refs[n_faces:],
    )
    copies = []

    def send(source, target):
        copies.append(pltpu.make_async_copy(source, target, sems.at[len(copies)]))
        copies[-1].start()

    send(source_ref, source_out)
    layers = les_outer(load_faces(face_refs, counts, 0, 5))
    for c in range(5):
        part = [(0.5 * low[c], 0.5 * high[c]) for low, high in layers]
        for x, plane in enumerate(with_layers(les_base_ref[c], part)):
            les_ref[c, x] = plane
        send(les_ref.at[c], les_out.at[c])
    layers = acoustic_outer(read_all(mean_ref), load_faces(face_refs, counts, 5, 9))
    step = 0.5 * acoustic_step
    for c in range(4):
        part = [(step * low[c], step * high[c]) for low, high in layers]
        for x, plane in enumerate(with_layers(wave_base_ref[c], part)):
            wave_ref[c, x] = plane
        send(wave_ref.at[c], wave_out.at[c])
    for copy in copies:
        copy.wait()


VMEM = pl.BlockSpec(memory_space=pltpu.VMEM)
SMEM = pl.BlockSpec(memory_space=pltpu.SMEM)


ANY = pl.BlockSpec(memory_space=pl.ANY)


def call(kernel, in_specs, out_shapes, name, cost, scratch=(), room=24, out_spec=VMEM):
    return pl.pallas_call(
        kernel,
        in_specs=in_specs,
        out_specs=[out_spec] * len(out_shapes),
        out_shape=out_shapes,
        scratch_shapes=list(scratch),
        name=name,
        cost_estimate=pl.CostEstimate(flops=cost, bytes_accessed=800000, transcendentals=0),
        compiler_params=pltpu.CompilerParams(vmem_limit_bytes=room * 1024 * 1024),
    )


def local(counts, les, wave, mean, projection, owner, slot):
    shape = les.shape[1:]
    faces = face_shapes(counts, 9)
    n_faces = len(faces)
    like = lambda n: jax.ShapeDtypeStruct((n,) + shape, f32)

    table = derivative_matrix()
    deriv = jnp.asarray(table, f32)
    along_z = np.kron(np.eye(16), table.T).astype(np.float32)
    high = along_z.astype(jnp.bfloat16)
    low = (along_z - high.astype(np.float32)).astype(jnp.bfloat16)
    tables = (deriv, jnp.asarray(high), jnp.asarray(low))

    x_sets = len(pairings(counts[0]))
    sent = call(
        functools.partial(x_faces_kernel, counts),
        [ANY] * 2,
        faces[:x_sets],
        "x_faces",
        10000,
        [pltpu.SemaphoreType.DMA((x_sets, 2))],
        56,
    )(les, wave)
    sent += call(
        functools.partial(faces_kernel, counts), [VMEM] * 2, faces[x_sets:], "faces", 100000
    )(les, wave)
    got = exchange(sent, counts)

    sets = partners(counts[0])
    n_plans = 4 * ((len(sets) + 3) // 4)
    plan = call(
        functools.partial(plan_kernel, counts),
        [SMEM] * 2,
        [
            jax.ShapeDtypeStruct((n_plans, 8, 128), jnp.int32),
            jax.ShapeDtypeStruct((len(sets), 8, 128), f32),
        ],
        "plan",
        4000000,
        [pltpu.SMEM((8,), jnp.int32)],
    )(owner, slot)
    pieces = call(
        functools.partial(lamb_kernel, counts, n_faces),
        [SMEM] + [VMEM] * (4 + n_faces),
        [jax.ShapeDtypeStruct((7, 8, 128), f32)] * len(sets),
        "lamb_blocks",
        10000000,
    )(projection, projection, *plan, les, *got)
    moved = [None] * len(sets)
    for k in reversed(range(len(sets))):
        still = all(i == j for i, j in sets[k])
        moved[k] = pieces[k] if still else lax.ppermute(pieces[k], "gx", sets[k])
    section, rate = call(
        functools.partial(first_kernel, counts, n_faces),
        [VMEM] * (6 + n_faces),
        [like(5), like(4)],
        "first_rates",
        40000000,
    )(*tables, les, wave, mean, *got)

    source, middle, carry, *sent = call(
        functools.partial(source_kernel, counts),
        [VMEM] * (4 + len(moved)),
        [like(3), like(4), like(4)] + faces,
        "source_and_faces",
        10000000,
    )(projection, wave, rate, section, *moved[::-1])
    got = exchange(sent, counts)
    les_base, wave_base = call(
        inner_kernel,
        [VMEM] * 8,
        [like(5), like(4)],
        "second_rates_inner",
        40000000,
    )(*tables, les, section, middle, carry, mean)
    return tuple(
        call(
            functools.partial(last_kernel, counts, n_faces),
            [VMEM] * (4 + n_faces),
            [like(5), like(3), like(4)],
            "second_rates_outer",
            4000000,
            [
                pltpu.VMEM(les.shape, f32),
                pltpu.VMEM(wave.shape, f32),
                pltpu.SemaphoreType.DMA((10,)),
            ],
            out_spec=ANY,
        )(source, les_base, wave_base, mean, *got)
    )


def solution(mesh):
    counts = tuple(mesh.shape[axis] for axis in axes)
    field = P(None, *axes)
    return jax.shard_map(
        functools.partial(local, counts),
        mesh=mesh,
        in_specs=(field, field, field, P(), P(*axes), P(*axes)),
        out_specs=(field, field, field),
        check_vma=False,
    )
```

```python
import functools

import jax
import jax.numpy as jnp
import numpy as np
from jax import lax
from jax.experimental import pallas as pl
from jax.experimental.pallas import tpu as pltpu
from jax.sharding import PartitionSpec as P

lobatto_points = np.array(
    [
        -1.0,
        -0.8717401485096066,
        -0.5917001814331423,
        -0.2092992179024789,
        0.2092992179024789,
        0.5917001814331423,
        0.8717401485096066,
        1.0,
    ]
)
flux_half = 0.08
gamma_less = 0.4
acoustic_step = 0.01
upwind_speed = 1.5
face_lift = 28.0
free_stream = (1.0, 0.0, 0.0, 0.0, 2.5)
axes = ("gx", "gy", "gz")
window = 4
f32 = jnp.float32


def derivative_matrix():
    points = lobatto_points
    products = [np.prod([points[i] - points[j] for j in range(8) if j != i]) for i in range(8)]
    matrix = np.zeros((8, 8))
    for i in range(8):
        for j in range(8):
            if j != i:
                matrix[i, j] = products[i] / (products[j] * (points[i] - points[j]))
        matrix[i, i] = -np.sum(matrix[i])
    return matrix


def sublane(shape):
    return lax.broadcasted_iota(jnp.int32, shape, len(shape) - 2)


def lane(shape):
    return lax.broadcasted_iota(jnp.int32, shape, len(shape) - 1)


def shifted(field, axis, step, outer):
    if axis == 0:
        if step == 1:
            return jnp.concatenate([field[1:], outer[None]], axis=0)
        return jnp.concatenate([outer[None], field[:-1]], axis=0)
    count = field.shape[axis]
    moved = pltpu.roll(field, count - 1 if step == 1 else 1, axis)
    edge = count - 1 if step == 1 else 0
    if axis == 1:
        return jnp.where(sublane(field.shape) == edge, outer[:, None, :], moved)
    columns = jnp.stack([outer[:, x : x + 1] for x in range(8)], axis=0)
    return jnp.where(lane(field.shape) == edge, columns, moved)


def fluid(state):
    density, mx, my, mz, energy = [s + r for s, r in zip(state, free_stream)]
    inverse = 1.0 / density
    momentum = (mx, my, mz)
    velocity = [m * inverse for m in momentum]
    pressure = gamma_less * (
        energy - 0.5 * (mx * velocity[0] + my * velocity[1] + mz * velocity[2])
    )
    return momentum, velocity, pressure, energy + pressure


def split_flux(state, parts, axis, sign):
    momentum, velocity, pressure, enthalpy = parts
    speed = velocity[axis]
    flux = [momentum[axis]]
    for c in range(3):
        term = momentum[c] * speed
        flux.append(term + pressure if c == axis else term)
    flux.append(enthalpy * speed)
    if sign > 0:
        return [flux_half * (s + f) for s, f in zip(state, flux)]
    return [flux_half * (s - f) for s, f in zip(state, flux)]


def les_rate(state, halos):
    parts = fluid(state)
    total = [-6.0 * flux_half * s for s in state]
    nothing = jnp.zeros((8, 128), f32)
    for axis in range(3):
        ahead = split_flux(state, parts, axis, -1)
        behind = split_flux(state, parts, axis, 1)
        ahead_outer = behind_outer = [nothing] * 5
        if halos is not None:
            before, after = halos[axis]
            ahead_outer = split_flux(after, fluid(after), axis, -1)
            behind_outer = split_flux(before, fluid(before), axis, 1)
        for c in range(5):
            total[c] = total[c] + (
                shifted(ahead[c], axis, 1, ahead_outer[c])
                + shifted(behind[c], axis, -1, behind_outer[c])
            )
    return total


def les_outer(halos):
    return [
        (
            split_flux(before, fluid(before), axis, 1),
            split_flux(after, fluid(after), axis, -1),
        )
        for axis, (before, after) in enumerate(halos)
    ]


def with_layers(field, layers):
    (x0, x1), (y0, y1), (z0, z1) = layers
    row, column = sublane((8, 128)), lane((8, 128))
    planes = []
    for x in range(8):
        plane = field[x]
        if x == 0:
            plane = plane + x0
        if x == 7:
            plane = plane + x1
        plane = plane + jnp.where(
            row == 0, y0[x : x + 1], jnp.where(row == 7, y1[x : x + 1], 0.0)
        )
        plane = plane + jnp.where(
            column == 0, z0[:, x : x + 1], jnp.where(column == 127, z1[:, x : x + 1], 0.0)
        )
        planes.append(plane)
    return planes


def wave_flux(state, mean, axis):
    speed = mean[axis]
    pressure = state[0]
    rows = [speed * pressure + state[1 + axis]]
    for c in range(3):
        term = speed * state[1 + c]
        rows.append(term + pressure if c == axis else term)
    return rows


def dot3(left, right):
    high = left.astype(jnp.bfloat16)
    low = (left - high.astype(f32)).astype(jnp.bfloat16)
    dot = functools.partial(jnp.dot, preferred_element_type=f32)
    return dot(high, right[0]) + (dot(low, right[0]) + dot(high, right[1]))


def acoustic_rate(state, mean, halos, deriv, along_z):
    shape = state[0].shape
    table = derivative_matrix()
    flux = wave_flux(state, mean, 0)
    if halos is None:
        halos = [([jnp.zeros((8, 128), f32)] * 4,) * 2] * 3
    before, after = halos[0]
    low_mean, high_mean = [m[0] for m in mean], [m[7] for m in mean]
    low_jump = [b - s[0] for b, s in zip(before, state)]
    high_jump = [a - s[7] for a, s in zip(after, state)]
    low_flux = wave_flux(low_jump, low_mean, 0)
    high_flux = wave_flux(high_jump, high_mean, 0)
    half, lift = 0.5 * face_lift, 0.5 * face_lift * upwind_speed
    total = []
    for c in range(4):
        planes = []
        for i in range(8):
            plane = -float(table[i, 0]) * flux[c][0]
            for a in range(1, 8):
                if abs(table[i, a]) > 1e-12:
                    plane = plane - float(table[i, a]) * flux[c][a]
            if i == 0:
                plane = plane + (half * low_flux[c] + lift * low_jump[c])
            if i == 7:
                plane = plane - (half * high_flux[c] - lift * high_jump[c])
            planes.append(plane)
        total.append(jnp.stack(planes, axis=0))
    flux = wave_flux(state, mean, 1)
    before, after = halos[1]
    row = sublane(shape)
    sign = jnp.where(row == 0, half, jnp.where(row == 7, -half, 0.0))
    jump = [
        jnp.where(row == 0, b[:, None, :], jnp.where(row == 7, a[:, None, :], s)) - s
        for s, b, a in zip(state, before, after)
    ]
    jump_flux = wave_flux(jump, mean, 1)
    for c in range(4):
        change = lift * jump[c] + sign * jump_flux[c]
        for b in range(8):
            change = change - deriv[:, b : b + 1][None] * flux[c][:, b : b + 1, :]
        total[c] = total[c] + change
    flux = wave_flux(state, mean, 2)
    before, after = halos[2]
    column = lane(shape)
    place = lax.rem(column, 8)
    sign = jnp.where(place == 0, half, jnp.where(place == 7, -half, 0.0))
    jump = [
        jnp.where(
            place == 0,
            shifted(s, 2, -1, b),
            jnp.where(place == 7, shifted(s, 2, 1, a), s),
        )
        - s
        for s, b, a in zip(state, before, after)
    ]
    jump_flux = wave_flux(jump, mean, 2)
    for c in range(4):
        slope = dot3(flux[c].reshape(64, 128), along_z).reshape(shape)
        total[c] = total[c] + (lift * jump[c] + sign * jump_flux[c] - slope)
    return total


def acoustic_outer(mean, halos):
    half, lift = 0.5 * face_lift, 0.5 * face_lift * upwind_speed
    layers = []
    for axis, (before, after) in enumerate(halos):
        if axis == 0:
            low, high = [m[0] for m in mean], [m[7] for m in mean]
        elif axis == 1:
            low, high = [m[:, 0, :] for m in mean], [m[:, 7, :] for m in mean]
        else:
            low, high = [z_layer(m, 0) for m in mean], [z_layer(m, 127) for m in mean]
        low_flux = wave_flux(before, low, axis)
        high_flux = wave_flux(after, high, axis)
        layers.append(
            (
                [half * f + lift * b for f, b in zip(low_flux, before)],
                [lift * a - half * f for f, a in zip(high_flux, after)],
            )
        )
    return layers


def tile_rows(matrix, transposed):
    spread = (lax.rem(lane((8, 128)), 8) == sublane((8, 128))).astype(f32)
    contract = ((1,), (0,)) if transposed else ((0,), (0,))
    return lax.dot_general(
        matrix, spread, (contract, ((), ())),
        precision=lax.Precision.HIGHEST, preferred_element_type=f32,
    )


def pairings(count):
    sets = []
    for first in (0, 1):
        pairs = [(i, i + 1) for i in range(first, count - 1, 2)]
        if pairs:
            sets.append(pairs)
    return sets


def routes(counts):
    places = [(x, y, z) for x in range(counts[0]) for y in range(counts[1]) for z in range(counts[2])]
    number = {place: n for n, place in enumerate(places)}
    found = []
    for axis in range(3):
        for pairs in pairings(counts[axis]):
            swap = dict(pairs + [(j, i) for i, j in pairs])
            alone = [i for i in range(counts[axis]) if i not in swap]
            spare = 0 if axis else 2
            route = []
            for place in places:
                other = list(place)
                if place[axis] in swap:
                    other[axis] = swap[place[axis]]
                elif axis == 0 and len(alone) == 2:
                    other[axis] = sum(alone) - place[axis]
                elif counts[spare] % 2 == 0:
                    other[spare] = place[spare] ^ 1
                route.append((number[place], number[tuple(other)]))
            found.append(route)
    return found


def z_layer(field, at):
    packed = jnp.zeros((8, 128), f32)
    column = lane((8, 128))
    for x in range(8):
        packed = jnp.where(column == x, field[x][:, at : at + 1], packed)
    return packed


def store_faces(fields, out_refs, counts):
    at = 0
    for axis in range(3):
        even = lax.rem(lax.axis_index(axes[axis]), 2) == 0
        sets = len(pairings(counts[axis]))
        for c, field in enumerate(fields):
            if axis == 0:
                low, high = field[0], field[7]
            elif axis == 1:
                low, high = field[:, 0, :], field[:, 7, :]
            else:
                low, high = z_layer(field, 0), z_layer(field, 127)
            for s in range(sets):
                out_refs[at + s][c] = jnp.where(even == (s == 0), high, low)
        at += sets


def sending_order(counts):
    where = [(axis, s) for axis in range(3) for s in range(len(pairings(counts[axis])))]
    wanted = ((0, 1), (2, 1), (2, 0), (1, 1), (1, 0), (0, 0))
    return [where.index(p) for p in wanted if p in where]


def load_faces(sent_refs, counts, first, last):
    in_refs = [None] * len(sent_refs)
    for ref, at in zip(sent_refs, sending_order(counts)):
        in_refs[at] = ref
    halos = []
    at = 0
    for axis in range(3):
        even = lax.rem(lax.axis_index(axes[axis]), 2) == 0
        sets = len(pairings(counts[axis]))
        got = [[in_refs[at + s][c] for c in range(first, last)] for s in range(sets)]
        while len(got) < 2:
            got.append([jnp.zeros((8, 128), f32)] * (last - first))
        place = lax.axis_index(axes[axis])
        before = [
            jnp.where(place == 0, 0.0, jnp.where(even, b, a)) for a, b in zip(*got)
        ]
        after = [
            jnp.where(place == counts[axis] - 1, 0.0, jnp.where(even, a, b))
            for a, b in zip(*got)
        ]
        halos.append((before, after))
        at += sets
    return halos


def face_shapes(counts, width):
    total = sum(len(pairings(count)) for count in counts)
    return [jax.ShapeDtypeStruct((width, 8, 128), f32)] * total


def exchange(faces, counts):
    ways = routes(counts)
    return [lax.ppermute(faces[at], axes, ways[at]) for at in sending_order(counts)]


def read_all(ref):
    return [ref[c] for c in range(ref.shape[0])]


def load_kernel(counts, les_hbm, wave_hbm, les_ref, wave_ref, *refs):
    out_refs, sems = refs[:-1], refs[-1]
    copies = []
    for source, target in ((les_hbm, les_ref), (wave_hbm, wave_ref)):
        for c in range(source.shape[0]):
            copies.append(
                pltpu.make_async_copy(source.at[c], target.at[c], sems.at[len(copies)])
            )
    for copy in copies:
        copy.start()
    for n, copy in enumerate(copies):
        copy.wait()
        field = les_ref[n] if n < 5 else wave_ref[n - 5]
        store_faces([field], [ref.at[n : n + 1] for ref in out_refs], counts)


def partners(count):
    if count == window:
        return [[(i, i ^ mask) for i in range(count)] for mask in range(count)]
    turns = sorted({d % count for d in range(1 - window, window)})
    return [[(i, (i + turn) % count) for i in range(count)] for turn in turns]


def plan_kernel(counts, owner_ref, slot_ref, order_ref, marks_ref, counter):
    count = counts[0]
    n_sets = len(partners(count))
    groups = 4 * ((n_sets + 3) // 4)
    own = lax.axis_index("gx")
    for g in range(groups):
        counter[g] = 0
    places = []
    for n in range(owner_ref.shape[-1]):
        if count == window:
            group = lax.bitwise_xor(owner_ref[0, 0, n], own)
        else:
            turn = lax.rem(owner_ref[0, 0, n] - own + count, count)
            group = turn if n_sets == count else jnp.where(
                turn < window, turn, turn - (count - n_sets)
            )
        taken = counter[group]
        counter[group] = taken + 1
        places.append(group * window + taken)
    column = lane((8, 128))
    quarter = column // 32
    for s in range(groups // 4):
        labels = jnp.full((8, 128), -1.0, f32)
        order = column
        for n, place in enumerate(places):
            here = column // 8 == place - 16 * s
            labels = jnp.where(here, slot_ref[0, 0, n].astype(f32), labels)
            order = jnp.where(here, 8 * n + lax.rem(column, 8), order)
        for t in range(4):
            order_ref[4 * s + t] = pltpu.roll(order, 32 * t, 1) if t else order
        for r in range(min(4, n_sets - 4 * s)):
            marks = labels
            for t in range(1, 4):
                marks = jnp.where(quarter == (r + t) % 4, pltpu.roll(labels, 32 * t, 1), marks)
            marks_ref[4 * s + r] = marks


def lamb_kernel(counts, n_faces, proj_smem, proj_ref, order_ref, marks_ref, les_ref, *refs):
    face_refs, out_refs = refs[:n_faces], refs[n_faces:]
    halos = load_faces(face_refs, counts, 0, 4)

    def speeds(state):
        inverse = 1.0 / (state[0] + 1.0)
        return [state[c] * inverse for c in (1, 2, 3)]

    velocity = speeds([les_ref[c] for c in range(4)])
    outer = [(speeds(before), speeds(after)) for before, after in halos]

    def slope(c, axis):
        return 0.5 * (
            shifted(velocity[c], axis, 1, outer[axis][1][c])
            - shifted(velocity[c], axis, -1, outer[axis][0][c])
        )

    vort = [slope(2, 1) - slope(1, 2), slope(0, 2) - slope(2, 0), slope(1, 0) - slope(0, 1)]
    lamb = [
        vort[1] * velocity[2] - vort[2] * velocity[1],
        vort[2] * velocity[0] - vort[0] * velocity[2],
        vort[0] * velocity[1] - vort[1] * velocity[0],
    ]
    proj = proj_ref[...]
    blocks = []
    for field in lamb:
        along_y = proj[:, 0:1][None] * field[:, 0:1, :]
        for b in range(1, 8):
            along_y = along_y + proj[:, b : b + 1][None] * field[:, b : b + 1, :]
        for i in range(8):
            plane = proj_smem[i, 0] * along_y[0]
            for a in range(1, 8):
                plane = plane + proj_smem[i, a] * along_y[a]
            blocks.append(plane)

    quarter = lane((8, 128)) // 32
    for s in range((len(out_refs) + 3) // 4):
        ordered = [
            jnp.take_along_axis(block, order_ref[4 * s + k % 4], axis=1)
            for k, block in enumerate(blocks)
        ]
        for r in range(min(4, len(out_refs) - 4 * s)):
            out = out_refs[4 * s + r]
            for q in range(6):
                packed = ordered[4 * q]
                for t in range(1, 4):
                    packed = jnp.where(quarter == (r + t) % 4, ordered[4 * q + t], packed)
                out[q] = packed
            out[6] = marks_ref[4 * s + r]


def first_kernel(
    counts, n_faces, deriv_ref, high_ref, low_ref, les_ref, wave_ref, mean_ref, *refs
):
    face_refs, (section_ref, rate_ref) = refs[:n_faces], refs[n_faces:]
    state = read_all(les_ref)
    rate = les_rate(state, load_faces(face_refs, counts, 0, 5))
    for c in range(5):
        section_ref[c] = state[c] + rate[c]
    rate = acoustic_rate(
        read_all(wave_ref), read_all(mean_ref), load_faces(face_refs, counts, 5, 9),
        deriv_ref[...], (high_ref[...], low_ref[...]),
    )
    for c in range(4):
        rate_ref[c] = rate[c]


def source_kernel(counts, proj_ref, wave_ref, rate_ref, section_ref, *refs):
    n_pieces = len(partners(counts[0]))
    pieces, refs = refs[:n_pieces][::-1], refs[n_pieces:]
    (source_ref, middle_ref, carry_ref), face_refs = refs[:3], refs[3:]
    quarter = lane((8, 128)) // 32
    tile = tile_rows(proj_ref[...], True)
    tile_high = tile.astype(jnp.bfloat16).astype(f32)
    tile_low = tile - tile_high
    total = None
    for s in range((n_pieces + 3) // 4):
        count = min(4, n_pieces - 4 * s)

        def gathered(q, t):
            value = jnp.full((8, 128), -1.0 if q == 6 else 0.0, f32)
            for r in range(count):
                value = jnp.where(quarter == (r + t) % 4, pieces[4 * s + r][q], value)
            return value

        here = [gathered(6, 0).astype(jnp.int32) == slot for slot in range(16)]
        chosen_high, chosen_low = [
            jnp.concatenate([jnp.where(h, part, 0.0) for h in here], axis=0).astype(jnp.bfloat16)
            for part in (tile_high, tile_low)
        ]
        data = []
        for k in range(24):
            piece = gathered(k // 4, k % 4)
            data.append(pltpu.roll(piece, 128 - 32 * (k % 4), 1) if k % 4 else piece)
        data = jnp.concatenate(data, axis=0)
        high = data.astype(jnp.bfloat16)
        low = (data - high.astype(f32)).astype(jnp.bfloat16)
        dot = functools.partial(
            lax.dot_general,
            dimension_numbers=(((1,), (1,)), ((), ())),
            preferred_element_type=f32,
        )
        moved = dot(high, chosen_high) + (dot(low, chosen_high) + dot(high, chosen_low))
        total = moved if total is None else total + moved
    source = [total[64 * c : 64 * c + 64].reshape(8, 8, 128) for c in range(3)]
    middle = []
    for c in range(4):
        rate = rate_ref[c]
        if c:
            source_ref[c - 1] = source[c - 1]
            rate = rate + source[c - 1]
        middle.append(wave_ref[c] + acoustic_step * rate)
        middle_ref[c] = middle[c]
        carry = wave_ref[c] + middle[c]
        carry_ref[c] = carry + acoustic_step * source[c - 1] if c else carry
    store_faces(read_all(section_ref) + middle, face_refs, counts)


def inner_kernel(
    deriv_ref, high_ref, low_ref, les_ref, section_ref, middle_ref, carry_ref, mean_ref,
    les_base_ref, wave_base_ref,
):
    section = read_all(section_ref)
    rate = les_rate(section, None)
    for c in range(5):
        les_base_ref[c] = 0.5 * ((les_ref[c] + section[c]) + rate[c])
    rate = acoustic_rate(
        read_all(middle_ref), read_all(mean_ref), None,
        deriv_ref[...], (high_ref[...], low_ref[...]),
    )
    for c in range(4):
        wave_base_ref[c] = 0.5 * (carry_ref[c] + acoustic_step * rate[c])


def last_kernel(counts, n_faces, source_ref, les_base_ref, wave_base_ref, mean_ref, *refs):
    face_refs, (les_out, source_out, wave_out, les_ref, wave_ref, sems) = (
        refs[:n_faces], refs[n_faces:],
    )
    copies = []

    def send(source, target):
        copies.append(pltpu.make_async_copy(source, target, sems.at[len(copies)]))
        copies[-1].start()

    send(source_ref, source_out)
    layers = les_outer(load_faces(face_refs, counts, 0, 5))
    for c in range(5):
        part = [(0.5 * low[c], 0.5 * high[c]) for low, high in layers]
        for x, plane in enumerate(with_layers(les_base_ref[c], part)):
            les_ref[c, x] = plane
        send(les_ref.at[c], les_out.at[c])
    layers = acoustic_outer(read_all(mean_ref), load_faces(face_refs, counts, 5, 9))
    step = 0.5 * acoustic_step
    for c in range(4):
        part = [(step * low[c], step * high[c]) for low, high in layers]
        for x, plane in enumerate(with_layers(wave_base_ref[c], part)):
            wave_ref[c, x] = plane
        send(wave_ref.at[c], wave_out.at[c])
    for copy in copies:
        copy.wait()


VMEM = pl.BlockSpec(memory_space=pltpu.VMEM)
SMEM = pl.BlockSpec(memory_space=pltpu.SMEM)


ANY = pl.BlockSpec(memory_space=pl.ANY)


def call(kernel, in_specs, out_shapes, name, cost, scratch=(), room=24, out_spec=VMEM):
    return pl.pallas_call(
        kernel,
        in_specs=in_specs,
        out_specs=[out_spec] * len(out_shapes),
        out_shape=out_shapes,
        scratch_shapes=list(scratch),
        name=name,
        cost_estimate=pl.CostEstimate(flops=cost, bytes_accessed=800000, transcendentals=0),
        compiler_params=pltpu.CompilerParams(vmem_limit_bytes=room * 1024 * 1024),
    )


def local(counts, les, wave, mean, projection, owner, slot):
    shape = les.shape[1:]
    faces = face_shapes(counts, 9)
    n_faces = len(faces)
    like = lambda n: jax.ShapeDtypeStruct((n,) + shape, f32)

    table = derivative_matrix()
    deriv = jnp.asarray(table, f32)
    along_z = np.kron(np.eye(16), table.T).astype(np.float32)
    high = along_z.astype(jnp.bfloat16)
    low = (along_z - high.astype(np.float32)).astype(jnp.bfloat16)
    tables = (deriv, jnp.asarray(high), jnp.asarray(low))

    les_hbm, wave_hbm = les, wave
    les, wave, *sent = call(
        functools.partial(load_kernel, counts),
        [ANY] * 2,
        [like(5), like(4)] + faces,
        "load_and_faces",
        100000,
        [pltpu.SemaphoreType.DMA((9,))],
        56,
    )(les_hbm, wave_hbm)
    got = exchange(sent, counts)

    sets = partners(counts[0])
    n_plans = 4 * ((len(sets) + 3) // 4)
    plan = call(
        functools.partial(plan_kernel, counts),
        [SMEM] * 2,
        [
            jax.ShapeDtypeStruct((n_plans, 8, 128), jnp.int32),
            jax.ShapeDtypeStruct((len(sets), 8, 128), f32),
        ],
        "plan",
        4000000,
        [pltpu.SMEM((8,), jnp.int32)],
    )(owner, slot)
    pieces = call(
        functools.partial(lamb_kernel, counts, n_faces),
        [SMEM] + [VMEM] * (4 + n_faces),
        [jax.ShapeDtypeStruct((7, 8, 128), f32)] * len(sets),
        "lamb_blocks",
        10000000,
    )(projection, projection, *plan, les, *got)
    moved = [None] * len(sets)
    for k in reversed(range(len(sets))):
        still = all(i == j for i, j in sets[k])
        moved[k] = pieces[k] if still else lax.ppermute(pieces[k], "gx", sets[k])
    section, rate = call(
        functools.partial(first_kernel, counts, n_faces),
        [VMEM] * (6 + n_faces),
        [like(5), like(4)],
        "first_rates",
        40000000,
    )(*tables, les, wave, mean, *got)

    source, middle, carry, *sent = call(
        functools.partial(source_kernel, counts),
        [VMEM] * (4 + len(moved)),
        [like(3), like(4), like(4)] + faces,
        "source_and_faces",
        10000000,
    )(projection, wave, rate, section, *moved[::-1])
    got = exchange(sent, counts)
    les_base, wave_base = call(
        inner_kernel,
        [VMEM] * 8,
        [like(5), like(4)],
        "second_rates_inner",
        40000000,
    )(*tables, les, section, middle, carry, mean)
    return tuple(
        call(
            functools.partial(last_kernel, counts, n_faces),
            [VMEM] * (4 + n_faces),
            [like(5), like(3), like(4)],
            "second_rates_outer",
            4000000,
            [
                pltpu.VMEM(les.shape, f32),
                pltpu.VMEM(wave.shape, f32),
                pltpu.SemaphoreType.DMA((10,)),
            ],
            out_spec=ANY,
        )(source, les_base, wave_base, mean, *got)
    )


def solution(mesh):
    counts = tuple(mesh.shape[axis] for axis in axes)
    field = P(None, *axes)
    return jax.shard_map(
        functools.partial(local, counts),
        mesh=mesh,
        in_specs=(field, field, field, P(), P(*axes), P(*axes)),
        out_specs=(field, field, field),
        check_vma=False,
    )
```

```python
import functools

import jax
import jax.numpy as jnp
import numpy as np
from jax import lax
from jax.experimental import pallas as pl
from jax.experimental.pallas import tpu as pltpu
from jax.sharding import PartitionSpec as P

lobatto_points = np.array(
    [
        -1.0,
        -0.8717401485096066,
        -0.5917001814331423,
        -0.2092992179024789,
        0.2092992179024789,
        0.5917001814331423,
        0.8717401485096066,
        1.0,
    ]
)
flux_half = 0.08
gamma_less = 0.4
acoustic_step = 0.01
upwind_speed = 1.5
face_lift = 28.0
free_stream = (1.0, 0.0, 0.0, 0.0, 2.5)
axes = ("gx", "gy", "gz")
window = 4
f32 = jnp.float32


def derivative_matrix():
    points = lobatto_points
    products = [np.prod([points[i] - points[j] for j in range(8) if j != i]) for i in range(8)]
    matrix = np.zeros((8, 8))
    for i in range(8):
        for j in range(8):
            if j != i:
                matrix[i, j] = products[i] / (products[j] * (points[i] - points[j]))
        matrix[i, i] = -np.sum(matrix[i])
    return matrix


def sublane(shape):
    return lax.broadcasted_iota(jnp.int32, shape, len(shape) - 2)


def lane(shape):
    return lax.broadcasted_iota(jnp.int32, shape, len(shape) - 1)


def shifted(field, axis, step, outer):
    if axis == 0:
        if step == 1:
            return jnp.concatenate([field[1:], outer[None]], axis=0)
        return jnp.concatenate([outer[None], field[:-1]], axis=0)
    count = field.shape[axis]
    moved = pltpu.roll(field, count - 1 if step == 1 else 1, axis)
    edge = count - 1 if step == 1 else 0
    if axis == 1:
        return jnp.where(sublane(field.shape) == edge, outer[:, None, :], moved)
    columns = jnp.stack([outer[:, x : x + 1] for x in range(8)], axis=0)
    return jnp.where(lane(field.shape) == edge, columns, moved)


def fluid(state):
    density, mx, my, mz, energy = [s + r for s, r in zip(state, free_stream)]
    inverse = 1.0 / density
    momentum = (mx, my, mz)
    velocity = [m * inverse for m in momentum]
    pressure = gamma_less * (
        energy - 0.5 * (mx * velocity[0] + my * velocity[1] + mz * velocity[2])
    )
    return momentum, velocity, pressure, energy + pressure


def split_flux(state, parts, axis, sign):
    momentum, velocity, pressure, enthalpy = parts
    speed = velocity[axis]
    flux = [momentum[axis]]
    for c in range(3):
        term = momentum[c] * speed
        flux.append(term + pressure if c == axis else term)
    flux.append(enthalpy * speed)
    if sign > 0:
        return [flux_half * (s + f) for s, f in zip(state, flux)]
    return [flux_half * (s - f) for s, f in zip(state, flux)]


def les_rate(state, halos):
    parts = fluid(state)
    total = [-6.0 * flux_half * s for s in state]
    nothing = jnp.zeros((8, 128), f32)
    for axis in range(3):
        ahead = split_flux(state, parts, axis, -1)
        behind = split_flux(state, parts, axis, 1)
        ahead_outer = behind_outer = [nothing] * 5
        if halos is not None:
            before, after = halos[axis]
            ahead_outer = split_flux(after, fluid(after), axis, -1)
            behind_outer = split_flux(before, fluid(before), axis, 1)
        for c in range(5):
            total[c] = total[c] + (
                shifted(ahead[c], axis, 1, ahead_outer[c])
                + shifted(behind[c], axis, -1, behind_outer[c])
            )
    return total


def les_outer(halos):
    return [
        (
            split_flux(before, fluid(before), axis, 1),
            split_flux(after, fluid(after), axis, -1),
        )
        for axis, (before, after) in enumerate(halos)
    ]


def with_layers(field, layers):
    (x0, x1), (y0, y1), (z0, z1) = layers
    row, column = sublane((8, 128)), lane((8, 128))
    planes = []
    for x in range(8):
        plane = field[x]
        if x == 0:
            plane = plane + x0
        if x == 7:
            plane = plane + x1
        plane = plane + jnp.where(
            row == 0, y0[x : x + 1], jnp.where(row == 7, y1[x : x + 1], 0.0)
        )
        plane = plane + jnp.where(
            column == 0, z0[:, x : x + 1], jnp.where(column == 127, z1[:, x : x + 1], 0.0)
        )
        planes.append(plane)
    return planes


def wave_flux(state, mean, axis):
    speed = mean[axis]
    pressure = state[0]
    rows = [speed * pressure + state[1 + axis]]
    for c in range(3):
        term = speed * state[1 + c]
        rows.append(term + pressure if c == axis else term)
    return rows


def dot3(left, right):
    high = left.astype(jnp.bfloat16)
    low = (left - high.astype(f32)).astype(jnp.bfloat16)
    dot = functools.partial(jnp.dot, preferred_element_type=f32)
    return dot(high, right[0]) + (dot(low, right[0]) + dot(high, right[1]))


def acoustic_rate(state, mean, halos, deriv, along_z):
    shape = state[0].shape
    table = derivative_matrix()
    flux = wave_flux(state, mean, 0)
    if halos is None:
        halos = [([jnp.zeros((8, 128), f32)] * 4,) * 2] * 3
    before, after = halos[0]
    low_mean, high_mean = [m[0] for m in mean], [m[7] for m in mean]
    low_jump = [b - s[0] for b, s in zip(before, state)]
    high_jump = [a - s[7] for a, s in zip(after, state)]
    low_flux = wave_flux(low_jump, low_mean, 0)
    high_flux = wave_flux(high_jump, high_mean, 0)
    half, lift = 0.5 * face_lift, 0.5 * face_lift * upwind_speed
    total = []
    for c in range(4):
        planes = []
        for i in range(8):
            plane = -float(table[i, 0]) * flux[c][0]
            for a in range(1, 8):
                if abs(table[i, a]) > 1e-12:
                    plane = plane - float(table[i, a]) * flux[c][a]
            if i == 0:
                plane = plane + (half * low_flux[c] + lift * low_jump[c])
            if i == 7:
                plane = plane - (half * high_flux[c] - lift * high_jump[c])
            planes.append(plane)
        total.append(jnp.stack(planes, axis=0))
    flux = wave_flux(state, mean, 1)
    before, after = halos[1]
    row = sublane(shape)
    sign = jnp.where(row == 0, half, jnp.where(row == 7, -half, 0.0))
    jump = [
        jnp.where(row == 0, b[:, None, :], jnp.where(row == 7, a[:, None, :], s)) - s
        for s, b, a in zip(state, before, after)
    ]
    jump_flux = wave_flux(jump, mean, 1)
    for c in range(4):
        change = lift * jump[c] + sign * jump_flux[c]
        for b in range(8):
            change = change - deriv[:, b : b + 1][None] * flux[c][:, b : b + 1, :]
        total[c] = total[c] + change
    flux = wave_flux(state, mean, 2)
    before, after = halos[2]
    column = lane(shape)
    place = lax.rem(column, 8)
    sign = jnp.where(place == 0, half, jnp.where(place == 7, -half, 0.0))
    jump = [
        jnp.where(
            place == 0,
            shifted(s, 2, -1, b),
            jnp.where(place == 7, shifted(s, 2, 1, a), s),
        )
        - s
        for s, b, a in zip(state, before, after)
    ]
    jump_flux = wave_flux(jump, mean, 2)
    for c in range(4):
        slope = dot3(flux[c].reshape(64, 128), along_z).reshape(shape)
        total[c] = total[c] + (lift * jump[c] + sign * jump_flux[c] - slope)
    return total


def acoustic_outer(mean, halos):
    half, lift = 0.5 * face_lift, 0.5 * face_lift * upwind_speed
    layers = []
    for axis, (before, after) in enumerate(halos):
        if axis == 0:
            low, high = [m[0] for m in mean], [m[7] for m in mean]
        elif axis == 1:
            low, high = [m[:, 0, :] for m in mean], [m[:, 7, :] for m in mean]
        else:
            low, high = [z_layer(m, 0) for m in mean], [z_layer(m, 127) for m in mean]
        low_flux = wave_flux(before, low, axis)
        high_flux = wave_flux(after, high, axis)
        layers.append(
            (
                [half * f + lift * b for f, b in zip(low_flux, before)],
                [lift * a - half * f for f, a in zip(high_flux, after)],
            )
        )
    return layers


def tile_rows(matrix, transposed):
    spread = (lax.rem(lane((8, 128)), 8) == sublane((8, 128))).astype(f32)
    contract = ((1,), (0,)) if transposed else ((0,), (0,))
    return lax.dot_general(
        matrix, spread, (contract, ((), ())),
        precision=lax.Precision.HIGHEST, preferred_element_type=f32,
    )


def pairings(count):
    sets = []
    for first in (0, 1):
        pairs = [(i, i + 1) for i in range(first, count - 1, 2)]
        if pairs:
            sets.append(pairs)
    return sets


def routes(counts):
    places = [(x, y, z) for x in range(counts[0]) for y in range(counts[1]) for z in range(counts[2])]
    number = {place: n for n, place in enumerate(places)}
    found = []
    for axis in range(3):
        for pairs in pairings(counts[axis]):
            swap = dict(pairs + [(j, i) for i, j in pairs])
            alone = [i for i in range(counts[axis]) if i not in swap]
            spare = 0 if axis else 2
            route = []
            for place in places:
                other = list(place)
                if place[axis] in swap:
                    other[axis] = swap[place[axis]]
                elif axis == 0 and len(alone) == 2:
                    other[axis] = sum(alone) - place[axis]
                elif counts[spare] % 2 == 0:
                    other[spare] = place[spare] ^ 1
                route.append((number[place], number[tuple(other)]))
            found.append(route)
    return found


def z_layer(field, at):
    packed = jnp.zeros((8, 128), f32)
    column = lane((8, 128))
    for x in range(8):
        packed = jnp.where(column == x, field[x][:, at : at + 1], packed)
    return packed


def store_faces(fields, out_refs, counts):
    at = 0
    for axis in range(3):
        even = lax.rem(lax.axis_index(axes[axis]), 2) == 0
        sets = len(pairings(counts[axis]))
        for c, field in enumerate(fields):
            if axis == 0:
                low, high = field[0], field[7]
            elif axis == 1:
                low, high = field[:, 0, :], field[:, 7, :]
            else:
                low, high = z_layer(field, 0), z_layer(field, 127)
            for s in range(sets):
                out_refs[at + s][c] = jnp.where(even == (s == 0), high, low)
        at += sets


def sending_order(counts):
    where = [(axis, s) for axis in range(3) for s in range(len(pairings(counts[axis])))]
    wanted = ((0, 1), (2, 1), (2, 0), (1, 1), (1, 0), (0, 0))
    return [where.index(p) for p in wanted if p in where]


def load_faces(sent_refs, counts, first, last):
    in_refs = [None] * len(sent_refs)
    for ref, at in zip(sent_refs, sending_order(counts)):
        in_refs[at] = ref
    halos = []
    at = 0
    for axis in range(3):
        even = lax.rem(lax.axis_index(axes[axis]), 2) == 0
        sets = len(pairings(counts[axis]))
        got = [[in_refs[at + s][c] for c in range(first, last)] for s in range(sets)]
        while len(got) < 2:
            got.append([jnp.zeros((8, 128), f32)] * (last - first))
        place = lax.axis_index(axes[axis])
        before = [
            jnp.where(place == 0, 0.0, jnp.where(even, b, a)) for a, b in zip(*got)
        ]
        after = [
            jnp.where(place == counts[axis] - 1, 0.0, jnp.where(even, a, b))
            for a, b in zip(*got)
        ]
        halos.append((before, after))
        at += sets
    return halos


def face_shapes(counts, width):
    total = sum(len(pairings(count)) for count in counts)
    return [jax.ShapeDtypeStruct((width, 8, 128), f32)] * total


def exchange(faces, counts):
    ways = routes(counts)
    return [lax.ppermute(faces[at], axes, ways[at]) for at in sending_order(counts)]


def read_all(ref):
    return [ref[c] for c in range(ref.shape[0])]


def load_kernel(counts, les_hbm, wave_hbm, les_ref, wave_ref, *refs):
    out_refs, sems = refs[:-1], refs[-1]
    copies = []
    for source, target in ((les_hbm, les_ref), (wave_hbm, wave_ref)):
        for c in range(source.shape[0]):
            copies.append(
                pltpu.make_async_copy(source.at[c], target.at[c], sems.at[len(copies)])
            )
    for copy in copies:
        copy.start()
    for n, copy in enumerate(copies):
        copy.wait()
        field = les_ref[n] if n < 5 else wave_ref[n - 5]
        store_faces([field], [ref.at[n : n + 1] for ref in out_refs], counts)


def partners(count):
    if count == window:
        return [[(i, i ^ mask) for i in range(count)] for mask in range(count)]
    turns = sorted({d % count for d in range(1 - window, window)})
    return [[(i, (i + turn) % count) for i in range(count)] for turn in turns]


def plan_kernel(counts, owner_ref, slot_ref, order_ref, marks_ref, counter):
    count = counts[0]
    n_sets = len(partners(count))
    groups = 4 * ((n_sets + 3) // 4)
    own = lax.axis_index("gx")
    for g in range(groups):
        counter[g] = 0
    places = []
    for n in range(owner_ref.shape[-1]):
        if count == window:
            group = lax.bitwise_xor(owner_ref[0, 0, n], own)
        else:
            turn = lax.rem(owner_ref[0, 0, n] - own + count, count)
            group = turn if n_sets == count else jnp.where(
                turn < window, turn, turn - (count - n_sets)
            )
        taken = counter[group]
        counter[group] = taken + 1
        places.append(group * window + taken)
    column = lane((8, 128))
    quarter = column // 32
    for s in range(groups // 4):
        labels = jnp.full((8, 128), -1.0, f32)
        order = column
        for n, place in enumerate(places):
            here = column // 8 == place - 16 * s
            labels = jnp.where(here, slot_ref[0, 0, n].astype(f32), labels)
            order = jnp.where(here, 8 * n + lax.rem(column, 8), order)
        for t in range(4):
            order_ref[4 * s + t] = pltpu.roll(order, 32 * t, 1) if t else order
        for r in range(min(4, n_sets - 4 * s)):
            marks = labels
            for t in range(1, 4):
                marks = jnp.where(quarter == (r + t) % 4, pltpu.roll(labels, 32 * t, 1), marks)
            marks_ref[4 * s + r] = marks


def lamb_kernel(counts, n_faces, proj_smem, proj_ref, order_ref, marks_ref, les_ref, *refs):
    face_refs, out_refs = refs[:n_faces], refs[n_faces:]
    halos = load_faces(face_refs, counts, 0, 4)

    def speeds(state):
        inverse = 1.0 / (state[0] + 1.0)
        return [state[c] * inverse for c in (1, 2, 3)]

    velocity = speeds([les_ref[c] for c in range(4)])
    outer = [(speeds(before), speeds(after)) for before, after in halos]

    def slope(c, axis):
        return 0.5 * (
            shifted(velocity[c], axis, 1, outer[axis][1][c])
            - shifted(velocity[c], axis, -1, outer[axis][0][c])
        )

    vort = [slope(2, 1) - slope(1, 2), slope(0, 2) - slope(2, 0), slope(1, 0) - slope(0, 1)]
    lamb = [
        vort[1] * velocity[2] - vort[2] * velocity[1],
        vort[2] * velocity[0] - vort[0] * velocity[2],
        vort[0] * velocity[1] - vort[1] * velocity[0],
    ]
    proj = proj_ref[...]
    blocks = []
    for field in lamb:
        along_y = proj[:, 0:1][None] * field[:, 0:1, :]
        for b in range(1, 8):
            along_y = along_y + proj[:, b : b + 1][None] * field[:, b : b + 1, :]
        for i in range(8):
            plane = proj_smem[i, 0] * along_y[0]
            for a in range(1, 8):
                plane = plane + proj_smem[i, a] * along_y[a]
            blocks.append(plane)

    quarter = lane((8, 128)) // 32
    for s in range((len(out_refs) + 3) // 4):
        ordered = [
            jnp.take_along_axis(block, order_ref[4 * s + k % 4], axis=1)
            for k, block in enumerate(blocks)
        ]
        for r in range(min(4, len(out_refs) - 4 * s)):
            out = out_refs[4 * s + r]
            for q in range(6):
                packed = ordered[4 * q]
                for t in range(1, 4):
                    packed = jnp.where(quarter == (r + t) % 4, ordered[4 * q + t], packed)
                out[q] = packed
            out[6] = marks_ref[4 * s + r]


def first_kernel(
    counts, n_faces, deriv_ref, high_ref, low_ref, les_ref, wave_ref, mean_ref, *refs
):
    face_refs, (section_ref, rate_ref) = refs[:n_faces], refs[n_faces:]
    state = read_all(les_ref)
    rate = les_rate(state, load_faces(face_refs, counts, 0, 5))
    for c in range(5):
        section_ref[c] = state[c] + rate[c]
    rate = acoustic_rate(
        read_all(wave_ref), read_all(mean_ref), load_faces(face_refs, counts, 5, 9),
        deriv_ref[...], (high_ref[...], low_ref[...]),
    )
    for c in range(4):
        rate_ref[c] = rate[c]


def source_kernel(counts, proj_ref, wave_ref, rate_ref, section_ref, *refs):
    n_pieces = len(partners(counts[0]))
    pieces, refs = refs[:n_pieces][::-1], refs[n_pieces:]
    (source_ref, middle_ref, carry_ref), face_refs = refs[:3], refs[3:]
    quarter = lane((8, 128)) // 32
    tile = tile_rows(proj_ref[...], True)
    tile_high = tile.astype(jnp.bfloat16).astype(f32)
    tile_low = tile - tile_high
    total = None
    for s in range((n_pieces + 3) // 4):
        count = min(4, n_pieces - 4 * s)

        def gathered(q, t):
            value = jnp.full((8, 128), -1.0 if q == 6 else 0.0, f32)
            for r in range(count):
                value = jnp.where(quarter == (r + t) % 4, pieces[4 * s + r][q], value)
            return value

        here = [gathered(6, 0).astype(jnp.int32) == slot for slot in range(16)]
        chosen_high, chosen_low = [
            jnp.concatenate([jnp.where(h, part, 0.0) for h in here], axis=0).astype(jnp.bfloat16)
            for part in (tile_high, tile_low)
        ]
        data = []
        for k in range(24):
            piece = gathered(k // 4, k % 4)
            data.append(pltpu.roll(piece, 128 - 32 * (k % 4), 1) if k % 4 else piece)
        data = jnp.concatenate(data, axis=0)
        high = data.astype(jnp.bfloat16)
        low = (data - high.astype(f32)).astype(jnp.bfloat16)
        dot = functools.partial(
            lax.dot_general,
            dimension_numbers=(((1,), (1,)), ((), ())),
            preferred_element_type=f32,
        )
        moved = dot(high, chosen_high) + (dot(low, chosen_high) + dot(high, chosen_low))
        total = moved if total is None else total + moved
    source = [total[64 * c : 64 * c + 64].reshape(8, 8, 128) for c in range(3)]
    middle = []
    for c in range(4):
        rate = rate_ref[c]
        if c:
            source_ref[c - 1] = source[c - 1]
            rate = rate + source[c - 1]
        middle.append(wave_ref[c] + acoustic_step * rate)
        middle_ref[c] = middle[c]
        carry = wave_ref[c] + middle[c]
        carry_ref[c] = carry + acoustic_step * source[c - 1] if c else carry
    store_faces(read_all(section_ref) + middle, face_refs, counts)


def inner_kernel(
    deriv_ref, high_ref, low_ref, les_ref, section_ref, middle_ref, carry_ref, mean_ref,
    les_base_ref, wave_base_ref,
):
    section = read_all(section_ref)
    rate = les_rate(section, None)
    for c in range(5):
        les_base_ref[c] = 0.5 * ((les_ref[c] + section[c]) + rate[c])
    rate = acoustic_rate(
        read_all(middle_ref), read_all(mean_ref), None,
        deriv_ref[...], (high_ref[...], low_ref[...]),
    )
    for c in range(4):
        wave_base_ref[c] = 0.5 * (carry_ref[c] + acoustic_step * rate[c])


def last_kernel(counts, n_faces, source_ref, les_base_ref, wave_base_ref, mean_ref, *refs):
    face_refs, (les_out, source_out, wave_out, les_ref, wave_ref, sems) = (
        refs[:n_faces], refs[n_faces:],
    )
    copies = []

    def send(source, target):
        copies.append(pltpu.make_async_copy(source, target, sems.at[len(copies)]))
        copies[-1].start()

    send(source_ref, source_out)
    layers = les_outer(load_faces(face_refs, counts, 0, 5))
    for c in range(5):
        part = [(0.5 * low[c], 0.5 * high[c]) for low, high in layers]
        for x, plane in enumerate(with_layers(les_base_ref[c], part)):
            les_ref[c, x] = plane
        send(les_ref.at[c], les_out.at[c])
    layers = acoustic_outer(read_all(mean_ref), load_faces(face_refs, counts, 5, 9))
    step = 0.5 * acoustic_step
    for c in range(4):
        part = [(step * low[c], step * high[c]) for low, high in layers]
        for x, plane in enumerate(with_layers(wave_base_ref[c], part)):
            wave_ref[c, x] = plane
        send(wave_ref.at[c], wave_out.at[c])
    for copy in copies:
        copy.wait()


VMEM = pl.BlockSpec(memory_space=pltpu.VMEM)
SMEM = pl.BlockSpec(memory_space=pltpu.SMEM)


HBM = pl.BlockSpec(memory_space=pltpu.HBM)


def call(kernel, in_specs, out_shapes, name, cost, scratch=(), out_spec=VMEM):
    return pl.pallas_call(
        kernel,
        in_specs=in_specs,
        out_specs=[out_spec] * len(out_shapes),
        out_shape=out_shapes,
        scratch_shapes=list(scratch),
        name=name,
        cost_estimate=pl.CostEstimate(flops=cost, bytes_accessed=800000, transcendentals=0),
        compiler_params=pltpu.CompilerParams(vmem_limit_bytes=24 * 1024 * 1024),
    )


def local(counts, les, wave, mean, projection, owner, slot):
    shape = les.shape[1:]
    faces = face_shapes(counts, 9)
    n_faces = len(faces)
    like = lambda n: jax.ShapeDtypeStruct((n,) + shape, f32)

    table = derivative_matrix()
    deriv = jnp.asarray(table, f32)
    along_z = np.kron(np.eye(16), table.T).astype(np.float32)
    high = along_z.astype(jnp.bfloat16)
    low = (along_z - high.astype(np.float32)).astype(jnp.bfloat16)
    tables = (deriv, jnp.asarray(high), jnp.asarray(low))

    les_hbm, wave_hbm = les, wave
    les, wave, *sent = call(
        functools.partial(load_kernel, counts),
        [HBM] * 2,
        [like(5), like(4)] + faces,
        "load_and_faces",
        100000,
        [pltpu.SemaphoreType.DMA((9,))],
    )(*(pltpu.with_memory_space_constraint(a, pltpu.HBM) for a in (les_hbm, wave_hbm)))
    got = exchange(sent, counts)

    sets = partners(counts[0])
    n_plans = 4 * ((len(sets) + 3) // 4)
    plan = call(
        functools.partial(plan_kernel, counts),
        [SMEM] * 2,
        [
            jax.ShapeDtypeStruct((n_plans, 8, 128), jnp.int32),
            jax.ShapeDtypeStruct((len(sets), 8, 128), f32),
        ],
        "plan",
        4000000,
        [pltpu.SMEM((8,), jnp.int32)],
    )(owner, slot)
    pieces = call(
        functools.partial(lamb_kernel, counts, n_faces),
        [SMEM] + [VMEM] * (4 + n_faces),
        [jax.ShapeDtypeStruct((7, 8, 128), f32)] * len(sets),
        "lamb_blocks",
        10000000,
    )(projection, projection, *plan, les, *got)
    moved = [None] * len(sets)
    for k in reversed(range(len(sets))):
        still = all(i == j for i, j in sets[k])
        moved[k] = pieces[k] if still else lax.ppermute(pieces[k], "gx", sets[k])
    section, rate = call(
        functools.partial(first_kernel, counts, n_faces),
        [VMEM] * (6 + n_faces),
        [like(5), like(4)],
        "first_rates",
        40000000,
    )(*tables, les, wave, mean, *got)

    source, middle, carry, *sent = call(
        functools.partial(source_kernel, counts),
        [VMEM] * (4 + len(moved)),
        [like(3), like(4), like(4)] + faces,
        "source_and_faces",
        10000000,
    )(projection, wave, rate, section, *moved[::-1])
    got = exchange(sent, counts)
    les_base, wave_base = call(
        inner_kernel,
        [VMEM] * 8,
        [like(5), like(4)],
        "second_rates_inner",
        40000000,
    )(*tables, les, section, middle, carry, mean)
    return tuple(
        call(
            functools.partial(last_kernel, counts, n_faces),
            [VMEM] * (4 + n_faces),
            [like(5), like(3), like(4)],
            "second_rates_outer",
            4000000,
            [
                pltpu.VMEM(les.shape, f32),
                pltpu.VMEM(wave.shape, f32),
                pltpu.SemaphoreType.DMA((10,)),
            ],
            out_spec=HBM,
        )(source, les_base, wave_base, mean, *got)
    )


def solution(mesh):
    counts = tuple(mesh.shape[axis] for axis in axes)
    field = P(None, *axes)
    return jax.shard_map(
        functools.partial(local, counts),
        mesh=mesh,
        in_specs=(field, field, field, P(), P(*axes), P(*axes)),
        out_specs=(field, field, field),
        check_vma=False,
    )
```

```python
import functools

import jax
import jax.numpy as jnp
import numpy as np
from jax import lax
from jax.experimental import pallas as pl
from jax.experimental.pallas import tpu as pltpu
from jax.sharding import PartitionSpec as P

lobatto_points = np.array(
    [
        -1.0,
        -0.8717401485096066,
        -0.5917001814331423,
        -0.2092992179024789,
        0.2092992179024789,
        0.5917001814331423,
        0.8717401485096066,
        1.0,
    ]
)
flux_half = 0.08
gamma_less = 0.4
acoustic_step = 0.01
upwind_speed = 1.5
face_lift = 28.0
free_stream = (1.0, 0.0, 0.0, 0.0, 2.5)
axes = ("gx", "gy", "gz")
window = 4
f32 = jnp.float32


def derivative_matrix():
    points = lobatto_points
    products = [np.prod([points[i] - points[j] for j in range(8) if j != i]) for i in range(8)]
    matrix = np.zeros((8, 8))
    for i in range(8):
        for j in range(8):
            if j != i:
                matrix[i, j] = products[i] / (products[j] * (points[i] - points[j]))
        matrix[i, i] = -np.sum(matrix[i])
    return matrix


def sublane(shape):
    return lax.broadcasted_iota(jnp.int32, shape, len(shape) - 2)


def lane(shape):
    return lax.broadcasted_iota(jnp.int32, shape, len(shape) - 1)


def rolled(tile, amount, axis):
    amount = amount % tile.shape[axis]
    return pltpu.roll(tile, amount, axis) if amount else tile


def shifted(field, axis, step, outer=None):
    if axis == 0:
        outer = jnp.zeros((8, 128), f32) if outer is None else outer
        if step == 1:
            return jnp.concatenate([field[1:], outer[None]], axis=0)
        return jnp.concatenate([outer[None], field[:-1]], axis=0)
    count = (8, 128)[axis - 1]
    edge = count - 1 if step == 1 else 0
    at_edge = (sublane if axis == 1 else lane)((8, 128)) == edge
    planes = []
    for x in range(8):
        layer = 0.0 if outer is None else rolled(outer, edge - axis * x, axis - 1)
        planes.append(jnp.where(at_edge, layer, rolled(field[x], -step, axis - 1)))
    return jnp.stack(planes, axis=0)


def fluid(state):
    density, mx, my, mz, energy = [s + r for s, r in zip(state, free_stream)]
    inverse = 1.0 / density
    momentum = (mx, my, mz)
    velocity = [m * inverse for m in momentum]
    pressure = gamma_less * (
        energy - 0.5 * (mx * velocity[0] + my * velocity[1] + mz * velocity[2])
    )
    return momentum, velocity, pressure, energy + pressure


def split_flux(state, parts, axis, sign):
    momentum, velocity, pressure, enthalpy = parts
    speed = velocity[axis]
    flux = [momentum[axis]]
    for c in range(3):
        term = momentum[c] * speed
        flux.append(term + pressure if c == axis else term)
    flux.append(enthalpy * speed)
    if sign > 0:
        return [flux_half * (s + f) for s, f in zip(state, flux)]
    return [flux_half * (s - f) for s, f in zip(state, flux)]


def les_rate(state, halos):
    parts = fluid(state)
    total = [-6.0 * flux_half * s for s in state]
    for axis in range(3):
        ahead = split_flux(state, parts, axis, -1)
        behind = split_flux(state, parts, axis, 1)
        ahead_outer = behind_outer = [None] * 5
        if halos is not None:
            before, after = halos[axis]
            ahead_outer = split_flux(after, fluid(after), axis, -1)
            behind_outer = split_flux(before, fluid(before), axis, 1)
        for c in range(5):
            total[c] = total[c] + (
                shifted(ahead[c], axis, 1, ahead_outer[c])
                + shifted(behind[c], axis, -1, behind_outer[c])
            )
    return total


def les_outer(halos):
    return [
        (
            split_flux(before, fluid(before), axis, 1),
            split_flux(after, fluid(after), axis, -1),
        )
        for axis, (before, after) in enumerate(halos)
    ]


def with_layers(field, layers):
    row, column = sublane((8, 128)), lane((8, 128))
    along_z = layers[2]
    if along_z is not None:
        along_z = jnp.where(lax.rem(column, 2) == 0, along_z[0], rolled(along_z[1], -1, 1))
    planes = []
    for x in range(8):
        plane = field[x]
        if layers[0] is not None and x in (0, 7):
            plane = plane + layers[0][x // 7]
        if layers[1] is not None:
            low, high = layers[1]
            plane = plane + jnp.where(
                row == 0, rolled(low, -x, 0), jnp.where(row == 7, rolled(high, 7 - x, 0), 0.0)
            )
        if along_z is not None:
            ends = (column == 0) | (column == 127)
            plane = plane + jnp.where(ends, rolled(along_z, -2 * x, 1), 0.0)
        planes.append(plane)
    return planes


def wave_flux(state, mean, axis):
    speed = mean[axis]
    pressure = state[0]
    rows = [speed * pressure + state[1 + axis]]
    for c in range(3):
        term = speed * state[1 + c]
        rows.append(term + pressure if c == axis else term)
    return rows


def dot3(left, right):
    high = left.astype(jnp.bfloat16)
    low = (left - high.astype(f32)).astype(jnp.bfloat16)
    dot = functools.partial(jnp.dot, preferred_element_type=f32)
    return dot(high, right[0]) + (dot(low, right[0]) + dot(high, right[1]))


def acoustic_rate(state, mean, halos, deriv, along_z):
    shape = state[0].shape
    table = derivative_matrix()
    flux = wave_flux(state, mean, 0)
    if halos is None:
        halos = [([jnp.zeros((8, 128), f32)] * 4,) * 2] + [([None] * 4,) * 2] * 2
    before, after = halos[0]
    low_mean, high_mean = [m[0] for m in mean], [m[7] for m in mean]
    low_jump = [b - s[0] for b, s in zip(before, state)]
    high_jump = [a - s[7] for a, s in zip(after, state)]
    low_flux = wave_flux(low_jump, low_mean, 0)
    high_flux = wave_flux(high_jump, high_mean, 0)
    half, lift = 0.5 * face_lift, 0.5 * face_lift * upwind_speed
    total = []
    for c in range(4):
        planes = []
        for i in range(8):
            plane = -float(table[i, 0]) * flux[c][0]
            for a in range(1, 8):
                if abs(table[i, a]) > 1e-12:
                    plane = plane - float(table[i, a]) * flux[c][a]
            if i == 0:
                plane = plane + (half * low_flux[c] + lift * low_jump[c])
            if i == 7:
                plane = plane - (half * high_flux[c] - lift * high_jump[c])
            planes.append(plane)
        total.append(jnp.stack(planes, axis=0))
    flux = wave_flux(state, mean, 1)
    before, after = halos[1]
    row = sublane(shape)
    sign = jnp.where(row == 0, half, jnp.where(row == 7, -half, 0.0))
    jump = []
    for s, b, a in zip(state, before, after):
        planes = []
        for x in range(8):
            low = 0.0 if b is None else rolled(b, -x, 0)
            high = 0.0 if a is None else rolled(a, 7 - x, 0)
            planes.append(jnp.where(row[x] == 0, low, jnp.where(row[x] == 7, high, s[x])) - s[x])
        jump.append(jnp.stack(planes, axis=0))
    jump_flux = wave_flux(jump, mean, 1)
    for c in range(4):
        change = lift * jump[c] + sign * jump_flux[c]
        for b in range(8):
            change = change - deriv[:, b : b + 1][None] * flux[c][:, b : b + 1, :]
        total[c] = total[c] + change
    flux = wave_flux(state, mean, 2)
    before, after = halos[2]
    column = lane(shape)
    place = lax.rem(column, 8)
    sign = jnp.where(place == 0, half, jnp.where(place == 7, -half, 0.0))
    jump = [
        jnp.where(
            place == 0,
            shifted(s, 2, -1, b),
            jnp.where(place == 7, shifted(s, 2, 1, a), s),
        )
        - s
        for s, b, a in zip(state, before, after)
    ]
    jump_flux = wave_flux(jump, mean, 2)
    for c in range(4):
        slope = dot3(flux[c].reshape(64, 128), along_z).reshape(shape)
        total[c] = total[c] + (lift * jump[c] + sign * jump_flux[c] - slope)
    return total


def acoustic_outer(mean, halos):
    half, lift = 0.5 * face_lift, 0.5 * face_lift * upwind_speed
    layers = []
    for axis, (before, after) in enumerate(halos):
        if axis == 0:
            low, high = [m[0] for m in mean], [m[7] for m in mean]
        elif axis == 1:
            low, high = [m[:, 0, :] for m in mean], [m[:, 7, :] for m in mean]
        else:
            low, high = [z_layer(m, 0) for m in mean], [z_layer(m, 127) for m in mean]
        low_flux = wave_flux(before, low, axis)
        high_flux = wave_flux(after, high, axis)
        layers.append(
            (
                [half * f + lift * b for f, b in zip(low_flux, before)],
                [lift * a - half * f for f, a in zip(high_flux, after)],
            )
        )
    return layers


def tile_rows(matrix, transposed):
    spread = (lax.rem(lane((8, 128)), 8) == sublane((8, 128))).astype(f32)
    contract = ((1,), (0,)) if transposed else ((0,), (0,))
    return lax.dot_general(
        matrix, spread, (contract, ((), ())),
        precision=lax.Precision.HIGHEST, preferred_element_type=f32,
    )


def pairings(count):
    sets = []
    for first in (0, 1):
        pairs = [(i, i + 1) for i in range(first, count - 1, 2)]
        if pairs:
            sets.append(pairs)
    return sets


def routes(counts):
    places = [(x, y, z) for x in range(counts[0]) for y in range(counts[1]) for z in range(counts[2])]
    number = {place: n for n, place in enumerate(places)}
    found = []
    for axis in range(3):
        for pairs in pairings(counts[axis]):
            swap = dict(pairs + [(j, i) for i, j in pairs])
            alone = [i for i in range(counts[axis]) if i not in swap]
            spare = 0 if axis else 2
            route = []
            for place in places:
                other = list(place)
                if place[axis] in swap:
                    other[axis] = swap[place[axis]]
                elif axis == 0 and len(alone) == 2:
                    other[axis] = sum(alone) - place[axis]
                elif counts[spare] % 2 == 0:
                    other[spare] = place[spare] ^ 1
                route.append((number[place], number[tuple(other)]))
            found.append(route)
    return found


def z_layer(field, at):
    packed = jnp.zeros((8, 128), f32)
    column = lane((8, 128))
    for x in range(8):
        packed = jnp.where(column == 2 * x, rolled(field[x], 2 * x - at, 1), packed)
    return packed


def store_faces(fields, out_refs, counts):
    at = 0
    for axis in range(3):
        even = lax.rem(lax.axis_index(axes[axis]), 2) == 0
        sets = len(pairings(counts[axis]))
        for c, field in enumerate(fields):
            if axis == 0:
                low, high = field[0], field[7]
            elif axis == 1:
                low, high = field[:, 0, :], field[:, 7, :]
            else:
                low, high = z_layer(field, 0), z_layer(field, 127)
            for s in range(sets):
                out_refs[at + s][c] = jnp.where(even == (s == 0), high, low)
        at += sets


def sending_order(counts):
    where = [(axis, s) for axis in range(3) for s in range(len(pairings(counts[axis])))]
    wanted = ((0, 1), (2, 1), (2, 0), (1, 1), (1, 0), (0, 0))
    return [where.index(p) for p in wanted if p in where]


def load_faces(sent_refs, counts, first, last):
    in_refs = [None] * len(sent_refs)
    for ref, at in zip(sent_refs, sending_order(counts)):
        in_refs[at] = ref
    halos = []
    at = 0
    for axis in range(3):
        even = lax.rem(lax.axis_index(axes[axis]), 2) == 0
        sets = len(pairings(counts[axis]))
        got = [[in_refs[at + s][c] for c in range(first, last)] for s in range(sets)]
        while len(got) < 2:
            got.append([jnp.zeros((8, 128), f32)] * (last - first))
        place = lax.axis_index(axes[axis])
        before = [
            jnp.where(place == 0, 0.0, jnp.where(even, b, a)) for a, b in zip(*got)
        ]
        after = [
            jnp.where(place == counts[axis] - 1, 0.0, jnp.where(even, a, b))
            for a, b in zip(*got)
        ]
        halos.append((before, after))
        at += sets
    return halos


def face_shapes(counts, width):
    total = sum(len(pairings(count)) for count in counts)
    return [jax.ShapeDtypeStruct((width, 8, 128), f32)] * total


def exchange(faces, counts):
    ways = routes(counts)
    return [lax.ppermute(faces[at], axes, ways[at]) for at in sending_order(counts)]


def read_all(ref):
    return [ref[c] for c in range(ref.shape[0])]


def load_kernel(counts, les_hbm, wave_hbm, les_ref, wave_ref, *refs):
    out_refs, sems = refs[:-1], refs[-1]
    states = ((les_hbm, les_ref, 0), (wave_hbm, wave_ref, 5))
    copies = [
        pltpu.make_async_copy(source, target, sems.at[n])
        for n, (source, target, _) in enumerate(states)
    ]
    for copy in copies:
        copy.start()
    for copy, (_, target, first) in zip(copies, states):
        copy.wait()
        count = target.shape[0]
        store_faces(read_all(target), [ref.at[first : first + count] for ref in out_refs], counts)


def partners(count):
    if count == window:
        return [[(i, i ^ mask) for i in range(count)] for mask in range(count)]
    turns = sorted({d % count for d in range(1 - window, window)})
    return [[(i, (i + turn) % count) for i in range(count)] for turn in turns]


def plan_kernel(counts, owner_ref, slot_ref, order_ref, marks_ref, counter):
    count = counts[0]
    n_sets = len(partners(count))
    groups = 4 * ((n_sets + 3) // 4)
    own = lax.axis_index("gx")
    for g in range(groups):
        counter[g] = 0
    places = []
    for n in range(owner_ref.shape[-1]):
        if count == window:
            group = lax.bitwise_xor(owner_ref[0, 0, n], own)
        else:
            turn = lax.rem(owner_ref[0, 0, n] - own + count, count)
            group = turn if n_sets == count else jnp.where(
                turn < window, turn, turn - (count - n_sets)
            )
        taken = counter[group]
        counter[group] = taken + 1
        places.append(group * window + taken)
    column = lane((8, 128))
    quarter = column // 32
    for s in range(groups // 4):
        labels = jnp.full((8, 128), -1.0, f32)
        order = column
        for n, place in enumerate(places):
            here = column // 8 == place - 16 * s
            labels = jnp.where(here, slot_ref[0, 0, n].astype(f32), labels)
            order = jnp.where(here, 8 * n + lax.rem(column, 8), order)
        for t in range(4):
            order_ref[4 * s + t] = pltpu.roll(order, 32 * t, 1) if t else order
        for r in range(min(4, n_sets - 4 * s)):
            marks = labels
            for t in range(1, 4):
                marks = jnp.where(quarter == (r + t) % 4, pltpu.roll(labels, 32 * t, 1), marks)
            marks_ref[4 * s + r] = marks


def speeds(state):
    inverse = 1.0 / (state[0] + 1.0)
    return [state[c] * inverse for c in (1, 2, 3)]


def vorticity_kernel(les_ref, velocity_ref, vort_ref):
    velocity = speeds([les_ref[c] for c in range(4)])

    def slope(c, axis):
        return shifted(velocity[c], axis, 1) - shifted(velocity[c], axis, -1)

    vort = [slope(2, 1) - slope(1, 2), slope(0, 2) - slope(2, 0), slope(1, 0) - slope(0, 1)]
    for c in range(3):
        velocity_ref[c] = velocity[c]
        vort_ref[c] = vort[c]


def lamb_kernel(
    counts, n_faces, proj_smem, proj_ref, order_ref, marks_ref, velocity_ref, vort_ref, *refs
):
    face_refs, out_refs = refs[:n_faces], refs[n_faces:]
    outer = [
        (speeds(before), speeds(after)) for before, after in load_faces(face_refs, counts, 0, 4)
    ]

    def rise(c, axis):
        return -outer[axis][0][c], outer[axis][1][c]

    def fall(c, axis):
        return outer[axis][0][c], -outer[axis][1][c]

    layers = [
        (None, rise(2, 1), fall(1, 2)),
        (fall(2, 0), None, rise(0, 2)),
        (rise(1, 0), fall(0, 1), None),
    ]
    vort = [0.5 * jnp.stack(with_layers(vort_ref[c], layers[c]), axis=0) for c in range(3)]
    velocity = read_all(velocity_ref)
    lamb = [
        vort[1] * velocity[2] - vort[2] * velocity[1],
        vort[2] * velocity[0] - vort[0] * velocity[2],
        vort[0] * velocity[1] - vort[1] * velocity[0],
    ]
    proj = proj_ref[...]
    blocks = []
    for field in lamb:
        along_y = proj[:, 0:1][None] * field[:, 0:1, :]
        for b in range(1, 8):
            along_y = along_y + proj[:, b : b + 1][None] * field[:, b : b + 1, :]
        for i in range(8):
            plane = proj_smem[i, 0] * along_y[0]
            for a in range(1, 8):
                plane = plane + proj_smem[i, a] * along_y[a]
            blocks.append(plane)

    quarter = lane((8, 128)) // 32
    for s in range((len(out_refs) + 3) // 4):
        ordered = [
            jnp.take_along_axis(block, order_ref[4 * s + k % 4], axis=1)
            for k, block in enumerate(blocks)
        ]
        for r in range(min(4, len(out_refs) - 4 * s)):
            out = out_refs[4 * s + r]
            for q in range(6):
                packed = ordered[4 * q]
                for t in range(1, 4):
                    packed = jnp.where(quarter == (r + t) % 4, ordered[4 * q + t], packed)
                out[q] = packed
            out[6] = marks_ref[4 * s + r]


def first_kernel(
    counts, n_faces, deriv_ref, high_ref, low_ref, les_ref, wave_ref, mean_ref, *refs
):
    face_refs, (section_ref, rate_ref) = refs[:n_faces], refs[n_faces:]
    state = read_all(les_ref)
    rate = les_rate(state, load_faces(face_refs, counts, 0, 5))
    for c in range(5):
        section_ref[c] = state[c] + rate[c]
    rate = acoustic_rate(
        read_all(wave_ref), read_all(mean_ref), load_faces(face_refs, counts, 5, 9),
        deriv_ref[...], (high_ref[...], low_ref[...]),
    )
    for c in range(4):
        rate_ref[c] = rate[c]


def source_kernel(counts, proj_ref, wave_ref, rate_ref, section_ref, *refs):
    n_pieces = len(partners(counts[0]))
    pieces, refs = refs[:n_pieces][::-1], refs[n_pieces:]
    (source_ref, middle_ref, carry_ref), face_refs = refs[:3], refs[3:]
    quarter = lane((8, 128)) // 32
    tile = tile_rows(proj_ref[...], True)
    tile_high = tile.astype(jnp.bfloat16).astype(f32)
    tile_low = tile - tile_high
    total = None
    for s in range((n_pieces + 3) // 4):
        count = min(4, n_pieces - 4 * s)

        def gathered(q, t):
            value = jnp.full((8, 128), -1.0 if q == 6 else 0.0, f32)
            for r in range(count):
                value = jnp.where(quarter == (r + t) % 4, pieces[4 * s + r][q], value)
            return value

        here = [gathered(6, 0).astype(jnp.int32) == slot for slot in range(16)]
        chosen_high, chosen_low = [
            jnp.concatenate([jnp.where(h, part, 0.0) for h in here], axis=0).astype(jnp.bfloat16)
            for part in (tile_high, tile_low)
        ]
        data = []
        for k in range(24):
            piece = gathered(k // 4, k % 4)
            data.append(pltpu.roll(piece, 128 - 32 * (k % 4), 1) if k % 4 else piece)
        data = jnp.concatenate(data, axis=0)
        high = data.astype(jnp.bfloat16)
        low = (data - high.astype(f32)).astype(jnp.bfloat16)
        dot = functools.partial(
            lax.dot_general,
            dimension_numbers=(((1,), (1,)), ((), ())),
            preferred_element_type=f32,
        )
        moved = dot(high, chosen_high) + (dot(low, chosen_high) + dot(high, chosen_low))
        total = moved if total is None else total + moved
    source = [total[64 * c : 64 * c + 64].reshape(8, 8, 128) for c in range(3)]
    middle = []
    for c in range(4):
        rate = rate_ref[c]
        if c:
            source_ref[c - 1] = source[c - 1]
            rate = rate + source[c - 1]
        middle.append(wave_ref[c] + acoustic_step * rate)
        middle_ref[c] = middle[c]
        carry = wave_ref[c] + middle[c]
        carry_ref[c] = carry + acoustic_step * source[c - 1] if c else carry
    store_faces(read_all(section_ref) + middle, face_refs, counts)


def inner_kernel(
    deriv_ref, high_ref, low_ref, les_ref, section_ref, middle_ref, carry_ref, mean_ref, source_ref,
    les_base_ref, wave_base_ref, source_out, sem,
):
    copy = pltpu.make_async_copy(source_ref, source_out, sem)
    copy.start()
    section = read_all(section_ref)
    rate = les_rate(section, None)
    for c in range(5):
        les_base_ref[c] = 0.5 * ((les_ref[c] + section[c]) + rate[c])
    rate = acoustic_rate(
        read_all(middle_ref), read_all(mean_ref), None,
        deriv_ref[...], (high_ref[...], low_ref[...]),
    )
    for c in range(4):
        wave_base_ref[c] = 0.5 * (carry_ref[c] + acoustic_step * rate[c])
    copy.wait()


def last_kernel(counts, n_faces, les_base_ref, wave_base_ref, mean_ref, *refs):
    face_refs, (les_out, wave_out, les_ref, wave_ref, sems) = (
        refs[:n_faces], refs[n_faces:],
    )
    copies = []

    def send(source, target):
        copies.append(pltpu.make_async_copy(source, target, sems.at[len(copies)]))
        copies[-1].start()

    layers = les_outer(load_faces(face_refs, counts, 0, 5))
    for c in range(5):
        part = [(0.5 * low[c], 0.5 * high[c]) for low, high in layers]
        for x, plane in enumerate(with_layers(les_base_ref[c], part)):
            les_ref[c, x] = plane
        send(les_ref.at[c], les_out.at[c])
    layers = acoustic_outer(read_all(mean_ref), load_faces(face_refs, counts, 5, 9))
    step = 0.5 * acoustic_step
    for c in range(4):
        part = [(step * low[c], step * high[c]) for low, high in layers]
        for x, plane in enumerate(with_layers(wave_base_ref[c], part)):
            wave_ref[c, x] = plane
        send(wave_ref.at[c], wave_out.at[c])
    for copy in copies:
        copy.wait()


VMEM = pl.BlockSpec(memory_space=pltpu.VMEM)
SMEM = pl.BlockSpec(memory_space=pltpu.SMEM)


HBM = pl.BlockSpec(memory_space=pltpu.HBM)


def call(kernel, in_specs, out_shapes, name, cost, scratch=(), out_spec=None):
    return pl.pallas_call(
        kernel,
        in_specs=in_specs,
        out_specs=out_spec or [VMEM] * len(out_shapes),
        out_shape=out_shapes,
        scratch_shapes=list(scratch),
        name=name,
        cost_estimate=pl.CostEstimate(flops=cost, bytes_accessed=800000, transcendentals=0),
        compiler_params=pltpu.CompilerParams(vmem_limit_bytes=24 * 1024 * 1024),
    )


def local(counts, les, wave, mean, projection, owner, slot):
    shape = les.shape[1:]
    faces = face_shapes(counts, 9)
    n_faces = len(faces)
    like = lambda n: jax.ShapeDtypeStruct((n,) + shape, f32)

    table = derivative_matrix()
    deriv = jnp.asarray(table, f32)
    along_z = np.kron(np.eye(16), table.T).astype(np.float32)
    high = along_z.astype(jnp.bfloat16)
    low = (along_z - high.astype(np.float32)).astype(jnp.bfloat16)
    tables = (deriv, jnp.asarray(high), jnp.asarray(low))

    les_hbm, wave_hbm = les, wave
    les, wave, *sent = call(
        functools.partial(load_kernel, counts),
        [HBM] * 2,
        [like(5), like(4)] + faces,
        "load_and_faces",
        100000,
        [pltpu.SemaphoreType.DMA((2,))],
    )(*(pltpu.with_memory_space_constraint(a, pltpu.HBM) for a in (les_hbm, wave_hbm)))
    got = exchange(sent, counts)

    sets = partners(counts[0])
    n_plans = 4 * ((len(sets) + 3) // 4)
    plan = call(
        functools.partial(plan_kernel, counts),
        [SMEM] * 2,
        [
            jax.ShapeDtypeStruct((n_plans, 8, 128), jnp.int32),
            jax.ShapeDtypeStruct((len(sets), 8, 128), f32),
        ],
        "plan",
        4000000,
        [pltpu.SMEM((8,), jnp.int32)],
    )(owner, slot)
    turning = call(vorticity_kernel, [VMEM], [like(3)] * 2, "vorticity", 1000000)(les)
    pieces = call(
        functools.partial(lamb_kernel, counts, n_faces),
        [SMEM] + [VMEM] * (5 + n_faces),
        [jax.ShapeDtypeStruct((7, 8, 128), f32)] * len(sets),
        "lamb_blocks",
        10000000,
    )(projection, projection, *plan, *turning, *got)
    moved = [None] * len(sets)
    for k in reversed(range(len(sets))):
        still = all(i == j for i, j in sets[k])
        moved[k] = pieces[k] if still else lax.ppermute(pieces[k], "gx", sets[k])
    section, rate = call(
        functools.partial(first_kernel, counts, n_faces),
        [VMEM] * (6 + n_faces),
        [like(5), like(4)],
        "first_rates",
        40000000,
    )(*tables, les, wave, mean, *got)

    source, middle, carry, *sent = call(
        functools.partial(source_kernel, counts),
        [VMEM] * (4 + len(moved)),
        [like(3), like(4), like(4)] + faces,
        "source_and_faces",
        10000000,
    )(projection, wave, rate, section, *moved[::-1])
    got = exchange(sent, counts)
    les_base, wave_base, source_out = call(
        inner_kernel,
        [VMEM] * 9,
        [like(5), like(4), like(3)],
        "second_rates_inner",
        40000000,
        [pltpu.SemaphoreType.DMA],
        out_spec=[VMEM, VMEM, HBM],
    )(*tables, les, section, middle, carry, mean, source)
    les_next, wave_next = call(
        functools.partial(last_kernel, counts, n_faces),
        [VMEM] * (3 + n_faces),
        [like(5), like(4)],
        "second_rates_outer",
        4000000,
        [
            pltpu.VMEM(les.shape, f32),
            pltpu.VMEM(wave.shape, f32),
            pltpu.SemaphoreType.DMA((9,)),
        ],
        out_spec=[HBM, HBM],
    )(les_base, wave_base, mean, *got)
    return les_next, source_out, wave_next


def solution(mesh):
    counts = tuple(mesh.shape[axis] for axis in axes)
    field = P(None, *axes)
    return jax.shard_map(
        functools.partial(local, counts),
        mesh=mesh,
        in_specs=(field, field, field, P(), P(*axes), P(*axes)),
        out_specs=(field, field, field),
        check_vma=False,
    )
```

```python
import functools

import jax
import jax.numpy as jnp
import numpy as np
from jax import lax
from jax.experimental import pallas as pl
from jax.experimental.pallas import tpu as pltpu
from jax.sharding import PartitionSpec as P

lobatto_points = np.array(
    [
        -1.0,
        -0.8717401485096066,
        -0.5917001814331423,
        -0.2092992179024789,
        0.2092992179024789,
        0.5917001814331423,
        0.8717401485096066,
        1.0,
    ]
)
flux_half = 0.08
gamma_less = 0.4
acoustic_step = 0.01
upwind_speed = 1.5
face_lift = 28.0
free_stream = (1.0, 0.0, 0.0, 0.0, 2.5)
axes = ("gx", "gy", "gz")
window = 4
f32 = jnp.float32


def derivative_matrix():
    points = lobatto_points
    products = [np.prod([points[i] - points[j] for j in range(8) if j != i]) for i in range(8)]
    matrix = np.zeros((8, 8))
    for i in range(8):
        for j in range(8):
            if j != i:
                matrix[i, j] = products[i] / (products[j] * (points[i] - points[j]))
        matrix[i, i] = -np.sum(matrix[i])
    return matrix


def sublane(shape):
    return lax.broadcasted_iota(jnp.int32, shape, len(shape) - 2)


def lane(shape):
    return lax.broadcasted_iota(jnp.int32, shape, len(shape) - 1)


def rolled(tile, amount, axis):
    amount = amount % tile.shape[axis]
    return pltpu.roll(tile, amount, axis) if amount else tile


def shifted(field, axis, step, outer=None):
    if axis == 0:
        outer = jnp.zeros((8, 128), f32) if outer is None else outer
        if step == 1:
            return jnp.concatenate([field[1:], outer[None]], axis=0)
        return jnp.concatenate([outer[None], field[:-1]], axis=0)
    count = (8, 128)[axis - 1]
    edge = count - 1 if step == 1 else 0
    at_edge = (sublane if axis == 1 else lane)((8, 128)) == edge
    planes = []
    for x in range(8):
        layer = 0.0 if outer is None else rolled(outer, edge - axis * x, axis - 1)
        planes.append(jnp.where(at_edge, layer, rolled(field[x], -step, axis - 1)))
    return jnp.stack(planes, axis=0)


def fluid(state):
    density, mx, my, mz, energy = [s + r for s, r in zip(state, free_stream)]
    inverse = 1.0 / density
    momentum = (mx, my, mz)
    velocity = [m * inverse for m in momentum]
    pressure = gamma_less * (
        energy - 0.5 * (mx * velocity[0] + my * velocity[1] + mz * velocity[2])
    )
    return momentum, velocity, pressure, energy + pressure


def split_flux(state, parts, axis, sign):
    momentum, velocity, pressure, enthalpy = parts
    speed = velocity[axis]
    flux = [momentum[axis]]
    for c in range(3):
        term = momentum[c] * speed
        flux.append(term + pressure if c == axis else term)
    flux.append(enthalpy * speed)
    if sign > 0:
        return [flux_half * (s + f) for s, f in zip(state, flux)]
    return [flux_half * (s - f) for s, f in zip(state, flux)]


def les_rate(state, halos):
    parts = fluid(state)
    total = [-6.0 * flux_half * s for s in state]
    for axis in range(3):
        ahead = split_flux(state, parts, axis, -1)
        behind = split_flux(state, parts, axis, 1)
        ahead_outer = behind_outer = [None] * 5
        if halos is not None:
            before, after = halos[axis]
            ahead_outer = split_flux(after, fluid(after), axis, -1)
            behind_outer = split_flux(before, fluid(before), axis, 1)
        for c in range(5):
            total[c] = total[c] + (
                shifted(ahead[c], axis, 1, ahead_outer[c])
                + shifted(behind[c], axis, -1, behind_outer[c])
            )
    return total


def les_outer(halos):
    return [
        (
            split_flux(before, fluid(before), axis, 1),
            split_flux(after, fluid(after), axis, -1),
        )
        for axis, (before, after) in enumerate(halos)
    ]


def with_layers(field, layers):
    row, column = sublane((8, 128)), lane((8, 128))
    along_z = layers[2]
    if along_z is not None:
        along_z = jnp.where(lax.rem(column, 2) == 0, along_z[0], rolled(along_z[1], -1, 1))
    planes = []
    for x in range(8):
        plane = field[x]
        if layers[0] is not None and x in (0, 7):
            plane = plane + layers[0][x // 7]
        if layers[1] is not None:
            low, high = layers[1]
            plane = plane + jnp.where(
                row == 0, rolled(low, -x, 0), jnp.where(row == 7, rolled(high, 7 - x, 0), 0.0)
            )
        if along_z is not None:
            ends = (column == 0) | (column == 127)
            plane = plane + jnp.where(ends, rolled(along_z, -2 * x, 1), 0.0)
        planes.append(plane)
    return planes


def wave_flux(state, mean, axis):
    speed = mean[axis]
    pressure = state[0]
    rows = [speed * pressure + state[1 + axis]]
    for c in range(3):
        term = speed * state[1 + c]
        rows.append(term + pressure if c == axis else term)
    return rows


def dot3(left, right):
    high = left.astype(jnp.bfloat16)
    low = (left - high.astype(f32)).astype(jnp.bfloat16)
    dot = functools.partial(jnp.dot, preferred_element_type=f32)
    return dot(high, right[0]) + (dot(low, right[0]) + dot(high, right[1]))


def acoustic_rate(state, mean, halos, deriv, along_z):
    shape = state[0].shape
    table = derivative_matrix()
    flux = wave_flux(state, mean, 0)
    if halos is None:
        halos = [([jnp.zeros((8, 128), f32)] * 4,) * 2] + [([None] * 4,) * 2] * 2
    before, after = halos[0]
    low_mean, high_mean = [m[0] for m in mean], [m[7] for m in mean]
    low_jump = [b - s[0] for b, s in zip(before, state)]
    high_jump = [a - s[7] for a, s in zip(after, state)]
    low_flux = wave_flux(low_jump, low_mean, 0)
    high_flux = wave_flux(high_jump, high_mean, 0)
    half, lift = 0.5 * face_lift, 0.5 * face_lift * upwind_speed
    total = []
    for c in range(4):
        planes = []
        for i in range(8):
            plane = -float(table[i, 0]) * flux[c][0]
            for a in range(1, 8):
                if abs(table[i, a]) > 1e-12:
                    plane = plane - float(table[i, a]) * flux[c][a]
            if i == 0:
                plane = plane + (half * low_flux[c] + lift * low_jump[c])
            if i == 7:
                plane = plane - (half * high_flux[c] - lift * high_jump[c])
            planes.append(plane)
        total.append(jnp.stack(planes, axis=0))
    flux = wave_flux(state, mean, 1)
    before, after = halos[1]
    row = sublane(shape)
    sign = jnp.where(row == 0, half, jnp.where(row == 7, -half, 0.0))
    jump = []
    for s, b, a in zip(state, before, after):
        planes = []
        for x in range(8):
            low = 0.0 if b is None else rolled(b, -x, 0)
            high = 0.0 if a is None else rolled(a, 7 - x, 0)
            planes.append(jnp.where(row[x] == 0, low, jnp.where(row[x] == 7, high, s[x])) - s[x])
        jump.append(jnp.stack(planes, axis=0))
    jump_flux = wave_flux(jump, mean, 1)
    for c in range(4):
        change = lift * jump[c] + sign * jump_flux[c]
        for b in range(8):
            change = change - deriv[:, b : b + 1][None] * flux[c][:, b : b + 1, :]
        total[c] = total[c] + change
    flux = wave_flux(state, mean, 2)
    before, after = halos[2]
    column = lane(shape)
    place = lax.rem(column, 8)
    sign = jnp.where(place == 0, half, jnp.where(place == 7, -half, 0.0))
    jump = [
        jnp.where(
            place == 0,
            shifted(s, 2, -1, b),
            jnp.where(place == 7, shifted(s, 2, 1, a), s),
        )
        - s
        for s, b, a in zip(state, before, after)
    ]
    jump_flux = wave_flux(jump, mean, 2)
    for c in range(4):
        slope = dot3(flux[c].reshape(64, 128), along_z).reshape(shape)
        total[c] = total[c] + (lift * jump[c] + sign * jump_flux[c] - slope)
    return total


def acoustic_outer(mean, halos):
    half, lift = 0.5 * face_lift, 0.5 * face_lift * upwind_speed
    layers = []
    for axis, (before, after) in enumerate(halos):
        if axis == 0:
            low, high = [m[0] for m in mean], [m[7] for m in mean]
        elif axis == 1:
            low, high = [m[:, 0, :] for m in mean], [m[:, 7, :] for m in mean]
        else:
            low, high = [[z_layer(m, jnp.int32(at)) for m in mean] for at in (0, 127)]
        low_flux = wave_flux(before, low, axis)
        high_flux = wave_flux(after, high, axis)
        layers.append(
            (
                [half * f + lift * b for f, b in zip(low_flux, before)],
                [lift * a - half * f for f, a in zip(high_flux, after)],
            )
        )
    return layers


def tile_rows(matrix):
    spread = (lax.rem(lane((8, 128)), 8) == sublane((8, 128))).astype(f32)
    return jnp.dot(
        matrix, spread, precision=lax.Precision.HIGHEST, preferred_element_type=f32
    )


def pairings(count):
    sets = []
    for first in (0, 1):
        pairs = [(i, i + 1) for i in range(first, count - 1, 2)]
        if pairs:
            sets.append(pairs)
    return sets


def routes(counts):
    places = [(x, y, z) for x in range(counts[0]) for y in range(counts[1]) for z in range(counts[2])]
    number = {place: n for n, place in enumerate(places)}
    found = []
    for axis in range(3):
        for pairs in pairings(counts[axis]):
            swap = dict(pairs + [(j, i) for i, j in pairs])
            alone = [i for i in range(counts[axis]) if i not in swap]
            spare = 0 if axis else 2
            route = []
            for place in places:
                other = list(place)
                if place[axis] in swap:
                    other[axis] = swap[place[axis]]
                elif axis == 0 and len(alone) == 2:
                    other[axis] = sum(alone) - place[axis]
                elif counts[spare] % 2 == 0:
                    other[spare] = place[spare] ^ 1
                route.append((number[place], number[tuple(other)]))
            found.append(route)
    return found


def z_layer(field, at):
    packed = jnp.zeros((8, 128), f32)
    column = lane((8, 128))
    for x in range(8):
        turned = pltpu.roll(field[x], lax.rem(2 * x - at + 128, 128), 1)
        packed = jnp.where(column == 2 * x, turned, packed)
    return packed


def store_faces(fields, out_refs, counts):
    at = 0
    for axis in range(3):
        even = lax.rem(lax.axis_index(axes[axis]), 2) == 0
        sets = len(pairings(counts[axis]))
        for c, field in enumerate(fields):
            if axis == 0:
                low, high = field[0], field[7]
            elif axis == 1:
                low, high = field[:, 0, :], field[:, 7, :]
            for s in range(sets):
                upper = even == (s == 0)
                if axis == 2:
                    out_refs[at + s][c] = z_layer(field, jnp.where(upper, 127, 0))
                else:
                    out_refs[at + s][c] = jnp.where(upper, high, low)
        at += sets


def sending_order(counts, stage):
    where = [(axis, s) for axis in range(3) for s in range(len(pairings(counts[axis])))]
    along_y = ((1, 1), (1, 0)) if stage == 1 else ((1, 0), (1, 1))
    wanted = ((2, 1), (2, 0)) + along_y + ((0, 1), (0, 0))
    return [where.index(p) for p in wanted if p in where]


def load_faces(sent_refs, counts, stage, first, last):
    in_refs = [None] * len(sent_refs)
    for ref, at in zip(sent_refs, sending_order(counts, stage)):
        in_refs[at] = ref
    halos = []
    at = 0
    for axis in range(3):
        even = lax.rem(lax.axis_index(axes[axis]), 2) == 0
        sets = len(pairings(counts[axis]))
        got = [[in_refs[at + s][c] for c in range(first, last)] for s in range(sets)]
        while len(got) < 2:
            got.append([jnp.zeros((8, 128), f32)] * (last - first))
        place = lax.axis_index(axes[axis])
        before = [
            jnp.where(place == 0, 0.0, jnp.where(even, b, a)) for a, b in zip(*got)
        ]
        after = [
            jnp.where(place == counts[axis] - 1, 0.0, jnp.where(even, a, b))
            for a, b in zip(*got)
        ]
        halos.append((before, after))
        at += sets
    return halos


def face_shapes(counts, width):
    total = sum(len(pairings(count)) for count in counts)
    return [jax.ShapeDtypeStruct((width, 8, 128), f32)] * total


def exchange(faces, counts, stage):
    ways = routes(counts)
    return [lax.ppermute(faces[at], axes, ways[at]) for at in sending_order(counts, stage)]


def read_all(ref):
    return [ref[c] for c in range(ref.shape[0])]


def load_kernel(counts, *refs):
    sources, targets, out_refs, sems = refs[:5], refs[5:10], refs[10:-1], refs[-1]
    copies = [
        pltpu.make_async_copy(source, target, sems.at[n])
        for n, (source, target) in enumerate(zip(sources, targets))
    ]
    for copy in copies:
        copy.start()
    for copy, target, first in zip(copies, targets, (0, 5)):
        copy.wait()
        count = target.shape[0]
        store_faces(read_all(target), [ref.at[first : first + count] for ref in out_refs], counts)
    for copy in copies[2:]:
        copy.wait()


def partners(count):
    if count == window:
        return [[(i, i ^ mask) for i in range(count)] for mask in range(count)]
    turns = sorted({d % count for d in range(1 - window, window)})
    return [[(i, (i + turn) % count) for i in range(count)] for turn in turns]


def sending_sets(count):
    return [2, 3, 1, 0] if count == window else list(range(count))


def plan_kernel(
    counts, owner_ref, slot_ref, proj_ref, order_ref, marks_ref, along_x_ref, along_y_ref, tile_ref
):
    count = counts[0]
    n_sets = len(partners(count))
    own = lax.axis_index("gx")
    n_blocks = owner_ref.shape[-1]
    square = (n_blocks, n_blocks)
    block, other = sublane(square), lane(square)

    def spread(ref):
        by_lane = jnp.broadcast_to(ref[0], square)
        here = jnp.where(block == other, by_lane, 0).astype(f32)
        return by_lane, jnp.sum(here, axis=1, keepdims=True).astype(jnp.int32)

    def group_of(owner):
        if count == window:
            return lax.bitwise_xor(owner, own)
        turn = lax.rem(owner - own + count, count)
        if n_sets == count:
            return turn
        return jnp.where(turn < window, turn, turn - (count - n_sets))

    owner_by_lane, owner = spread(owner_ref)
    slot = spread(slot_ref)[1]
    group = group_of(owner)
    before = (group_of(owner_by_lane) == group) & (other < block)
    taken = jnp.sum(before.astype(f32), axis=1, keepdims=True).astype(jnp.int32)
    wide = (n_blocks, 128)
    place = jnp.broadcast_to(group * window + taken, wide)
    column = lane((8, 128))
    quarter = column // 32
    for s in range((n_sets + 3) // 4):
        here = place - 16 * s == lane(wide) // 8
        label = jnp.sum(jnp.where(here, (slot + 1).astype(f32), 0.0), axis=0, keepdims=True) - 1.0
        source = jnp.sum(
            jnp.where(here, (8 * sublane(wide)).astype(f32), 0.0), axis=0, keepdims=True
        )
        labels = jnp.broadcast_to(label, (8, 128))
        order = jnp.broadcast_to(source, (8, 128)).astype(jnp.int32) + lax.rem(column, 8)
        for t in range(4):
            order_ref[4 * s + t] = rolled(order, 32 * t, 1)
        for r in range(min(4, n_sets - 4 * s)):
            marks = labels
            for t in range(1, 4):
                marks = jnp.where(quarter == (r + t) % 4, rolled(labels, 32 * t, 1), marks)
            marks_ref[4 * s + r] = marks
    proj = proj_ref[...]
    for a in range(8):
        along_y = jnp.broadcast_to(proj[:, a : a + 1], (8, 128))
        along_y_ref[a] = along_y
        for i in range(8):
            along_x_ref[8 * i + a] = jnp.broadcast_to(along_y[i : i + 1], (8, 128))
    tile = tile_rows(proj)
    high = tile.astype(jnp.bfloat16).astype(f32)
    tile_ref[0] = high
    tile_ref[1] = tile - high


def speeds(state):
    inverse = 1.0 / (state[0] + 1.0)
    return [state[c] * inverse for c in (1, 2, 3)]


def vorticity_kernel(les_ref, velocity_ref, vort_ref):
    velocity = speeds([les_ref[c] for c in range(4)])

    def slope(c, axis):
        return shifted(velocity[c], axis, 1) - shifted(velocity[c], axis, -1)

    vort = [slope(2, 1) - slope(1, 2), slope(0, 2) - slope(2, 0), slope(1, 0) - slope(0, 1)]
    for c in range(3):
        velocity_ref[c] = velocity[c]
        vort_ref[c] = vort[c]


def lamb_kernel(
    counts, n_faces, order_ref, marks_ref, along_x_ref, along_y_ref, velocity_ref, vort_ref, *refs
):
    face_refs, out_refs = refs[:n_faces], refs[n_faces:]
    outer = [
        (speeds(before), speeds(after)) for before, after in load_faces(face_refs, counts, 1, 0, 4)
    ]

    def rise(c, axis):
        return -outer[axis][0][c], outer[axis][1][c]

    def fall(c, axis):
        return outer[axis][0][c], -outer[axis][1][c]

    layers = [
        (None, rise(2, 1), fall(1, 2)),
        (fall(2, 0), None, rise(0, 2)),
        (rise(1, 0), fall(0, 1), None),
    ]
    vort = [0.5 * jnp.stack(with_layers(vort_ref[c], layers[c]), axis=0) for c in range(3)]
    velocity = read_all(velocity_ref)
    lamb = [
        vort[1] * velocity[2] - vort[2] * velocity[1],
        vort[2] * velocity[0] - vort[0] * velocity[2],
        vort[0] * velocity[1] - vort[1] * velocity[0],
    ]
    blocks = []
    for field in lamb:
        along_y = along_y_ref[0][None] * field[:, 0:1, :]
        for b in range(1, 8):
            along_y = along_y + along_y_ref[b][None] * field[:, b : b + 1, :]
        for i in range(8):
            plane = along_x_ref[8 * i] * along_y[0]
            for a in range(1, 8):
                plane = plane + along_x_ref[8 * i + a] * along_y[a]
            blocks.append(plane)

    quarter = lane((8, 128)) // 32
    for s in range((len(out_refs) + 3) // 4):
        ordered = [
            jnp.take_along_axis(block, order_ref[4 * s + k % 4], axis=1)
            for k, block in enumerate(blocks)
        ]
        for r in range(min(4, len(out_refs) - 4 * s)):
            out = out_refs[4 * s + r]
            for q in range(6):
                packed = ordered[4 * q]
                for t in range(1, 4):
                    packed = jnp.where(quarter == (r + t) % 4, ordered[4 * q + t], packed)
                out[q] = packed
            out[6] = marks_ref[4 * s + r]


def first_kernel(
    counts, n_faces, deriv_ref, high_ref, low_ref, les_ref, wave_ref, mean_ref, *refs
):
    face_refs, (section_ref, rate_ref), out_refs = (
        refs[:n_faces], refs[n_faces : n_faces + 2], refs[n_faces + 2 :],
    )
    state = read_all(les_ref)
    rate = les_rate(state, load_faces(face_refs, counts, 1, 0, 5))
    section = [s + r for s, r in zip(state, rate)]
    for c in range(5):
        section_ref[c] = section[c]
    store_faces(section, out_refs, counts)
    rate = acoustic_rate(
        read_all(wave_ref), read_all(mean_ref), load_faces(face_refs, counts, 1, 5, 9),
        deriv_ref[...], (high_ref[...], low_ref[...]),
    )
    for c in range(4):
        rate_ref[c] = rate[c]


def source_kernel(counts, n_faces, tile_ref, wave_ref, rate_ref, *refs):
    n_pieces = len(partners(counts[0]))
    pieces = [None] * n_pieces
    for ref, k in zip(refs, sending_sets(n_pieces)):
        pieces[k] = ref
    refs = refs[n_pieces:]
    section_faces, (source_ref, middle_ref, carry_ref), face_refs = (
        refs[:n_faces], refs[n_faces : n_faces + 3], refs[n_faces + 3 :],
    )
    quarter = lane((8, 128)) // 32
    tile_high, tile_low = tile_ref[0], tile_ref[1]
    total = None
    for s in range((n_pieces + 3) // 4):
        count = min(4, n_pieces - 4 * s)

        def gathered(q, t):
            value = jnp.full((8, 128), -1.0 if q == 6 else 0.0, f32)
            for r in range(count):
                value = jnp.where(quarter == (r + t) % 4, pieces[4 * s + r][q], value)
            return value

        here = [gathered(6, 0).astype(jnp.int32) == slot for slot in range(16)]
        chosen_high, chosen_low = [
            jnp.concatenate([jnp.where(h, part, 0.0) for h in here], axis=0).astype(jnp.bfloat16)
            for part in (tile_high, tile_low)
        ]
        data = []
        for k in range(24):
            piece = gathered(k // 4, k % 4)
            data.append(pltpu.roll(piece, 128 - 32 * (k % 4), 1) if k % 4 else piece)
        data = jnp.concatenate(data, axis=0)
        high = data.astype(jnp.bfloat16)
        low = (data - high.astype(f32)).astype(jnp.bfloat16)
        dot = functools.partial(
            lax.dot_general,
            dimension_numbers=(((1,), (1,)), ((), ())),
            preferred_element_type=f32,
        )
        moved = dot(high, chosen_high) + (dot(low, chosen_high) + dot(high, chosen_low))
        total = moved if total is None else total + moved
    source = [total[64 * c : 64 * c + 64].reshape(8, 8, 128) for c in range(3)]
    middle = []
    for c in range(4):
        rate = rate_ref[c]
        if c:
            source_ref[c - 1] = source[c - 1]
            rate = rate + source[c - 1]
        middle.append(wave_ref[c] + acoustic_step * rate)
        middle_ref[c] = middle[c]
        carry = wave_ref[c] + middle[c]
        carry_ref[c] = carry + acoustic_step * source[c - 1] if c else carry
    for ready, face in zip(section_faces, face_refs):
        face[0:5] = ready[...]
    store_faces(middle, [face.at[5:9] for face in face_refs], counts)


def inner_kernel(
    deriv_ref, high_ref, low_ref, les_ref, section_ref, middle_ref, carry_ref, mean_ref, source_ref,
    les_base_ref, wave_base_ref, source_out, sem,
):
    copy = pltpu.make_async_copy(source_ref, source_out, sem)
    copy.start()
    section = read_all(section_ref)
    rate = les_rate(section, None)
    for c in range(5):
        les_base_ref[c] = 0.5 * ((les_ref[c] + section[c]) + rate[c])
    rate = acoustic_rate(
        read_all(middle_ref), read_all(mean_ref), None,
        deriv_ref[...], (high_ref[...], low_ref[...]),
    )
    for c in range(4):
        wave_base_ref[c] = 0.5 * (carry_ref[c] + acoustic_step * rate[c])
    copy.wait()


def last_kernel(counts, n_faces, les_base_ref, wave_base_ref, mean_ref, *refs):
    face_refs, (les_out, wave_out, les_ref, wave_ref, sems) = (
        refs[:n_faces], refs[n_faces:],
    )
    copies = []

    def send(source, target):
        copies.append(pltpu.make_async_copy(source, target, sems.at[len(copies)]))
        copies[-1].start()

    layers = les_outer(load_faces(face_refs, counts, 2, 0, 5))
    for c in range(5):
        part = [(0.5 * low[c], 0.5 * high[c]) for low, high in layers]
        for x, plane in enumerate(with_layers(les_base_ref[c], part)):
            les_ref[c, x] = plane
        send(les_ref.at[c], les_out.at[c])
    layers = acoustic_outer(read_all(mean_ref), load_faces(face_refs, counts, 2, 5, 9))
    step = 0.5 * acoustic_step
    for c in range(4):
        part = [(step * low[c], step * high[c]) for low, high in layers]
        for x, plane in enumerate(with_layers(wave_base_ref[c], part)):
            wave_ref[c, x] = plane
        send(wave_ref.at[c], wave_out.at[c])
    for copy in copies:
        copy.wait()


VMEM = pl.BlockSpec(memory_space=pltpu.VMEM)


HBM = pl.BlockSpec(memory_space=pltpu.HBM)


def call(kernel, in_specs, out_shapes, name, cost, scratch=(), out_spec=None):
    return pl.pallas_call(
        kernel,
        in_specs=in_specs,
        out_specs=out_spec or [VMEM] * len(out_shapes),
        out_shape=out_shapes,
        scratch_shapes=list(scratch),
        name=name,
        cost_estimate=pl.CostEstimate(flops=cost, bytes_accessed=800000, transcendentals=0),
        compiler_params=pltpu.CompilerParams(vmem_limit_bytes=24 * 1024 * 1024),
    )


def local(counts, les, wave, mean, projection, owner, slot):
    shape = les.shape[1:]
    faces = face_shapes(counts, 9)
    n_faces = len(faces)
    like = lambda n: jax.ShapeDtypeStruct((n,) + shape, f32)

    table = derivative_matrix()
    deriv = jnp.asarray(table, f32)
    along_z = np.kron(np.eye(16), table.T).astype(np.float32)
    high = along_z.astype(jnp.bfloat16)
    low = (along_z - high.astype(np.float32)).astype(jnp.bfloat16)
    tables = (deriv, jnp.asarray(high), jnp.asarray(low))

    arguments = (les, wave, owner, slot, projection)
    les, wave, owner, slot, projection, *sent = call(
        functools.partial(load_kernel, counts),
        [HBM] * 5,
        [jax.ShapeDtypeStruct(a.shape, a.dtype) for a in arguments] + faces,
        "load_and_faces",
        100000,
        [pltpu.SemaphoreType.DMA((5,))],
    )(*(pltpu.with_memory_space_constraint(a, pltpu.HBM) for a in arguments))
    got = exchange(sent, counts, 1)

    sets = partners(counts[0])
    n_plans = 4 * ((len(sets) + 3) // 4)
    order, marks, along_x, along_y, tile = call(
        functools.partial(plan_kernel, counts),
        [VMEM] * 3,
        [
            jax.ShapeDtypeStruct((n_plans, 8, 128), jnp.int32),
            jax.ShapeDtypeStruct((len(sets), 8, 128), f32),
            jax.ShapeDtypeStruct((64, 8, 128), f32),
            jax.ShapeDtypeStruct((8, 8, 128), f32),
            jax.ShapeDtypeStruct((2, 8, 128), f32),
        ],
        "plan",
        1000000,
    )(owner, slot, projection)
    turning = call(vorticity_kernel, [VMEM], [like(3)] * 2, "vorticity", 1000000)(les)
    pieces = call(
        functools.partial(lamb_kernel, counts, n_faces),
        [VMEM] * (6 + n_faces),
        [jax.ShapeDtypeStruct((7, 8, 128), f32)] * len(sets),
        "lamb_blocks",
        10000000,
    )(order, marks, along_x, along_y, *turning, *got)
    moved = []
    for k in sending_sets(len(sets)):
        still = all(i == j for i, j in sets[k])
        moved.append(pieces[k] if still else lax.ppermute(pieces[k], "gx", sets[k]))
    section, rate, *section_faces = call(
        functools.partial(first_kernel, counts, n_faces),
        [VMEM] * (6 + n_faces),
        [like(5), like(4)] + face_shapes(counts, 5),
        "first_rates",
        40000000,
    )(*tables, les, wave, mean, *got)

    source, middle, carry, *sent = call(
        functools.partial(source_kernel, counts, n_faces),
        [VMEM] * (3 + len(moved) + n_faces),
        [like(3), like(4), like(4)] + faces,
        "source_and_faces",
        10000000,
    )(tile, wave, rate, *moved, *section_faces)
    got = exchange(sent, counts, 2)
    les_base, wave_base, source_out = call(
        inner_kernel,
        [VMEM] * 9,
        [like(5), like(4), like(3)],
        "second_rates_inner",
        40000000,
        [pltpu.SemaphoreType.DMA],
        out_spec=[VMEM, VMEM, HBM],
    )(*tables, les, section, middle, carry, mean, source)
    les_next, wave_next = call(
        functools.partial(last_kernel, counts, n_faces),
        [VMEM] * (3 + n_faces),
        [like(5), like(4)],
        "second_rates_outer",
        4000000,
        [
            pltpu.VMEM(les.shape, f32),
            pltpu.VMEM(wave.shape, f32),
            pltpu.SemaphoreType.DMA((9,)),
        ],
        out_spec=[HBM, HBM],
    )(les_base, wave_base, mean, *got)
    return les_next, source_out, wave_next


def solution(mesh):
    counts = tuple(mesh.shape[axis] for axis in axes)
    field = P(None, *axes)
    return jax.shard_map(
        functools.partial(local, counts),
        mesh=mesh,
        in_specs=(field, field, field, P(), P(*axes), P(*axes)),
        out_specs=(field, field, field),
        check_vma=False,
    )
```

```python
import functools

import jax
import jax.numpy as jnp
import numpy as np
from jax import lax
from jax.experimental import pallas as pl
from jax.experimental.pallas import tpu as pltpu
from jax.sharding import PartitionSpec as P

lobatto_points = np.array(
    [
        -1.0,
        -0.8717401485096066,
        -0.5917001814331423,
        -0.2092992179024789,
        0.2092992179024789,
        0.5917001814331423,
        0.8717401485096066,
        1.0,
    ]
)
flux_half = 0.08
gamma_less = 0.4
acoustic_step = 0.01
upwind_speed = 1.5
face_lift = 28.0
free_stream = (1.0, 0.0, 0.0, 0.0, 2.5)
axes = ("gx", "gy", "gz")
window = 4
f32 = jnp.float32


def derivative_matrix():
    points = lobatto_points
    products = [np.prod([points[i] - points[j] for j in range(8) if j != i]) for i in range(8)]
    matrix = np.zeros((8, 8))
    for i in range(8):
        for j in range(8):
            if j != i:
                matrix[i, j] = products[i] / (products[j] * (points[i] - points[j]))
        matrix[i, i] = -np.sum(matrix[i])
    return matrix


def sublane(shape):
    return lax.broadcasted_iota(jnp.int32, shape, len(shape) - 2)


def lane(shape):
    return lax.broadcasted_iota(jnp.int32, shape, len(shape) - 1)


def rolled(tile, amount, axis):
    amount = amount % tile.shape[axis]
    return pltpu.roll(tile, amount, axis) if amount else tile


def shifted(field, axis, step, outer=None):
    if axis == 0:
        outer = jnp.zeros((8, 128), f32) if outer is None else outer
        if step == 1:
            return jnp.concatenate([field[1:], outer[None]], axis=0)
        return jnp.concatenate([outer[None], field[:-1]], axis=0)
    count = (8, 128)[axis - 1]
    edge = count - 1 if step == 1 else 0
    at_edge = (sublane if axis == 1 else lane)((8, 128)) == edge
    planes = []
    for x in range(8):
        layer = 0.0 if outer is None else rolled(outer, edge - axis * x, axis - 1)
        planes.append(jnp.where(at_edge, layer, rolled(field[x], -step, axis - 1)))
    return jnp.stack(planes, axis=0)


def fluid(state):
    density, mx, my, mz, energy = [s + r for s, r in zip(state, free_stream)]
    inverse = 1.0 / density
    momentum = (mx, my, mz)
    velocity = [m * inverse for m in momentum]
    pressure = gamma_less * (
        energy - 0.5 * (mx * velocity[0] + my * velocity[1] + mz * velocity[2])
    )
    return momentum, velocity, pressure, energy + pressure


def split_flux(state, parts, axis, sign):
    momentum, velocity, pressure, enthalpy = parts
    speed = velocity[axis]
    flux = [momentum[axis]]
    for c in range(3):
        term = momentum[c] * speed
        flux.append(term + pressure if c == axis else term)
    flux.append(enthalpy * speed)
    if sign > 0:
        return [flux_half * (s + f) for s, f in zip(state, flux)]
    return [flux_half * (s - f) for s, f in zip(state, flux)]


def les_rate(state, halos):
    parts = fluid(state)
    total = [-6.0 * flux_half * s for s in state]
    for axis in range(3):
        ahead = split_flux(state, parts, axis, -1)
        behind = split_flux(state, parts, axis, 1)
        ahead_outer = behind_outer = [None] * 5
        if halos is not None:
            before, after = halos[axis]
            ahead_outer = split_flux(after, fluid(after), axis, -1)
            behind_outer = split_flux(before, fluid(before), axis, 1)
        for c in range(5):
            total[c] = total[c] + (
                shifted(ahead[c], axis, 1, ahead_outer[c])
                + shifted(behind[c], axis, -1, behind_outer[c])
            )
    return total


def les_outer(halos):
    return [
        (
            split_flux(before, fluid(before), axis, 1),
            split_flux(after, fluid(after), axis, -1),
        )
        for axis, (before, after) in enumerate(halos)
    ]


def with_layers(field, layers):
    row, column = sublane((8, 128)), lane((8, 128))
    along_z = layers[2]
    if along_z is not None:
        along_z = jnp.where(lax.rem(column, 2) == 0, along_z[0], rolled(along_z[1], -1, 1))
    planes = []
    for x in range(8):
        plane = field[x]
        if layers[0] is not None and x in (0, 7):
            plane = plane + layers[0][x // 7]
        if layers[1] is not None:
            low, high = layers[1]
            plane = plane + jnp.where(
                row == 0, rolled(low, -x, 0), jnp.where(row == 7, rolled(high, 7 - x, 0), 0.0)
            )
        if along_z is not None:
            ends = (column == 0) | (column == 127)
            plane = plane + jnp.where(ends, rolled(along_z, -2 * x, 1), 0.0)
        planes.append(plane)
    return planes


def wave_flux(state, mean, axis):
    speed = mean[axis]
    pressure = state[0]
    rows = [speed * pressure + state[1 + axis]]
    for c in range(3):
        term = speed * state[1 + c]
        rows.append(term + pressure if c == axis else term)
    return rows


def dot3(left, right):
    high = left.astype(jnp.bfloat16)
    low = (left - high.astype(f32)).astype(jnp.bfloat16)
    dot = functools.partial(jnp.dot, preferred_element_type=f32)
    return dot(high, right[0]) + (dot(low, right[0]) + dot(high, right[1]))


def acoustic_rate(state, mean, halos, deriv, along_z):
    shape = state[0].shape
    table = derivative_matrix()
    flux = wave_flux(state, mean, 0)
    if halos is None:
        halos = [([jnp.zeros((8, 128), f32)] * 4,) * 2] + [([None] * 4,) * 2] * 2
    before, after = halos[0]
    low_mean, high_mean = [m[0] for m in mean], [m[7] for m in mean]
    low_jump = [b - s[0] for b, s in zip(before, state)]
    high_jump = [a - s[7] for a, s in zip(after, state)]
    low_flux = wave_flux(low_jump, low_mean, 0)
    high_flux = wave_flux(high_jump, high_mean, 0)
    half, lift = 0.5 * face_lift, 0.5 * face_lift * upwind_speed
    total = []
    for c in range(4):
        planes = []
        for i in range(8):
            plane = -float(table[i, 0]) * flux[c][0]
            for a in range(1, 8):
                if abs(table[i, a]) > 1e-12:
                    plane = plane - float(table[i, a]) * flux[c][a]
            if i == 0:
                plane = plane + (half * low_flux[c] + lift * low_jump[c])
            if i == 7:
                plane = plane - (half * high_flux[c] - lift * high_jump[c])
            planes.append(plane)
        total.append(jnp.stack(planes, axis=0))
    flux = wave_flux(state, mean, 1)
    before, after = halos[1]
    row = sublane(shape)
    sign = jnp.where(row == 0, half, jnp.where(row == 7, -half, 0.0))
    jump = []
    for s, b, a in zip(state, before, after):
        planes = []
        for x in range(8):
            low = 0.0 if b is None else rolled(b, -x, 0)
            high = 0.0 if a is None else rolled(a, 7 - x, 0)
            planes.append(jnp.where(row[x] == 0, low, jnp.where(row[x] == 7, high, s[x])) - s[x])
        jump.append(jnp.stack(planes, axis=0))
    jump_flux = wave_flux(jump, mean, 1)
    for c in range(4):
        change = lift * jump[c] + sign * jump_flux[c]
        for b in range(8):
            change = change - deriv[:, b : b + 1][None] * flux[c][:, b : b + 1, :]
        total[c] = total[c] + change
    flux = wave_flux(state, mean, 2)
    before, after = halos[2]
    column = lane(shape)
    place = lax.rem(column, 8)
    sign = jnp.where(place == 0, half, jnp.where(place == 7, -half, 0.0))
    jump = [
        jnp.where(
            place == 0,
            shifted(s, 2, -1, b),
            jnp.where(place == 7, shifted(s, 2, 1, a), s),
        )
        - s
        for s, b, a in zip(state, before, after)
    ]
    jump_flux = wave_flux(jump, mean, 2)
    for c in range(4):
        slope = dot3(flux[c].reshape(64, 128), along_z).reshape(shape)
        total[c] = total[c] + (lift * jump[c] + sign * jump_flux[c] - slope)
    return total


def mean_layers(mean):
    return [
        [m[0] for m in mean],
        [m[7] for m in mean],
        [m[:, 0, :] for m in mean],
        [m[:, 7, :] for m in mean],
        [z_layer(m, jnp.int32(0)) for m in mean],
        [z_layer(m, jnp.int32(127)) for m in mean],
    ]


def acoustic_outer(mean_faces, halos):
    half, lift = 0.5 * face_lift, 0.5 * face_lift * upwind_speed
    layers = []
    for axis, (before, after) in enumerate(halos):
        low_flux = wave_flux(before, mean_faces[2 * axis], axis)
        high_flux = wave_flux(after, mean_faces[2 * axis + 1], axis)
        layers.append(
            (
                [half * f + lift * b for f, b in zip(low_flux, before)],
                [lift * a - half * f for f, a in zip(high_flux, after)],
            )
        )
    return layers


def tile_rows(matrix):
    spread = (lax.rem(lane((8, 128)), 8) == sublane((8, 128))).astype(f32)
    return jnp.dot(
        matrix, spread, precision=lax.Precision.HIGHEST, preferred_element_type=f32
    )


def pairings(count):
    sets = []
    for first in (0, 1):
        pairs = [(i, i + 1) for i in range(first, count - 1, 2)]
        if pairs:
            sets.append(pairs)
    return sets


def routes(counts):
    places = [(x, y, z) for x in range(counts[0]) for y in range(counts[1]) for z in range(counts[2])]
    number = {place: n for n, place in enumerate(places)}
    found = []
    for axis in range(3):
        for pairs in pairings(counts[axis]):
            swap = dict(pairs + [(j, i) for i, j in pairs])
            alone = [i for i in range(counts[axis]) if i not in swap]
            spare = 0 if axis else 2
            route = []
            for place in places:
                other = list(place)
                if place[axis] in swap:
                    other[axis] = swap[place[axis]]
                elif axis == 0 and len(alone) == 2:
                    other[axis] = sum(alone) - place[axis]
                elif counts[spare] % 2 == 0:
                    other[spare] = place[spare] ^ 1
                route.append((number[place], number[tuple(other)]))
            found.append(route)
    return found


def z_layer(field, at):
    packed = jnp.zeros((8, 128), f32)
    column = lane((8, 128))
    for x in range(8):
        turned = pltpu.roll(field[x], lax.rem(2 * x - at + 128, 128), 1)
        packed = jnp.where(column == 2 * x, turned, packed)
    return packed


def store_faces(fields, out_refs, counts):
    at = 0
    for axis in range(3):
        even = lax.rem(lax.axis_index(axes[axis]), 2) == 0
        sets = len(pairings(counts[axis]))
        for c, field in enumerate(fields):
            if axis == 0:
                low, high = field[0], field[7]
            elif axis == 1:
                low, high = field[:, 0, :], field[:, 7, :]
            for s in range(sets):
                upper = even == (s == 0)
                if axis == 2:
                    out_refs[at + s][c] = z_layer(field, jnp.where(upper, 127, 0))
                else:
                    out_refs[at + s][c] = jnp.where(upper, high, low)
        at += sets


def sending_order(counts, stage):
    where = [(axis, s) for axis in range(3) for s in range(len(pairings(counts[axis])))]
    if stage == 1:
        wanted = ((2, 1), (2, 0), (1, 1), (1, 0), (0, 1), (0, 0))
    else:
        wanted = ((2, 1), (2, 0), (1, 0), (0, 1), (1, 1), (0, 0))
    return [where.index(p) for p in wanted if p in where]


def load_faces(sent_refs, counts, stage, first, last):
    in_refs = [None] * len(sent_refs)
    for ref, at in zip(sent_refs, sending_order(counts, stage)):
        in_refs[at] = ref
    halos = []
    at = 0
    for axis in range(3):
        even = lax.rem(lax.axis_index(axes[axis]), 2) == 0
        sets = len(pairings(counts[axis]))
        got = [[in_refs[at + s][c] for c in range(first, last)] for s in range(sets)]
        while len(got) < 2:
            got.append([jnp.zeros((8, 128), f32)] * (last - first))
        place = lax.axis_index(axes[axis])
        before = [
            jnp.where(place == 0, 0.0, jnp.where(even, b, a)) for a, b in zip(*got)
        ]
        after = [
            jnp.where(place == counts[axis] - 1, 0.0, jnp.where(even, a, b))
            for a, b in zip(*got)
        ]
        halos.append((before, after))
        at += sets
    return halos


def face_shapes(counts, width):
    total = sum(len(pairings(count)) for count in counts)
    return [jax.ShapeDtypeStruct((width, 8, 128), f32)] * total


def exchange(faces, counts, stage):
    ways = routes(counts)
    return [lax.ppermute(faces[at], axes, ways[at]) for at in sending_order(counts, stage)]


def read_all(ref):
    return [ref[c] for c in range(ref.shape[0])]


def load_kernel(counts, *refs):
    sources, targets, out_refs, sems = refs[:5], refs[5:10], refs[10:-1], refs[-1]
    copies = [
        pltpu.make_async_copy(source, target, sems.at[n])
        for n, (source, target) in enumerate(zip(sources, targets))
    ]
    for copy in copies:
        copy.start()
    for copy, target, first in zip(copies, targets, (0, 5)):
        copy.wait()
        count = target.shape[0]
        store_faces(read_all(target), [ref.at[first : first + count] for ref in out_refs], counts)
    for copy in copies[2:]:
        copy.wait()


def partners(count):
    if count == window:
        return [[(i, i ^ mask) for i in range(count)] for mask in range(count)]
    turns = sorted({d % count for d in range(1 - window, window)})
    return [[(i, (i + turn) % count) for i in range(count)] for turn in turns]


def sending_sets(count):
    return [3, 2, 1, 0] if count == window else list(range(count))


def plan_kernel(
    counts, owner_ref, slot_ref, proj_ref, order_ref, marks_ref, along_x_ref, along_y_ref, tile_ref
):
    count = counts[0]
    n_sets = len(partners(count))
    own = lax.axis_index("gx")
    n_blocks = owner_ref.shape[-1]
    square = (n_blocks, n_blocks)
    block, other = sublane(square), lane(square)

    def spread(ref):
        by_lane = jnp.broadcast_to(ref[0], square)
        here = jnp.where(block == other, by_lane, 0).astype(f32)
        return by_lane, jnp.sum(here, axis=1, keepdims=True).astype(jnp.int32)

    def group_of(owner):
        if count == window:
            return lax.bitwise_xor(owner, own)
        turn = lax.rem(owner - own + count, count)
        if n_sets == count:
            return turn
        return jnp.where(turn < window, turn, turn - (count - n_sets))

    owner_by_lane, owner = spread(owner_ref)
    slot = spread(slot_ref)[1]
    group = group_of(owner)
    before = (group_of(owner_by_lane) == group) & (other < block)
    taken = jnp.sum(before.astype(f32), axis=1, keepdims=True).astype(jnp.int32)
    wide = (n_blocks, 128)
    place = jnp.broadcast_to(group * window + taken, wide)
    column = lane((8, 128))
    quarter = column // 32
    for s in range((n_sets + 3) // 4):
        here = place - 16 * s == lane(wide) // 8
        label = jnp.sum(jnp.where(here, (slot + 1).astype(f32), 0.0), axis=0, keepdims=True) - 1.0
        source = jnp.sum(
            jnp.where(here, (8 * sublane(wide)).astype(f32), 0.0), axis=0, keepdims=True
        )
        labels = jnp.broadcast_to(label, (8, 128))
        order = jnp.broadcast_to(source, (8, 128)).astype(jnp.int32) + lax.rem(column, 8)
        for t in range(4):
            order_ref[4 * s + t] = rolled(order, 32 * t, 1)
        for r in range(min(4, n_sets - 4 * s)):
            marks = labels
            for t in range(1, 4):
                marks = jnp.where(quarter == (r + t) % 4, rolled(labels, 32 * t, 1), marks)
            marks_ref[4 * s + r] = marks
    proj = proj_ref[...]
    for a in range(8):
        along_y = jnp.broadcast_to(proj[:, a : a + 1], (8, 128))
        along_y_ref[a] = along_y
        for i in range(8):
            along_x_ref[8 * i + a] = jnp.broadcast_to(along_y[i : i + 1], (8, 128))
    tile = tile_rows(proj)
    high = tile.astype(jnp.bfloat16).astype(f32)
    tile_ref[0] = high
    tile_ref[1] = tile - high


def speeds(state):
    inverse = 1.0 / (state[0] + 1.0)
    return [state[c] * inverse for c in (1, 2, 3)]


def vorticity_kernel(les_ref, velocity_ref, vort_ref):
    velocity = speeds([les_ref[c] for c in range(4)])

    def slope(c, axis):
        return shifted(velocity[c], axis, 1) - shifted(velocity[c], axis, -1)

    vort = [slope(2, 1) - slope(1, 2), slope(0, 2) - slope(2, 0), slope(1, 0) - slope(0, 1)]
    for c in range(3):
        velocity_ref[c] = velocity[c]
        vort_ref[c] = vort[c]


def lamb_kernel(
    counts, n_faces, order_ref, marks_ref, along_x_ref, along_y_ref, velocity_ref, vort_ref, *refs
):
    face_refs, out_refs = refs[:n_faces], refs[n_faces:]
    outer = [
        (speeds(before), speeds(after)) for before, after in load_faces(face_refs, counts, 1, 0, 4)
    ]

    def rise(c, axis):
        return -outer[axis][0][c], outer[axis][1][c]

    def fall(c, axis):
        return outer[axis][0][c], -outer[axis][1][c]

    layers = [
        (None, rise(2, 1), fall(1, 2)),
        (fall(2, 0), None, rise(0, 2)),
        (rise(1, 0), fall(0, 1), None),
    ]
    vort = [0.5 * jnp.stack(with_layers(vort_ref[c], layers[c]), axis=0) for c in range(3)]
    velocity = read_all(velocity_ref)
    lamb = [
        vort[1] * velocity[2] - vort[2] * velocity[1],
        vort[2] * velocity[0] - vort[0] * velocity[2],
        vort[0] * velocity[1] - vort[1] * velocity[0],
    ]
    blocks = []
    for field in lamb:
        along_y = along_y_ref[0][None] * field[:, 0:1, :]
        for b in range(1, 8):
            along_y = along_y + along_y_ref[b][None] * field[:, b : b + 1, :]
        for i in range(8):
            plane = along_x_ref[8 * i] * along_y[0]
            for a in range(1, 8):
                plane = plane + along_x_ref[8 * i + a] * along_y[a]
            blocks.append(plane)

    quarter = lane((8, 128)) // 32
    for s in range((len(out_refs) + 3) // 4):
        ordered = [
            jnp.take_along_axis(block, order_ref[4 * s + k % 4], axis=1)
            for k, block in enumerate(blocks)
        ]
        for r in range(min(4, len(out_refs) - 4 * s)):
            out = out_refs[4 * s + r]
            for q in range(6):
                packed = ordered[4 * q]
                for t in range(1, 4):
                    packed = jnp.where(quarter == (r + t) % 4, ordered[4 * q + t], packed)
                out[q] = packed
            out[6] = marks_ref[4 * s + r]


def first_kernel(
    counts, n_faces, deriv_ref, high_ref, low_ref, les_ref, wave_ref, mean_ref, *refs
):
    face_refs, (section_ref, rate_ref), out_refs = (
        refs[:n_faces], refs[n_faces : n_faces + 2], refs[n_faces + 2 :],
    )
    state = read_all(les_ref)
    rate = les_rate(state, load_faces(face_refs, counts, 1, 0, 5))
    section = [s + r for s, r in zip(state, rate)]
    for c in range(5):
        section_ref[c] = section[c]
    store_faces(section, out_refs, counts)
    rate = acoustic_rate(
        read_all(wave_ref), read_all(mean_ref), load_faces(face_refs, counts, 1, 5, 9),
        deriv_ref[...], (high_ref[...], low_ref[...]),
    )
    for c in range(4):
        rate_ref[c] = rate[c]


def source_kernel(counts, n_faces, tile_ref, wave_ref, rate_ref, *refs):
    n_pieces = len(partners(counts[0]))
    pieces = [None] * n_pieces
    for ref, k in zip(refs, sending_sets(n_pieces)):
        pieces[k] = ref
    refs = refs[n_pieces:]
    section_faces, (source_ref, middle_ref, carry_ref), face_refs = (
        refs[:n_faces], refs[n_faces : n_faces + 3], refs[n_faces + 3 :],
    )
    quarter = lane((8, 128)) // 32
    tile_high, tile_low = tile_ref[0], tile_ref[1]
    total = None
    for s in range((n_pieces + 3) // 4):
        count = min(4, n_pieces - 4 * s)

        def gathered(q, t):
            value = jnp.full((8, 128), -1.0 if q == 6 else 0.0, f32)
            for r in range(count):
                value = jnp.where(quarter == (r + t) % 4, pieces[4 * s + r][q], value)
            return value

        here = [gathered(6, 0).astype(jnp.int32) == slot for slot in range(16)]
        chosen_high, chosen_low = [
            jnp.concatenate([jnp.where(h, part, 0.0) for h in here], axis=0).astype(jnp.bfloat16)
            for part in (tile_high, tile_low)
        ]
        data = []
        for k in range(24):
            piece = gathered(k // 4, k % 4)
            data.append(pltpu.roll(piece, 128 - 32 * (k % 4), 1) if k % 4 else piece)
        data = jnp.concatenate(data, axis=0)
        high = data.astype(jnp.bfloat16)
        low = (data - high.astype(f32)).astype(jnp.bfloat16)
        dot = functools.partial(
            lax.dot_general,
            dimension_numbers=(((1,), (1,)), ((), ())),
            preferred_element_type=f32,
        )
        moved = dot(high, chosen_high) + (dot(low, chosen_high) + dot(high, chosen_low))
        total = moved if total is None else total + moved
    source = [total[64 * c : 64 * c + 64].reshape(8, 8, 128) for c in range(3)]
    middle = []
    for c in range(4):
        rate = rate_ref[c]
        if c:
            source_ref[c - 1] = source[c - 1]
            rate = rate + source[c - 1]
        middle.append(wave_ref[c] + acoustic_step * rate)
        middle_ref[c] = middle[c]
        carry = wave_ref[c] + middle[c]
        carry_ref[c] = carry + acoustic_step * source[c - 1] if c else carry
    for ready, face in zip(section_faces, face_refs):
        face[0:5] = ready[...]
    store_faces(middle, [face.at[5:9] for face in face_refs], counts)


def inner_kernel(
    deriv_ref, high_ref, low_ref, les_ref, section_ref, middle_ref, carry_ref, mean_ref, source_ref,
    les_base_ref, wave_base_ref, mean_faces_ref, source_out, sem,
):
    copy = pltpu.make_async_copy(source_ref, source_out, sem)
    copy.start()
    section = read_all(section_ref)
    rate = les_rate(section, None)
    for c in range(5):
        les_base_ref[c] = 0.5 * ((les_ref[c] + section[c]) + rate[c])
    mean = read_all(mean_ref)
    for n, face in enumerate(mean_layers(mean)):
        for c in range(3):
            mean_faces_ref[n, c] = face[c]
    rate = acoustic_rate(
        read_all(middle_ref), mean, None, deriv_ref[...], (high_ref[...], low_ref[...])
    )
    for c in range(4):
        wave_base_ref[c] = 0.5 * (carry_ref[c] + acoustic_step * rate[c])
    copy.wait()


def last_kernel(counts, n_faces, les_base_ref, wave_base_ref, mean_faces_ref, *refs):
    face_refs, (les_out, wave_out, les_ref, wave_ref, sems) = (
        refs[:n_faces], refs[n_faces:],
    )
    copies = []

    def send(source, target):
        copies.append(pltpu.make_async_copy(source, target, sems.at[len(copies)]))
        copies[-1].start()

    layers = les_outer(load_faces(face_refs, counts, 2, 0, 5))
    for c in range(5):
        part = [(0.5 * low[c], 0.5 * high[c]) for low, high in layers]
        for x, plane in enumerate(with_layers(les_base_ref[c], part)):
            les_ref[c, x] = plane
        send(les_ref.at[c], les_out.at[c])
    mean_faces = [[mean_faces_ref[n, c] for c in range(3)] for n in range(6)]
    layers = acoustic_outer(mean_faces, load_faces(face_refs, counts, 2, 5, 9))
    step = 0.5 * acoustic_step
    for c in range(4):
        part = [(step * low[c], step * high[c]) for low, high in layers]
        for x, plane in enumerate(with_layers(wave_base_ref[c], part)):
            wave_ref[c, x] = plane
        send(wave_ref.at[c], wave_out.at[c])
    for copy in copies:
        copy.wait()


VMEM = pl.BlockSpec(memory_space=pltpu.VMEM)


HBM = pl.BlockSpec(memory_space=pltpu.HBM)


def call(kernel, in_specs, out_shapes, name, cost, scratch=(), out_spec=None):
    return pl.pallas_call(
        kernel,
        in_specs=in_specs,
        out_specs=out_spec or [VMEM] * len(out_shapes),
        out_shape=out_shapes,
        scratch_shapes=list(scratch),
        name=name,
        cost_estimate=pl.CostEstimate(flops=cost, bytes_accessed=800000, transcendentals=0),
        compiler_params=pltpu.CompilerParams(vmem_limit_bytes=24 * 1024 * 1024),
    )


def local(counts, les, wave, mean, projection, owner, slot):
    shape = les.shape[1:]
    faces = face_shapes(counts, 9)
    n_faces = len(faces)
    like = lambda n: jax.ShapeDtypeStruct((n,) + shape, f32)

    table = derivative_matrix()
    deriv = jnp.asarray(table, f32)
    along_z = np.kron(np.eye(16), table.T).astype(np.float32)
    high = along_z.astype(jnp.bfloat16)
    low = (along_z - high.astype(np.float32)).astype(jnp.bfloat16)
    tables = (deriv, jnp.asarray(high), jnp.asarray(low))

    arguments = (les, wave, owner, slot, projection)
    les, wave, owner, slot, projection, *sent = call(
        functools.partial(load_kernel, counts),
        [HBM] * 5,
        [jax.ShapeDtypeStruct(a.shape, a.dtype) for a in arguments] + faces,
        "load_and_faces",
        100000,
        [pltpu.SemaphoreType.DMA((5,))],
    )(*(pltpu.with_memory_space_constraint(a, pltpu.HBM) for a in arguments))
    got = exchange(sent, counts, 1)

    sets = partners(counts[0])
    n_plans = 4 * ((len(sets) + 3) // 4)
    order, marks, along_x, along_y, tile = call(
        functools.partial(plan_kernel, counts),
        [VMEM] * 3,
        [
            jax.ShapeDtypeStruct((n_plans, 8, 128), jnp.int32),
            jax.ShapeDtypeStruct((len(sets), 8, 128), f32),
            jax.ShapeDtypeStruct((64, 8, 128), f32),
            jax.ShapeDtypeStruct((8, 8, 128), f32),
            jax.ShapeDtypeStruct((2, 8, 128), f32),
        ],
        "plan",
        1000000,
    )(owner, slot, projection)
    turning = call(vorticity_kernel, [VMEM], [like(3)] * 2, "vorticity", 1000000)(les)
    pieces = call(
        functools.partial(lamb_kernel, counts, n_faces),
        [VMEM] * (6 + n_faces),
        [jax.ShapeDtypeStruct((7, 8, 128), f32)] * len(sets),
        "lamb_blocks",
        10000000,
    )(order, marks, along_x, along_y, *turning, *got)
    moved = []
    for k in sending_sets(len(sets)):
        still = all(i == j for i, j in sets[k])
        moved.append(pieces[k] if still else lax.ppermute(pieces[k], "gx", sets[k]))
    section, rate, *section_faces = call(
        functools.partial(first_kernel, counts, n_faces),
        [VMEM] * (6 + n_faces),
        [like(5), like(4)] + face_shapes(counts, 5),
        "first_rates",
        40000000,
    )(*tables, les, wave, mean, *got)

    source, middle, carry, *sent = call(
        functools.partial(source_kernel, counts, n_faces),
        [VMEM] * (3 + len(moved) + n_faces),
        [like(3), like(4), like(4)] + faces,
        "source_and_faces",
        10000000,
    )(tile, wave, rate, *moved, *section_faces)
    got = exchange(sent, counts, 2)
    les_base, wave_base, mean_faces, source_out = call(
        inner_kernel,
        [VMEM] * 9,
        [like(5), like(4), jax.ShapeDtypeStruct((6, 3, 8, 128), f32), like(3)],
        "second_rates_inner",
        40000000,
        [pltpu.SemaphoreType.DMA],
        out_spec=[VMEM, VMEM, VMEM, HBM],
    )(*tables, les, section, middle, carry, mean, source)
    les_next, wave_next = call(
        functools.partial(last_kernel, counts, n_faces),
        [VMEM] * (3 + n_faces),
        [like(5), like(4)],
        "second_rates_outer",
        4000000,
        [
            pltpu.VMEM(les.shape, f32),
            pltpu.VMEM(wave.shape, f32),
            pltpu.SemaphoreType.DMA((9,)),
        ],
        out_spec=[HBM, HBM],
    )(les_base, wave_base, mean_faces, *got)
    return les_next, source_out, wave_next


def solution(mesh):
    counts = tuple(mesh.shape[axis] for axis in axes)
    field = P(None, *axes)
    return jax.shard_map(
        functools.partial(local, counts),
        mesh=mesh,
        in_specs=(field, field, field, P(), P(*axes), P(*axes)),
        out_specs=(field, field, field),
        check_vma=False,
    )
```

```python
import functools

import jax
import jax.numpy as jnp
import numpy as np
from jax import lax
from jax.experimental import pallas as pl
from jax.experimental.pallas import tpu as pltpu
from jax.sharding import PartitionSpec as P

lobatto_points = np.array(
    [
        -1.0,
        -0.8717401485096066,
        -0.5917001814331423,
        -0.2092992179024789,
        0.2092992179024789,
        0.5917001814331423,
        0.8717401485096066,
        1.0,
    ]
)
flux_half = 0.08
gamma_less = 0.4
acoustic_step = 0.01
upwind_speed = 1.5
face_lift = 28.0
free_stream = (1.0, 0.0, 0.0, 0.0, 2.5)
axes = ("gx", "gy", "gz")
window = 4
f32 = jnp.float32


def derivative_matrix():
    points = lobatto_points
    products = [np.prod([points[i] - points[j] for j in range(8) if j != i]) for i in range(8)]
    matrix = np.zeros((8, 8))
    for i in range(8):
        for j in range(8):
            if j != i:
                matrix[i, j] = products[i] / (products[j] * (points[i] - points[j]))
        matrix[i, i] = -np.sum(matrix[i])
    return matrix


def sublane(shape):
    return lax.broadcasted_iota(jnp.int32, shape, len(shape) - 2)


def lane(shape):
    return lax.broadcasted_iota(jnp.int32, shape, len(shape) - 1)


def rolled(tile, amount, axis):
    amount = amount % tile.shape[axis]
    return pltpu.roll(tile, amount, axis) if amount else tile


def shifted(field, axis, step, outer=None):
    if axis == 0:
        outer = jnp.zeros((8, 128), f32) if outer is None else outer
        if step == 1:
            return jnp.concatenate([field[1:], outer[None]], axis=0)
        return jnp.concatenate([outer[None], field[:-1]], axis=0)
    count = (8, 128)[axis - 1]
    edge = count - 1 if step == 1 else 0
    at_edge = (sublane if axis == 1 else lane)((8, 128)) == edge
    planes = []
    for x in range(8):
        layer = 0.0 if outer is None else rolled(outer, edge - axis * x, axis - 1)
        planes.append(jnp.where(at_edge, layer, rolled(field[x], -step, axis - 1)))
    return jnp.stack(planes, axis=0)


def fluid(state):
    density, mx, my, mz, energy = [s + r for s, r in zip(state, free_stream)]
    inverse = 1.0 / density
    momentum = (mx, my, mz)
    velocity = [m * inverse for m in momentum]
    pressure = gamma_less * (
        energy - 0.5 * (mx * velocity[0] + my * velocity[1] + mz * velocity[2])
    )
    return momentum, velocity, pressure, energy + pressure


def split_flux(state, parts, axis, sign):
    momentum, velocity, pressure, enthalpy = parts
    speed = velocity[axis]
    flux = [momentum[axis]]
    for c in range(3):
        term = momentum[c] * speed
        flux.append(term + pressure if c == axis else term)
    flux.append(enthalpy * speed)
    if sign > 0:
        return [flux_half * (s + f) for s, f in zip(state, flux)]
    return [flux_half * (s - f) for s, f in zip(state, flux)]


def les_rate(state, halos):
    parts = fluid(state)
    total = [-6.0 * flux_half * s for s in state]
    for axis in range(3):
        ahead = split_flux(state, parts, axis, -1)
        behind = split_flux(state, parts, axis, 1)
        ahead_outer = behind_outer = [None] * 5
        if halos is not None:
            before, after = halos[axis]
            ahead_outer = split_flux(after, fluid(after), axis, -1)
            behind_outer = split_flux(before, fluid(before), axis, 1)
        for c in range(5):
            total[c] = total[c] + (
                shifted(ahead[c], axis, 1, ahead_outer[c])
                + shifted(behind[c], axis, -1, behind_outer[c])
            )
    return total


def les_outer(halos):
    return [
        (
            split_flux(before, fluid(before), axis, 1),
            split_flux(after, fluid(after), axis, -1),
        )
        for axis, (before, after) in enumerate(halos)
    ]


def with_layers(field, layers):
    row, column = sublane((8, 128)), lane((8, 128))
    along_z = layers[2]
    if along_z is not None:
        along_z = jnp.where(lax.rem(column, 2) == 0, along_z[0], rolled(along_z[1], -1, 1))
    planes = []
    for x in range(8):
        plane = field[x]
        if layers[0] is not None and x in (0, 7):
            plane = plane + layers[0][x // 7]
        if layers[1] is not None:
            low, high = layers[1]
            plane = plane + jnp.where(
                row == 0, rolled(low, -x, 0), jnp.where(row == 7, rolled(high, 7 - x, 0), 0.0)
            )
        if along_z is not None:
            ends = (column == 0) | (column == 127)
            plane = plane + jnp.where(ends, rolled(along_z, -2 * x, 1), 0.0)
        planes.append(plane)
    return planes


def wave_flux(state, mean, axis):
    speed = mean[axis]
    pressure = state[0]
    rows = [speed * pressure + state[1 + axis]]
    for c in range(3):
        term = speed * state[1 + c]
        rows.append(term + pressure if c == axis else term)
    return rows


def dot3(left, right):
    high = left.astype(jnp.bfloat16)
    low = (left - high.astype(f32)).astype(jnp.bfloat16)
    dot = functools.partial(jnp.dot, preferred_element_type=f32)
    return dot(high, right[0]) + (dot(low, right[0]) + dot(high, right[1]))


def acoustic_rate(state, mean, halos, deriv, along_z):
    shape = state[0].shape
    table = derivative_matrix()
    flux = wave_flux(state, mean, 0)
    if halos is None:
        halos = [([jnp.zeros((8, 128), f32)] * 4,) * 2] + [([None] * 4,) * 2] * 2
    before, after = halos[0]
    low_mean, high_mean = [m[0] for m in mean], [m[7] for m in mean]
    low_jump = [b - s[0] for b, s in zip(before, state)]
    high_jump = [a - s[7] for a, s in zip(after, state)]
    low_flux = wave_flux(low_jump, low_mean, 0)
    high_flux = wave_flux(high_jump, high_mean, 0)
    half, lift = 0.5 * face_lift, 0.5 * face_lift * upwind_speed
    total = []
    for c in range(4):
        planes = []
        for i in range(8):
            plane = -float(table[i, 0]) * flux[c][0]
            for a in range(1, 8):
                if abs(table[i, a]) > 1e-12:
                    plane = plane - float(table[i, a]) * flux[c][a]
            if i == 0:
                plane = plane + (half * low_flux[c] + lift * low_jump[c])
            if i == 7:
                plane = plane - (half * high_flux[c] - lift * high_jump[c])
            planes.append(plane)
        total.append(jnp.stack(planes, axis=0))
    flux = wave_flux(state, mean, 1)
    before, after = halos[1]
    row = sublane(shape)
    sign = jnp.where(row == 0, half, jnp.where(row == 7, -half, 0.0))
    jump = []
    for s, b, a in zip(state, before, after):
        planes = []
        for x in range(8):
            low = 0.0 if b is None else rolled(b, -x, 0)
            high = 0.0 if a is None else rolled(a, 7 - x, 0)
            planes.append(jnp.where(row[x] == 0, low, jnp.where(row[x] == 7, high, s[x])) - s[x])
        jump.append(jnp.stack(planes, axis=0))
    jump_flux = wave_flux(jump, mean, 1)
    for c in range(4):
        change = lift * jump[c] + sign * jump_flux[c]
        for b in range(8):
            change = change - deriv[:, b : b + 1][None] * flux[c][:, b : b + 1, :]
        total[c] = total[c] + change
    flux = wave_flux(state, mean, 2)
    before, after = halos[2]
    column = lane(shape)
    place = lax.rem(column, 8)
    sign = jnp.where(place == 0, half, jnp.where(place == 7, -half, 0.0))
    jump = [
        jnp.where(
            place == 0,
            shifted(s, 2, -1, b),
            jnp.where(place == 7, shifted(s, 2, 1, a), s),
        )
        - s
        for s, b, a in zip(state, before, after)
    ]
    jump_flux = wave_flux(jump, mean, 2)
    for c in range(4):
        slope = dot3(flux[c].reshape(64, 128), along_z).reshape(shape)
        total[c] = total[c] + (lift * jump[c] + sign * jump_flux[c] - slope)
    return total


def mean_layers(mean):
    return [
        [m[0] for m in mean],
        [m[7] for m in mean],
        [m[:, 0, :] for m in mean],
        [m[:, 7, :] for m in mean],
        [z_layer(m, jnp.int32(0)) for m in mean],
        [z_layer(m, jnp.int32(127)) for m in mean],
    ]


def acoustic_outer(mean_faces, halos):
    half, lift = 0.5 * face_lift, 0.5 * face_lift * upwind_speed
    layers = []
    for axis, (before, after) in enumerate(halos):
        low_flux = wave_flux(before, mean_faces[2 * axis], axis)
        high_flux = wave_flux(after, mean_faces[2 * axis + 1], axis)
        layers.append(
            (
                [half * f + lift * b for f, b in zip(low_flux, before)],
                [lift * a - half * f for f, a in zip(high_flux, after)],
            )
        )
    return layers


def tile_rows(matrix):
    spread = (lax.rem(lane((8, 128)), 8) == sublane((8, 128))).astype(f32)
    return jnp.dot(
        matrix, spread, precision=lax.Precision.HIGHEST, preferred_element_type=f32
    )


def pairings(count):
    sets = []
    for first in (0, 1):
        pairs = [(i, i + 1) for i in range(first, count - 1, 2)]
        if pairs:
            sets.append(pairs)
    return sets


def routes(counts):
    places = [(x, y, z) for x in range(counts[0]) for y in range(counts[1]) for z in range(counts[2])]
    number = {place: n for n, place in enumerate(places)}
    found = []
    for axis in range(3):
        for pairs in pairings(counts[axis]):
            swap = dict(pairs + [(j, i) for i, j in pairs])
            alone = [i for i in range(counts[axis]) if i not in swap]
            spare = 0 if axis else 2
            route = []
            for place in places:
                other = list(place)
                if place[axis] in swap:
                    other[axis] = swap[place[axis]]
                elif axis == 0 and len(alone) == 2:
                    other[axis] = sum(alone) - place[axis]
                elif counts[spare] % 2 == 0:
                    other[spare] = place[spare] ^ 1
                route.append((number[place], number[tuple(other)]))
            found.append(route)
    return found


def z_layer(field, at):
    packed = jnp.zeros((8, 128), f32)
    column = lane((8, 128))
    for x in range(8):
        turned = pltpu.roll(field[x], lax.rem(2 * x - at + 128, 128), 1)
        packed = jnp.where(column == 2 * x, turned, packed)
    return packed


def store_faces(fields, out_refs, counts):
    at = 0
    for axis in range(3):
        even = lax.rem(lax.axis_index(axes[axis]), 2) == 0
        sets = len(pairings(counts[axis]))
        for c, field in enumerate(fields):
            if axis == 0:
                low, high = field[0], field[7]
            elif axis == 1:
                low, high = field[:, 0, :], field[:, 7, :]
            for s in range(sets):
                upper = even == (s == 0)
                if axis == 2:
                    out_refs[at + s][c] = z_layer(field, jnp.where(upper, 127, 0))
                else:
                    out_refs[at + s][c] = jnp.where(upper, high, low)
        at += sets


def sending_order(counts, stage):
    where = [(axis, s) for axis in range(3) for s in range(len(pairings(counts[axis])))]
    if stage == 1:
        wanted = ((2, 1), (2, 0), (0, 1), (1, 0), (1, 1), (0, 0))
    else:
        wanted = ((0, 1), (2, 1), (2, 0), (1, 0), (1, 1), (0, 0))
    return [where.index(p) for p in wanted if p in where]


def load_faces(sent_refs, counts, stage, first, last):
    in_refs = [None] * len(sent_refs)
    for ref, at in zip(sent_refs, sending_order(counts, stage)):
        in_refs[at] = ref
    halos = []
    at = 0
    for axis in range(3):
        even = lax.rem(lax.axis_index(axes[axis]), 2) == 0
        sets = len(pairings(counts[axis]))
        got = [[in_refs[at + s][c] for c in range(first, last)] for s in range(sets)]
        while len(got) < 2:
            got.append([jnp.zeros((8, 128), f32)] * (last - first))
        place = lax.axis_index(axes[axis])
        before = [
            jnp.where(place == 0, 0.0, jnp.where(even, b, a)) for a, b in zip(*got)
        ]
        after = [
            jnp.where(place == counts[axis] - 1, 0.0, jnp.where(even, a, b))
            for a, b in zip(*got)
        ]
        halos.append((before, after))
        at += sets
    return halos


def face_shapes(counts, width):
    total = sum(len(pairings(count)) for count in counts)
    return [jax.ShapeDtypeStruct((width, 8, 128), f32)] * total


def exchange(faces, counts, stage):
    ways = routes(counts)
    return [lax.ppermute(faces[at], axes, ways[at]) for at in sending_order(counts, stage)]


def read_all(ref):
    return [ref[c] for c in range(ref.shape[0])]


def load_kernel(counts, *refs):
    sources, targets, out_refs, sems = refs[:5], refs[5:10], refs[10:-1], refs[-1]
    copies = [
        pltpu.make_async_copy(source, target, sems.at[n])
        for n, (source, target) in enumerate(zip(sources, targets))
    ]
    for copy in copies:
        copy.start()
    for copy, target, first in zip(copies, targets, (0, 5)):
        copy.wait()
        count = target.shape[0]
        store_faces(read_all(target), [ref.at[first : first + count] for ref in out_refs], counts)
    for copy in copies[2:]:
        copy.wait()


def partners(count):
    if count == window:
        return [[(i, i ^ mask) for i in range(count)] for mask in range(count)]
    turns = sorted({d % count for d in range(1 - window, window)})
    return [[(i, (i + turn) % count) for i in range(count)] for turn in turns]


def sending_sets(count):
    return [3, 2, 1, 0] if count == window else list(range(count))


def plan_kernel(
    counts, owner_ref, slot_ref, proj_ref, order_ref, marks_ref, along_x_ref, along_y_ref, tile_ref
):
    count = counts[0]
    n_sets = len(partners(count))
    own = lax.axis_index("gx")
    n_blocks = owner_ref.shape[-1]
    square = (n_blocks, n_blocks)
    block, other = sublane(square), lane(square)

    def spread(ref):
        by_lane = jnp.broadcast_to(ref[0], square)
        here = jnp.where(block == other, by_lane, 0).astype(f32)
        return by_lane, jnp.sum(here, axis=1, keepdims=True).astype(jnp.int32)

    def group_of(owner):
        if count == window:
            return lax.bitwise_xor(owner, own)
        turn = lax.rem(owner - own + count, count)
        if n_sets == count:
            return turn
        return jnp.where(turn < window, turn, turn - (count - n_sets))

    owner_by_lane, owner = spread(owner_ref)
    slot = spread(slot_ref)[1]
    group = group_of(owner)
    before = (group_of(owner_by_lane) == group) & (other < block)
    taken = jnp.sum(before.astype(f32), axis=1, keepdims=True).astype(jnp.int32)
    wide = (n_blocks, 128)
    place = jnp.broadcast_to(group * window + taken, wide)
    column = lane((8, 128))
    quarter = column // 32
    for s in range((n_sets + 3) // 4):
        here = place - 16 * s == lane(wide) // 8
        label = jnp.sum(jnp.where(here, (slot + 1).astype(f32), 0.0), axis=0, keepdims=True) - 1.0
        source = jnp.sum(
            jnp.where(here, (8 * sublane(wide)).astype(f32), 0.0), axis=0, keepdims=True
        )
        labels = jnp.broadcast_to(label, (8, 128))
        order = jnp.broadcast_to(source, (8, 128)).astype(jnp.int32) + lax.rem(column, 8)
        for t in range(4):
            order_ref[4 * s + t] = rolled(order, 32 * t, 1)
        for r in range(min(4, n_sets - 4 * s)):
            marks = labels
            for t in range(1, 4):
                marks = jnp.where(quarter == (r + t) % 4, rolled(labels, 32 * t, 1), marks)
            marks_ref[4 * s + r] = marks
    proj = proj_ref[...]
    for a in range(8):
        along_y = jnp.broadcast_to(proj[:, a : a + 1], (8, 128))
        along_y_ref[a] = along_y
        for i in range(8):
            along_x_ref[8 * i + a] = jnp.broadcast_to(along_y[i : i + 1], (8, 128))
    tile = tile_rows(proj)
    high = tile.astype(jnp.bfloat16).astype(f32)
    tile_ref[0] = high
    tile_ref[1] = tile - high


def speeds(state):
    inverse = 1.0 / (state[0] + 1.0)
    return [state[c] * inverse for c in (1, 2, 3)]


def vorticity_kernel(les_ref, velocity_ref, vort_ref):
    velocity = speeds([les_ref[c] for c in range(4)])

    def slope(c, axis):
        return shifted(velocity[c], axis, 1) - shifted(velocity[c], axis, -1)

    vort = [slope(2, 1) - slope(1, 2), slope(0, 2) - slope(2, 0), slope(1, 0) - slope(0, 1)]
    for c in range(3):
        velocity_ref[c] = velocity[c]
        vort_ref[c] = vort[c]


def lamb_kernel(
    counts, n_faces, order_ref, marks_ref, along_x_ref, along_y_ref, velocity_ref, vort_ref, *refs
):
    face_refs, out_refs = refs[:n_faces], refs[n_faces:]
    outer = [
        (speeds(before), speeds(after)) for before, after in load_faces(face_refs, counts, 1, 0, 4)
    ]

    def rise(c, axis):
        return -outer[axis][0][c], outer[axis][1][c]

    def fall(c, axis):
        return outer[axis][0][c], -outer[axis][1][c]

    layers = [
        (None, rise(2, 1), fall(1, 2)),
        (fall(2, 0), None, rise(0, 2)),
        (rise(1, 0), fall(0, 1), None),
    ]
    vort = [0.5 * jnp.stack(with_layers(vort_ref[c], layers[c]), axis=0) for c in range(3)]
    velocity = read_all(velocity_ref)
    lamb = [
        vort[1] * velocity[2] - vort[2] * velocity[1],
        vort[2] * velocity[0] - vort[0] * velocity[2],
        vort[0] * velocity[1] - vort[1] * velocity[0],
    ]
    blocks = []
    for field in lamb:
        along_y = along_y_ref[0][None] * field[:, 0:1, :]
        for b in range(1, 8):
            along_y = along_y + along_y_ref[b][None] * field[:, b : b + 1, :]
        for i in range(8):
            plane = along_x_ref[8 * i] * along_y[0]
            for a in range(1, 8):
                plane = plane + along_x_ref[8 * i + a] * along_y[a]
            blocks.append(plane)

    quarter = lane((8, 128)) // 32
    for s in range((len(out_refs) + 3) // 4):
        ordered = [
            jnp.take_along_axis(block, order_ref[4 * s + k % 4], axis=1)
            for k, block in enumerate(blocks)
        ]
        for r in range(min(4, len(out_refs) - 4 * s)):
            out = out_refs[4 * s + r]
            for q in range(6):
                packed = ordered[4 * q]
                for t in range(1, 4):
                    packed = jnp.where(quarter == (r + t) % 4, ordered[4 * q + t], packed)
                out[q] = packed
            out[6] = marks_ref[4 * s + r]


def first_kernel(
    counts, n_faces, deriv_ref, high_ref, low_ref, les_ref, wave_ref, mean_ref, *refs
):
    face_refs, (section_ref, rate_ref), out_refs = (
        refs[:n_faces], refs[n_faces : n_faces + 2], refs[n_faces + 2 :],
    )
    state = read_all(les_ref)
    rate = les_rate(state, load_faces(face_refs, counts, 1, 0, 5))
    section = [s + r for s, r in zip(state, rate)]
    for c in range(5):
        section_ref[c] = section[c]
    store_faces(section, out_refs, counts)
    rate = acoustic_rate(
        read_all(wave_ref), read_all(mean_ref), load_faces(face_refs, counts, 1, 5, 9),
        deriv_ref[...], (high_ref[...], low_ref[...]),
    )
    for c in range(4):
        rate_ref[c] = rate[c]


def source_kernel(counts, n_faces, tile_ref, wave_ref, rate_ref, *refs):
    n_pieces = len(partners(counts[0]))
    pieces = [None] * n_pieces
    for ref, k in zip(refs, sending_sets(n_pieces)):
        pieces[k] = ref
    refs = refs[n_pieces:]
    section_faces, (source_ref, middle_ref, carry_ref), face_refs = (
        refs[:n_faces], refs[n_faces : n_faces + 3], refs[n_faces + 3 :],
    )
    quarter = lane((8, 128)) // 32
    tile_high, tile_low = tile_ref[0], tile_ref[1]
    total = None
    for s in range((n_pieces + 3) // 4):
        count = min(4, n_pieces - 4 * s)

        def gathered(q, t):
            value = jnp.full((8, 128), -1.0 if q == 6 else 0.0, f32)
            for r in range(count):
                value = jnp.where(quarter == (r + t) % 4, pieces[4 * s + r][q], value)
            return value

        here = [gathered(6, 0).astype(jnp.int32) == slot for slot in range(16)]
        chosen_high, chosen_low = [
            jnp.concatenate([jnp.where(h, part, 0.0) for h in here], axis=0).astype(jnp.bfloat16)
            for part in (tile_high, tile_low)
        ]
        data = []
        for k in range(24):
            piece = gathered(k // 4, k % 4)
            data.append(pltpu.roll(piece, 128 - 32 * (k % 4), 1) if k % 4 else piece)
        data = jnp.concatenate(data, axis=0)
        high = data.astype(jnp.bfloat16)
        low = (data - high.astype(f32)).astype(jnp.bfloat16)
        dot = functools.partial(
            lax.dot_general,
            dimension_numbers=(((1,), (1,)), ((), ())),
            preferred_element_type=f32,
        )
        moved = dot(high, chosen_high) + (dot(low, chosen_high) + dot(high, chosen_low))
        total = moved if total is None else total + moved
    source = [total[64 * c : 64 * c + 64].reshape(8, 8, 128) for c in range(3)]
    middle = []
    for c in range(4):
        rate = rate_ref[c]
        if c:
            source_ref[c - 1] = source[c - 1]
            rate = rate + source[c - 1]
        middle.append(wave_ref[c] + acoustic_step * rate)
        middle_ref[c] = middle[c]
        carry = wave_ref[c] + middle[c]
        carry_ref[c] = carry + acoustic_step * source[c - 1] if c else carry
    for ready, face in zip(section_faces, face_refs):
        face[0:5] = ready[...]
    store_faces(middle, [face.at[5:9] for face in face_refs], counts)


def inner_kernel(
    deriv_ref, high_ref, low_ref, les_ref, section_ref, middle_ref, carry_ref, mean_ref, source_ref,
    les_base_ref, wave_base_ref, mean_faces_ref, source_out, sem,
):
    copy = pltpu.make_async_copy(source_ref, source_out, sem)
    copy.start()
    section = read_all(section_ref)
    rate = les_rate(section, None)
    for c in range(5):
        les_base_ref[c] = 0.5 * ((les_ref[c] + section[c]) + rate[c])
    mean = read_all(mean_ref)
    for n, face in enumerate(mean_layers(mean)):
        for c in range(3):
            mean_faces_ref[n, c] = face[c]
    rate = acoustic_rate(
        read_all(middle_ref), mean, None, deriv_ref[...], (high_ref[...], low_ref[...])
    )
    for c in range(4):
        wave_base_ref[c] = 0.5 * (carry_ref[c] + acoustic_step * rate[c])
    copy.wait()


def last_kernel(counts, n_faces, les_base_ref, wave_base_ref, mean_faces_ref, *refs):
    face_refs, (les_out, wave_out, les_ref, wave_ref, sems) = (
        refs[:n_faces], refs[n_faces:],
    )
    copies = []

    def send(source, target):
        copies.append(pltpu.make_async_copy(source, target, sems.at[len(copies)]))
        copies[-1].start()

    layers = les_outer(load_faces(face_refs, counts, 2, 0, 5))
    for c in range(5):
        part = [(0.5 * low[c], 0.5 * high[c]) for low, high in layers]
        for x, plane in enumerate(with_layers(les_base_ref[c], part)):
            les_ref[c, x] = plane
        send(les_ref.at[c], les_out.at[c])
    mean_faces = [[mean_faces_ref[n, c] for c in range(3)] for n in range(6)]
    layers = acoustic_outer(mean_faces, load_faces(face_refs, counts, 2, 5, 9))
    step = 0.5 * acoustic_step
    for c in range(4):
        part = [(step * low[c], step * high[c]) for low, high in layers]
        for x, plane in enumerate(with_layers(wave_base_ref[c], part)):
            wave_ref[c, x] = plane
        send(wave_ref.at[c], wave_out.at[c])
    for copy in copies:
        copy.wait()


VMEM = pl.BlockSpec(memory_space=pltpu.VMEM)


HBM = pl.BlockSpec(memory_space=pltpu.HBM)


def call(kernel, in_specs, out_shapes, name, cost, scratch=(), out_spec=None):
    return pl.pallas_call(
        kernel,
        in_specs=in_specs,
        out_specs=out_spec or [VMEM] * len(out_shapes),
        out_shape=out_shapes,
        scratch_shapes=list(scratch),
        name=name,
        cost_estimate=pl.CostEstimate(flops=cost, bytes_accessed=800000, transcendentals=0),
        compiler_params=pltpu.CompilerParams(vmem_limit_bytes=24 * 1024 * 1024),
    )


def local(counts, les, wave, mean, projection, owner, slot):
    shape = les.shape[1:]
    faces = face_shapes(counts, 9)
    n_faces = len(faces)
    like = lambda n: jax.ShapeDtypeStruct((n,) + shape, f32)

    table = derivative_matrix()
    deriv = jnp.asarray(table, f32)
    along_z = np.kron(np.eye(16), table.T).astype(np.float32)
    high = along_z.astype(jnp.bfloat16)
    low = (along_z - high.astype(np.float32)).astype(jnp.bfloat16)
    tables = (deriv, jnp.asarray(high), jnp.asarray(low))

    arguments = (les, wave, owner, slot, projection)
    les, wave, owner, slot, projection, *sent = call(
        functools.partial(load_kernel, counts),
        [HBM] * 5,
        [jax.ShapeDtypeStruct(a.shape, a.dtype) for a in arguments] + faces,
        "load_and_faces",
        100000,
        [pltpu.SemaphoreType.DMA((5,))],
    )(*(pltpu.with_memory_space_constraint(a, pltpu.HBM) for a in arguments))
    got = exchange(sent, counts, 1)

    sets = partners(counts[0])
    n_plans = 4 * ((len(sets) + 3) // 4)
    order, marks, along_x, along_y, tile = call(
        functools.partial(plan_kernel, counts),
        [VMEM] * 3,
        [
            jax.ShapeDtypeStruct((n_plans, 8, 128), jnp.int32),
            jax.ShapeDtypeStruct((len(sets), 8, 128), f32),
            jax.ShapeDtypeStruct((64, 8, 128), f32),
            jax.ShapeDtypeStruct((8, 8, 128), f32),
            jax.ShapeDtypeStruct((2, 8, 128), f32),
        ],
        "plan",
        1000000,
    )(owner, slot, projection)
    turning = call(vorticity_kernel, [VMEM], [like(3)] * 2, "vorticity", 1000000)(les)
    pieces = call(
        functools.partial(lamb_kernel, counts, n_faces),
        [VMEM] * (6 + n_faces),
        [jax.ShapeDtypeStruct((7, 8, 128), f32)] * len(sets),
        "lamb_blocks",
        10000000,
    )(order, marks, along_x, along_y, *turning, *got)
    moved = []
    for k in sending_sets(len(sets)):
        still = all(i == j for i, j in sets[k])
        moved.append(pieces[k] if still else lax.ppermute(pieces[k], "gx", sets[k]))
    section, rate, *section_faces = call(
        functools.partial(first_kernel, counts, n_faces),
        [VMEM] * (6 + n_faces),
        [like(5), like(4)] + face_shapes(counts, 5),
        "first_rates",
        40000000,
    )(*tables, les, wave, mean, *got)

    source, middle, carry, *sent = call(
        functools.partial(source_kernel, counts, n_faces),
        [VMEM] * (3 + len(moved) + n_faces),
        [like(3), like(4), like(4)] + faces,
        "source_and_faces",
        10000000,
    )(tile, wave, rate, *moved, *section_faces)
    got = exchange(sent, counts, 2)
    les_base, wave_base, mean_faces, source_out = call(
        inner_kernel,
        [VMEM] * 9,
        [like(5), like(4), jax.ShapeDtypeStruct((6, 3, 8, 128), f32), like(3)],
        "second_rates_inner",
        40000000,
        [pltpu.SemaphoreType.DMA],
        out_spec=[VMEM, VMEM, VMEM, HBM],
    )(*tables, les, section, middle, carry, mean, source)
    les_next, wave_next = call(
        functools.partial(last_kernel, counts, n_faces),
        [VMEM] * (3 + n_faces),
        [like(5), like(4)],
        "second_rates_outer",
        4000000,
        [
            pltpu.VMEM(les.shape, f32),
            pltpu.VMEM(wave.shape, f32),
            pltpu.SemaphoreType.DMA((9,)),
        ],
        out_spec=[HBM, HBM],
    )(les_base, wave_base, mean_faces, *got)
    return les_next, source_out, wave_next


def solution(mesh):
    counts = tuple(mesh.shape[axis] for axis in axes)
    field = P(None, *axes)
    return jax.shard_map(
        functools.partial(local, counts),
        mesh=mesh,
        in_specs=(field, field, field, P(), P(*axes), P(*axes)),
        out_specs=(field, field, field),
        check_vma=False,
    )
```

```python
import functools

import jax
import jax.numpy as jnp
import numpy as np
from jax import lax
from jax.experimental import pallas as pl
from jax.experimental.pallas import tpu as pltpu
from jax.sharding import PartitionSpec as P

lobatto_points = np.array(
    [
        -1.0,
        -0.8717401485096066,
        -0.5917001814331423,
        -0.2092992179024789,
        0.2092992179024789,
        0.5917001814331423,
        0.8717401485096066,
        1.0,
    ]
)
flux_half = 0.08
gamma_less = 0.4
acoustic_step = 0.01
upwind_speed = 1.5
face_lift = 28.0
free_stream = (1.0, 0.0, 0.0, 0.0, 2.5)
axes = ("gx", "gy", "gz")
window = 4
f32 = jnp.float32


def derivative_matrix():
    points = lobatto_points
    products = [np.prod([points[i] - points[j] for j in range(8) if j != i]) for i in range(8)]
    matrix = np.zeros((8, 8))
    for i in range(8):
        for j in range(8):
            if j != i:
                matrix[i, j] = products[i] / (products[j] * (points[i] - points[j]))
        matrix[i, i] = -np.sum(matrix[i])
    return matrix


def sublane(shape):
    return lax.broadcasted_iota(jnp.int32, shape, len(shape) - 2)


def lane(shape):
    return lax.broadcasted_iota(jnp.int32, shape, len(shape) - 1)


def rolled(tile, amount, axis):
    amount = amount % tile.shape[axis]
    return pltpu.roll(tile, amount, axis) if amount else tile


def shifted(field, axis, step, outer=None):
    if axis == 0:
        outer = jnp.zeros((8, 128), f32) if outer is None else outer
        if step == 1:
            return jnp.concatenate([field[1:], outer[None]], axis=0)
        return jnp.concatenate([outer[None], field[:-1]], axis=0)
    count = (8, 128)[axis - 1]
    edge = count - 1 if step == 1 else 0
    at_edge = (sublane if axis == 1 else lane)((8, 128)) == edge
    planes = []
    for x in range(8):
        layer = 0.0 if outer is None else rolled(outer, edge - axis * x, axis - 1)
        planes.append(jnp.where(at_edge, layer, rolled(field[x], -step, axis - 1)))
    return jnp.stack(planes, axis=0)


def fluid(state):
    density, mx, my, mz, energy = [s + r for s, r in zip(state, free_stream)]
    inverse = 1.0 / density
    momentum = (mx, my, mz)
    velocity = [m * inverse for m in momentum]
    pressure = gamma_less * (
        energy - 0.5 * (mx * velocity[0] + my * velocity[1] + mz * velocity[2])
    )
    return momentum, velocity, pressure, energy + pressure


def split_flux(state, parts, axis, sign):
    momentum, velocity, pressure, enthalpy = parts
    speed = velocity[axis]
    flux = [momentum[axis]]
    for c in range(3):
        term = momentum[c] * speed
        flux.append(term + pressure if c == axis else term)
    flux.append(enthalpy * speed)
    if sign > 0:
        return [flux_half * (s + f) for s, f in zip(state, flux)]
    return [flux_half * (s - f) for s, f in zip(state, flux)]


def les_rate(state, halos):
    parts = fluid(state)
    total = [-6.0 * flux_half * s for s in state]
    for axis in range(3):
        ahead = split_flux(state, parts, axis, -1)
        behind = split_flux(state, parts, axis, 1)
        ahead_outer = behind_outer = [None] * 5
        if halos is not None:
            before, after = halos[axis]
            ahead_outer = split_flux(after, fluid(after), axis, -1)
            behind_outer = split_flux(before, fluid(before), axis, 1)
        for c in range(5):
            total[c] = total[c] + (
                shifted(ahead[c], axis, 1, ahead_outer[c])
                + shifted(behind[c], axis, -1, behind_outer[c])
            )
    return total


def les_outer(halos):
    return [
        (
            split_flux(before, fluid(before), axis, 1),
            split_flux(after, fluid(after), axis, -1),
        )
        for axis, (before, after) in enumerate(halos)
    ]


def with_layers(field, layers):
    row, column = sublane((8, 128)), lane((8, 128))
    along_z = layers[2]
    if along_z is not None:
        along_z = jnp.where(lax.rem(column, 2) == 0, along_z[0], rolled(along_z[1], -1, 1))
    planes = []
    for x in range(8):
        plane = field[x]
        if layers[0] is not None and x in (0, 7):
            plane = plane + layers[0][x // 7]
        if layers[1] is not None:
            low, high = layers[1]
            plane = plane + jnp.where(
                row == 0, rolled(low, -x, 0), jnp.where(row == 7, rolled(high, 7 - x, 0), 0.0)
            )
        if along_z is not None:
            ends = (column == 0) | (column == 127)
            plane = plane + jnp.where(ends, rolled(along_z, -2 * x, 1), 0.0)
        planes.append(plane)
    return planes


def wave_flux(state, mean, axis):
    speed = mean[axis]
    pressure = state[0]
    rows = [speed * pressure + state[1 + axis]]
    for c in range(3):
        term = speed * state[1 + c]
        rows.append(term + pressure if c == axis else term)
    return rows


def dot3(left, right):
    high = left.astype(jnp.bfloat16)
    low = (left - high.astype(f32)).astype(jnp.bfloat16)
    dot = functools.partial(jnp.dot, preferred_element_type=f32)
    return dot(high, right[0]) + (dot(low, right[0]) + dot(high, right[1]))


def acoustic_rate(state, mean, halos, deriv, along_z):
    shape = state[0].shape
    table = derivative_matrix()
    flux = wave_flux(state, mean, 0)
    if halos is None:
        halos = [([jnp.zeros((8, 128), f32)] * 4,) * 2] + [([None] * 4,) * 2] * 2
    before, after = halos[0]
    low_mean, high_mean = [m[0] for m in mean], [m[7] for m in mean]
    low_jump = [b - s[0] for b, s in zip(before, state)]
    high_jump = [a - s[7] for a, s in zip(after, state)]
    low_flux = wave_flux(low_jump, low_mean, 0)
    high_flux = wave_flux(high_jump, high_mean, 0)
    half, lift = 0.5 * face_lift, 0.5 * face_lift * upwind_speed
    total = []
    for c in range(4):
        planes = []
        for i in range(8):
            plane = -float(table[i, 0]) * flux[c][0]
            for a in range(1, 8):
                if abs(table[i, a]) > 1e-12:
                    plane = plane - float(table[i, a]) * flux[c][a]
            if i == 0:
                plane = plane + (half * low_flux[c] + lift * low_jump[c])
            if i == 7:
                plane = plane - (half * high_flux[c] - lift * high_jump[c])
            planes.append(plane)
        total.append(jnp.stack(planes, axis=0))
    flux = wave_flux(state, mean, 1)
    before, after = halos[1]
    row = sublane(shape)
    sign = jnp.where(row == 0, half, jnp.where(row == 7, -half, 0.0))
    jump = []
    for s, b, a in zip(state, before, after):
        planes = []
        for x in range(8):
            low = 0.0 if b is None else rolled(b, -x, 0)
            high = 0.0 if a is None else rolled(a, 7 - x, 0)
            planes.append(jnp.where(row[x] == 0, low, jnp.where(row[x] == 7, high, s[x])) - s[x])
        jump.append(jnp.stack(planes, axis=0))
    jump_flux = wave_flux(jump, mean, 1)
    for c in range(4):
        change = lift * jump[c] + sign * jump_flux[c]
        for b in range(8):
            change = change - deriv[:, b : b + 1][None] * flux[c][:, b : b + 1, :]
        total[c] = total[c] + change
    flux = wave_flux(state, mean, 2)
    before, after = halos[2]
    column = lane(shape)
    place = lax.rem(column, 8)
    sign = jnp.where(place == 0, half, jnp.where(place == 7, -half, 0.0))
    jump = [
        jnp.where(
            place == 0,
            shifted(s, 2, -1, b),
            jnp.where(place == 7, shifted(s, 2, 1, a), s),
        )
        - s
        for s, b, a in zip(state, before, after)
    ]
    jump_flux = wave_flux(jump, mean, 2)
    for c in range(4):
        slope = dot3(flux[c].reshape(64, 128), along_z).reshape(shape)
        total[c] = total[c] + (lift * jump[c] + sign * jump_flux[c] - slope)
    return total


def mean_layers(mean):
    return [
        [m[0] for m in mean],
        [m[7] for m in mean],
        [m[:, 0, :] for m in mean],
        [m[:, 7, :] for m in mean],
        [z_layer(m, jnp.int32(0)) for m in mean],
        [z_layer(m, jnp.int32(127)) for m in mean],
    ]


def acoustic_outer(mean_faces, halos):
    half, lift = 0.5 * face_lift, 0.5 * face_lift * upwind_speed
    layers = []
    for axis, (before, after) in enumerate(halos):
        low_flux = wave_flux(before, mean_faces[2 * axis], axis)
        high_flux = wave_flux(after, mean_faces[2 * axis + 1], axis)
        layers.append(
            (
                [half * f + lift * b for f, b in zip(low_flux, before)],
                [lift * a - half * f for f, a in zip(high_flux, after)],
            )
        )
    return layers


def tile_rows(matrix):
    spread = (lax.rem(lane((8, 128)), 8) == sublane((8, 128))).astype(f32)
    return jnp.dot(
        matrix, spread, precision=lax.Precision.HIGHEST, preferred_element_type=f32
    )


def pairings(count):
    sets = []
    for first in (0, 1):
        pairs = [(i, i + 1) for i in range(first, count - 1, 2)]
        if pairs:
            sets.append(pairs)
    return sets


def slots(counts):
    found = [(axis, n) for axis in range(3) for n in range(len(pairings(counts[axis])))]
    lower = ((2, 1), (2, 0), (0, 1), (1, 0), (1, 1), (0, 0))
    upper = ((2, 1), (0, 1), (2, 0), (0, 0), (1, 1), (1, 0))
    lower = [swap for swap in lower if swap in found]
    upper = [swap for swap in upper if swap in found] if counts[1] == 4 else lower
    return list(zip(lower, upper))


def in_upper_half(counts):
    return lax.axis_index("gy") >= counts[1] // 2


def routes(counts):
    places = [(x, y, z) for x in range(counts[0]) for y in range(counts[1]) for z in range(counts[2])]
    number = {place: n for n, place in enumerate(places)}

    def partner(place, axis, n):
        pairs = pairings(counts[axis])[n]
        swap = dict(pairs + [(j, i) for i, j in pairs])
        alone = [i for i in range(counts[axis]) if i not in swap]
        spare = 0 if axis else 2
        other = list(place)
        if place[axis] in swap:
            other[axis] = swap[place[axis]]
        elif axis == 0 and len(alone) == 2:
            other[axis] = sum(alone) - place[axis]
        elif counts[spare] % 2 == 0:
            other[spare] = place[spare] ^ 1
        return number[tuple(other)]

    return [
        [
            (number[place], partner(place, *(upper if place[1] >= counts[1] // 2 else lower)))
            for place in places
        ]
        for lower, upper in slots(counts)
    ]


def z_layer(field, at):
    packed = jnp.zeros((8, 128), f32)
    column = lane((8, 128))
    for x in range(8):
        turned = pltpu.roll(field[x], lax.rem(2 * x - at + 128, 128), 1)
        packed = jnp.where(column == 2 * x, turned, packed)
    return packed


def store_faces(fields, out_refs, counts):
    high_half = in_upper_half(counts)
    for c, field in enumerate(fields):
        faces = {}
        for axis in range(3):
            even = lax.rem(lax.axis_index(axes[axis]), 2) == 0
            if axis == 0:
                low, high = field[0], field[7]
            elif axis == 1:
                low, high = field[:, 0, :], field[:, 7, :]
            for n in range(len(pairings(counts[axis]))):
                last = even == (n == 0)
                if axis == 2:
                    faces[axis, n] = z_layer(field, jnp.where(last, 127, 0))
                else:
                    faces[axis, n] = jnp.where(last, high, low)
        for ref, (lower, upper) in zip(out_refs, slots(counts)):
            if lower == upper:
                ref[c] = faces[lower]
            else:
                ref[c] = jnp.where(high_half, faces[upper], faces[lower])


def load_faces(in_refs, counts, first, last):
    high_half = in_upper_half(counts)
    lower, upper = zip(*slots(counts))
    halos = []
    for axis in range(3):
        place = lax.axis_index(axes[axis])
        even = lax.rem(place, 2) == 0
        got = []
        for n in range(len(pairings(counts[axis]))):
            a, b = in_refs[lower.index((axis, n))], in_refs[upper.index((axis, n))]
            got.append(
                [a[c] if a is b else jnp.where(high_half, b[c], a[c]) for c in range(first, last)]
            )
        while len(got) < 2:
            got.append([jnp.zeros((8, 128), f32)] * (last - first))
        before = [jnp.where(place == 0, 0.0, jnp.where(even, b, a)) for a, b in zip(*got)]
        after = [
            jnp.where(place == counts[axis] - 1, 0.0, jnp.where(even, a, b))
            for a, b in zip(*got)
        ]
        halos.append((before, after))
    return halos


def face_shapes(counts, width):
    total = sum(len(pairings(count)) for count in counts)
    return [jax.ShapeDtypeStruct((width, 8, 128), f32)] * total


def exchange(faces, counts):
    return [lax.ppermute(face, axes, way) for face, way in zip(faces, routes(counts))]


def read_all(ref):
    return [ref[c] for c in range(ref.shape[0])]


def load_kernel(counts, *refs):
    sources, targets, out_refs, sems = refs[:5], refs[5:10], refs[10:-1], refs[-1]
    copies = [
        pltpu.make_async_copy(source, target, sems.at[n])
        for n, (source, target) in enumerate(zip(sources, targets))
    ]
    for copy in copies:
        copy.start()
    for copy, target, first in zip(copies, targets, (0, 5)):
        copy.wait()
        count = target.shape[0]
        store_faces(read_all(target), [ref.at[first : first + count] for ref in out_refs], counts)
    for copy in copies[2:]:
        copy.wait()


def partners(count):
    if count == window:
        return [[(i, i ^ mask) for i in range(count)] for mask in range(count)]
    turns = sorted({d % count for d in range(1 - window, window)})
    return [[(i, (i + turn) % count) for i in range(count)] for turn in turns]


def sending_sets(count):
    return [3, 2, 1, 0] if count == window else list(range(count))


def plan_kernel(
    counts, owner_ref, slot_ref, proj_ref, order_ref, marks_ref, along_x_ref, along_y_ref, tile_ref
):
    count = counts[0]
    n_sets = len(partners(count))
    own = lax.axis_index("gx")
    n_blocks = owner_ref.shape[-1]
    square = (n_blocks, n_blocks)
    block, other = sublane(square), lane(square)

    def spread(ref):
        by_lane = jnp.broadcast_to(ref[0], square)
        here = jnp.where(block == other, by_lane, 0).astype(f32)
        return by_lane, jnp.sum(here, axis=1, keepdims=True).astype(jnp.int32)

    def group_of(owner):
        if count == window:
            return lax.bitwise_xor(owner, own)
        turn = lax.rem(owner - own + count, count)
        if n_sets == count:
            return turn
        return jnp.where(turn < window, turn, turn - (count - n_sets))

    owner_by_lane, owner = spread(owner_ref)
    slot = spread(slot_ref)[1]
    group = group_of(owner)
    before = (group_of(owner_by_lane) == group) & (other < block)
    taken = jnp.sum(before.astype(f32), axis=1, keepdims=True).astype(jnp.int32)
    wide = (n_blocks, 128)
    place = jnp.broadcast_to(group * window + taken, wide)
    column = lane((8, 128))
    quarter = column // 32
    for s in range((n_sets + 3) // 4):
        here = place - 16 * s == lane(wide) // 8
        label = jnp.sum(jnp.where(here, (slot + 1).astype(f32), 0.0), axis=0, keepdims=True) - 1.0
        source = jnp.sum(
            jnp.where(here, (8 * sublane(wide)).astype(f32), 0.0), axis=0, keepdims=True
        )
        labels = jnp.broadcast_to(label, (8, 128))
        order = jnp.broadcast_to(source, (8, 128)).astype(jnp.int32) + lax.rem(column, 8)
        for t in range(4):
            order_ref[4 * s + t] = rolled(order, 32 * t, 1)
        for r in range(min(4, n_sets - 4 * s)):
            marks = labels
            for t in range(1, 4):
                marks = jnp.where(quarter == (r + t) % 4, rolled(labels, 32 * t, 1), marks)
            marks_ref[4 * s + r] = marks
    proj = proj_ref[...]
    for a in range(8):
        along_y = jnp.broadcast_to(proj[:, a : a + 1], (8, 128))
        along_y_ref[a] = along_y
        for i in range(8):
            along_x_ref[8 * i + a] = jnp.broadcast_to(along_y[i : i + 1], (8, 128))
    tile = tile_rows(proj)
    high = tile.astype(jnp.bfloat16).astype(f32)
    tile_ref[0] = high
    tile_ref[1] = tile - high


def speeds(state):
    inverse = 1.0 / (state[0] + 1.0)
    return [state[c] * inverse for c in (1, 2, 3)]


def vorticity_kernel(les_ref, velocity_ref, vort_ref):
    velocity = speeds([les_ref[c] for c in range(4)])

    def slope(c, axis):
        return shifted(velocity[c], axis, 1) - shifted(velocity[c], axis, -1)

    vort = [slope(2, 1) - slope(1, 2), slope(0, 2) - slope(2, 0), slope(1, 0) - slope(0, 1)]
    for c in range(3):
        velocity_ref[c] = velocity[c]
        vort_ref[c] = vort[c]


def lamb_kernel(
    counts, n_faces, order_ref, marks_ref, along_x_ref, along_y_ref, velocity_ref, vort_ref, *refs
):
    face_refs, out_refs = refs[:n_faces], refs[n_faces:]
    outer = [
        (speeds(before), speeds(after)) for before, after in load_faces(face_refs, counts, 0, 4)
    ]

    def rise(c, axis):
        return -outer[axis][0][c], outer[axis][1][c]

    def fall(c, axis):
        return outer[axis][0][c], -outer[axis][1][c]

    layers = [
        (None, rise(2, 1), fall(1, 2)),
        (fall(2, 0), None, rise(0, 2)),
        (rise(1, 0), fall(0, 1), None),
    ]
    vort = [0.5 * jnp.stack(with_layers(vort_ref[c], layers[c]), axis=0) for c in range(3)]
    velocity = read_all(velocity_ref)
    lamb = [
        vort[1] * velocity[2] - vort[2] * velocity[1],
        vort[2] * velocity[0] - vort[0] * velocity[2],
        vort[0] * velocity[1] - vort[1] * velocity[0],
    ]
    blocks = []
    for field in lamb:
        along_y = along_y_ref[0][None] * field[:, 0:1, :]
        for b in range(1, 8):
            along_y = along_y + along_y_ref[b][None] * field[:, b : b + 1, :]
        for i in range(8):
            plane = along_x_ref[8 * i] * along_y[0]
            for a in range(1, 8):
                plane = plane + along_x_ref[8 * i + a] * along_y[a]
            blocks.append(plane)

    quarter = lane((8, 128)) // 32
    for s in range((len(out_refs) + 3) // 4):
        ordered = [
            jnp.take_along_axis(block, order_ref[4 * s + k % 4], axis=1)
            for k, block in enumerate(blocks)
        ]
        for r in range(min(4, len(out_refs) - 4 * s)):
            out = out_refs[4 * s + r]
            for q in range(6):
                packed = ordered[4 * q]
                for t in range(1, 4):
                    packed = jnp.where(quarter == (r + t) % 4, ordered[4 * q + t], packed)
                out[q] = packed
            out[6] = marks_ref[4 * s + r]


def first_kernel(
    counts, n_faces, deriv_ref, high_ref, low_ref, les_ref, wave_ref, mean_ref, *refs
):
    face_refs, (section_ref, rate_ref), out_refs = (
        refs[:n_faces], refs[n_faces : n_faces + 2], refs[n_faces + 2 :],
    )
    state = read_all(les_ref)
    rate = les_rate(state, load_faces(face_refs, counts, 0, 5))
    section = [s + r for s, r in zip(state, rate)]
    for c in range(5):
        section_ref[c] = section[c]
    store_faces(section, out_refs, counts)
    rate = acoustic_rate(
        read_all(wave_ref), read_all(mean_ref), load_faces(face_refs, counts, 5, 9),
        deriv_ref[...], (high_ref[...], low_ref[...]),
    )
    for c in range(4):
        rate_ref[c] = rate[c]


def source_kernel(counts, n_faces, tile_ref, wave_ref, rate_ref, *refs):
    n_pieces = len(partners(counts[0]))
    pieces = [None] * n_pieces
    for ref, k in zip(refs, sending_sets(n_pieces)):
        pieces[k] = ref
    refs = refs[n_pieces:]
    section_faces, (source_ref, middle_ref, carry_ref), face_refs = (
        refs[:n_faces], refs[n_faces : n_faces + 3], refs[n_faces + 3 :],
    )
    quarter = lane((8, 128)) // 32
    tile_high, tile_low = tile_ref[0], tile_ref[1]
    total = None
    for s in range((n_pieces + 3) // 4):
        count = min(4, n_pieces - 4 * s)

        def gathered(q, t):
            value = jnp.full((8, 128), -1.0 if q == 6 else 0.0, f32)
            for r in range(count):
                value = jnp.where(quarter == (r + t) % 4, pieces[4 * s + r][q], value)
            return value

        here = [gathered(6, 0).astype(jnp.int32) == slot for slot in range(16)]
        chosen_high, chosen_low = [
            jnp.concatenate([jnp.where(h, part, 0.0) for h in here], axis=0).astype(jnp.bfloat16)
            for part in (tile_high, tile_low)
        ]
        data = []
        for k in range(24):
            piece = gathered(k // 4, k % 4)
            data.append(pltpu.roll(piece, 128 - 32 * (k % 4), 1) if k % 4 else piece)
        data = jnp.concatenate(data, axis=0)
        high = data.astype(jnp.bfloat16)
        low = (data - high.astype(f32)).astype(jnp.bfloat16)
        dot = functools.partial(
            lax.dot_general,
            dimension_numbers=(((1,), (1,)), ((), ())),
            preferred_element_type=f32,
        )
        moved = dot(high, chosen_high) + (dot(low, chosen_high) + dot(high, chosen_low))
        total = moved if total is None else total + moved
    source = [total[64 * c : 64 * c + 64].reshape(8, 8, 128) for c in range(3)]
    middle = []
    for c in range(4):
        rate = rate_ref[c]
        if c:
            source_ref[c - 1] = source[c - 1]
            rate = rate + source[c - 1]
        middle.append(wave_ref[c] + acoustic_step * rate)
        middle_ref[c] = middle[c]
        carry = wave_ref[c] + middle[c]
        carry_ref[c] = carry + acoustic_step * source[c - 1] if c else carry
    for ready, face in zip(section_faces, face_refs):
        face[0:5] = ready[...]
    store_faces(middle, [face.at[5:9] for face in face_refs], counts)


def inner_kernel(
    deriv_ref, high_ref, low_ref, les_ref, section_ref, middle_ref, carry_ref, mean_ref, source_ref,
    les_base_ref, wave_base_ref, mean_faces_ref, source_out, sem,
):
    copy = pltpu.make_async_copy(source_ref, source_out, sem)
    copy.start()
    section = read_all(section_ref)
    rate = les_rate(section, None)
    for c in range(5):
        les_base_ref[c] = 0.5 * ((les_ref[c] + section[c]) + rate[c])
    mean = read_all(mean_ref)
    for n, face in enumerate(mean_layers(mean)):
        for c in range(3):
            mean_faces_ref[n, c] = face[c]
    rate = acoustic_rate(
        read_all(middle_ref), mean, None, deriv_ref[...], (high_ref[...], low_ref[...])
    )
    for c in range(4):
        wave_base_ref[c] = 0.5 * (carry_ref[c] + acoustic_step * rate[c])
    copy.wait()


def last_kernel(counts, n_faces, les_base_ref, wave_base_ref, mean_faces_ref, *refs):
    face_refs, (les_out, wave_out, les_ref, wave_ref, sems) = (
        refs[:n_faces], refs[n_faces:],
    )
    copies = []

    def send(source, target):
        copies.append(pltpu.make_async_copy(source, target, sems.at[len(copies)]))
        copies[-1].start()

    layers = les_outer(load_faces(face_refs, counts, 0, 5))
    for c in range(5):
        part = [(0.5 * low[c], 0.5 * high[c]) for low, high in layers]
        for x, plane in enumerate(with_layers(les_base_ref[c], part)):
            les_ref[c, x] = plane
        send(les_ref.at[c], les_out.at[c])
    mean_faces = [[mean_faces_ref[n, c] for c in range(3)] for n in range(6)]
    layers = acoustic_outer(mean_faces, load_faces(face_refs, counts, 5, 9))
    step = 0.5 * acoustic_step
    for c in range(4):
        part = [(step * low[c], step * high[c]) for low, high in layers]
        for x, plane in enumerate(with_layers(wave_base_ref[c], part)):
            wave_ref[c, x] = plane
        send(wave_ref.at[c], wave_out.at[c])
    for copy in copies:
        copy.wait()


VMEM = pl.BlockSpec(memory_space=pltpu.VMEM)


HBM = pl.BlockSpec(memory_space=pltpu.HBM)


def call(kernel, in_specs, out_shapes, name, cost, scratch=(), out_spec=None):
    return pl.pallas_call(
        kernel,
        in_specs=in_specs,
        out_specs=out_spec or [VMEM] * len(out_shapes),
        out_shape=out_shapes,
        scratch_shapes=list(scratch),
        name=name,
        cost_estimate=pl.CostEstimate(flops=cost, bytes_accessed=800000, transcendentals=0),
        compiler_params=pltpu.CompilerParams(vmem_limit_bytes=24 * 1024 * 1024),
    )


def local(counts, les, wave, mean, projection, owner, slot):
    shape = les.shape[1:]
    faces = face_shapes(counts, 9)
    n_faces = len(faces)
    like = lambda n: jax.ShapeDtypeStruct((n,) + shape, f32)

    table = derivative_matrix()
    deriv = jnp.asarray(table, f32)
    along_z = np.kron(np.eye(16), table.T).astype(np.float32)
    high = along_z.astype(jnp.bfloat16)
    low = (along_z - high.astype(np.float32)).astype(jnp.bfloat16)
    tables = (deriv, jnp.asarray(high), jnp.asarray(low))

    arguments = (les, wave, owner, slot, projection)
    les, wave, owner, slot, projection, *sent = call(
        functools.partial(load_kernel, counts),
        [HBM] * 5,
        [jax.ShapeDtypeStruct(a.shape, a.dtype) for a in arguments] + faces,
        "load_and_faces",
        100000,
        [pltpu.SemaphoreType.DMA((5,))],
    )(*(pltpu.with_memory_space_constraint(a, pltpu.HBM) for a in arguments))
    got = exchange(sent, counts)

    sets = partners(counts[0])
    n_plans = 4 * ((len(sets) + 3) // 4)
    order, marks, along_x, along_y, tile = call(
        functools.partial(plan_kernel, counts),
        [VMEM] * 3,
        [
            jax.ShapeDtypeStruct((n_plans, 8, 128), jnp.int32),
            jax.ShapeDtypeStruct((len(sets), 8, 128), f32),
            jax.ShapeDtypeStruct((64, 8, 128), f32),
            jax.ShapeDtypeStruct((8, 8, 128), f32),
            jax.ShapeDtypeStruct((2, 8, 128), f32),
        ],
        "plan",
        1000000,
    )(owner, slot, projection)
    turning = call(vorticity_kernel, [VMEM], [like(3)] * 2, "vorticity", 1000000)(les)
    pieces = call(
        functools.partial(lamb_kernel, counts, n_faces),
        [VMEM] * (6 + n_faces),
        [jax.ShapeDtypeStruct((7, 8, 128), f32)] * len(sets),
        "lamb_blocks",
        10000000,
    )(order, marks, along_x, along_y, *turning, *got)
    moved = []
    for k in sending_sets(len(sets)):
        still = all(i == j for i, j in sets[k])
        moved.append(pieces[k] if still else lax.ppermute(pieces[k], "gx", sets[k]))
    section, rate, *section_faces = call(
        functools.partial(first_kernel, counts, n_faces),
        [VMEM] * (6 + n_faces),
        [like(5), like(4)] + face_shapes(counts, 5),
        "first_rates",
        40000000,
    )(*tables, les, wave, mean, *got)

    source, middle, carry, *sent = call(
        functools.partial(source_kernel, counts, n_faces),
        [VMEM] * (3 + len(moved) + n_faces),
        [like(3), like(4), like(4)] + faces,
        "source_and_faces",
        10000000,
    )(tile, wave, rate, *moved, *section_faces)
    got = exchange(sent, counts)
    les_base, wave_base, mean_faces, source_out = call(
        inner_kernel,
        [VMEM] * 9,
        [like(5), like(4), jax.ShapeDtypeStruct((6, 3, 8, 128), f32), like(3)],
        "second_rates_inner",
        40000000,
        [pltpu.SemaphoreType.DMA],
        out_spec=[VMEM, VMEM, VMEM, HBM],
    )(*tables, les, section, middle, carry, mean, source)
    les_next, wave_next = call(
        functools.partial(last_kernel, counts, n_faces),
        [VMEM] * (3 + n_faces),
        [like(5), like(4)],
        "second_rates_outer",
        4000000,
        [
            pltpu.VMEM(les.shape, f32),
            pltpu.VMEM(wave.shape, f32),
            pltpu.SemaphoreType.DMA((9,)),
        ],
        out_spec=[HBM, HBM],
    )(les_base, wave_base, mean_faces, *got)
    return les_next, source_out, wave_next


def solution(mesh):
    counts = tuple(mesh.shape[axis] for axis in axes)
    field = P(None, *axes)
    return jax.shard_map(
        functools.partial(local, counts),
        mesh=mesh,
        in_specs=(field, field, field, P(), P(*axes), P(*axes)),
        out_specs=(field, field, field),
        check_vma=False,
    )
```

```python
import functools

import jax
import jax.numpy as jnp
import numpy as np
from jax import lax
from jax.experimental import pallas as pl
from jax.experimental.pallas import tpu as pltpu
from jax.sharding import PartitionSpec as P

lobatto_points = np.array(
    [
        -1.0,
        -0.8717401485096066,
        -0.5917001814331423,
        -0.2092992179024789,
        0.2092992179024789,
        0.5917001814331423,
        0.8717401485096066,
        1.0,
    ]
)
flux_half = 0.08
gamma_less = 0.4
acoustic_step = 0.01
upwind_speed = 1.5
face_lift = 28.0
free_stream = (1.0, 0.0, 0.0, 0.0, 2.5)
axes = ("gx", "gy", "gz")
window = 4
f32 = jnp.float32


def derivative_matrix():
    points = lobatto_points
    products = [np.prod([points[i] - points[j] for j in range(8) if j != i]) for i in range(8)]
    matrix = np.zeros((8, 8))
    for i in range(8):
        for j in range(8):
            if j != i:
                matrix[i, j] = products[i] / (products[j] * (points[i] - points[j]))
        matrix[i, i] = -np.sum(matrix[i])
    return matrix


def sublane(shape):
    return lax.broadcasted_iota(jnp.int32, shape, len(shape) - 2)


def lane(shape):
    return lax.broadcasted_iota(jnp.int32, shape, len(shape) - 1)


def rolled(tile, amount, axis):
    amount = amount % tile.shape[axis]
    return pltpu.roll(tile, amount, axis) if amount else tile


def shifted(field, axis, step, outer=None):
    if axis == 0:
        outer = jnp.zeros((8, 128), f32) if outer is None else outer
        if step == 1:
            return jnp.concatenate([field[1:], outer[None]], axis=0)
        return jnp.concatenate([outer[None], field[:-1]], axis=0)
    count = (8, 128)[axis - 1]
    edge = count - 1 if step == 1 else 0
    at_edge = (sublane if axis == 1 else lane)((8, 128)) == edge
    planes = []
    for x in range(8):
        layer = 0.0 if outer is None else rolled(outer, edge - axis * x, axis - 1)
        planes.append(jnp.where(at_edge, layer, rolled(field[x], -step, axis - 1)))
    return jnp.stack(planes, axis=0)


def fluid(state):
    density, mx, my, mz, energy = [s + r for s, r in zip(state, free_stream)]
    inverse = 1.0 / density
    momentum = (mx, my, mz)
    velocity = [m * inverse for m in momentum]
    pressure = gamma_less * (
        energy - 0.5 * (mx * velocity[0] + my * velocity[1] + mz * velocity[2])
    )
    return momentum, velocity, pressure, energy + pressure


def split_flux(state, parts, axis, sign):
    momentum, velocity, pressure, enthalpy = parts
    speed = velocity[axis]
    flux = [momentum[axis]]
    for c in range(3):
        term = momentum[c] * speed
        flux.append(term + pressure if c == axis else term)
    flux.append(enthalpy * speed)
    if sign > 0:
        return [flux_half * (s + f) for s, f in zip(state, flux)]
    return [flux_half * (s - f) for s, f in zip(state, flux)]


def les_rate(state, halos):
    parts = fluid(state)
    total = [-6.0 * flux_half * s for s in state]
    for axis in range(3):
        ahead = split_flux(state, parts, axis, -1)
        behind = split_flux(state, parts, axis, 1)
        ahead_outer = behind_outer = [None] * 5
        if halos is not None:
            before, after = halos[axis]
            ahead_outer = split_flux(after, fluid(after), axis, -1)
            behind_outer = split_flux(before, fluid(before), axis, 1)
        for c in range(5):
            total[c] = total[c] + (
                shifted(ahead[c], axis, 1, ahead_outer[c])
                + shifted(behind[c], axis, -1, behind_outer[c])
            )
    return total


def les_outer(halos):
    return [
        (
            split_flux(before, fluid(before), axis, 1),
            split_flux(after, fluid(after), axis, -1),
        )
        for axis, (before, after) in enumerate(halos)
    ]


def with_layers(field, layers):
    row, column = sublane((8, 128)), lane((8, 128))
    along_z = layers[2]
    if along_z is not None:
        along_z = jnp.where(lax.rem(column, 2) == 0, along_z[0], rolled(along_z[1], -1, 1))
    planes = []
    for x in range(8):
        plane = field[x]
        if layers[0] is not None and x in (0, 7):
            plane = plane + layers[0][x // 7]
        if layers[1] is not None:
            low, high = layers[1]
            plane = plane + jnp.where(
                row == 0, rolled(low, -x, 0), jnp.where(row == 7, rolled(high, 7 - x, 0), 0.0)
            )
        if along_z is not None:
            ends = (column == 0) | (column == 127)
            plane = plane + jnp.where(ends, rolled(along_z, -2 * x, 1), 0.0)
        planes.append(plane)
    return planes


def wave_flux(state, mean, axis):
    speed = mean[axis]
    pressure = state[0]
    rows = [speed * pressure + state[1 + axis]]
    for c in range(3):
        term = speed * state[1 + c]
        rows.append(term + pressure if c == axis else term)
    return rows


def dot3(left, right):
    high = left.astype(jnp.bfloat16)
    low = (left - high.astype(f32)).astype(jnp.bfloat16)
    dot = functools.partial(jnp.dot, preferred_element_type=f32)
    return dot(high, right[0]) + (dot(low, right[0]) + dot(high, right[1]))


def acoustic_rate(state, mean, halos, deriv, along_z):
    shape = state[0].shape
    table = derivative_matrix()
    flux = wave_flux(state, mean, 0)
    if halos is None:
        halos = [([jnp.zeros((8, 128), f32)] * 4,) * 2] + [([None] * 4,) * 2] * 2
    before, after = halos[0]
    low_mean, high_mean = [m[0] for m in mean], [m[7] for m in mean]
    low_jump = [b - s[0] for b, s in zip(before, state)]
    high_jump = [a - s[7] for a, s in zip(after, state)]
    low_flux = wave_flux(low_jump, low_mean, 0)
    high_flux = wave_flux(high_jump, high_mean, 0)
    half, lift = 0.5 * face_lift, 0.5 * face_lift * upwind_speed
    total = []
    for c in range(4):
        planes = []
        for i in range(8):
            plane = -float(table[i, 0]) * flux[c][0]
            for a in range(1, 8):
                if abs(table[i, a]) > 1e-12:
                    plane = plane - float(table[i, a]) * flux[c][a]
            if i == 0:
                plane = plane + (half * low_flux[c] + lift * low_jump[c])
            if i == 7:
                plane = plane - (half * high_flux[c] - lift * high_jump[c])
            planes.append(plane)
        total.append(jnp.stack(planes, axis=0))
    flux = wave_flux(state, mean, 1)
    before, after = halos[1]
    row = sublane(shape)
    sign = jnp.where(row == 0, half, jnp.where(row == 7, -half, 0.0))
    jump = []
    for s, b, a in zip(state, before, after):
        planes = []
        for x in range(8):
            low = 0.0 if b is None else rolled(b, -x, 0)
            high = 0.0 if a is None else rolled(a, 7 - x, 0)
            planes.append(jnp.where(row[x] == 0, low, jnp.where(row[x] == 7, high, s[x])) - s[x])
        jump.append(jnp.stack(planes, axis=0))
    jump_flux = wave_flux(jump, mean, 1)
    for c in range(4):
        change = lift * jump[c] + sign * jump_flux[c]
        for b in range(8):
            change = change - deriv[:, b : b + 1][None] * flux[c][:, b : b + 1, :]
        total[c] = total[c] + change
    flux = wave_flux(state, mean, 2)
    before, after = halos[2]
    column = lane(shape)
    place = lax.rem(column, 8)
    sign = jnp.where(place == 0, half, jnp.where(place == 7, -half, 0.0))
    jump = [
        jnp.where(
            place == 0,
            shifted(s, 2, -1, b),
            jnp.where(place == 7, shifted(s, 2, 1, a), s),
        )
        - s
        for s, b, a in zip(state, before, after)
    ]
    jump_flux = wave_flux(jump, mean, 2)
    for c in range(4):
        slope = dot3(flux[c].reshape(64, 128), along_z).reshape(shape)
        total[c] = total[c] + (lift * jump[c] + sign * jump_flux[c] - slope)
    return total


def mean_layers(mean):
    return [
        [m[0] for m in mean],
        [m[7] for m in mean],
        [m[:, 0, :] for m in mean],
        [m[:, 7, :] for m in mean],
        [z_layer(m, jnp.int32(0)) for m in mean],
        [z_layer(m, jnp.int32(127)) for m in mean],
    ]


def acoustic_outer(mean_faces, halos):
    half, lift = 0.5 * face_lift, 0.5 * face_lift * upwind_speed
    layers = []
    for axis, (before, after) in enumerate(halos):
        low_flux = wave_flux(before, mean_faces[2 * axis], axis)
        high_flux = wave_flux(after, mean_faces[2 * axis + 1], axis)
        layers.append(
            (
                [half * f + lift * b for f, b in zip(low_flux, before)],
                [lift * a - half * f for f, a in zip(high_flux, after)],
            )
        )
    return layers


def tile_rows(matrix):
    spread = (lax.rem(lane((8, 128)), 8) == sublane((8, 128))).astype(f32)
    return jnp.dot(
        matrix, spread, precision=lax.Precision.HIGHEST, preferred_element_type=f32
    )


def pairings(count):
    sets = []
    for first in (0, 1):
        pairs = [(i, i + 1) for i in range(first, count - 1, 2)]
        if pairs:
            sets.append(pairs)
    return sets


def slots(counts):
    found = [(axis, n) for axis in range(3) for n in range(len(pairings(counts[axis])))]
    lower = ((2, 1), (2, 0), (0, 1), (1, 0), (1, 1), (0, 0))
    upper = ((2, 1), (0, 1), (2, 0), (0, 0), (1, 1), (1, 0))
    lower = [swap for swap in lower if swap in found]
    upper = [swap for swap in upper if swap in found] if counts[1] == 4 else lower
    return list(zip(lower, upper))


def in_upper_half(counts):
    return lax.axis_index("gy") >= counts[1] // 2


def routes(counts):
    places = [(x, y, z) for x in range(counts[0]) for y in range(counts[1]) for z in range(counts[2])]
    number = {place: n for n, place in enumerate(places)}

    def partner(place, axis, n):
        pairs = pairings(counts[axis])[n]
        swap = dict(pairs + [(j, i) for i, j in pairs])
        alone = [i for i in range(counts[axis]) if i not in swap]
        spare = 0 if axis else 2
        other = list(place)
        if place[axis] in swap:
            other[axis] = swap[place[axis]]
        elif axis == 0 and len(alone) == 2:
            other[axis] = sum(alone) - place[axis]
        elif counts[spare] % 2 == 0:
            other[spare] = place[spare] ^ 1
        return number[tuple(other)]

    return [
        [
            (number[place], partner(place, *(upper if place[1] >= counts[1] // 2 else lower)))
            for place in places
        ]
        for lower, upper in slots(counts)
    ]


def z_layer(field, at):
    packed = jnp.zeros((8, 128), f32)
    column = lane((8, 128))
    for x in range(8):
        turned = pltpu.roll(field[x], lax.rem(2 * x - at + 128, 128), 1)
        packed = jnp.where(column == 2 * x, turned, packed)
    return packed


def store_faces(fields, out_refs, counts):
    high_half = in_upper_half(counts)
    for c, field in enumerate(fields):
        faces = {}
        for axis in range(3):
            even = lax.rem(lax.axis_index(axes[axis]), 2) == 0
            if axis == 0:
                low, high = field[0], field[7]
            elif axis == 1:
                low, high = field[:, 0, :], field[:, 7, :]
            for n in range(len(pairings(counts[axis]))):
                last = even == (n == 0)
                if axis == 2:
                    faces[axis, n] = z_layer(field, jnp.where(last, 127, 0))
                else:
                    faces[axis, n] = jnp.where(last, high, low)
        for ref, (lower, upper) in zip(out_refs, slots(counts)):
            if lower == upper:
                ref[c] = faces[lower]
            else:
                ref[c] = jnp.where(high_half, faces[upper], faces[lower])


def load_faces(in_refs, counts, first, last):
    high_half = in_upper_half(counts)
    lower, upper = zip(*slots(counts))
    halos = []
    for axis in range(3):
        place = lax.axis_index(axes[axis])
        even = lax.rem(place, 2) == 0
        got = []
        for n in range(len(pairings(counts[axis]))):
            a, b = in_refs[lower.index((axis, n))], in_refs[upper.index((axis, n))]
            got.append(
                [a[c] if a is b else jnp.where(high_half, b[c], a[c]) for c in range(first, last)]
            )
        while len(got) < 2:
            got.append([jnp.zeros((8, 128), f32)] * (last - first))
        before = [jnp.where(place == 0, 0.0, jnp.where(even, b, a)) for a, b in zip(*got)]
        after = [
            jnp.where(place == counts[axis] - 1, 0.0, jnp.where(even, a, b))
            for a, b in zip(*got)
        ]
        halos.append((before, after))
    return halos


def face_shapes(counts, width):
    total = sum(len(pairings(count)) for count in counts)
    return [jax.ShapeDtypeStruct((width, 8, 128), f32)] * total


def exchange(faces, counts):
    return [lax.ppermute(face, axes, way) for face, way in zip(faces, routes(counts))]


def read_all(ref):
    return [ref[c] for c in range(ref.shape[0])]


def load_kernel(counts, les_hbm, wave_hbm, les_ref, wave_ref, *refs):
    out_refs, sems = refs[:-1], refs[-1]
    copies = [
        pltpu.make_async_copy(les_hbm, les_ref, sems.at[0]),
        pltpu.make_async_copy(wave_hbm, wave_ref, sems.at[1]),
    ]
    for copy in copies:
        copy.start()
    for copy, target, first in zip(copies, (les_ref, wave_ref), (0, 5)):
        copy.wait()
        count = target.shape[0]
        store_faces(read_all(target), [ref.at[first : first + count] for ref in out_refs], counts)


def partners(count):
    if count == window:
        return [[(i, i ^ mask) for i in range(count)] for mask in range(count)]
    turns = sorted({d % count for d in range(1 - window, window)})
    return [[(i, (i + turn) % count) for i in range(count)] for turn in turns]


def speeds(state):
    inverse = 1.0 / (state[0] + 1.0)
    return [state[c] * inverse for c in (1, 2, 3)]


def vorticity(les_ref, velocity_ref, vort_ref):
    velocity = speeds([les_ref[c] for c in range(4)])

    def slope(c, axis):
        return shifted(velocity[c], axis, 1) - shifted(velocity[c], axis, -1)

    vort = [slope(2, 1) - slope(1, 2), slope(0, 2) - slope(2, 0), slope(1, 0) - slope(0, 1)]
    for c in range(3):
        velocity_ref[c] = velocity[c]
        vort_ref[c] = vort[c]


def sending_sets(count):
    return [3, 2, 1, 0] if count == window else list(range(count))


def plan_kernel(
    counts, owner_hbm, slot_hbm, proj_hbm, les_ref, order_ref, marks_ref, along_x_ref, along_y_ref,
    tile_ref, velocity_ref, vort_ref, owner_ref, slot_ref, proj_ref, sems,
):
    copies = [
        pltpu.make_async_copy(source, target, sems.at[n])
        for n, (source, target) in enumerate(
            ((owner_hbm, owner_ref), (slot_hbm, slot_ref), (proj_hbm, proj_ref))
        )
    ]
    for copy in copies:
        copy.start()
    vorticity(les_ref, velocity_ref, vort_ref)
    for copy in copies:
        copy.wait()
    count = counts[0]
    n_sets = len(partners(count))
    own = lax.axis_index("gx")
    n_blocks = owner_ref.shape[-1]
    square = (n_blocks, n_blocks)
    block, other = sublane(square), lane(square)

    def spread(ref):
        by_lane = jnp.broadcast_to(ref[0], square)
        here = jnp.where(block == other, by_lane, 0).astype(f32)
        return by_lane, jnp.sum(here, axis=1, keepdims=True).astype(jnp.int32)

    def group_of(owner):
        if count == window:
            return lax.bitwise_xor(owner, own)
        turn = lax.rem(owner - own + count, count)
        if n_sets == count:
            return turn
        return jnp.where(turn < window, turn, turn - (count - n_sets))

    owner_by_lane, owner = spread(owner_ref)
    slot = spread(slot_ref)[1]
    group = group_of(owner)
    before = (group_of(owner_by_lane) == group) & (other < block)
    taken = jnp.sum(before.astype(f32), axis=1, keepdims=True).astype(jnp.int32)
    wide = (n_blocks, 128)
    place = jnp.broadcast_to(group * window + taken, wide)
    column = lane((8, 128))
    quarter = column // 32
    for s in range((n_sets + 3) // 4):
        here = place - 16 * s == lane(wide) // 8
        label = jnp.sum(jnp.where(here, (slot + 1).astype(f32), 0.0), axis=0, keepdims=True) - 1.0
        source = jnp.sum(
            jnp.where(here, (8 * sublane(wide)).astype(f32), 0.0), axis=0, keepdims=True
        )
        labels = jnp.broadcast_to(label, (8, 128))
        order = jnp.broadcast_to(source, (8, 128)).astype(jnp.int32) + lax.rem(column, 8)
        for t in range(4):
            order_ref[4 * s + t] = rolled(order, 32 * t, 1)
        for r in range(min(4, n_sets - 4 * s)):
            marks = labels
            for t in range(1, 4):
                marks = jnp.where(quarter == (r + t) % 4, rolled(labels, 32 * t, 1), marks)
            marks_ref[4 * s + r] = marks
    proj = proj_ref[...]
    for a in range(8):
        along_y = jnp.broadcast_to(proj[:, a : a + 1], (8, 128))
        along_y_ref[a] = along_y
        for i in range(8):
            along_x_ref[8 * i + a] = jnp.broadcast_to(along_y[i : i + 1], (8, 128))
    tile = tile_rows(proj)
    high = tile.astype(jnp.bfloat16).astype(f32)
    tile_ref[0] = high
    tile_ref[1] = tile - high


def lamb_kernel(
    counts, n_faces, order_ref, marks_ref, along_x_ref, along_y_ref, velocity_ref, vort_ref, *refs
):
    face_refs, out_refs = refs[:n_faces], refs[n_faces:]
    outer = [
        (speeds(before), speeds(after)) for before, after in load_faces(face_refs, counts, 0, 4)
    ]

    def rise(c, axis):
        return -outer[axis][0][c], outer[axis][1][c]

    def fall(c, axis):
        return outer[axis][0][c], -outer[axis][1][c]

    layers = [
        (None, rise(2, 1), fall(1, 2)),
        (fall(2, 0), None, rise(0, 2)),
        (rise(1, 0), fall(0, 1), None),
    ]
    vort = [0.5 * jnp.stack(with_layers(vort_ref[c], layers[c]), axis=0) for c in range(3)]
    velocity = read_all(velocity_ref)
    lamb = [
        vort[1] * velocity[2] - vort[2] * velocity[1],
        vort[2] * velocity[0] - vort[0] * velocity[2],
        vort[0] * velocity[1] - vort[1] * velocity[0],
    ]
    blocks = []
    for field in lamb:
        along_y = along_y_ref[0][None] * field[:, 0:1, :]
        for b in range(1, 8):
            along_y = along_y + along_y_ref[b][None] * field[:, b : b + 1, :]
        for i in range(8):
            plane = along_x_ref[8 * i] * along_y[0]
            for a in range(1, 8):
                plane = plane + along_x_ref[8 * i + a] * along_y[a]
            blocks.append(plane)

    quarter = lane((8, 128)) // 32
    for s in range((len(out_refs) + 3) // 4):
        ordered = [
            jnp.take_along_axis(block, order_ref[4 * s + k % 4], axis=1)
            for k, block in enumerate(blocks)
        ]
        for r in range(min(4, len(out_refs) - 4 * s)):
            out = out_refs[4 * s + r]
            for q in range(6):
                packed = ordered[4 * q]
                for t in range(1, 4):
                    packed = jnp.where(quarter == (r + t) % 4, ordered[4 * q + t], packed)
                out[q] = packed
            out[6] = marks_ref[4 * s + r]


def first_kernel(
    counts, n_faces, deriv_ref, high_ref, low_ref, les_ref, wave_ref, mean_ref, *refs
):
    face_refs, (section_ref, rate_ref), out_refs = (
        refs[:n_faces], refs[n_faces : n_faces + 2], refs[n_faces + 2 :],
    )
    state = read_all(les_ref)
    rate = les_rate(state, load_faces(face_refs, counts, 0, 5))
    section = [s + r for s, r in zip(state, rate)]
    for c in range(5):
        section_ref[c] = section[c]
    store_faces(section, out_refs, counts)
    rate = acoustic_rate(
        read_all(wave_ref), read_all(mean_ref), load_faces(face_refs, counts, 5, 9),
        deriv_ref[...], (high_ref[...], low_ref[...]),
    )
    for c in range(4):
        rate_ref[c] = rate[c]


def source_kernel(counts, n_faces, tile_ref, wave_ref, rate_ref, *refs):
    n_pieces = len(partners(counts[0]))
    pieces = [None] * n_pieces
    for ref, k in zip(refs, sending_sets(n_pieces)):
        pieces[k] = ref
    refs = refs[n_pieces:]
    section_faces, (source_ref, middle_ref, carry_ref), face_refs = (
        refs[:n_faces], refs[n_faces : n_faces + 3], refs[n_faces + 3 :],
    )
    quarter = lane((8, 128)) // 32
    tile_high, tile_low = tile_ref[0], tile_ref[1]
    total = None
    for s in range((n_pieces + 3) // 4):
        count = min(4, n_pieces - 4 * s)

        def gathered(q, t):
            value = jnp.full((8, 128), -1.0 if q == 6 else 0.0, f32)
            for r in range(count):
                value = jnp.where(quarter == (r + t) % 4, pieces[4 * s + r][q], value)
            return value

        here = [gathered(6, 0).astype(jnp.int32) == slot for slot in range(16)]
        chosen_high, chosen_low = [
            jnp.concatenate([jnp.where(h, part, 0.0) for h in here], axis=0).astype(jnp.bfloat16)
            for part in (tile_high, tile_low)
        ]
        data = []
        for k in range(24):
            piece = gathered(k // 4, k % 4)
            data.append(pltpu.roll(piece, 128 - 32 * (k % 4), 1) if k % 4 else piece)
        data = jnp.concatenate(data, axis=0)
        high = data.astype(jnp.bfloat16)
        low = (data - high.astype(f32)).astype(jnp.bfloat16)
        dot = functools.partial(
            lax.dot_general,
            dimension_numbers=(((1,), (1,)), ((), ())),
            preferred_element_type=f32,
        )
        moved = dot(high, chosen_high) + (dot(low, chosen_high) + dot(high, chosen_low))
        total = moved if total is None else total + moved
    source = [total[64 * c : 64 * c + 64].reshape(8, 8, 128) for c in range(3)]
    middle = []
    for c in range(4):
        rate = rate_ref[c]
        if c:
            source_ref[c - 1] = source[c - 1]
            rate = rate + source[c - 1]
        middle.append(wave_ref[c] + acoustic_step * rate)
        middle_ref[c] = middle[c]
        carry = wave_ref[c] + middle[c]
        carry_ref[c] = carry + acoustic_step * source[c - 1] if c else carry
    for ready, face in zip(section_faces, face_refs):
        face[0:5] = ready[...]
    store_faces(middle, [face.at[5:9] for face in face_refs], counts)


def inner_kernel(
    deriv_ref, high_ref, low_ref, les_ref, section_ref, middle_ref, carry_ref, mean_ref, source_ref,
    les_base_ref, wave_base_ref, mean_faces_ref, source_out, sem,
):
    copy = pltpu.make_async_copy(source_ref, source_out, sem)
    copy.start()
    section = read_all(section_ref)
    rate = les_rate(section, None)
    for c in range(5):
        les_base_ref[c] = 0.5 * ((les_ref[c] + section[c]) + rate[c])
    mean = read_all(mean_ref)
    for n, face in enumerate(mean_layers(mean)):
        for c in range(3):
            mean_faces_ref[n, c] = face[c]
    rate = acoustic_rate(
        read_all(middle_ref), mean, None, deriv_ref[...], (high_ref[...], low_ref[...])
    )
    for c in range(4):
        wave_base_ref[c] = 0.5 * (carry_ref[c] + acoustic_step * rate[c])
    copy.wait()


def last_kernel(counts, n_faces, les_base_ref, wave_base_ref, mean_faces_ref, *refs):
    face_refs, (les_out, wave_out, les_ref, wave_ref, sems) = (
        refs[:n_faces], refs[n_faces:],
    )
    copies = []

    def send(source, target):
        copies.append(pltpu.make_async_copy(source, target, sems.at[len(copies)]))
        copies[-1].start()

    layers = les_outer(load_faces(face_refs, counts, 0, 5))
    for c in range(5):
        part = [(0.5 * low[c], 0.5 * high[c]) for low, high in layers]
        for x, plane in enumerate(with_layers(les_base_ref[c], part)):
            les_ref[c, x] = plane
    send(les_ref, les_out)
    mean_faces = [[mean_faces_ref[n, c] for c in range(3)] for n in range(6)]
    layers = acoustic_outer(mean_faces, load_faces(face_refs, counts, 5, 9))
    step = 0.5 * acoustic_step
    for c in range(4):
        part = [(step * low[c], step * high[c]) for low, high in layers]
        for x, plane in enumerate(with_layers(wave_base_ref[c], part)):
            wave_ref[c, x] = plane
    send(wave_ref, wave_out)
    for copy in copies:
        copy.wait()


VMEM = pl.BlockSpec(memory_space=pltpu.VMEM)


HBM = pl.BlockSpec(memory_space=pltpu.HBM)


def call(kernel, in_specs, out_shapes, name, cost, scratch=(), out_spec=None):
    return pl.pallas_call(
        kernel,
        in_specs=in_specs,
        out_specs=out_spec or [VMEM] * len(out_shapes),
        out_shape=out_shapes,
        scratch_shapes=list(scratch),
        name=name,
        cost_estimate=pl.CostEstimate(flops=cost, bytes_accessed=800000, transcendentals=0),
        compiler_params=pltpu.CompilerParams(vmem_limit_bytes=24 * 1024 * 1024),
    )


def local(counts, les, wave, mean, projection, owner, slot):
    shape = les.shape[1:]
    faces = face_shapes(counts, 9)
    n_faces = len(faces)
    like = lambda n: jax.ShapeDtypeStruct((n,) + shape, f32)

    table = derivative_matrix()
    deriv = jnp.asarray(table, f32)
    along_z = np.kron(np.eye(16), table.T).astype(np.float32)
    high = along_z.astype(jnp.bfloat16)
    low = (along_z - high.astype(np.float32)).astype(jnp.bfloat16)
    tables = (deriv, jnp.asarray(high), jnp.asarray(low))

    in_hbm = lambda *arrays: [pltpu.with_memory_space_constraint(a, pltpu.HBM) for a in arrays]
    les, wave, *sent = call(
        functools.partial(load_kernel, counts),
        [HBM] * 2,
        [like(5), like(4)] + faces,
        "load_and_faces",
        100000,
        [pltpu.SemaphoreType.DMA((2,))],
    )(*in_hbm(les, wave))
    got = exchange(sent, counts)

    sets = partners(counts[0])
    n_plans = 4 * ((len(sets) + 3) // 4)
    small = (owner, slot, projection)
    order, marks, along_x, along_y, tile, *turning = call(
        functools.partial(plan_kernel, counts),
        [HBM] * 3 + [VMEM],
        [
            jax.ShapeDtypeStruct((n_plans, 8, 128), jnp.int32),
            jax.ShapeDtypeStruct((len(sets), 8, 128), f32),
            jax.ShapeDtypeStruct((64, 8, 128), f32),
            jax.ShapeDtypeStruct((8, 8, 128), f32),
            jax.ShapeDtypeStruct((2, 8, 128), f32),
            like(3),
            like(3),
        ],
        "plan_and_vorticity",
        1000000,
        [pltpu.VMEM(a.shape, a.dtype) for a in small] + [pltpu.SemaphoreType.DMA((3,))],
    )(*in_hbm(*small), les)
    pieces = call(
        functools.partial(lamb_kernel, counts, n_faces),
        [VMEM] * (6 + n_faces),
        [jax.ShapeDtypeStruct((7, 8, 128), f32)] * len(sets),
        "lamb_blocks",
        10000000,
    )(order, marks, along_x, along_y, *turning, *got)
    moved = []
    for k in sending_sets(len(sets)):
        still = all(i == j for i, j in sets[k])
        moved.append(pieces[k] if still else lax.ppermute(pieces[k], "gx", sets[k]))
    section, rate, *section_faces = call(
        functools.partial(first_kernel, counts, n_faces),
        [VMEM] * (6 + n_faces),
        [like(5), like(4)] + face_shapes(counts, 5),
        "first_rates",
        40000000,
    )(*tables, les, wave, mean, *got)

    source, middle, carry, *sent = call(
        functools.partial(source_kernel, counts, n_faces),
        [VMEM] * (3 + len(moved) + n_faces),
        [like(3), like(4), like(4)] + faces,
        "source_and_faces",
        10000000,
    )(tile, wave, rate, *moved, *section_faces)
    got = exchange(sent, counts)
    les_base, wave_base, mean_faces, source_out = call(
        inner_kernel,
        [VMEM] * 9,
        [like(5), like(4), jax.ShapeDtypeStruct((6, 3, 8, 128), f32), like(3)],
        "second_rates_inner",
        40000000,
        [pltpu.SemaphoreType.DMA],
        out_spec=[VMEM, VMEM, VMEM, HBM],
    )(*tables, les, section, middle, carry, mean, source)
    les_next, wave_next = call(
        functools.partial(last_kernel, counts, n_faces),
        [VMEM] * (3 + n_faces),
        [like(5), like(4)],
        "second_rates_outer",
        4000000,
        [
            pltpu.VMEM(les.shape, f32),
            pltpu.VMEM(wave.shape, f32),
            pltpu.SemaphoreType.DMA((2,)),
        ],
        out_spec=[HBM, HBM],
    )(les_base, wave_base, mean_faces, *got)
    return les_next, source_out, wave_next


def solution(mesh):
    counts = tuple(mesh.shape[axis] for axis in axes)
    field = P(None, *axes)
    return jax.shard_map(
        functools.partial(local, counts),
        mesh=mesh,
        in_specs=(field, field, field, P(), P(*axes), P(*axes)),
        out_specs=(field, field, field),
        check_vma=False,
    )
```

```python
import functools

import jax
import jax.numpy as jnp
import numpy as np
from jax import lax
from jax.experimental import pallas as pl
from jax.experimental.pallas import tpu as pltpu
from jax.sharding import PartitionSpec as P

lobatto_points = np.array(
    [
        -1.0,
        -0.8717401485096066,
        -0.5917001814331423,
        -0.2092992179024789,
        0.2092992179024789,
        0.5917001814331423,
        0.8717401485096066,
        1.0,
    ]
)
flux_half = 0.08
gamma_less = 0.4
acoustic_step = 0.01
upwind_speed = 1.5
face_lift = 28.0
free_stream = (1.0, 0.0, 0.0, 0.0, 2.5)
axes = ("gx", "gy", "gz")
window = 4
f32 = jnp.float32


def derivative_matrix():
    points = lobatto_points
    products = [np.prod([points[i] - points[j] for j in range(8) if j != i]) for i in range(8)]
    matrix = np.zeros((8, 8))
    for i in range(8):
        for j in range(8):
            if j != i:
                matrix[i, j] = products[i] / (products[j] * (points[i] - points[j]))
        matrix[i, i] = -np.sum(matrix[i])
    return matrix


def sublane(shape):
    return lax.broadcasted_iota(jnp.int32, shape, len(shape) - 2)


def lane(shape):
    return lax.broadcasted_iota(jnp.int32, shape, len(shape) - 1)


def rolled(tile, amount, axis):
    amount = amount % tile.shape[axis]
    return pltpu.roll(tile, amount, axis) if amount else tile


def shifted(field, axis, step, outer=None):
    if axis == 0:
        outer = jnp.zeros((8, 128), f32) if outer is None else outer
        if step == 1:
            return jnp.concatenate([field[1:], outer[None]], axis=0)
        return jnp.concatenate([outer[None], field[:-1]], axis=0)
    count = (8, 128)[axis - 1]
    edge = count - 1 if step == 1 else 0
    at_edge = (sublane if axis == 1 else lane)((8, 128)) == edge
    planes = []
    for x in range(8):
        layer = 0.0 if outer is None else rolled(outer, edge - axis * x, axis - 1)
        planes.append(jnp.where(at_edge, layer, rolled(field[x], -step, axis - 1)))
    return jnp.stack(planes, axis=0)


def fluid(state):
    density, mx, my, mz, energy = [s + r for s, r in zip(state, free_stream)]
    inverse = 1.0 / density
    momentum = (mx, my, mz)
    velocity = [m * inverse for m in momentum]
    pressure = gamma_less * (
        energy - 0.5 * (mx * velocity[0] + my * velocity[1] + mz * velocity[2])
    )
    return momentum, velocity, pressure, energy + pressure


def split_flux(state, parts, axis, sign):
    momentum, velocity, pressure, enthalpy = parts
    speed = velocity[axis]
    flux = [momentum[axis]]
    for c in range(3):
        term = momentum[c] * speed
        flux.append(term + pressure if c == axis else term)
    flux.append(enthalpy * speed)
    if sign > 0:
        return [flux_half * (s + f) for s, f in zip(state, flux)]
    return [flux_half * (s - f) for s, f in zip(state, flux)]


def les_rate(state, halos):
    parts = fluid(state)
    total = [-6.0 * flux_half * s for s in state]
    for axis in range(3):
        ahead = split_flux(state, parts, axis, -1)
        behind = split_flux(state, parts, axis, 1)
        ahead_outer = behind_outer = [None] * 5
        if halos is not None:
            before, after = halos[axis]
            ahead_outer = split_flux(after, fluid(after), axis, -1)
            behind_outer = split_flux(before, fluid(before), axis, 1)
        for c in range(5):
            total[c] = total[c] + (
                shifted(ahead[c], axis, 1, ahead_outer[c])
                + shifted(behind[c], axis, -1, behind_outer[c])
            )
    return total


def les_outer(halos):
    return [
        (
            split_flux(before, fluid(before), axis, 1),
            split_flux(after, fluid(after), axis, -1),
        )
        for axis, (before, after) in enumerate(halos)
    ]


def with_layers(field, layers):
    row, column = sublane((8, 128)), lane((8, 128))
    along_z = layers[2]
    if along_z is not None:
        along_z = jnp.where(lax.rem(column, 2) == 0, along_z[0], rolled(along_z[1], -1, 1))
    planes = []
    for x in range(8):
        plane = field[x]
        if layers[0] is not None and x in (0, 7):
            plane = plane + layers[0][x // 7]
        if layers[1] is not None:
            low, high = layers[1]
            plane = plane + jnp.where(
                row == 0, rolled(low, -x, 0), jnp.where(row == 7, rolled(high, 7 - x, 0), 0.0)
            )
        if along_z is not None:
            ends = (column == 0) | (column == 127)
            plane = plane + jnp.where(ends, rolled(along_z, -2 * x, 1), 0.0)
        planes.append(plane)
    return planes


def wave_flux(state, mean, axis):
    speed = mean[axis]
    pressure = state[0]
    rows = [speed * pressure + state[1 + axis]]
    for c in range(3):
        term = speed * state[1 + c]
        rows.append(term + pressure if c == axis else term)
    return rows


def dot3(left, right):
    high = left.astype(jnp.bfloat16)
    low = (left - high.astype(f32)).astype(jnp.bfloat16)
    dot = functools.partial(jnp.dot, preferred_element_type=f32)
    return dot(high, right[0]) + (dot(low, right[0]) + dot(high, right[1]))


def acoustic_rate(state, mean, halos, deriv, along_z):
    shape = state[0].shape
    table = derivative_matrix()
    flux = wave_flux(state, mean, 0)
    if halos is None:
        halos = [([jnp.zeros((8, 128), f32)] * 4,) * 2] + [([None] * 4,) * 2] * 2
    before, after = halos[0]
    low_mean, high_mean = [m[0] for m in mean], [m[7] for m in mean]
    low_jump = [b - s[0] for b, s in zip(before, state)]
    high_jump = [a - s[7] for a, s in zip(after, state)]
    low_flux = wave_flux(low_jump, low_mean, 0)
    high_flux = wave_flux(high_jump, high_mean, 0)
    half, lift = 0.5 * face_lift, 0.5 * face_lift * upwind_speed
    total = []
    for c in range(4):
        planes = []
        for i in range(8):
            plane = -float(table[i, 0]) * flux[c][0]
            for a in range(1, 8):
                if abs(table[i, a]) > 1e-12:
                    plane = plane - float(table[i, a]) * flux[c][a]
            if i == 0:
                plane = plane + (half * low_flux[c] + lift * low_jump[c])
            if i == 7:
                plane = plane - (half * high_flux[c] - lift * high_jump[c])
            planes.append(plane)
        total.append(jnp.stack(planes, axis=0))
    flux = wave_flux(state, mean, 1)
    before, after = halos[1]
    row = sublane(shape)
    sign = jnp.where(row == 0, half, jnp.where(row == 7, -half, 0.0))
    jump = []
    for s, b, a in zip(state, before, after):
        planes = []
        for x in range(8):
            low = 0.0 if b is None else rolled(b, -x, 0)
            high = 0.0 if a is None else rolled(a, 7 - x, 0)
            planes.append(jnp.where(row[x] == 0, low, jnp.where(row[x] == 7, high, s[x])) - s[x])
        jump.append(jnp.stack(planes, axis=0))
    jump_flux = wave_flux(jump, mean, 1)
    for c in range(4):
        change = lift * jump[c] + sign * jump_flux[c]
        for b in range(8):
            change = change - deriv[:, b : b + 1][None] * flux[c][:, b : b + 1, :]
        total[c] = total[c] + change
    flux = wave_flux(state, mean, 2)
    before, after = halos[2]
    column = lane(shape)
    place = lax.rem(column, 8)
    sign = jnp.where(place == 0, half, jnp.where(place == 7, -half, 0.0))
    jump = [
        jnp.where(
            place == 0,
            shifted(s, 2, -1, b),
            jnp.where(place == 7, shifted(s, 2, 1, a), s),
        )
        - s
        for s, b, a in zip(state, before, after)
    ]
    jump_flux = wave_flux(jump, mean, 2)
    for c in range(4):
        slope = dot3(flux[c].reshape(64, 128), along_z).reshape(shape)
        total[c] = total[c] + (lift * jump[c] + sign * jump_flux[c] - slope)
    return total


def mean_layers(mean):
    return [
        [m[0] for m in mean],
        [m[7] for m in mean],
        [m[:, 0, :] for m in mean],
        [m[:, 7, :] for m in mean],
        [z_layer(m, jnp.int32(0)) for m in mean],
        [z_layer(m, jnp.int32(127)) for m in mean],
    ]


def acoustic_outer(mean_faces, halos):
    half, lift = 0.5 * face_lift, 0.5 * face_lift * upwind_speed
    layers = []
    for axis, (before, after) in enumerate(halos):
        low_flux = wave_flux(before, mean_faces[2 * axis], axis)
        high_flux = wave_flux(after, mean_faces[2 * axis + 1], axis)
        layers.append(
            (
                [half * f + lift * b for f, b in zip(low_flux, before)],
                [lift * a - half * f for f, a in zip(high_flux, after)],
            )
        )
    return layers


def tile_rows(matrix):
    spread = (lax.rem(lane((8, 128)), 8) == sublane((8, 128))).astype(f32)
    return jnp.dot(
        matrix, spread, precision=lax.Precision.HIGHEST, preferred_element_type=f32
    )


def pairings(count):
    sets = []
    for first in (0, 1):
        pairs = [(i, i + 1) for i in range(first, count - 1, 2)]
        if pairs:
            sets.append(pairs)
    return sets


def slots(counts):
    found = [(axis, n) for axis in range(3) for n in range(len(pairings(counts[axis])))]
    lower = ((2, 1), (2, 0), (0, 1), (1, 0), (1, 1), (0, 0))
    upper = ((2, 1), (0, 1), (2, 0), (0, 0), (1, 1), (1, 0))
    lower = [swap for swap in lower if swap in found]
    upper = [swap for swap in upper if swap in found] if counts[1] == 4 else lower
    return list(zip(lower, upper))


def in_upper_half(counts):
    return lax.axis_index("gy") >= counts[1] // 2


def routes(counts):
    places = [(x, y, z) for x in range(counts[0]) for y in range(counts[1]) for z in range(counts[2])]
    number = {place: n for n, place in enumerate(places)}

    def partner(place, axis, n):
        pairs = pairings(counts[axis])[n]
        swap = dict(pairs + [(j, i) for i, j in pairs])
        alone = [i for i in range(counts[axis]) if i not in swap]
        spare = 0 if axis else 2
        other = list(place)
        if place[axis] in swap:
            other[axis] = swap[place[axis]]
        elif axis == 0 and len(alone) == 2:
            other[axis] = sum(alone) - place[axis]
        elif counts[spare] % 2 == 0:
            other[spare] = place[spare] ^ 1
        return number[tuple(other)]

    return [
        [
            (number[place], partner(place, *(upper if place[1] >= counts[1] // 2 else lower)))
            for place in places
        ]
        for lower, upper in slots(counts)
    ]


def z_layer(field, at):
    packed = jnp.zeros((8, 128), f32)
    column = lane((8, 128))
    for x in range(8):
        turned = pltpu.roll(field[x], lax.rem(2 * x - at + 128, 128), 1)
        packed = jnp.where(column == 2 * x, turned, packed)
    return packed


def store_faces(source_ref, out_refs, counts, first=0):
    high_half = in_upper_half(counts)

    def store(c, carry):
        field = source_ref[c]
        faces = {}
        for axis in range(3):
            even = lax.rem(lax.axis_index(axes[axis]), 2) == 0
            if axis == 0:
                low, high = field[0], field[7]
            elif axis == 1:
                low, high = field[:, 0, :], field[:, 7, :]
            for n in range(len(pairings(counts[axis]))):
                last = even == (n == 0)
                if axis == 2:
                    faces[axis, n] = z_layer(field, jnp.where(last, 127, 0))
                else:
                    faces[axis, n] = jnp.where(last, high, low)
        for ref, (lower, upper) in zip(out_refs, slots(counts)):
            if lower == upper:
                ref[first + c] = faces[lower]
            else:
                ref[first + c] = jnp.where(high_half, faces[upper], faces[lower])
        return carry

    lax.fori_loop(0, source_ref.shape[0], store, 0)


def load_faces(in_refs, counts, first, last):
    high_half = in_upper_half(counts)
    lower, upper = zip(*slots(counts))
    halos = []
    for axis in range(3):
        place = lax.axis_index(axes[axis])
        even = lax.rem(place, 2) == 0
        got = []
        for n in range(len(pairings(counts[axis]))):
            a, b = in_refs[lower.index((axis, n))], in_refs[upper.index((axis, n))]
            got.append(
                [a[c] if a is b else jnp.where(high_half, b[c], a[c]) for c in range(first, last)]
            )
        while len(got) < 2:
            got.append([jnp.zeros((8, 128), f32)] * (last - first))
        before = [jnp.where(place == 0, 0.0, jnp.where(even, b, a)) for a, b in zip(*got)]
        after = [
            jnp.where(place == counts[axis] - 1, 0.0, jnp.where(even, a, b))
            for a, b in zip(*got)
        ]
        halos.append((before, after))
    return halos


def face_shapes(counts, width):
    total = sum(len(pairings(count)) for count in counts)
    return [jax.ShapeDtypeStruct((width, 8, 128), f32)] * total


def exchange(faces, counts):
    return [lax.ppermute(face, axes, way) for face, way in zip(faces, routes(counts))]


def read_all(ref):
    return [ref[c] for c in range(ref.shape[0])]


def load_kernel(counts, *refs):
    sources, targets, out_refs, sems = refs[:5], refs[5:10], refs[10:-1], refs[-1]
    copies = [
        pltpu.make_async_copy(source, target, sems.at[n])
        for n, (source, target) in enumerate(zip(sources, targets))
    ]
    for copy in copies:
        copy.start()
    for copy, target, first in zip(copies, targets, (0, 5)):
        copy.wait()
        store_faces(target, out_refs, counts, first)
    for copy in copies[2:]:
        copy.wait()


def partners(count):
    if count == window:
        return [[(i, i ^ mask) for i in range(count)] for mask in range(count)]
    turns = sorted({d % count for d in range(1 - window, window)})
    return [[(i, (i + turn) % count) for i in range(count)] for turn in turns]


def sending_sets(count):
    return [3, 2, 1, 0] if count == window else list(range(count))


def plan_kernel(
    counts, owner_ref, slot_ref, proj_ref, order_ref, marks_ref, along_x_ref, along_y_ref, tile_ref
):
    count = counts[0]
    n_sets = len(partners(count))
    own = lax.axis_index("gx")
    n_blocks = owner_ref.shape[-1]
    square = (n_blocks, n_blocks)
    block, other = sublane(square), lane(square)

    def spread(ref):
        by_lane = jnp.broadcast_to(ref[0], square)
        here = jnp.where(block == other, by_lane, 0).astype(f32)
        return by_lane, jnp.sum(here, axis=1, keepdims=True).astype(jnp.int32)

    def group_of(owner):
        if count == window:
            return lax.bitwise_xor(owner, own)
        turn = lax.rem(owner - own + count, count)
        if n_sets == count:
            return turn
        return jnp.where(turn < window, turn, turn - (count - n_sets))

    owner_by_lane, owner = spread(owner_ref)
    slot = spread(slot_ref)[1]
    group = group_of(owner)
    before = (group_of(owner_by_lane) == group) & (other < block)
    taken = jnp.sum(before.astype(f32), axis=1, keepdims=True).astype(jnp.int32)
    wide = (n_blocks, 128)
    place = jnp.broadcast_to(group * window + taken, wide)
    column = lane((8, 128))
    quarter = column // 32
    for s in range((n_sets + 3) // 4):
        here = place - 16 * s == lane(wide) // 8
        label = jnp.sum(jnp.where(here, (slot + 1).astype(f32), 0.0), axis=0, keepdims=True) - 1.0
        source = jnp.sum(
            jnp.where(here, (8 * sublane(wide)).astype(f32), 0.0), axis=0, keepdims=True
        )
        labels = jnp.broadcast_to(label, (8, 128))
        order = jnp.broadcast_to(source, (8, 128)).astype(jnp.int32) + lax.rem(column, 8)
        for t in range(4):
            order_ref[4 * s + t] = rolled(order, 32 * t, 1)
        for r in range(min(4, n_sets - 4 * s)):
            marks = labels
            for t in range(1, 4):
                marks = jnp.where(quarter == (r + t) % 4, rolled(labels, 32 * t, 1), marks)
            marks_ref[4 * s + r] = marks
    proj = proj_ref[...]
    for a in range(8):
        along_y = jnp.broadcast_to(proj[:, a : a + 1], (8, 128))
        along_y_ref[a] = along_y
        for i in range(8):
            along_x_ref[8 * i + a] = jnp.broadcast_to(along_y[i : i + 1], (8, 128))
    tile = tile_rows(proj)
    high = tile.astype(jnp.bfloat16).astype(f32)
    tile_ref[0] = high
    tile_ref[1] = tile - high


def speeds(state):
    inverse = 1.0 / (state[0] + 1.0)
    return [state[c] * inverse for c in (1, 2, 3)]


def vorticity_kernel(les_ref, velocity_ref, vort_ref):
    velocity = speeds([les_ref[c] for c in range(4)])

    def slope(c, axis):
        return shifted(velocity[c], axis, 1) - shifted(velocity[c], axis, -1)

    vort = [slope(2, 1) - slope(1, 2), slope(0, 2) - slope(2, 0), slope(1, 0) - slope(0, 1)]
    for c in range(3):
        velocity_ref[c] = velocity[c]
        vort_ref[c] = vort[c]


def lamb_kernel(
    counts, n_faces, order_ref, marks_ref, along_x_ref, along_y_ref, velocity_ref, vort_ref, *refs
):
    face_refs, out_refs, lamb_ref = refs[:n_faces], refs[n_faces:-1], refs[-1]
    outer = [
        (speeds(before), speeds(after)) for before, after in load_faces(face_refs, counts, 0, 4)
    ]

    def rise(c, axis):
        return -outer[axis][0][c], outer[axis][1][c]

    def fall(c, axis):
        return outer[axis][0][c], -outer[axis][1][c]

    layers = [
        (None, rise(2, 1), fall(1, 2)),
        (fall(2, 0), None, rise(0, 2)),
        (rise(1, 0), fall(0, 1), None),
    ]
    vort = [0.5 * jnp.stack(with_layers(vort_ref[c], layers[c]), axis=0) for c in range(3)]
    velocity = read_all(velocity_ref)
    lamb = [
        vort[1] * velocity[2] - vort[2] * velocity[1],
        vort[2] * velocity[0] - vort[0] * velocity[2],
        vort[0] * velocity[1] - vort[1] * velocity[0],
    ]
    for c in range(3):
        lamb_ref[c] = lamb[c]
    quarter = lane((8, 128)) // 32

    def project(c, carry):
        field = lamb_ref[c]
        along_y = along_y_ref[0][None] * field[:, 0:1, :]
        for b in range(1, 8):
            along_y = along_y + along_y_ref[b][None] * field[:, b : b + 1, :]
        blocks = []
        for i in range(8):
            plane = along_x_ref[8 * i] * along_y[0]
            for a in range(1, 8):
                plane = plane + along_x_ref[8 * i + a] * along_y[a]
            blocks.append(plane)
        for s in range((len(out_refs) + 3) // 4):
            ordered = [
                jnp.take_along_axis(block, order_ref[4 * s + i % 4], axis=1)
                for i, block in enumerate(blocks)
            ]
            for r in range(min(4, len(out_refs) - 4 * s)):
                for q in range(2):
                    packed = ordered[4 * q]
                    for t in range(1, 4):
                        packed = jnp.where(quarter == (r + t) % 4, ordered[4 * q + t], packed)
                    out_refs[4 * s + r][2 * c + q] = packed
        return carry

    lax.fori_loop(0, 3, project, 0)
    for out, marks in zip(out_refs, read_all(marks_ref)):
        out[6] = marks


def first_kernel(
    counts, n_faces, deriv_ref, high_ref, low_ref, les_ref, wave_ref, mean_ref, *refs
):
    face_refs, (section_ref, rate_ref), out_refs = (
        refs[:n_faces], refs[n_faces : n_faces + 2], refs[n_faces + 2 :],
    )
    state = read_all(les_ref)
    rate = les_rate(state, load_faces(face_refs, counts, 0, 5))
    section = [s + r for s, r in zip(state, rate)]
    for c in range(5):
        section_ref[c] = section[c]
    store_faces(section_ref, out_refs, counts)
    rate = acoustic_rate(
        read_all(wave_ref), read_all(mean_ref), load_faces(face_refs, counts, 5, 9),
        deriv_ref[...], (high_ref[...], low_ref[...]),
    )
    for c in range(4):
        rate_ref[c] = rate[c]


def source_kernel(counts, n_faces, tile_ref, wave_ref, rate_ref, *refs):
    n_pieces = len(partners(counts[0]))
    pieces = [None] * n_pieces
    for ref, k in zip(refs, sending_sets(n_pieces)):
        pieces[k] = ref
    refs = refs[n_pieces:]
    section_faces, (source_ref, middle_ref, carry_ref), face_refs = (
        refs[:n_faces], refs[n_faces : n_faces + 3], refs[n_faces + 3 :],
    )
    quarter = lane((8, 128)) // 32
    tile_high, tile_low = tile_ref[0], tile_ref[1]
    total = None
    for s in range((n_pieces + 3) // 4):
        count = min(4, n_pieces - 4 * s)

        def gathered(q, t):
            value = jnp.full((8, 128), -1.0 if q == 6 else 0.0, f32)
            for r in range(count):
                value = jnp.where(quarter == (r + t) % 4, pieces[4 * s + r][q], value)
            return value

        here = [gathered(6, 0).astype(jnp.int32) == slot for slot in range(16)]
        chosen_high, chosen_low = [
            jnp.concatenate([jnp.where(h, part, 0.0) for h in here], axis=0).astype(jnp.bfloat16)
            for part in (tile_high, tile_low)
        ]
        data = []
        for k in range(24):
            piece = gathered(k // 4, k % 4)
            data.append(pltpu.roll(piece, 128 - 32 * (k % 4), 1) if k % 4 else piece)
        data = jnp.concatenate(data, axis=0)
        high = data.astype(jnp.bfloat16)
        low = (data - high.astype(f32)).astype(jnp.bfloat16)
        dot = functools.partial(
            lax.dot_general,
            dimension_numbers=(((1,), (1,)), ((), ())),
            preferred_element_type=f32,
        )
        moved = dot(high, chosen_high) + (dot(low, chosen_high) + dot(high, chosen_low))
        total = moved if total is None else total + moved
    source = [total[64 * c : 64 * c + 64].reshape(8, 8, 128) for c in range(3)]
    middle = []
    for c in range(4):
        rate = rate_ref[c]
        if c:
            source_ref[c - 1] = source[c - 1]
            rate = rate + source[c - 1]
        middle.append(wave_ref[c] + acoustic_step * rate)
        middle_ref[c] = middle[c]
        carry = wave_ref[c] + middle[c]
        carry_ref[c] = carry + acoustic_step * source[c - 1] if c else carry
    for ready, face in zip(section_faces, face_refs):
        face[0:5] = ready[...]
    store_faces(middle_ref, face_refs, counts, 5)


def inner_kernel(
    deriv_ref, high_ref, low_ref, les_ref, section_ref, middle_ref, carry_ref, mean_ref, source_ref,
    les_base_ref, wave_base_ref, mean_faces_ref, source_out, sem,
):
    copy = pltpu.make_async_copy(source_ref, source_out, sem)
    copy.start()
    section = read_all(section_ref)
    rate = les_rate(section, None)
    for c in range(5):
        les_base_ref[c] = 0.5 * ((les_ref[c] + section[c]) + rate[c])
    mean = read_all(mean_ref)
    for n, face in enumerate(mean_layers(mean)):
        for c in range(3):
            mean_faces_ref[n, c] = face[c]
    rate = acoustic_rate(
        read_all(middle_ref), mean, None, deriv_ref[...], (high_ref[...], low_ref[...])
    )
    for c in range(4):
        wave_base_ref[c] = 0.5 * (carry_ref[c] + acoustic_step * rate[c])
    copy.wait()


def last_kernel(counts, n_faces, les_base_ref, wave_base_ref, mean_faces_ref, *refs):
    face_refs, (les_out, wave_out, les_ref, wave_ref, layers_ref, sems) = (
        refs[:n_faces], refs[n_faces:],
    )
    def stack_layers(layers, first, scale):
        for axis, sides in enumerate(layers):
            for side, parts in enumerate(sides):
                for c, part in enumerate(parts):
                    layers_ref[2 * axis + side, first + c] = scale * part

    def finish(base_ref, out_ref, target, first):
        def one(c, carry):
            part = [
                (layers_ref[2 * axis, first + c], layers_ref[2 * axis + 1, first + c])
                for axis in range(3)
            ]
            for x, plane in enumerate(with_layers(base_ref[c], part)):
                out_ref[c, x] = plane
            return carry

        lax.fori_loop(0, out_ref.shape[0], one, 0)
        copy = pltpu.make_async_copy(out_ref, target, sems.at[0 if first == 0 else 1])
        copy.start()
        return copy

    stack_layers(les_outer(load_faces(face_refs, counts, 0, 5)), 0, 0.5)
    copies = [finish(les_base_ref, les_ref, les_out, 0)]
    mean_faces = [[mean_faces_ref[n, c] for c in range(3)] for n in range(6)]
    layers = acoustic_outer(mean_faces, load_faces(face_refs, counts, 5, 9))
    stack_layers(layers, 5, 0.5 * acoustic_step)
    copies.append(finish(wave_base_ref, wave_ref, wave_out, 5))
    for copy in copies:
        copy.wait()


VMEM = pl.BlockSpec(memory_space=pltpu.VMEM)


HBM = pl.BlockSpec(memory_space=pltpu.HBM)


def call(kernel, in_specs, out_shapes, name, cost, scratch=(), out_spec=None):
    return pl.pallas_call(
        kernel,
        in_specs=in_specs,
        out_specs=out_spec or [VMEM] * len(out_shapes),
        out_shape=out_shapes,
        scratch_shapes=list(scratch),
        name=name,
        cost_estimate=pl.CostEstimate(flops=cost, bytes_accessed=800000, transcendentals=0),
        compiler_params=pltpu.CompilerParams(vmem_limit_bytes=24 * 1024 * 1024),
    )


def local(counts, les, wave, mean, projection, owner, slot):
    shape = les.shape[1:]
    faces = face_shapes(counts, 9)
    n_faces = len(faces)
    like = lambda n: jax.ShapeDtypeStruct((n,) + shape, f32)

    table = derivative_matrix()
    deriv = jnp.asarray(table, f32)
    along_z = np.kron(np.eye(16), table.T).astype(np.float32)
    high = along_z.astype(jnp.bfloat16)
    low = (along_z - high.astype(np.float32)).astype(jnp.bfloat16)
    tables = (deriv, jnp.asarray(high), jnp.asarray(low))

    arguments = (les, wave, owner, slot, projection)
    les, wave, owner, slot, projection, *sent = call(
        functools.partial(load_kernel, counts),
        [HBM] * 5,
        [jax.ShapeDtypeStruct(a.shape, a.dtype) for a in arguments] + faces,
        "load_and_faces",
        100000,
        [pltpu.SemaphoreType.DMA((5,))],
    )(*(pltpu.with_memory_space_constraint(a, pltpu.HBM) for a in arguments))
    got = exchange(sent, counts)

    sets = partners(counts[0])
    n_plans = 4 * ((len(sets) + 3) // 4)
    order, marks, along_x, along_y, tile = call(
        functools.partial(plan_kernel, counts),
        [VMEM] * 3,
        [
            jax.ShapeDtypeStruct((n_plans, 8, 128), jnp.int32),
            jax.ShapeDtypeStruct((len(sets), 8, 128), f32),
            jax.ShapeDtypeStruct((64, 8, 128), f32),
            jax.ShapeDtypeStruct((8, 8, 128), f32),
            jax.ShapeDtypeStruct((2, 8, 128), f32),
        ],
        "plan",
        1000000,
    )(owner, slot, projection)
    turning = call(vorticity_kernel, [VMEM], [like(3)] * 2, "vorticity", 1000000)(les)
    pieces = call(
        functools.partial(lamb_kernel, counts, n_faces),
        [VMEM] * (6 + n_faces),
        [jax.ShapeDtypeStruct((7, 8, 128), f32)] * len(sets),
        "lamb_blocks",
        10000000,
        [pltpu.VMEM((3,) + shape, f32)],
    )(order, marks, along_x, along_y, *turning, *got)
    moved = []
    for k in sending_sets(len(sets)):
        still = all(i == j for i, j in sets[k])
        moved.append(pieces[k] if still else lax.ppermute(pieces[k], "gx", sets[k]))
    section, rate, *section_faces = call(
        functools.partial(first_kernel, counts, n_faces),
        [VMEM] * (6 + n_faces),
        [like(5), like(4)] + face_shapes(counts, 5),
        "first_rates",
        40000000,
    )(*tables, les, wave, mean, *got)

    source, middle, carry, *sent = call(
        functools.partial(source_kernel, counts, n_faces),
        [VMEM] * (3 + len(moved) + n_faces),
        [like(3), like(4), like(4)] + faces,
        "source_and_faces",
        10000000,
    )(tile, wave, rate, *moved, *section_faces)
    got = exchange(sent, counts)
    les_base, wave_base, mean_faces, source_out = call(
        inner_kernel,
        [VMEM] * 9,
        [like(5), like(4), jax.ShapeDtypeStruct((6, 3, 8, 128), f32), like(3)],
        "second_rates_inner",
        40000000,
        [pltpu.SemaphoreType.DMA],
        out_spec=[VMEM, VMEM, VMEM, HBM],
    )(*tables, les, section, middle, carry, mean, source)
    les_next, wave_next = call(
        functools.partial(last_kernel, counts, n_faces),
        [VMEM] * (3 + n_faces),
        [like(5), like(4)],
        "second_rates_outer",
        4000000,
        [
            pltpu.VMEM(les.shape, f32),
            pltpu.VMEM(wave.shape, f32),
            pltpu.VMEM((6, 9, 8, 128), f32),
            pltpu.SemaphoreType.DMA((2,)),
        ],
        out_spec=[HBM, HBM],
    )(les_base, wave_base, mean_faces, *got)
    return les_next, source_out, wave_next


def solution(mesh):
    counts = tuple(mesh.shape[axis] for axis in axes)
    field = P(None, *axes)
    return jax.shard_map(
        functools.partial(local, counts),
        mesh=mesh,
        in_specs=(field, field, field, P(), P(*axes), P(*axes)),
        out_specs=(field, field, field),
        check_vma=False,
    )
```

```python
import functools

import jax
import jax.numpy as jnp
import numpy as np
from jax import lax
from jax.experimental import pallas as pl
from jax.experimental.pallas import tpu as pltpu
from jax.sharding import PartitionSpec as P

lobatto_points = np.array(
    [
        -1.0,
        -0.8717401485096066,
        -0.5917001814331423,
        -0.2092992179024789,
        0.2092992179024789,
        0.5917001814331423,
        0.8717401485096066,
        1.0,
    ]
)
flux_half = 0.08
gamma_less = 0.4
acoustic_step = 0.01
upwind_speed = 1.5
face_lift = 28.0
free_stream = (1.0, 0.0, 0.0, 0.0, 2.5)
axes = ("gx", "gy", "gz")
window = 4
f32 = jnp.float32


def derivative_matrix():
    points = lobatto_points
    products = [np.prod([points[i] - points[j] for j in range(8) if j != i]) for i in range(8)]
    matrix = np.zeros((8, 8))
    for i in range(8):
        for j in range(8):
            if j != i:
                matrix[i, j] = products[i] / (products[j] * (points[i] - points[j]))
        matrix[i, i] = -np.sum(matrix[i])
    return matrix


def sublane(shape):
    return lax.broadcasted_iota(jnp.int32, shape, len(shape) - 2)


def lane(shape):
    return lax.broadcasted_iota(jnp.int32, shape, len(shape) - 1)


def rolled(tile, amount, axis):
    amount = amount % tile.shape[axis]
    return pltpu.roll(tile, amount, axis) if amount else tile


def shifted(field, axis, step, outer=None):
    if axis == 0:
        outer = jnp.zeros((8, 128), f32) if outer is None else outer
        if step == 1:
            return jnp.concatenate([field[1:], outer[None]], axis=0)
        return jnp.concatenate([outer[None], field[:-1]], axis=0)
    count = (8, 128)[axis - 1]
    edge = count - 1 if step == 1 else 0
    at_edge = (sublane if axis == 1 else lane)((8, 128)) == edge
    planes = []
    for x in range(8):
        layer = 0.0 if outer is None else rolled(outer, edge - axis * x, axis - 1)
        planes.append(jnp.where(at_edge, layer, rolled(field[x], -step, axis - 1)))
    return jnp.stack(planes, axis=0)


def fluid(state):
    density, mx, my, mz, energy = [s + r for s, r in zip(state, free_stream)]
    inverse = 1.0 / density
    momentum = (mx, my, mz)
    velocity = [m * inverse for m in momentum]
    pressure = gamma_less * (
        energy - 0.5 * (mx * velocity[0] + my * velocity[1] + mz * velocity[2])
    )
    return momentum, velocity, pressure, energy + pressure


def split_flux(state, parts, axis, sign):
    momentum, velocity, pressure, enthalpy = parts
    speed = velocity[axis]
    flux = [momentum[axis]]
    for c in range(3):
        term = momentum[c] * speed
        flux.append(term + pressure if c == axis else term)
    flux.append(enthalpy * speed)
    if sign > 0:
        return [flux_half * (s + f) for s, f in zip(state, flux)]
    return [flux_half * (s - f) for s, f in zip(state, flux)]


def les_rate(state, halos):
    parts = fluid(state)
    total = [-6.0 * flux_half * s for s in state]
    for axis in range(3):
        ahead = split_flux(state, parts, axis, -1)
        behind = split_flux(state, parts, axis, 1)
        ahead_outer = behind_outer = [None] * 5
        if halos is not None:
            before, after = halos[axis]
            ahead_outer = split_flux(after, fluid(after), axis, -1)
            behind_outer = split_flux(before, fluid(before), axis, 1)
        for c in range(5):
            total[c] = total[c] + (
                shifted(ahead[c], axis, 1, ahead_outer[c])
                + shifted(behind[c], axis, -1, behind_outer[c])
            )
    return total


def les_outer(halos):
    return [
        halo
        and (
            split_flux(halo[0], fluid(halo[0]), axis, 1),
            split_flux(halo[1], fluid(halo[1]), axis, -1),
        )
        for axis, halo in enumerate(halos)
    ]


def with_layers(field, layers):
    row, column = sublane((8, 128)), lane((8, 128))
    along_z = layers[2]
    if along_z is not None:
        along_z = jnp.where(lax.rem(column, 2) == 0, along_z[0], rolled(along_z[1], -1, 1))
    planes = []
    for x in range(8):
        plane = field[x]
        if layers[0] is not None and x in (0, 7):
            plane = plane + layers[0][x // 7]
        if layers[1] is not None:
            low, high = layers[1]
            plane = plane + jnp.where(
                row == 0, rolled(low, -x, 0), jnp.where(row == 7, rolled(high, 7 - x, 0), 0.0)
            )
        if along_z is not None:
            ends = (column == 0) | (column == 127)
            plane = plane + jnp.where(ends, rolled(along_z, -2 * x, 1), 0.0)
        planes.append(plane)
    return planes


def wave_flux(state, mean, axis):
    speed = mean[axis]
    pressure = state[0]
    rows = [speed * pressure + state[1 + axis]]
    for c in range(3):
        term = speed * state[1 + c]
        rows.append(term + pressure if c == axis else term)
    return rows


def dot3(left, right):
    high = left.astype(jnp.bfloat16)
    low = (left - high.astype(f32)).astype(jnp.bfloat16)
    dot = functools.partial(jnp.dot, preferred_element_type=f32)
    return dot(high, right[0]) + (dot(low, right[0]) + dot(high, right[1]))


def acoustic_rate(state, mean, halos, deriv, along_z):
    shape = state[0].shape
    table = derivative_matrix()
    flux = wave_flux(state, mean, 0)
    if halos is None:
        halos = [([jnp.zeros((8, 128), f32)] * 4,) * 2] + [([None] * 4,) * 2] * 2
    before, after = halos[0]
    low_mean, high_mean = [m[0] for m in mean], [m[7] for m in mean]
    low_jump = [b - s[0] for b, s in zip(before, state)]
    high_jump = [a - s[7] for a, s in zip(after, state)]
    low_flux = wave_flux(low_jump, low_mean, 0)
    high_flux = wave_flux(high_jump, high_mean, 0)
    half, lift = 0.5 * face_lift, 0.5 * face_lift * upwind_speed
    total = []
    for c in range(4):
        planes = []
        for i in range(8):
            plane = -float(table[i, 0]) * flux[c][0]
            for a in range(1, 8):
                if abs(table[i, a]) > 1e-12:
                    plane = plane - float(table[i, a]) * flux[c][a]
            if i == 0:
                plane = plane + (half * low_flux[c] + lift * low_jump[c])
            if i == 7:
                plane = plane - (half * high_flux[c] - lift * high_jump[c])
            planes.append(plane)
        total.append(jnp.stack(planes, axis=0))
    flux = wave_flux(state, mean, 1)
    before, after = halos[1]
    row = sublane(shape)
    sign = jnp.where(row == 0, half, jnp.where(row == 7, -half, 0.0))
    jump = []
    for s, b, a in zip(state, before, after):
        planes = []
        for x in range(8):
            low = 0.0 if b is None else rolled(b, -x, 0)
            high = 0.0 if a is None else rolled(a, 7 - x, 0)
            planes.append(jnp.where(row[x] == 0, low, jnp.where(row[x] == 7, high, s[x])) - s[x])
        jump.append(jnp.stack(planes, axis=0))
    jump_flux = wave_flux(jump, mean, 1)
    for c in range(4):
        change = lift * jump[c] + sign * jump_flux[c]
        for b in range(8):
            change = change - deriv[:, b : b + 1][None] * flux[c][:, b : b + 1, :]
        total[c] = total[c] + change
    flux = wave_flux(state, mean, 2)
    before, after = halos[2]
    column = lane(shape)
    place = lax.rem(column, 8)
    sign = jnp.where(place == 0, half, jnp.where(place == 7, -half, 0.0))
    jump = [
        jnp.where(
            place == 0,
            shifted(s, 2, -1, b),
            jnp.where(place == 7, shifted(s, 2, 1, a), s),
        )
        - s
        for s, b, a in zip(state, before, after)
    ]
    jump_flux = wave_flux(jump, mean, 2)
    for c in range(4):
        slope = dot3(flux[c].reshape(64, 128), along_z).reshape(shape)
        total[c] = total[c] + (lift * jump[c] + sign * jump_flux[c] - slope)
    return total


def mean_layers(mean):
    return [
        [m[0] for m in mean],
        [m[7] for m in mean],
        [m[:, 0, :] for m in mean],
        [m[:, 7, :] for m in mean],
        [z_layer(m, jnp.int32(0)) for m in mean],
        [z_layer(m, jnp.int32(127)) for m in mean],
    ]


def acoustic_outer(mean_faces, halos):
    half, lift = 0.5 * face_lift, 0.5 * face_lift * upwind_speed
    layers = []
    for axis, halo in enumerate(halos):
        if halo is None:
            layers.append(None)
            continue
        before, after = halo
        low_flux = wave_flux(before, mean_faces[2 * axis], axis)
        high_flux = wave_flux(after, mean_faces[2 * axis + 1], axis)
        layers.append(
            (
                [half * f + lift * b for f, b in zip(low_flux, before)],
                [lift * a - half * f for f, a in zip(high_flux, after)],
            )
        )
    return layers


def tile_rows(matrix):
    spread = (lax.rem(lane((8, 128)), 8) == sublane((8, 128))).astype(f32)
    return jnp.dot(
        matrix, spread, precision=lax.Precision.HIGHEST, preferred_element_type=f32
    )


def pairings(count):
    sets = []
    for first in (0, 1):
        pairs = [(i, i + 1) for i in range(first, count - 1, 2)]
        if pairs:
            sets.append(pairs)
    return sets


def slots(counts):
    found = [(axis, n) for axis in range(3) for n in range(len(pairings(counts[axis])))]
    lower = ((2, 1), (2, 0), (0, 1), (1, 0), (1, 1), (0, 0))
    upper = ((2, 1), (0, 1), (2, 0), (0, 0), (1, 1), (1, 0))
    lower = [swap for swap in lower if swap in found]
    upper = [swap for swap in upper if swap in found] if counts[1] == 4 else lower
    return list(zip(lower, upper))


def in_upper_half(counts):
    return lax.axis_index("gy") >= counts[1] // 2


def routes(counts):
    places = [(x, y, z) for x in range(counts[0]) for y in range(counts[1]) for z in range(counts[2])]
    number = {place: n for n, place in enumerate(places)}

    def partner(place, axis, n):
        pairs = pairings(counts[axis])[n]
        swap = dict(pairs + [(j, i) for i, j in pairs])
        alone = [i for i in range(counts[axis]) if i not in swap]
        spare = 0 if axis else 2
        other = list(place)
        if place[axis] in swap:
            other[axis] = swap[place[axis]]
        elif axis == 0 and len(alone) == 2:
            other[axis] = sum(alone) - place[axis]
        elif counts[spare] % 2 == 0:
            other[spare] = place[spare] ^ 1
        return number[tuple(other)]

    return [
        [
            (number[place], partner(place, *(upper if place[1] >= counts[1] // 2 else lower)))
            for place in places
        ]
        for lower, upper in slots(counts)
    ]


def z_layer(field, at):
    packed = jnp.zeros((8, 128), f32)
    column = lane((8, 128))
    for x in range(8):
        turned = pltpu.roll(field[x], lax.rem(2 * x - at + 128, 128), 1)
        packed = jnp.where(column == 2 * x, turned, packed)
    return packed


def store_faces(fields, out_refs, counts):
    high_half = in_upper_half(counts)
    for c, field in enumerate(fields):
        faces = {}
        for axis in range(3):
            even = lax.rem(lax.axis_index(axes[axis]), 2) == 0
            if axis == 0:
                low, high = field[0], field[7]
            elif axis == 1:
                low, high = field[:, 0, :], field[:, 7, :]
            for n in range(len(pairings(counts[axis]))):
                last = even == (n == 0)
                if axis == 2:
                    faces[axis, n] = z_layer(field, jnp.where(last, 127, 0))
                else:
                    faces[axis, n] = jnp.where(last, high, low)
        for ref, (lower, upper) in zip(out_refs, slots(counts)):
            if lower == upper:
                ref[c] = faces[lower]
            else:
                ref[c] = jnp.where(high_half, faces[upper], faces[lower])


def load_faces(in_refs, counts, first, last, chosen=(0, 1, 2)):
    high_half = in_upper_half(counts)
    lower, upper = zip(*slots(counts))
    halos = []
    for axis in range(3):
        if axis not in chosen:
            halos.append(None)
            continue
        place = lax.axis_index(axes[axis])
        even = lax.rem(place, 2) == 0
        got = []
        for n in range(len(pairings(counts[axis]))):
            a, b = in_refs[lower.index((axis, n))], in_refs[upper.index((axis, n))]
            got.append(
                [a[c] if a is b else jnp.where(high_half, b[c], a[c]) for c in range(first, last)]
            )
        while len(got) < 2:
            got.append([jnp.zeros((8, 128), f32)] * (last - first))
        before = [jnp.where(place == 0, 0.0, jnp.where(even, b, a)) for a, b in zip(*got)]
        after = [
            jnp.where(place == counts[axis] - 1, 0.0, jnp.where(even, a, b))
            for a, b in zip(*got)
        ]
        halos.append((before, after))
    return halos


def face_shapes(counts, width):
    total = sum(len(pairings(count)) for count in counts)
    return [jax.ShapeDtypeStruct((width, 8, 128), f32)] * total


def exchange(faces, counts):
    return [lax.ppermute(face, axes, way) for face, way in zip(faces, routes(counts))]


def read_all(ref):
    return [ref[c] for c in range(ref.shape[0])]


def load_kernel(counts, *refs):
    sources, targets, out_refs, sems = refs[:5], refs[5:10], refs[10:-1], refs[-1]
    copies = [
        pltpu.make_async_copy(source, target, sems.at[n])
        for n, (source, target) in enumerate(zip(sources, targets))
    ]
    for copy in copies:
        copy.start()
    for copy, target, first in zip(copies, targets, (0, 5)):
        copy.wait()
        count = target.shape[0]
        store_faces(read_all(target), [ref.at[first : first + count] for ref in out_refs], counts)
    for copy in copies[2:]:
        copy.wait()


def partners(count):
    if count == window:
        return [[(i, i ^ mask) for i in range(count)] for mask in range(count)]
    turns = sorted({d % count for d in range(1 - window, window)})
    return [[(i, (i + turn) % count) for i in range(count)] for turn in turns]


def sending_sets(count):
    return [3, 2, 1, 0] if count == window else list(range(count))


def plan_kernel(
    counts, owner_ref, slot_ref, proj_ref, order_ref, marks_ref, along_x_ref, along_y_ref, tile_ref
):
    count = counts[0]
    n_sets = len(partners(count))
    own = lax.axis_index("gx")
    n_blocks = owner_ref.shape[-1]
    square = (n_blocks, n_blocks)
    block, other = sublane(square), lane(square)

    def spread(ref):
        by_lane = jnp.broadcast_to(ref[0], square)
        here = jnp.where(block == other, by_lane, 0).astype(f32)
        return by_lane, jnp.sum(here, axis=1, keepdims=True).astype(jnp.int32)

    def group_of(owner):
        if count == window:
            return lax.bitwise_xor(owner, own)
        turn = lax.rem(owner - own + count, count)
        if n_sets == count:
            return turn
        return jnp.where(turn < window, turn, turn - (count - n_sets))

    owner_by_lane, owner = spread(owner_ref)
    slot = spread(slot_ref)[1]
    group = group_of(owner)
    before = (group_of(owner_by_lane) == group) & (other < block)
    taken = jnp.sum(before.astype(f32), axis=1, keepdims=True).astype(jnp.int32)
    wide = (n_blocks, 128)
    place = jnp.broadcast_to(group * window + taken, wide)
    column = lane((8, 128))
    quarter = column // 32
    for s in range((n_sets + 3) // 4):
        here = place - 16 * s == lane(wide) // 8
        label = jnp.sum(jnp.where(here, (slot + 1).astype(f32), 0.0), axis=0, keepdims=True) - 1.0
        source = jnp.sum(
            jnp.where(here, (8 * sublane(wide)).astype(f32), 0.0), axis=0, keepdims=True
        )
        labels = jnp.broadcast_to(label, (8, 128))
        order = jnp.broadcast_to(source, (8, 128)).astype(jnp.int32) + lax.rem(column, 8)
        for t in range(4):
            order_ref[4 * s + t] = rolled(order, 32 * t, 1)
        for r in range(min(4, n_sets - 4 * s)):
            marks = labels
            for t in range(1, 4):
                marks = jnp.where(quarter == (r + t) % 4, rolled(labels, 32 * t, 1), marks)
            marks_ref[4 * s + r] = marks
    proj = proj_ref[...]
    for a in range(8):
        along_y = jnp.broadcast_to(proj[:, a : a + 1], (8, 128))
        along_y_ref[a] = along_y
        for i in range(8):
            along_x_ref[8 * i + a] = jnp.broadcast_to(along_y[i : i + 1], (8, 128))
    tile = tile_rows(proj)
    high = tile.astype(jnp.bfloat16).astype(f32)
    tile_ref[0] = high
    tile_ref[1] = tile - high


def speeds(state):
    inverse = 1.0 / (state[0] + 1.0)
    return [state[c] * inverse for c in (1, 2, 3)]


def vorticity_kernel(les_ref, velocity_ref, vort_ref):
    velocity = speeds([les_ref[c] for c in range(4)])

    def slope(c, axis):
        return shifted(velocity[c], axis, 1) - shifted(velocity[c], axis, -1)

    vort = [slope(2, 1) - slope(1, 2), slope(0, 2) - slope(2, 0), slope(1, 0) - slope(0, 1)]
    for c in range(3):
        velocity_ref[c] = velocity[c]
        vort_ref[c] = vort[c]


def vorticity_z_kernel(counts, present, vort_ref, *refs):
    refs = list(refs)
    face_refs = [refs.pop(0) if here else None for here in present]
    (out_ref,) = refs
    before, after = [speeds(layer) for layer in load_faces(face_refs, counts, 0, 4, (2,))[2]]
    for c, layer in ((0, (before[1], -after[1])), (1, (-before[0], after[0]))):
        for x, plane in enumerate(with_layers(vort_ref[c], (None, None, layer))):
            out_ref[c, x] = plane
    out_ref[2] = vort_ref[2]


def lamb_kernel(
    counts, n_faces, order_ref, marks_ref, along_x_ref, along_y_ref, velocity_ref, vort_ref, *refs
):
    face_refs, out_refs = refs[:n_faces], refs[n_faces:]
    outer = [
        halo and (speeds(halo[0]), speeds(halo[1]))
        for halo in load_faces(face_refs, counts, 0, 4, (0, 1))
    ]

    def rise(c, axis):
        return -outer[axis][0][c], outer[axis][1][c]

    def fall(c, axis):
        return outer[axis][0][c], -outer[axis][1][c]

    layers = [
        (None, rise(2, 1), None),
        (fall(2, 0), None, None),
        (rise(1, 0), fall(0, 1), None),
    ]
    vort = [0.5 * jnp.stack(with_layers(vort_ref[c], layers[c]), axis=0) for c in range(3)]
    velocity = read_all(velocity_ref)
    lamb = [
        vort[1] * velocity[2] - vort[2] * velocity[1],
        vort[2] * velocity[0] - vort[0] * velocity[2],
        vort[0] * velocity[1] - vort[1] * velocity[0],
    ]
    blocks = []
    for field in lamb:
        along_y = along_y_ref[0][None] * field[:, 0:1, :]
        for b in range(1, 8):
            along_y = along_y + along_y_ref[b][None] * field[:, b : b + 1, :]
        for i in range(8):
            plane = along_x_ref[8 * i] * along_y[0]
            for a in range(1, 8):
                plane = plane + along_x_ref[8 * i + a] * along_y[a]
            blocks.append(plane)

    quarter = lane((8, 128)) // 32
    for s in range((len(out_refs) + 3) // 4):
        ordered = [
            jnp.take_along_axis(block, order_ref[4 * s + k % 4], axis=1)
            for k, block in enumerate(blocks)
        ]
        for r in range(min(4, len(out_refs) - 4 * s)):
            out = out_refs[4 * s + r]
            for q in range(6):
                packed = ordered[4 * q]
                for t in range(1, 4):
                    packed = jnp.where(quarter == (r + t) % 4, ordered[4 * q + t], packed)
                out[q] = packed
            out[6] = marks_ref[4 * s + r]


def first_kernel(
    counts, n_faces, deriv_ref, high_ref, low_ref, les_ref, wave_ref, mean_ref, *refs
):
    face_refs, (section_ref, rate_ref, mean_faces_ref), out_refs = (
        refs[:n_faces], refs[n_faces : n_faces + 3], refs[n_faces + 3 :],
    )
    for n, face in enumerate(mean_layers(read_all(mean_ref))):
        for c in range(3):
            mean_faces_ref[n, c] = face[c]
    state = read_all(les_ref)
    rate = les_rate(state, load_faces(face_refs, counts, 0, 5))
    section = [s + r for s, r in zip(state, rate)]
    for c in range(5):
        section_ref[c] = section[c]
    store_faces(section, out_refs, counts)
    rate = acoustic_rate(
        read_all(wave_ref), read_all(mean_ref), load_faces(face_refs, counts, 5, 9),
        deriv_ref[...], (high_ref[...], low_ref[...]),
    )
    for c in range(4):
        rate_ref[c] = rate[c]


def source_kernel(counts, n_faces, tile_ref, wave_ref, rate_ref, *refs):
    n_pieces = len(partners(counts[0]))
    pieces = [None] * n_pieces
    for ref, k in zip(refs, sending_sets(n_pieces)):
        pieces[k] = ref
    refs = refs[n_pieces:]
    section_faces, (source_ref, middle_ref, carry_ref), face_refs = (
        refs[:n_faces], refs[n_faces : n_faces + 3], refs[n_faces + 3 :],
    )
    quarter = lane((8, 128)) // 32
    tile_high, tile_low = tile_ref[0], tile_ref[1]
    total = None
    for s in range((n_pieces + 3) // 4):
        count = min(4, n_pieces - 4 * s)

        def gathered(q, t):
            value = jnp.full((8, 128), -1.0 if q == 6 else 0.0, f32)
            for r in range(count):
                value = jnp.where(quarter == (r + t) % 4, pieces[4 * s + r][q], value)
            return value

        here = [gathered(6, 0).astype(jnp.int32) == slot for slot in range(16)]
        chosen_high, chosen_low = [
            jnp.concatenate([jnp.where(h, part, 0.0) for h in here], axis=0).astype(jnp.bfloat16)
            for part in (tile_high, tile_low)
        ]
        data = []
        for k in range(24):
            piece = gathered(k // 4, k % 4)
            data.append(pltpu.roll(piece, 128 - 32 * (k % 4), 1) if k % 4 else piece)
        data = jnp.concatenate(data, axis=0)
        high = data.astype(jnp.bfloat16)
        low = (data - high.astype(f32)).astype(jnp.bfloat16)
        dot = functools.partial(
            lax.dot_general,
            dimension_numbers=(((1,), (1,)), ((), ())),
            preferred_element_type=f32,
        )
        moved = dot(high, chosen_high) + (dot(low, chosen_high) + dot(high, chosen_low))
        total = moved if total is None else total + moved
    source = [total[64 * c : 64 * c + 64].reshape(8, 8, 128) for c in range(3)]
    middle = []
    for c in range(4):
        rate = rate_ref[c]
        if c:
            source_ref[c - 1] = source[c - 1]
            rate = rate + source[c - 1]
        middle.append(wave_ref[c] + acoustic_step * rate)
        middle_ref[c] = middle[c]
        carry = wave_ref[c] + middle[c]
        carry_ref[c] = carry + acoustic_step * source[c - 1] if c else carry
    for ready, face in zip(section_faces, face_refs):
        face[0:5] = ready[...]
    store_faces(middle, [face.at[5:9] for face in face_refs], counts)


def inner_kernel(
    deriv_ref, high_ref, low_ref, les_ref, section_ref, middle_ref, carry_ref, mean_ref, source_ref,
    les_base_ref, wave_base_ref, source_out, sem,
):
    copy = pltpu.make_async_copy(source_ref, source_out, sem)
    copy.start()
    section = read_all(section_ref)
    rate = les_rate(section, None)
    for c in range(5):
        les_base_ref[c] = 0.5 * ((les_ref[c] + section[c]) + rate[c])
    rate = acoustic_rate(
        read_all(middle_ref), read_all(mean_ref), None,
        deriv_ref[...], (high_ref[...], low_ref[...]),
    )
    for c in range(4):
        wave_base_ref[c] = 0.5 * (carry_ref[c] + acoustic_step * rate[c])
    copy.wait()


def add_layers(counts, chosen, face_refs, mean_faces_ref, les_base_ref, wave_base_ref, put):
    layers = les_outer(load_faces(face_refs, counts, 0, 5, chosen))
    for c in range(5):
        part = [layer and (0.5 * layer[0][c], 0.5 * layer[1][c]) for layer in layers]
        put(c, with_layers(les_base_ref[c], part))
    mean_faces = [[mean_faces_ref[n, c] for c in range(3)] for n in range(6)]
    layers = acoustic_outer(mean_faces, load_faces(face_refs, counts, 5, 9, chosen))
    step = 0.5 * acoustic_step
    for c in range(4):
        part = [layer and (step * layer[0][c], step * layer[1][c]) for layer in layers]
        put(5 + c, with_layers(wave_base_ref[c], part))


def z_faces(faces, counts):
    holds = [any(axis == 2 for axis, _ in pair) for pair in slots(counts)]
    return [face if hold else None for face, hold in zip(faces, holds)]


def z_kernel(counts, present, les_base_ref, wave_base_ref, mean_faces_ref, *refs):
    refs = list(refs)
    face_refs = [refs.pop(0) if here else None for here in present]
    les_ref, wave_ref = refs

    def put(c, planes):
        for x, plane in enumerate(planes):
            if c < 5:
                les_ref[c, x] = plane
            else:
                wave_ref[c - 5, x] = plane

    add_layers(counts, (2,), face_refs, mean_faces_ref, les_base_ref, wave_base_ref, put)


def last_kernel(counts, n_faces, les_base_ref, wave_base_ref, mean_faces_ref, *refs):
    face_refs, (les_out, wave_out, les_ref, wave_ref, sems) = (
        refs[:n_faces], refs[n_faces:],
    )
    copies = []

    def put(c, planes):
        kept, target = (les_ref.at[c], les_out.at[c]) if c < 5 else (
            wave_ref.at[c - 5], wave_out.at[c - 5]
        )
        for x, plane in enumerate(planes):
            kept[x] = plane
        copies.append(pltpu.make_async_copy(kept, target, sems.at[c]))
        copies[-1].start()

    add_layers(counts, (0, 1), face_refs, mean_faces_ref, les_base_ref, wave_base_ref, put)
    for copy in copies:
        copy.wait()


VMEM = pl.BlockSpec(memory_space=pltpu.VMEM)


HBM = pl.BlockSpec(memory_space=pltpu.HBM)


def call(kernel, in_specs, out_shapes, name, cost, scratch=(), out_spec=None):
    return pl.pallas_call(
        kernel,
        in_specs=in_specs,
        out_specs=out_spec or [VMEM] * len(out_shapes),
        out_shape=out_shapes,
        scratch_shapes=list(scratch),
        name=name,
        cost_estimate=pl.CostEstimate(flops=cost, bytes_accessed=800000, transcendentals=0),
        compiler_params=pltpu.CompilerParams(vmem_limit_bytes=24 * 1024 * 1024),
    )


def local(counts, les, wave, mean, projection, owner, slot):
    shape = les.shape[1:]
    faces = face_shapes(counts, 9)
    n_faces = len(faces)
    like = lambda n: jax.ShapeDtypeStruct((n,) + shape, f32)

    table = derivative_matrix()
    deriv = jnp.asarray(table, f32)
    along_z = np.kron(np.eye(16), table.T).astype(np.float32)
    high = along_z.astype(jnp.bfloat16)
    low = (along_z - high.astype(np.float32)).astype(jnp.bfloat16)
    tables = (deriv, jnp.asarray(high), jnp.asarray(low))

    arguments = (les, wave, owner, slot, projection)
    les, wave, owner, slot, projection, *sent = call(
        functools.partial(load_kernel, counts),
        [HBM] * 5,
        [jax.ShapeDtypeStruct(a.shape, a.dtype) for a in arguments] + faces,
        "load_and_faces",
        100000,
        [pltpu.SemaphoreType.DMA((5,))],
    )(*(pltpu.with_memory_space_constraint(a, pltpu.HBM) for a in arguments))
    got = exchange(sent, counts)

    sets = partners(counts[0])
    n_plans = 4 * ((len(sets) + 3) // 4)
    order, marks, along_x, along_y, tile = call(
        functools.partial(plan_kernel, counts),
        [VMEM] * 3,
        [
            jax.ShapeDtypeStruct((n_plans, 8, 128), jnp.int32),
            jax.ShapeDtypeStruct((len(sets), 8, 128), f32),
            jax.ShapeDtypeStruct((64, 8, 128), f32),
            jax.ShapeDtypeStruct((8, 8, 128), f32),
            jax.ShapeDtypeStruct((2, 8, 128), f32),
        ],
        "plan",
        1000000,
    )(owner, slot, projection)
    turning = list(call(vorticity_kernel, [VMEM], [like(3)] * 2, "vorticity", 1000000)(les))
    z_got = z_faces(got, counts)
    present = [face is not None for face in z_got]
    turning[1] = call(
        functools.partial(vorticity_z_kernel, counts, present),
        [VMEM] * (1 + sum(present)),
        [like(3)],
        "vorticity_z",
        1000000,
    )(turning[1], *(face for face in z_got if face is not None))[0]
    pieces = call(
        functools.partial(lamb_kernel, counts, n_faces),
        [VMEM] * (6 + n_faces),
        [jax.ShapeDtypeStruct((7, 8, 128), f32)] * len(sets),
        "lamb_blocks",
        10000000,
    )(order, marks, along_x, along_y, *turning, *got)
    moved = []
    for k in sending_sets(len(sets)):
        still = all(i == j for i, j in sets[k])
        moved.append(pieces[k] if still else lax.ppermute(pieces[k], "gx", sets[k]))
    section, rate, mean_faces, *section_faces = call(
        functools.partial(first_kernel, counts, n_faces),
        [VMEM] * (6 + n_faces),
        [like(5), like(4), jax.ShapeDtypeStruct((6, 3, 8, 128), f32)] + face_shapes(counts, 5),
        "first_rates",
        40000000,
    )(*tables, les, wave, mean, *got)

    source, middle, carry, *sent = call(
        functools.partial(source_kernel, counts, n_faces),
        [VMEM] * (3 + len(moved) + n_faces),
        [like(3), like(4), like(4)] + faces,
        "source_and_faces",
        10000000,
    )(tile, wave, rate, *moved, *section_faces)
    got = exchange(sent, counts)
    les_base, wave_base, source_out = call(
        inner_kernel,
        [VMEM] * 9,
        [like(5), like(4), like(3)],
        "second_rates_inner",
        40000000,
        [pltpu.SemaphoreType.DMA],
        out_spec=[VMEM, VMEM, HBM],
    )(*tables, les, section, middle, carry, mean, source)
    z_got = z_faces(got, counts)
    present = [face is not None for face in z_got]
    les_base, wave_base = call(
        functools.partial(z_kernel, counts, present),
        [VMEM] * (3 + sum(present)),
        [like(5), like(4)],
        "second_rates_z",
        1000000,
    )(les_base, wave_base, mean_faces, *(face for face in z_got if face is not None))
    les_next, wave_next = call(
        functools.partial(last_kernel, counts, n_faces),
        [VMEM] * (3 + n_faces),
        [like(5), like(4)],
        "second_rates_outer",
        4000000,
        [
            pltpu.VMEM(les.shape, f32),
            pltpu.VMEM(wave.shape, f32),
            pltpu.SemaphoreType.DMA((9,)),
        ],
        out_spec=[HBM, HBM],
    )(les_base, wave_base, mean_faces, *got)
    return les_next, source_out, wave_next


def solution(mesh):
    counts = tuple(mesh.shape[axis] for axis in axes)
    field = P(None, *axes)
    return jax.shard_map(
        functools.partial(local, counts),
        mesh=mesh,
        in_specs=(field, field, field, P(), P(*axes), P(*axes)),
        out_specs=(field, field, field),
        check_vma=False,
    )
```

```python
import functools

import jax
import jax.numpy as jnp
import numpy as np
from jax import lax
from jax.experimental import pallas as pl
from jax.experimental.pallas import tpu as pltpu
from jax.sharding import PartitionSpec as P

lobatto_points = np.array(
    [
        -1.0,
        -0.8717401485096066,
        -0.5917001814331423,
        -0.2092992179024789,
        0.2092992179024789,
        0.5917001814331423,
        0.8717401485096066,
        1.0,
    ]
)
flux_half = 0.08
gamma_less = 0.4
acoustic_step = 0.01
upwind_speed = 1.5
face_lift = 28.0
free_stream = (1.0, 0.0, 0.0, 0.0, 2.5)
axes = ("gx", "gy", "gz")
window = 4
f32 = jnp.float32


def derivative_matrix():
    points = lobatto_points
    products = [np.prod([points[i] - points[j] for j in range(8) if j != i]) for i in range(8)]
    matrix = np.zeros((8, 8))
    for i in range(8):
        for j in range(8):
            if j != i:
                matrix[i, j] = products[i] / (products[j] * (points[i] - points[j]))
        matrix[i, i] = -np.sum(matrix[i])
    return matrix


def sublane(shape):
    return lax.broadcasted_iota(jnp.int32, shape, len(shape) - 2)


def lane(shape):
    return lax.broadcasted_iota(jnp.int32, shape, len(shape) - 1)


def rolled(tile, amount, axis):
    amount = amount % tile.shape[axis]
    return pltpu.roll(tile, amount, axis) if amount else tile


def shifted(field, axis, step, outer=None):
    if axis == 0:
        outer = jnp.zeros((8, 128), f32) if outer is None else outer
        if step == 1:
            return jnp.concatenate([field[1:], outer[None]], axis=0)
        return jnp.concatenate([outer[None], field[:-1]], axis=0)
    count = (8, 128)[axis - 1]
    edge = count - 1 if step == 1 else 0
    at_edge = (sublane if axis == 1 else lane)((8, 128)) == edge
    planes = []
    for x in range(8):
        layer = 0.0 if outer is None else rolled(outer, edge - axis * x, axis - 1)
        planes.append(jnp.where(at_edge, layer, rolled(field[x], -step, axis - 1)))
    return jnp.stack(planes, axis=0)


def fluid(state):
    density, mx, my, mz, energy = [s + r for s, r in zip(state, free_stream)]
    inverse = 1.0 / density
    momentum = (mx, my, mz)
    velocity = [m * inverse for m in momentum]
    pressure = gamma_less * (
        energy - 0.5 * (mx * velocity[0] + my * velocity[1] + mz * velocity[2])
    )
    return momentum, velocity, pressure, energy + pressure


def split_flux(state, parts, axis, sign):
    momentum, velocity, pressure, enthalpy = parts
    speed = velocity[axis]
    flux = [momentum[axis]]
    for c in range(3):
        term = momentum[c] * speed
        flux.append(term + pressure if c == axis else term)
    flux.append(enthalpy * speed)
    if sign > 0:
        return [flux_half * (s + f) for s, f in zip(state, flux)]
    return [flux_half * (s - f) for s, f in zip(state, flux)]


def les_rate(state, halos):
    parts = fluid(state)
    total = [-6.0 * flux_half * s for s in state]
    for axis in range(3):
        ahead = split_flux(state, parts, axis, -1)
        behind = split_flux(state, parts, axis, 1)
        ahead_outer = behind_outer = [None] * 5
        if halos is not None:
            before, after = halos[axis]
            ahead_outer = split_flux(after, fluid(after), axis, -1)
            behind_outer = split_flux(before, fluid(before), axis, 1)
        for c in range(5):
            total[c] = total[c] + (
                shifted(ahead[c], axis, 1, ahead_outer[c])
                + shifted(behind[c], axis, -1, behind_outer[c])
            )
    return total


def les_outer(halos):
    return [
        halo
        and (
            split_flux(halo[0], fluid(halo[0]), axis, 1),
            split_flux(halo[1], fluid(halo[1]), axis, -1),
        )
        for axis, halo in enumerate(halos)
    ]


def with_layers(field, layers):
    row, column = sublane((8, 128)), lane((8, 128))
    along_z = layers[2]
    if along_z is not None:
        along_z = jnp.where(lax.rem(column, 2) == 0, along_z[0], rolled(along_z[1], -1, 1))
    planes = []
    for x in range(8):
        plane = field[x]
        if layers[0] is not None and x in (0, 7):
            plane = plane + layers[0][x // 7]
        if layers[1] is not None:
            low, high = layers[1]
            plane = plane + jnp.where(
                row == 0, rolled(low, -x, 0), jnp.where(row == 7, rolled(high, 7 - x, 0), 0.0)
            )
        if along_z is not None:
            ends = (column == 0) | (column == 127)
            plane = plane + jnp.where(ends, rolled(along_z, -2 * x, 1), 0.0)
        planes.append(plane)
    return planes


def wave_flux(state, mean, axis):
    speed = mean[axis]
    pressure = state[0]
    rows = [speed * pressure + state[1 + axis]]
    for c in range(3):
        term = speed * state[1 + c]
        rows.append(term + pressure if c == axis else term)
    return rows


def dot3(left, right):
    high = left.astype(jnp.bfloat16)
    low = (left - high.astype(f32)).astype(jnp.bfloat16)
    dot = functools.partial(jnp.dot, preferred_element_type=f32)
    return dot(high, right[0]) + (dot(low, right[0]) + dot(high, right[1]))


def acoustic_rate(state, mean, halos, deriv, along_z):
    shape = state[0].shape
    table = derivative_matrix()
    flux = wave_flux(state, mean, 0)
    if halos is None:
        halos = [([jnp.zeros((8, 128), f32)] * 4,) * 2] + [([None] * 4,) * 2] * 2
    before, after = halos[0]
    low_mean, high_mean = [m[0] for m in mean], [m[7] for m in mean]
    low_jump = [b - s[0] for b, s in zip(before, state)]
    high_jump = [a - s[7] for a, s in zip(after, state)]
    low_flux = wave_flux(low_jump, low_mean, 0)
    high_flux = wave_flux(high_jump, high_mean, 0)
    half, lift = 0.5 * face_lift, 0.5 * face_lift * upwind_speed
    total = []
    for c in range(4):
        planes = []
        for i in range(8):
            plane = -float(table[i, 0]) * flux[c][0]
            for a in range(1, 8):
                if abs(table[i, a]) > 1e-12:
                    plane = plane - float(table[i, a]) * flux[c][a]
            if i == 0:
                plane = plane + (half * low_flux[c] + lift * low_jump[c])
            if i == 7:
                plane = plane - (half * high_flux[c] - lift * high_jump[c])
            planes.append(plane)
        total.append(jnp.stack(planes, axis=0))
    flux = wave_flux(state, mean, 1)
    before, after = halos[1]
    row = sublane(shape)
    sign = jnp.where(row == 0, half, jnp.where(row == 7, -half, 0.0))
    jump = []
    for s, b, a in zip(state, before, after):
        planes = []
        for x in range(8):
            low = 0.0 if b is None else rolled(b, -x, 0)
            high = 0.0 if a is None else rolled(a, 7 - x, 0)
            planes.append(jnp.where(row[x] == 0, low, jnp.where(row[x] == 7, high, s[x])) - s[x])
        jump.append(jnp.stack(planes, axis=0))
    jump_flux = wave_flux(jump, mean, 1)
    for c in range(4):
        change = lift * jump[c] + sign * jump_flux[c]
        for b in range(8):
            change = change - deriv[:, b : b + 1][None] * flux[c][:, b : b + 1, :]
        total[c] = total[c] + change
    flux = wave_flux(state, mean, 2)
    before, after = halos[2]
    column = lane(shape)
    place = lax.rem(column, 8)
    sign = jnp.where(place == 0, half, jnp.where(place == 7, -half, 0.0))
    jump = [
        jnp.where(
            place == 0,
            shifted(s, 2, -1, b),
            jnp.where(place == 7, shifted(s, 2, 1, a), s),
        )
        - s
        for s, b, a in zip(state, before, after)
    ]
    jump_flux = wave_flux(jump, mean, 2)
    for c in range(4):
        slope = dot3(flux[c].reshape(64, 128), along_z).reshape(shape)
        total[c] = total[c] + (lift * jump[c] + sign * jump_flux[c] - slope)
    return total


def mean_layers(mean):
    return [
        [m[0] for m in mean],
        [m[7] for m in mean],
        [m[:, 0, :] for m in mean],
        [m[:, 7, :] for m in mean],
        [z_layer(m, jnp.int32(0)) for m in mean],
        [z_layer(m, jnp.int32(127)) for m in mean],
    ]


def acoustic_outer(mean_faces, halos):
    half, lift = 0.5 * face_lift, 0.5 * face_lift * upwind_speed
    layers = []
    for axis, halo in enumerate(halos):
        if halo is None:
            layers.append(None)
            continue
        before, after = halo
        low_flux = wave_flux(before, mean_faces[2 * axis], axis)
        high_flux = wave_flux(after, mean_faces[2 * axis + 1], axis)
        layers.append(
            (
                [half * f + lift * b for f, b in zip(low_flux, before)],
                [lift * a - half * f for f, a in zip(high_flux, after)],
            )
        )
    return layers


def tile_rows(matrix):
    spread = (lax.rem(lane((8, 128)), 8) == sublane((8, 128))).astype(f32)
    return jnp.dot(
        matrix, spread, precision=lax.Precision.HIGHEST, preferred_element_type=f32
    )


def pairings(count):
    sets = []
    for first in (0, 1):
        pairs = [(i, i + 1) for i in range(first, count - 1, 2)]
        if pairs:
            sets.append(pairs)
    return sets


def slots(counts):
    found = [(axis, n) for axis in range(3) for n in range(len(pairings(counts[axis])))]
    lower = ((2, 1), (2, 0), (0, 1), (1, 0), (1, 1), (0, 0))
    upper = ((2, 1), (0, 1), (2, 0), (0, 0), (1, 1), (1, 0))
    lower = [swap for swap in lower if swap in found]
    upper = [swap for swap in upper if swap in found] if counts[1] == 4 else lower
    return list(zip(lower, upper))


def in_upper_half(counts):
    return lax.axis_index("gy") >= counts[1] // 2


def routes(counts):
    places = [(x, y, z) for x in range(counts[0]) for y in range(counts[1]) for z in range(counts[2])]
    number = {place: n for n, place in enumerate(places)}

    def partner(place, axis, n):
        pairs = pairings(counts[axis])[n]
        swap = dict(pairs + [(j, i) for i, j in pairs])
        alone = [i for i in range(counts[axis]) if i not in swap]
        spare = 0 if axis else 2
        other = list(place)
        if place[axis] in swap:
            other[axis] = swap[place[axis]]
        elif axis == 0 and len(alone) == 2:
            other[axis] = sum(alone) - place[axis]
        elif counts[spare] % 2 == 0:
            other[spare] = place[spare] ^ 1
        return number[tuple(other)]

    return [
        [
            (number[place], partner(place, *(upper if place[1] >= counts[1] // 2 else lower)))
            for place in places
        ]
        for lower, upper in slots(counts)
    ]


def z_layer(field, at):
    packed = jnp.zeros((8, 128), f32)
    column = lane((8, 128))
    for x in range(8):
        turned = pltpu.roll(field[x], lax.rem(2 * x - at + 128, 128), 1)
        packed = jnp.where(column == 2 * x, turned, packed)
    return packed


def store_faces(fields, out_refs, counts):
    high_half = in_upper_half(counts)
    for c, field in enumerate(fields):
        faces = {}
        for axis in range(3):
            even = lax.rem(lax.axis_index(axes[axis]), 2) == 0
            if axis == 0:
                low, high = field[0], field[7]
            elif axis == 1:
                low, high = field[:, 0, :], field[:, 7, :]
            for n in range(len(pairings(counts[axis]))):
                last = even == (n == 0)
                if axis == 2:
                    faces[axis, n] = z_layer(field, jnp.where(last, 127, 0))
                else:
                    faces[axis, n] = jnp.where(last, high, low)
        for ref, (lower, upper) in zip(out_refs, slots(counts)):
            if lower == upper:
                ref[c] = faces[lower]
            else:
                ref[c] = jnp.where(high_half, faces[upper], faces[lower])


def load_faces(in_refs, counts, first, last, chosen=(0, 1, 2)):
    high_half = in_upper_half(counts)
    lower, upper = zip(*slots(counts))
    halos = []
    for axis in range(3):
        if axis not in chosen:
            halos.append(None)
            continue
        place = lax.axis_index(axes[axis])
        even = lax.rem(place, 2) == 0
        got = []
        for n in range(len(pairings(counts[axis]))):
            a, b = in_refs[lower.index((axis, n))], in_refs[upper.index((axis, n))]
            got.append(
                [a[c] if a is b else jnp.where(high_half, b[c], a[c]) for c in range(first, last)]
            )
        while len(got) < 2:
            got.append([jnp.zeros((8, 128), f32)] * (last - first))
        before = [jnp.where(place == 0, 0.0, jnp.where(even, b, a)) for a, b in zip(*got)]
        after = [
            jnp.where(place == counts[axis] - 1, 0.0, jnp.where(even, a, b))
            for a, b in zip(*got)
        ]
        halos.append((before, after))
    return halos


def face_shapes(counts, width):
    total = sum(len(pairings(count)) for count in counts)
    return [jax.ShapeDtypeStruct((width, 8, 128), f32)] * total


def exchange(faces, counts):
    return [lax.ppermute(face, axes, way) for face, way in zip(faces, routes(counts))]


def read_all(ref):
    return [ref[c] for c in range(ref.shape[0])]


def load_kernel(counts, *refs):
    sources, targets, out_refs, sems = refs[:5], refs[5:10], refs[10:-1], refs[-1]
    copies = [
        pltpu.make_async_copy(source, target, sems.at[n])
        for n, (source, target) in enumerate(zip(sources, targets))
    ]
    for copy in copies:
        copy.start()
    for copy, target, first in zip(copies, targets, (0, 5)):
        copy.wait()
        count = target.shape[0]
        store_faces(read_all(target), [ref.at[first : first + count] for ref in out_refs], counts)
    for copy in copies[2:]:
        copy.wait()


def partners(count):
    if count == window:
        return [[(i, i ^ mask) for i in range(count)] for mask in range(count)]
    turns = sorted({d % count for d in range(1 - window, window)})
    return [[(i, (i + turn) % count) for i in range(count)] for turn in turns]


def sending_sets(count):
    return [3, 2, 1, 0] if count == window else list(range(count))


def plan_kernel(
    counts, owner_ref, slot_ref, proj_ref, order_ref, marks_ref, along_x_ref, along_y_ref, tile_ref
):
    count = counts[0]
    n_sets = len(partners(count))
    own = lax.axis_index("gx")
    n_blocks = owner_ref.shape[-1]
    square = (n_blocks, n_blocks)
    block, other = sublane(square), lane(square)

    def spread(ref):
        by_lane = jnp.broadcast_to(ref[0], square)
        here = jnp.where(block == other, by_lane, 0).astype(f32)
        return by_lane, jnp.sum(here, axis=1, keepdims=True).astype(jnp.int32)

    def group_of(owner):
        if count == window:
            return lax.bitwise_xor(owner, own)
        turn = lax.rem(owner - own + count, count)
        if n_sets == count:
            return turn
        return jnp.where(turn < window, turn, turn - (count - n_sets))

    owner_by_lane, owner = spread(owner_ref)
    slot = spread(slot_ref)[1]
    group = group_of(owner)
    before = (group_of(owner_by_lane) == group) & (other < block)
    taken = jnp.sum(before.astype(f32), axis=1, keepdims=True).astype(jnp.int32)
    wide = (n_blocks, 128)
    place = jnp.broadcast_to(group * window + taken, wide)
    column = lane((8, 128))
    quarter = column // 32
    for s in range((n_sets + 3) // 4):
        here = place - 16 * s == lane(wide) // 8
        label = jnp.sum(jnp.where(here, (slot + 1).astype(f32), 0.0), axis=0, keepdims=True) - 1.0
        source = jnp.sum(
            jnp.where(here, (8 * sublane(wide)).astype(f32), 0.0), axis=0, keepdims=True
        )
        labels = jnp.broadcast_to(label, (8, 128))
        order = jnp.broadcast_to(source, (8, 128)).astype(jnp.int32) + lax.rem(column, 8)
        for t in range(4):
            order_ref[4 * s + t] = rolled(order, 32 * t, 1)
        for r in range(min(4, n_sets - 4 * s)):
            marks = labels
            for t in range(1, 4):
                marks = jnp.where(quarter == (r + t) % 4, rolled(labels, 32 * t, 1), marks)
            marks_ref[4 * s + r] = marks
    proj = proj_ref[...]
    for a in range(8):
        along_y = jnp.broadcast_to(proj[:, a : a + 1], (8, 128))
        along_y_ref[a] = along_y
        for i in range(8):
            along_x_ref[8 * i + a] = jnp.broadcast_to(along_y[i : i + 1], (8, 128))
    tile = tile_rows(proj)
    high = tile.astype(jnp.bfloat16).astype(f32)
    tile_ref[0] = high
    tile_ref[1] = tile - high


def speeds(state):
    inverse = 1.0 / (state[0] + 1.0)
    return [state[c] * inverse for c in (1, 2, 3)]


def vorticity_kernel(les_ref, velocity_ref, vort_ref):
    velocity = speeds([les_ref[c] for c in range(4)])

    def slope(c, axis):
        return shifted(velocity[c], axis, 1) - shifted(velocity[c], axis, -1)

    vort = [slope(2, 1) - slope(1, 2), slope(0, 2) - slope(2, 0), slope(1, 0) - slope(0, 1)]
    for c in range(3):
        velocity_ref[c] = velocity[c]
        vort_ref[c] = vort[c]


def vorticity_z_kernel(counts, present, vort_ref, *refs):
    refs = list(refs)
    face_refs = [refs.pop(0) if here else None for here in present]
    (out_ref,) = refs
    before, after = [speeds(layer) for layer in load_faces(face_refs, counts, 0, 4, (2,))[2]]
    for c, layer in ((0, (before[1], -after[1])), (1, (-before[0], after[0]))):
        for x, plane in enumerate(with_layers(vort_ref[c], (None, None, layer))):
            out_ref[c, x] = plane
    out_ref[2] = vort_ref[2]


def lamb_kernel(
    counts, n_faces, order_ref, marks_ref, along_x_ref, along_y_ref, velocity_ref, vort_ref, *refs
):
    face_refs, out_refs = refs[:n_faces], refs[n_faces:]
    outer = [
        halo and (speeds(halo[0]), speeds(halo[1]))
        for halo in load_faces(face_refs, counts, 0, 4, (0, 1))
    ]

    def rise(c, axis):
        return -outer[axis][0][c], outer[axis][1][c]

    def fall(c, axis):
        return outer[axis][0][c], -outer[axis][1][c]

    layers = [
        (None, rise(2, 1), None),
        (fall(2, 0), None, None),
        (rise(1, 0), fall(0, 1), None),
    ]
    vort = [0.5 * jnp.stack(with_layers(vort_ref[c], layers[c]), axis=0) for c in range(3)]
    velocity = read_all(velocity_ref)
    lamb = [
        vort[1] * velocity[2] - vort[2] * velocity[1],
        vort[2] * velocity[0] - vort[0] * velocity[2],
        vort[0] * velocity[1] - vort[1] * velocity[0],
    ]
    blocks = []
    for field in lamb:
        along_y = along_y_ref[0][None] * field[:, 0:1, :]
        for b in range(1, 8):
            along_y = along_y + along_y_ref[b][None] * field[:, b : b + 1, :]
        for i in range(8):
            plane = along_x_ref[8 * i] * along_y[0]
            for a in range(1, 8):
                plane = plane + along_x_ref[8 * i + a] * along_y[a]
            blocks.append(plane)

    quarter = lane((8, 128)) // 32
    for s in range((len(out_refs) + 3) // 4):
        ordered = [
            jnp.take_along_axis(block, order_ref[4 * s + k % 4], axis=1)
            for k, block in enumerate(blocks)
        ]
        for r in range(min(4, len(out_refs) - 4 * s)):
            out = out_refs[4 * s + r]
            for q in range(6):
                packed = ordered[4 * q]
                for t in range(1, 4):
                    packed = jnp.where(quarter == (r + t) % 4, ordered[4 * q + t], packed)
                out[q] = packed
            out[6] = marks_ref[4 * s + r]


def first_kernel(
    counts, n_faces, deriv_ref, high_ref, low_ref, les_ref, wave_ref, mean_ref, *refs
):
    face_refs, (section_ref, rate_ref, mean_faces_ref), out_refs = (
        refs[:n_faces], refs[n_faces : n_faces + 3], refs[n_faces + 3 :],
    )
    for n, face in enumerate(mean_layers(read_all(mean_ref))):
        for c in range(3):
            mean_faces_ref[n, c] = face[c]
    state = read_all(les_ref)
    rate = les_rate(state, load_faces(face_refs, counts, 0, 5))
    section = [s + r for s, r in zip(state, rate)]
    for c in range(5):
        section_ref[c] = section[c]
    rate = acoustic_rate(
        read_all(wave_ref), read_all(mean_ref), load_faces(face_refs, counts, 5, 9),
        deriv_ref[...], (high_ref[...], low_ref[...]),
    )
    for c in range(4):
        rate_ref[c] = rate[c]
    store_faces(section + [wave_ref[0] + acoustic_step * rate[0]], out_refs, counts)


def source_kernel(counts, n_faces, tile_ref, wave_ref, rate_ref, *refs):
    n_pieces = len(partners(counts[0]))
    pieces = [None] * n_pieces
    for ref, k in zip(refs, sending_sets(n_pieces)):
        pieces[k] = ref
    refs = refs[n_pieces:]
    ready_faces, source_ref, face_refs = refs[:n_faces], refs[n_faces], refs[n_faces + 1 :]
    quarter = lane((8, 128)) // 32
    tile_high, tile_low = tile_ref[0], tile_ref[1]
    total = None
    for s in range((n_pieces + 3) // 4):
        count = min(4, n_pieces - 4 * s)

        def gathered(q, t):
            value = jnp.full((8, 128), -1.0 if q == 6 else 0.0, f32)
            for r in range(count):
                value = jnp.where(quarter == (r + t) % 4, pieces[4 * s + r][q], value)
            return value

        here = [gathered(6, 0).astype(jnp.int32) == slot for slot in range(16)]
        chosen_high, chosen_low = [
            jnp.concatenate([jnp.where(h, part, 0.0) for h in here], axis=0).astype(jnp.bfloat16)
            for part in (tile_high, tile_low)
        ]
        data = []
        for k in range(24):
            piece = gathered(k // 4, k % 4)
            data.append(pltpu.roll(piece, 128 - 32 * (k % 4), 1) if k % 4 else piece)
        data = jnp.concatenate(data, axis=0)
        high = data.astype(jnp.bfloat16)
        low = (data - high.astype(f32)).astype(jnp.bfloat16)
        dot = functools.partial(
            lax.dot_general,
            dimension_numbers=(((1,), (1,)), ((), ())),
            preferred_element_type=f32,
        )
        moved = dot(high, chosen_high) + (dot(low, chosen_high) + dot(high, chosen_low))
        total = moved if total is None else total + moved
    source = [total[64 * c : 64 * c + 64].reshape(8, 8, 128) for c in range(3)]
    middle = []
    for c in range(3):
        source_ref[c] = source[c]
        middle.append(wave_ref[1 + c] + acoustic_step * (rate_ref[1 + c] + source[c]))
    for ready, face in zip(ready_faces, face_refs):
        face[0:6] = ready[...]
    store_faces(middle, [face.at[6:9] for face in face_refs], counts)


def inner_kernel(
    deriv_ref, high_ref, low_ref, les_ref, section_ref, wave_ref, rate_ref, mean_ref, source_ref,
    les_base_ref, wave_base_ref, source_out, sem,
):
    copy = pltpu.make_async_copy(source_ref, source_out, sem)
    copy.start()
    section = read_all(section_ref)
    rate = les_rate(section, None)
    for c in range(5):
        les_base_ref[c] = 0.5 * ((les_ref[c] + section[c]) + rate[c])
    first = read_all(rate_ref)
    middle = [wave_ref[0] + acoustic_step * first[0]]
    for c in range(1, 4):
        middle.append(wave_ref[c] + acoustic_step * (first[c] + source_ref[c - 1]))
    rate = acoustic_rate(
        middle, read_all(mean_ref), None, deriv_ref[...], (high_ref[...], low_ref[...])
    )
    for c in range(4):
        total = rate[c] + source_ref[c - 1] if c else rate[c]
        wave_base_ref[c] = 0.5 * (wave_ref[c] + middle[c] + acoustic_step * total)
    copy.wait()


def add_layers(counts, chosen, face_refs, mean_faces_ref, les_base_ref, wave_base_ref, put):
    layers = les_outer(load_faces(face_refs, counts, 0, 5, chosen))
    for c in range(5):
        part = [layer and (0.5 * layer[0][c], 0.5 * layer[1][c]) for layer in layers]
        put(c, with_layers(les_base_ref[c], part))
    mean_faces = [[mean_faces_ref[n, c] for c in range(3)] for n in range(6)]
    layers = acoustic_outer(mean_faces, load_faces(face_refs, counts, 5, 9, chosen))
    step = 0.5 * acoustic_step
    for c in range(4):
        part = [layer and (step * layer[0][c], step * layer[1][c]) for layer in layers]
        put(5 + c, with_layers(wave_base_ref[c], part))


def z_faces(faces, counts):
    holds = [any(axis == 2 for axis, _ in pair) for pair in slots(counts)]
    return [face if hold else None for face, hold in zip(faces, holds)]


def z_kernel(counts, present, les_base_ref, wave_base_ref, mean_faces_ref, *refs):
    refs = list(refs)
    face_refs = [refs.pop(0) if here else None for here in present]
    les_ref, wave_ref = refs

    def put(c, planes):
        for x, plane in enumerate(planes):
            if c < 5:
                les_ref[c, x] = plane
            else:
                wave_ref[c - 5, x] = plane

    add_layers(counts, (2,), face_refs, mean_faces_ref, les_base_ref, wave_base_ref, put)


def last_kernel(counts, n_faces, les_base_ref, wave_base_ref, mean_faces_ref, *refs):
    face_refs, (les_out, wave_out, les_ref, wave_ref, sems) = (
        refs[:n_faces], refs[n_faces:],
    )
    copies = []

    def put(c, planes):
        kept, target = (les_ref.at[c], les_out.at[c]) if c < 5 else (
            wave_ref.at[c - 5], wave_out.at[c - 5]
        )
        for x, plane in enumerate(planes):
            kept[x] = plane
        copies.append(pltpu.make_async_copy(kept, target, sems.at[c]))
        copies[-1].start()

    add_layers(counts, (0, 1), face_refs, mean_faces_ref, les_base_ref, wave_base_ref, put)
    for copy in copies:
        copy.wait()


VMEM = pl.BlockSpec(memory_space=pltpu.VMEM)


HBM = pl.BlockSpec(memory_space=pltpu.HBM)


def call(kernel, in_specs, out_shapes, name, cost, scratch=(), out_spec=None):
    return pl.pallas_call(
        kernel,
        in_specs=in_specs,
        out_specs=out_spec or [VMEM] * len(out_shapes),
        out_shape=out_shapes,
        scratch_shapes=list(scratch),
        name=name,
        cost_estimate=pl.CostEstimate(flops=cost, bytes_accessed=800000, transcendentals=0),
        compiler_params=pltpu.CompilerParams(vmem_limit_bytes=24 * 1024 * 1024),
    )


def local(counts, les, wave, mean, projection, owner, slot):
    shape = les.shape[1:]
    faces = face_shapes(counts, 9)
    n_faces = len(faces)
    like = lambda n: jax.ShapeDtypeStruct((n,) + shape, f32)

    table = derivative_matrix()
    deriv = jnp.asarray(table, f32)
    along_z = np.kron(np.eye(16), table.T).astype(np.float32)
    high = along_z.astype(jnp.bfloat16)
    low = (along_z - high.astype(np.float32)).astype(jnp.bfloat16)
    tables = (deriv, jnp.asarray(high), jnp.asarray(low))

    arguments = (les, wave, owner, slot, projection)
    les, wave, owner, slot, projection, *sent = call(
        functools.partial(load_kernel, counts),
        [HBM] * 5,
        [jax.ShapeDtypeStruct(a.shape, a.dtype) for a in arguments] + faces,
        "load_and_faces",
        100000,
        [pltpu.SemaphoreType.DMA((5,))],
    )(*(pltpu.with_memory_space_constraint(a, pltpu.HBM) for a in arguments))
    got = exchange(sent, counts)

    sets = partners(counts[0])
    n_plans = 4 * ((len(sets) + 3) // 4)
    order, marks, along_x, along_y, tile = call(
        functools.partial(plan_kernel, counts),
        [VMEM] * 3,
        [
            jax.ShapeDtypeStruct((n_plans, 8, 128), jnp.int32),
            jax.ShapeDtypeStruct((len(sets), 8, 128), f32),
            jax.ShapeDtypeStruct((64, 8, 128), f32),
            jax.ShapeDtypeStruct((8, 8, 128), f32),
            jax.ShapeDtypeStruct((2, 8, 128), f32),
        ],
        "plan",
        1000000,
    )(owner, slot, projection)
    turning = list(call(vorticity_kernel, [VMEM], [like(3)] * 2, "vorticity", 1000000)(les))
    z_got = z_faces(got, counts)
    present = [face is not None for face in z_got]
    turning[1] = call(
        functools.partial(vorticity_z_kernel, counts, present),
        [VMEM] * (1 + sum(present)),
        [like(3)],
        "vorticity_z",
        1000000,
    )(turning[1], *(face for face in z_got if face is not None))[0]
    pieces = call(
        functools.partial(lamb_kernel, counts, n_faces),
        [VMEM] * (6 + n_faces),
        [jax.ShapeDtypeStruct((7, 8, 128), f32)] * len(sets),
        "lamb_blocks",
        10000000,
    )(order, marks, along_x, along_y, *turning, *got)
    moved = []
    for k in sending_sets(len(sets)):
        still = all(i == j for i, j in sets[k])
        moved.append(pieces[k] if still else lax.ppermute(pieces[k], "gx", sets[k]))
    section, rate, mean_faces, *ready_faces = call(
        functools.partial(first_kernel, counts, n_faces),
        [VMEM] * (6 + n_faces),
        [like(5), like(4), jax.ShapeDtypeStruct((6, 3, 8, 128), f32)] + face_shapes(counts, 6),
        "first_rates",
        40000000,
    )(*tables, les, wave, mean, *got)

    source, *sent = call(
        functools.partial(source_kernel, counts, n_faces),
        [VMEM] * (3 + len(moved) + n_faces),
        [like(3)] + faces,
        "source_and_faces",
        10000000,
    )(tile, wave, rate, *moved, *ready_faces)
    got = exchange(sent, counts)
    les_base, wave_base, source_out = call(
        inner_kernel,
        [VMEM] * 9,
        [like(5), like(4), like(3)],
        "second_rates_inner",
        40000000,
        [pltpu.SemaphoreType.DMA],
        out_spec=[VMEM, VMEM, HBM],
    )(*tables, les, section, wave, rate, mean, source)
    z_got = z_faces(got, counts)
    present = [face is not None for face in z_got]
    les_base, wave_base = call(
        functools.partial(z_kernel, counts, present),
        [VMEM] * (3 + sum(present)),
        [like(5), like(4)],
        "second_rates_z",
        1000000,
    )(les_base, wave_base, mean_faces, *(face for face in z_got if face is not None))
    les_next, wave_next = call(
        functools.partial(last_kernel, counts, n_faces),
        [VMEM] * (3 + n_faces),
        [like(5), like(4)],
        "second_rates_outer",
        4000000,
        [
            pltpu.VMEM(les.shape, f32),
            pltpu.VMEM(wave.shape, f32),
            pltpu.SemaphoreType.DMA((9,)),
        ],
        out_spec=[HBM, HBM],
    )(les_base, wave_base, mean_faces, *got)
    return les_next, source_out, wave_next


def solution(mesh):
    counts = tuple(mesh.shape[axis] for axis in axes)
    field = P(None, *axes)
    return jax.shard_map(
        functools.partial(local, counts),
        mesh=mesh,
        in_specs=(field, field, field, P(), P(*axes), P(*axes)),
        out_specs=(field, field, field),
        check_vma=False,
    )
```

```python
import functools

import jax
import jax.numpy as jnp
import numpy as np
from jax import lax
from jax.experimental import pallas as pl
from jax.experimental.pallas import tpu as pltpu
from jax.sharding import PartitionSpec as P

lobatto_points = np.array(
    [
        -1.0,
        -0.8717401485096066,
        -0.5917001814331423,
        -0.2092992179024789,
        0.2092992179024789,
        0.5917001814331423,
        0.8717401485096066,
        1.0,
    ]
)
flux_half = 0.08
gamma_less = 0.4
acoustic_step = 0.01
upwind_speed = 1.5
face_lift = 28.0
free_stream = (1.0, 0.0, 0.0, 0.0, 2.5)
axes = ("gx", "gy", "gz")
window = 4
f32 = jnp.float32


def derivative_matrix():
    points = lobatto_points
    products = [np.prod([points[i] - points[j] for j in range(8) if j != i]) for i in range(8)]
    matrix = np.zeros((8, 8))
    for i in range(8):
        for j in range(8):
            if j != i:
                matrix[i, j] = products[i] / (products[j] * (points[i] - points[j]))
        matrix[i, i] = -np.sum(matrix[i])
    return matrix


def sublane(shape):
    return lax.broadcasted_iota(jnp.int32, shape, len(shape) - 2)


def lane(shape):
    return lax.broadcasted_iota(jnp.int32, shape, len(shape) - 1)


def rolled(tile, amount, axis):
    amount = amount % tile.shape[axis]
    return pltpu.roll(tile, amount, axis) if amount else tile


def shifted(field, axis, step, outer=None):
    if axis == 0:
        outer = jnp.zeros((8, 128), f32) if outer is None else outer
        if step == 1:
            return jnp.concatenate([field[1:], outer[None]], axis=0)
        return jnp.concatenate([outer[None], field[:-1]], axis=0)
    count = (8, 128)[axis - 1]
    edge = count - 1 if step == 1 else 0
    at_edge = (sublane if axis == 1 else lane)((8, 128)) == edge
    planes = []
    for x in range(8):
        layer = 0.0 if outer is None else rolled(outer, edge - axis * x, axis - 1)
        planes.append(jnp.where(at_edge, layer, rolled(field[x], -step, axis - 1)))
    return jnp.stack(planes, axis=0)


def fluid(state):
    density, mx, my, mz, energy = [s + r for s, r in zip(state, free_stream)]
    inverse = 1.0 / density
    momentum = (mx, my, mz)
    velocity = [m * inverse for m in momentum]
    pressure = gamma_less * (
        energy - 0.5 * (mx * velocity[0] + my * velocity[1] + mz * velocity[2])
    )
    return momentum, velocity, pressure, energy + pressure


def split_flux(state, parts, axis, sign):
    momentum, velocity, pressure, enthalpy = parts
    speed = velocity[axis]
    flux = [momentum[axis]]
    for c in range(3):
        term = momentum[c] * speed
        flux.append(term + pressure if c == axis else term)
    flux.append(enthalpy * speed)
    if sign > 0:
        return [flux_half * (s + f) for s, f in zip(state, flux)]
    return [flux_half * (s - f) for s, f in zip(state, flux)]


def les_rate(state, halos):
    parts = fluid(state)
    total = [-6.0 * flux_half * s for s in state]
    for axis in range(3):
        ahead = split_flux(state, parts, axis, -1)
        behind = split_flux(state, parts, axis, 1)
        ahead_outer = behind_outer = [None] * 5
        if halos is not None:
            before, after = halos[axis]
            ahead_outer = split_flux(after, fluid(after), axis, -1)
            behind_outer = split_flux(before, fluid(before), axis, 1)
        for c in range(5):
            total[c] = total[c] + (
                shifted(ahead[c], axis, 1, ahead_outer[c])
                + shifted(behind[c], axis, -1, behind_outer[c])
            )
    return total


def les_outer(halos):
    return [
        halo
        and (
            split_flux(halo[0], fluid(halo[0]), axis, 1),
            split_flux(halo[1], fluid(halo[1]), axis, -1),
        )
        for axis, halo in enumerate(halos)
    ]


def with_layers(field, layers):
    row, column = sublane((8, 128)), lane((8, 128))
    along_z = layers[2]
    if along_z is not None:
        along_z = jnp.where(lax.rem(column, 2) == 0, along_z[0], rolled(along_z[1], -1, 1))
    planes = []
    for x in range(8):
        plane = field[x]
        if layers[0] is not None and x in (0, 7):
            plane = plane + layers[0][x // 7]
        if layers[1] is not None:
            low, high = layers[1]
            plane = plane + jnp.where(
                row == 0, rolled(low, -x, 0), jnp.where(row == 7, rolled(high, 7 - x, 0), 0.0)
            )
        if along_z is not None:
            ends = (column == 0) | (column == 127)
            plane = plane + jnp.where(ends, rolled(along_z, -2 * x, 1), 0.0)
        planes.append(plane)
    return planes


def wave_flux(state, mean, axis):
    speed = mean[axis]
    pressure = state[0]
    rows = [speed * pressure + state[1 + axis]]
    for c in range(3):
        term = speed * state[1 + c]
        rows.append(term + pressure if c == axis else term)
    return rows


def dot3(left, right):
    high = left.astype(jnp.bfloat16)
    low = (left - high.astype(f32)).astype(jnp.bfloat16)
    dot = functools.partial(jnp.dot, preferred_element_type=f32)
    return dot(high, right[0]) + (dot(low, right[0]) + dot(high, right[1]))


def acoustic_rate(state, mean, halos, deriv, along_z):
    shape = state[0].shape
    table = derivative_matrix()
    flux = wave_flux(state, mean, 0)
    if halos is None:
        halos = [([jnp.zeros((8, 128), f32)] * 4,) * 2] + [([None] * 4,) * 2] * 2
    before, after = halos[0]
    low_mean, high_mean = [m[0] for m in mean], [m[7] for m in mean]
    low_jump = [b - s[0] for b, s in zip(before, state)]
    high_jump = [a - s[7] for a, s in zip(after, state)]
    low_flux = wave_flux(low_jump, low_mean, 0)
    high_flux = wave_flux(high_jump, high_mean, 0)
    half, lift = 0.5 * face_lift, 0.5 * face_lift * upwind_speed
    total = []
    for c in range(4):
        planes = []
        for i in range(8):
            plane = -float(table[i, 0]) * flux[c][0]
            for a in range(1, 8):
                if abs(table[i, a]) > 1e-12:
                    plane = plane - float(table[i, a]) * flux[c][a]
            if i == 0:
                plane = plane + (half * low_flux[c] + lift * low_jump[c])
            if i == 7:
                plane = plane - (half * high_flux[c] - lift * high_jump[c])
            planes.append(plane)
        total.append(jnp.stack(planes, axis=0))
    flux = wave_flux(state, mean, 1)
    before, after = halos[1]
    row = sublane(shape)
    sign = jnp.where(row == 0, half, jnp.where(row == 7, -half, 0.0))
    jump = []
    for s, b, a in zip(state, before, after):
        planes = []
        for x in range(8):
            low = 0.0 if b is None else rolled(b, -x, 0)
            high = 0.0 if a is None else rolled(a, 7 - x, 0)
            planes.append(jnp.where(row[x] == 0, low, jnp.where(row[x] == 7, high, s[x])) - s[x])
        jump.append(jnp.stack(planes, axis=0))
    jump_flux = wave_flux(jump, mean, 1)
    for c in range(4):
        change = lift * jump[c] + sign * jump_flux[c]
        for b in range(8):
            change = change - deriv[:, b : b + 1][None] * flux[c][:, b : b + 1, :]
        total[c] = total[c] + change
    flux = wave_flux(state, mean, 2)
    before, after = halos[2]
    column = lane(shape)
    place = lax.rem(column, 8)
    sign = jnp.where(place == 0, half, jnp.where(place == 7, -half, 0.0))
    jump = [
        jnp.where(
            place == 0,
            shifted(s, 2, -1, b),
            jnp.where(place == 7, shifted(s, 2, 1, a), s),
        )
        - s
        for s, b, a in zip(state, before, after)
    ]
    jump_flux = wave_flux(jump, mean, 2)
    for c in range(4):
        slope = dot3(flux[c].reshape(64, 128), along_z).reshape(shape)
        total[c] = total[c] + (lift * jump[c] + sign * jump_flux[c] - slope)
    return total


def mean_layers(mean):
    return [
        [m[0] for m in mean],
        [m[7] for m in mean],
        [m[:, 0, :] for m in mean],
        [m[:, 7, :] for m in mean],
        [z_layer(m, jnp.int32(0)) for m in mean],
        [z_layer(m, jnp.int32(127)) for m in mean],
    ]


def acoustic_outer(mean_faces, halos):
    half, lift = 0.5 * face_lift, 0.5 * face_lift * upwind_speed
    layers = []
    for axis, halo in enumerate(halos):
        if halo is None:
            layers.append(None)
            continue
        before, after = halo
        low_flux = wave_flux(before, mean_faces[2 * axis], axis)
        high_flux = wave_flux(after, mean_faces[2 * axis + 1], axis)
        layers.append(
            (
                [half * f + lift * b for f, b in zip(low_flux, before)],
                [lift * a - half * f for f, a in zip(high_flux, after)],
            )
        )
    return layers


def tile_rows(matrix):
    spread = (lax.rem(lane((8, 128)), 8) == sublane((8, 128))).astype(f32)
    return jnp.dot(
        matrix, spread, precision=lax.Precision.HIGHEST, preferred_element_type=f32
    )


def pairings(count):
    sets = []
    for first in (0, 1):
        pairs = [(i, i + 1) for i in range(first, count - 1, 2)]
        if pairs:
            sets.append(pairs)
    return sets


def slots(counts):
    found = [(axis, n) for axis in range(3) for n in range(len(pairings(counts[axis])))]
    lower = ((2, 1), (2, 0), (0, 1), (1, 0), (1, 1), (0, 0))
    upper = ((2, 1), (0, 1), (2, 0), (0, 0), (1, 1), (1, 0))
    lower = [swap for swap in lower if swap in found]
    upper = [swap for swap in upper if swap in found] if counts[1] == 4 else lower
    return list(zip(lower, upper))


def in_upper_half(counts):
    return lax.axis_index("gy") >= counts[1] // 2


def routes(counts):
    places = [(x, y, z) for x in range(counts[0]) for y in range(counts[1]) for z in range(counts[2])]
    number = {place: n for n, place in enumerate(places)}

    def partner(place, axis, n):
        pairs = pairings(counts[axis])[n]
        swap = dict(pairs + [(j, i) for i, j in pairs])
        alone = [i for i in range(counts[axis]) if i not in swap]
        spare = 0 if axis else 2
        other = list(place)
        if place[axis] in swap:
            other[axis] = swap[place[axis]]
        elif axis == 0 and len(alone) == 2:
            other[axis] = sum(alone) - place[axis]
        elif counts[spare] % 2 == 0:
            other[spare] = place[spare] ^ 1
        return number[tuple(other)]

    return [
        [
            (number[place], partner(place, *(upper if place[1] >= counts[1] // 2 else lower)))
            for place in places
        ]
        for lower, upper in slots(counts)
    ]


def z_layer(field, at):
    packed = jnp.zeros((8, 128), f32)
    column = lane((8, 128))
    for x in range(8):
        turned = pltpu.roll(field[x], lax.rem(2 * x - at + 128, 128), 1)
        packed = jnp.where(column == 2 * x, turned, packed)
    return packed


def store_faces(fields, out_refs, counts):
    high_half = in_upper_half(counts)
    for c, field in enumerate(fields):
        faces = {}
        for axis in range(3):
            even = lax.rem(lax.axis_index(axes[axis]), 2) == 0
            if axis == 0:
                low, high = field[0], field[7]
            elif axis == 1:
                low, high = field[:, 0, :], field[:, 7, :]
            for n in range(len(pairings(counts[axis]))):
                last = even == (n == 0)
                if axis == 2:
                    faces[axis, n] = z_layer(field, jnp.where(last, 127, 0))
                else:
                    faces[axis, n] = jnp.where(last, high, low)
        for ref, (lower, upper) in zip(out_refs, slots(counts)):
            if lower == upper:
                ref[c] = faces[lower]
            else:
                ref[c] = jnp.where(high_half, faces[upper], faces[lower])


def load_faces(in_refs, counts, first, last, chosen=(0, 1, 2)):
    high_half = in_upper_half(counts)
    lower, upper = zip(*slots(counts))
    halos = []
    for axis in range(3):
        if axis not in chosen:
            halos.append(None)
            continue
        place = lax.axis_index(axes[axis])
        even = lax.rem(place, 2) == 0
        got = []
        for n in range(len(pairings(counts[axis]))):
            a, b = in_refs[lower.index((axis, n))], in_refs[upper.index((axis, n))]
            got.append(
                [a[c] if a is b else jnp.where(high_half, b[c], a[c]) for c in range(first, last)]
            )
        while len(got) < 2:
            got.append([jnp.zeros((8, 128), f32)] * (last - first))
        before = [jnp.where(place == 0, 0.0, jnp.where(even, b, a)) for a, b in zip(*got)]
        after = [
            jnp.where(place == counts[axis] - 1, 0.0, jnp.where(even, a, b))
            for a, b in zip(*got)
        ]
        halos.append((before, after))
    return halos


def face_shapes(counts, width):
    total = sum(len(pairings(count)) for count in counts)
    return [jax.ShapeDtypeStruct((width, 8, 128), f32)] * total


def exchange(faces, counts):
    return [lax.ppermute(face, axes, way) for face, way in zip(faces, routes(counts))]


def read_all(ref):
    return [ref[c] for c in range(ref.shape[0])]


def load_kernel(counts, *refs):
    sources, targets, out_refs, sems = refs[:5], refs[5:10], refs[10:-1], refs[-1]
    copies = [
        pltpu.make_async_copy(source, target, sems.at[n])
        for n, (source, target) in enumerate(zip(sources, targets))
    ]
    for copy in copies:
        copy.start()
    for copy, target, first in zip(copies, targets, (0, 5)):
        copy.wait()
        count = target.shape[0]
        store_faces(read_all(target), [ref.at[first : first + count] for ref in out_refs], counts)
    for copy in copies[2:]:
        copy.wait()


def partners(count):
    if count == window:
        return [[(i, i ^ mask) for i in range(count)] for mask in range(count)]
    turns = sorted({d % count for d in range(1 - window, window)})
    return [[(i, (i + turn) % count) for i in range(count)] for turn in turns]


def sending_sets(count):
    return [3, 2, 1, 0] if count == window else list(range(count))


def plan_kernel(
    counts, owner_ref, slot_ref, proj_ref, order_ref, marks_ref, along_x_ref, along_y_ref, tile_ref
):
    count = counts[0]
    n_sets = len(partners(count))
    own = lax.axis_index("gx")
    n_blocks = owner_ref.shape[-1]
    square = (n_blocks, n_blocks)
    block, other = sublane(square), lane(square)

    def spread(ref):
        by_lane = jnp.broadcast_to(ref[0], square)
        here = jnp.where(block == other, by_lane, 0).astype(f32)
        return by_lane, jnp.sum(here, axis=1, keepdims=True).astype(jnp.int32)

    def group_of(owner):
        if count == window:
            return lax.bitwise_xor(owner, own)
        turn = lax.rem(owner - own + count, count)
        if n_sets == count:
            return turn
        return jnp.where(turn < window, turn, turn - (count - n_sets))

    owner_by_lane, owner = spread(owner_ref)
    slot = spread(slot_ref)[1]
    group = group_of(owner)
    before = (group_of(owner_by_lane) == group) & (other < block)
    taken = jnp.sum(before.astype(f32), axis=1, keepdims=True).astype(jnp.int32)
    wide = (n_blocks, 128)
    place = jnp.broadcast_to(group * window + taken, wide)
    column = lane((8, 128))
    quarter = column // 32
    for s in range((n_sets + 3) // 4):
        here = place - 16 * s == lane(wide) // 8
        label = jnp.sum(jnp.where(here, (slot + 1).astype(f32), 0.0), axis=0, keepdims=True) - 1.0
        source = jnp.sum(
            jnp.where(here, (8 * sublane(wide)).astype(f32), 0.0), axis=0, keepdims=True
        )
        labels = jnp.broadcast_to(label, (8, 128))
        order = jnp.broadcast_to(source, (8, 128)).astype(jnp.int32) + lax.rem(column, 8)
        for t in range(4):
            order_ref[4 * s + t] = rolled(order, 32 * t, 1)
        for r in range(min(4, n_sets - 4 * s)):
            marks = labels
            for t in range(1, 4):
                marks = jnp.where(quarter == (r + t) % 4, rolled(labels, 32 * t, 1), marks)
            marks_ref[4 * s + r] = marks
    proj = proj_ref[...]
    for a in range(8):
        along_y = jnp.broadcast_to(proj[:, a : a + 1], (8, 128))
        along_y_ref[a] = along_y
        for i in range(8):
            along_x_ref[8 * i + a] = jnp.broadcast_to(along_y[i : i + 1], (8, 128))
    tile = tile_rows(proj)
    high = tile.astype(jnp.bfloat16).astype(f32)
    tile_ref[0] = high
    tile_ref[1] = tile - high


def speeds(state):
    inverse = 1.0 / (state[0] + 1.0)
    return [state[c] * inverse for c in (1, 2, 3)]


def vorticity_kernel(les_ref, velocity_ref, vort_ref):
    velocity = speeds([les_ref[c] for c in range(4)])

    def slope(c, axis):
        return shifted(velocity[c], axis, 1) - shifted(velocity[c], axis, -1)

    vort = [slope(2, 1) - slope(1, 2), slope(0, 2) - slope(2, 0), slope(1, 0) - slope(0, 1)]
    for c in range(3):
        velocity_ref[c] = velocity[c]
        vort_ref[c] = vort[c]


def vorticity_z_kernel(counts, present, vort_ref, *refs):
    refs = list(refs)
    face_refs = [refs.pop(0) if here else None for here in present]
    (out_ref,) = refs
    before, after = [speeds(layer) for layer in load_faces(face_refs, counts, 0, 4, (2,))[2]]
    for c, layer in ((0, (before[1], -after[1])), (1, (-before[0], after[0]))):
        for x, plane in enumerate(with_layers(vort_ref[c], (None, None, layer))):
            out_ref[c, x] = plane
    out_ref[2] = vort_ref[2]


def lamb_kernel(
    counts, n_faces, order_ref, marks_ref, along_x_ref, along_y_ref, velocity_ref, vort_ref, *refs
):
    face_refs, out_refs = refs[:n_faces], refs[n_faces:]
    outer = [
        halo and (speeds(halo[0]), speeds(halo[1]))
        for halo in load_faces(face_refs, counts, 0, 4, (0, 1))
    ]

    def rise(c, axis):
        return -outer[axis][0][c], outer[axis][1][c]

    def fall(c, axis):
        return outer[axis][0][c], -outer[axis][1][c]

    layers = [
        (None, rise(2, 1), None),
        (fall(2, 0), None, None),
        (rise(1, 0), fall(0, 1), None),
    ]
    vort = [0.5 * jnp.stack(with_layers(vort_ref[c], layers[c]), axis=0) for c in range(3)]
    velocity = read_all(velocity_ref)
    lamb = [
        vort[1] * velocity[2] - vort[2] * velocity[1],
        vort[2] * velocity[0] - vort[0] * velocity[2],
        vort[0] * velocity[1] - vort[1] * velocity[0],
    ]
    blocks = []
    for field in lamb:
        along_y = along_y_ref[0][None] * field[:, 0:1, :]
        for b in range(1, 8):
            along_y = along_y + along_y_ref[b][None] * field[:, b : b + 1, :]
        for i in range(8):
            plane = along_x_ref[8 * i] * along_y[0]
            for a in range(1, 8):
                plane = plane + along_x_ref[8 * i + a] * along_y[a]
            blocks.append(plane)

    quarter = lane((8, 128)) // 32
    for s in range((len(out_refs) + 3) // 4):
        ordered = [
            jnp.take_along_axis(
                block, order_ref[4 * s + k % 4], axis=1, mode="promise_in_bounds"
            )
            for k, block in enumerate(blocks)
        ]
        for r in range(min(4, len(out_refs) - 4 * s)):
            out = out_refs[4 * s + r]
            for q in range(6):
                packed = ordered[4 * q]
                for t in range(1, 4):
                    packed = jnp.where(quarter == (r + t) % 4, ordered[4 * q + t], packed)
                out[q] = packed
            out[6] = marks_ref[4 * s + r]


def first_kernel(
    counts, n_faces, deriv_ref, high_ref, low_ref, les_ref, wave_ref, mean_ref, *refs
):
    face_refs, (section_ref, rate_ref, mean_faces_ref), out_refs = (
        refs[:n_faces], refs[n_faces : n_faces + 3], refs[n_faces + 3 :],
    )
    for n, face in enumerate(mean_layers(read_all(mean_ref))):
        for c in range(3):
            mean_faces_ref[n, c] = face[c]
    state = read_all(les_ref)
    rate = les_rate(state, load_faces(face_refs, counts, 0, 5))
    section = [s + r for s, r in zip(state, rate)]
    for c in range(5):
        section_ref[c] = section[c]
    rate = acoustic_rate(
        read_all(wave_ref), read_all(mean_ref), load_faces(face_refs, counts, 5, 9),
        deriv_ref[...], (high_ref[...], low_ref[...]),
    )
    for c in range(4):
        rate_ref[c] = rate[c]
    store_faces(section + [wave_ref[0] + acoustic_step * rate[0]], out_refs, counts)


def source_kernel(counts, n_faces, tile_ref, wave_ref, rate_ref, *refs):
    n_pieces = len(partners(counts[0]))
    pieces = [None] * n_pieces
    for ref, k in zip(refs, sending_sets(n_pieces)):
        pieces[k] = ref
    refs = refs[n_pieces:]
    ready_faces, source_ref, face_refs = refs[:n_faces], refs[n_faces], refs[n_faces + 1 :]
    quarter = lane((8, 128)) // 32
    tile_high, tile_low = tile_ref[0], tile_ref[1]
    total = None
    for s in range((n_pieces + 3) // 4):
        count = min(4, n_pieces - 4 * s)

        def gathered(q, t):
            value = jnp.full((8, 128), -1.0 if q == 6 else 0.0, f32)
            for r in range(count):
                value = jnp.where(quarter == (r + t) % 4, pieces[4 * s + r][q], value)
            return value

        here = [gathered(6, 0).astype(jnp.int32) == slot for slot in range(16)]
        chosen_high, chosen_low = [
            jnp.concatenate([jnp.where(h, part, 0.0) for h in here], axis=0).astype(jnp.bfloat16)
            for part in (tile_high, tile_low)
        ]
        data = []
        for k in range(24):
            piece = gathered(k // 4, k % 4)
            data.append(pltpu.roll(piece, 128 - 32 * (k % 4), 1) if k % 4 else piece)
        data = jnp.concatenate(data, axis=0)
        high = data.astype(jnp.bfloat16)
        low = (data - high.astype(f32)).astype(jnp.bfloat16)
        dot = functools.partial(
            lax.dot_general,
            dimension_numbers=(((1,), (1,)), ((), ())),
            preferred_element_type=f32,
        )
        moved = dot(high, chosen_high) + (dot(low, chosen_high) + dot(high, chosen_low))
        total = moved if total is None else total + moved
    source = [total[64 * c : 64 * c + 64].reshape(8, 8, 128) for c in range(3)]
    middle = []
    for c in range(3):
        source_ref[c] = source[c]
        middle.append(wave_ref[1 + c] + acoustic_step * (rate_ref[1 + c] + source[c]))
    for ready, face in zip(ready_faces, face_refs):
        face[0:6] = ready[...]
    store_faces(middle, [face.at[6:9] for face in face_refs], counts)


def inner_kernel(
    deriv_ref, high_ref, low_ref, les_ref, section_ref, wave_ref, rate_ref, mean_ref, source_ref,
    les_base_ref, wave_base_ref, source_out, sem,
):
    copy = pltpu.make_async_copy(source_ref, source_out, sem)
    copy.start()
    section = read_all(section_ref)
    rate = les_rate(section, None)
    for c in range(5):
        les_base_ref[c] = 0.5 * ((les_ref[c] + section[c]) + rate[c])
    first = read_all(rate_ref)
    middle = [wave_ref[0] + acoustic_step * first[0]]
    for c in range(1, 4):
        middle.append(wave_ref[c] + acoustic_step * (first[c] + source_ref[c - 1]))
    rate = acoustic_rate(
        middle, read_all(mean_ref), None, deriv_ref[...], (high_ref[...], low_ref[...])
    )
    for c in range(4):
        total = rate[c] + source_ref[c - 1] if c else rate[c]
        wave_base_ref[c] = 0.5 * (wave_ref[c] + middle[c] + acoustic_step * total)
    copy.wait()


def add_layers(counts, chosen, face_refs, mean_faces_ref, les_base_ref, wave_base_ref, put):
    mean_faces = [[mean_faces_ref[n, c] for c in range(3)] for n in range(6)]
    layers = acoustic_outer(mean_faces, load_faces(face_refs, counts, 5, 9, chosen))
    step = 0.5 * acoustic_step
    for c in range(4):
        part = [layer and (step * layer[0][c], step * layer[1][c]) for layer in layers]
        put(5 + c, with_layers(wave_base_ref[c], part))
    layers = les_outer(load_faces(face_refs, counts, 0, 5, chosen))
    for c in range(5):
        part = [layer and (0.5 * layer[0][c], 0.5 * layer[1][c]) for layer in layers]
        put(c, with_layers(les_base_ref[c], part))


def z_faces(faces, counts):
    holds = [any(axis == 2 for axis, _ in pair) for pair in slots(counts)]
    return [face if hold else None for face, hold in zip(faces, holds)]


def z_kernel(counts, present, les_base_ref, wave_base_ref, mean_faces_ref, *refs):
    refs = list(refs)
    face_refs = [refs.pop(0) if here else None for here in present]
    les_ref, wave_ref = refs

    def put(c, planes):
        for x, plane in enumerate(planes):
            if c < 5:
                les_ref[c, x] = plane
            else:
                wave_ref[c - 5, x] = plane

    add_layers(counts, (2,), face_refs, mean_faces_ref, les_base_ref, wave_base_ref, put)


def last_kernel(counts, n_faces, les_base_ref, wave_base_ref, mean_faces_ref, *refs):
    face_refs, (les_out, wave_out, les_ref, wave_ref, sems) = (
        refs[:n_faces], refs[n_faces:],
    )
    copies = []

    def put(c, planes):
        kept, target = (les_ref.at[c], les_out.at[c]) if c < 5 else (
            wave_ref.at[c - 5], wave_out.at[c - 5]
        )
        for x, plane in enumerate(planes):
            kept[x] = plane
        copies.append(pltpu.make_async_copy(kept, target, sems.at[c]))
        copies[-1].start()

    add_layers(counts, (0, 1), face_refs, mean_faces_ref, les_base_ref, wave_base_ref, put)
    for copy in copies:
        copy.wait()


VMEM = pl.BlockSpec(memory_space=pltpu.VMEM)


HBM = pl.BlockSpec(memory_space=pltpu.HBM)


def call(kernel, in_specs, out_shapes, name, cost, scratch=(), out_spec=None):
    return pl.pallas_call(
        kernel,
        in_specs=in_specs,
        out_specs=out_spec or [VMEM] * len(out_shapes),
        out_shape=out_shapes,
        scratch_shapes=list(scratch),
        name=name,
        cost_estimate=pl.CostEstimate(flops=cost, bytes_accessed=800000, transcendentals=0),
        compiler_params=pltpu.CompilerParams(vmem_limit_bytes=24 * 1024 * 1024),
    )


def local(counts, les, wave, mean, projection, owner, slot):
    shape = les.shape[1:]
    faces = face_shapes(counts, 9)
    n_faces = len(faces)
    like = lambda n: jax.ShapeDtypeStruct((n,) + shape, f32)

    table = derivative_matrix()
    deriv = jnp.asarray(table, f32)
    along_z = np.kron(np.eye(16), table.T).astype(np.float32)
    high = along_z.astype(jnp.bfloat16)
    low = (along_z - high.astype(np.float32)).astype(jnp.bfloat16)
    tables = (deriv, jnp.asarray(high), jnp.asarray(low))

    arguments = (les, wave, owner, slot, projection)
    les, wave, owner, slot, projection, *sent = call(
        functools.partial(load_kernel, counts),
        [HBM] * 5,
        [jax.ShapeDtypeStruct(a.shape, a.dtype) for a in arguments] + faces,
        "load_and_faces",
        100000,
        [pltpu.SemaphoreType.DMA((5,))],
    )(*(pltpu.with_memory_space_constraint(a, pltpu.HBM) for a in arguments))
    got = exchange(sent, counts)

    sets = partners(counts[0])
    n_plans = 4 * ((len(sets) + 3) // 4)
    order, marks, along_x, along_y, tile = call(
        functools.partial(plan_kernel, counts),
        [VMEM] * 3,
        [
            jax.ShapeDtypeStruct((n_plans, 8, 128), jnp.int32),
            jax.ShapeDtypeStruct((len(sets), 8, 128), f32),
            jax.ShapeDtypeStruct((64, 8, 128), f32),
            jax.ShapeDtypeStruct((8, 8, 128), f32),
            jax.ShapeDtypeStruct((2, 8, 128), f32),
        ],
        "plan",
        1000000,
    )(owner, slot, projection)
    turning = list(call(vorticity_kernel, [VMEM], [like(3)] * 2, "vorticity", 1000000)(les))
    z_got = z_faces(got, counts)
    present = [face is not None for face in z_got]
    turning[1] = call(
        functools.partial(vorticity_z_kernel, counts, present),
        [VMEM] * (1 + sum(present)),
        [like(3)],
        "vorticity_z",
        1000000,
    )(turning[1], *(face for face in z_got if face is not None))[0]
    pieces = call(
        functools.partial(lamb_kernel, counts, n_faces),
        [VMEM] * (6 + n_faces),
        [jax.ShapeDtypeStruct((7, 8, 128), f32)] * len(sets),
        "lamb_blocks",
        10000000,
    )(order, marks, along_x, along_y, *turning, *got)
    moved = []
    for k in sending_sets(len(sets)):
        still = all(i == j for i, j in sets[k])
        moved.append(pieces[k] if still else lax.ppermute(pieces[k], "gx", sets[k]))
    section, rate, mean_faces, *ready_faces = call(
        functools.partial(first_kernel, counts, n_faces),
        [VMEM] * (6 + n_faces),
        [like(5), like(4), jax.ShapeDtypeStruct((6, 3, 8, 128), f32)] + face_shapes(counts, 6),
        "first_rates",
        40000000,
    )(*tables, les, wave, mean, *got)

    source, *sent = call(
        functools.partial(source_kernel, counts, n_faces),
        [VMEM] * (3 + len(moved) + n_faces),
        [like(3)] + faces,
        "source_and_faces",
        10000000,
    )(tile, wave, rate, *moved, *ready_faces)
    got = exchange(sent, counts)
    les_base, wave_base, source_out = call(
        inner_kernel,
        [VMEM] * 9,
        [like(5), like(4), like(3)],
        "second_rates_inner",
        40000000,
        [pltpu.SemaphoreType.DMA],
        out_spec=[VMEM, VMEM, HBM],
    )(*tables, les, section, wave, rate, mean, source)
    z_got = z_faces(got, counts)
    present = [face is not None for face in z_got]
    les_base, wave_base = call(
        functools.partial(z_kernel, counts, present),
        [VMEM] * (3 + sum(present)),
        [like(5), like(4)],
        "second_rates_z",
        1000000,
    )(les_base, wave_base, mean_faces, *(face for face in z_got if face is not None))
    les_next, wave_next = call(
        functools.partial(last_kernel, counts, n_faces),
        [VMEM] * (3 + n_faces),
        [like(5), like(4)],
        "second_rates_outer",
        4000000,
        [
            pltpu.VMEM(les.shape, f32),
            pltpu.VMEM(wave.shape, f32),
            pltpu.SemaphoreType.DMA((9,)),
        ],
        out_spec=[HBM, HBM],
    )(les_base, wave_base, mean_faces, *got)
    return les_next, source_out, wave_next


def solution(mesh):
    counts = tuple(mesh.shape[axis] for axis in axes)
    field = P(None, *axes)
    return jax.shard_map(
        functools.partial(local, counts),
        mesh=mesh,
        in_specs=(field, field, field, P(), P(*axes), P(*axes)),
        out_specs=(field, field, field),
        check_vma=False,
    )
```

```python
import functools

import jax
import jax.numpy as jnp
import numpy as np
from jax import lax
from jax.experimental import pallas as pl
from jax.experimental.pallas import tpu as pltpu
from jax.sharding import PartitionSpec as P

lobatto_points = np.array(
    [
        -1.0,
        -0.8717401485096066,
        -0.5917001814331423,
        -0.2092992179024789,
        0.2092992179024789,
        0.5917001814331423,
        0.8717401485096066,
        1.0,
    ]
)
flux_half = 0.08
gamma_less = 0.4
acoustic_step = 0.01
upwind_speed = 1.5
face_lift = 28.0
free_stream = (1.0, 0.0, 0.0, 0.0, 2.5)
axes = ("gx", "gy", "gz")
window = 4
f32 = jnp.float32


def derivative_matrix():
    points = lobatto_points
    products = [np.prod([points[i] - points[j] for j in range(8) if j != i]) for i in range(8)]
    matrix = np.zeros((8, 8))
    for i in range(8):
        for j in range(8):
            if j != i:
                matrix[i, j] = products[i] / (products[j] * (points[i] - points[j]))
        matrix[i, i] = -np.sum(matrix[i])
    return matrix


def sublane(shape):
    return lax.broadcasted_iota(jnp.int32, shape, len(shape) - 2)


def lane(shape):
    return lax.broadcasted_iota(jnp.int32, shape, len(shape) - 1)


def rolled(tile, amount, axis):
    amount = amount % tile.shape[axis]
    return pltpu.roll(tile, amount, axis) if amount else tile


def shifted(field, axis, step, outer=None):
    if axis == 0:
        outer = jnp.zeros((8, 128), f32) if outer is None else outer
        if step == 1:
            return jnp.concatenate([field[1:], outer[None]], axis=0)
        return jnp.concatenate([outer[None], field[:-1]], axis=0)
    count = (8, 128)[axis - 1]
    edge = count - 1 if step == 1 else 0
    at_edge = (sublane if axis == 1 else lane)((8, 128)) == edge
    planes = []
    for x in range(8):
        layer = 0.0 if outer is None else rolled(outer, edge - axis * x, axis - 1)
        planes.append(jnp.where(at_edge, layer, rolled(field[x], -step, axis - 1)))
    return jnp.stack(planes, axis=0)


def fluid(state):
    density, mx, my, mz, energy = [s + r for s, r in zip(state, free_stream)]
    inverse = 1.0 / density
    momentum = (mx, my, mz)
    velocity = [m * inverse for m in momentum]
    pressure = gamma_less * (
        energy - 0.5 * (mx * velocity[0] + my * velocity[1] + mz * velocity[2])
    )
    return momentum, velocity, pressure, energy + pressure


def split_flux(state, parts, axis, sign):
    momentum, velocity, pressure, enthalpy = parts
    speed = velocity[axis]
    flux = [momentum[axis]]
    for c in range(3):
        term = momentum[c] * speed
        flux.append(term + pressure if c == axis else term)
    flux.append(enthalpy * speed)
    if sign > 0:
        return [flux_half * (s + f) for s, f in zip(state, flux)]
    return [flux_half * (s - f) for s, f in zip(state, flux)]


def les_rate(state, halos):
    parts = fluid(state)
    total = [-6.0 * flux_half * s for s in state]
    for axis in range(3):
        ahead = split_flux(state, parts, axis, -1)
        behind = split_flux(state, parts, axis, 1)
        ahead_outer = behind_outer = [None] * 5
        if halos is not None:
            before, after = halos[axis]
            ahead_outer = split_flux(after, fluid(after), axis, -1)
            behind_outer = split_flux(before, fluid(before), axis, 1)
        for c in range(5):
            total[c] = total[c] + (
                shifted(ahead[c], axis, 1, ahead_outer[c])
                + shifted(behind[c], axis, -1, behind_outer[c])
            )
    return total


def les_outer(halos):
    return [
        halo
        and (
            split_flux(halo[0], fluid(halo[0]), axis, 1),
            split_flux(halo[1], fluid(halo[1]), axis, -1),
        )
        for axis, halo in enumerate(halos)
    ]


def with_layers(field, layers):
    row, column = sublane((8, 128)), lane((8, 128))
    along_z = layers[2]
    if along_z is not None:
        along_z = jnp.where(lax.rem(column, 2) == 0, along_z[0], rolled(along_z[1], -1, 1))
    planes = []
    for x in range(8):
        plane = field[x]
        if layers[0] is not None and x in (0, 7):
            plane = plane + layers[0][x // 7]
        if layers[1] is not None:
            low, high = layers[1]
            plane = plane + jnp.where(
                row == 0, rolled(low, -x, 0), jnp.where(row == 7, rolled(high, 7 - x, 0), 0.0)
            )
        if along_z is not None:
            ends = (column == 0) | (column == 127)
            plane = plane + jnp.where(ends, rolled(along_z, -2 * x, 1), 0.0)
        planes.append(plane)
    return planes


def wave_flux(state, mean, axis):
    speed = mean[axis]
    pressure = state[0]
    rows = [speed * pressure + state[1 + axis]]
    for c in range(3):
        term = speed * state[1 + c]
        rows.append(term + pressure if c == axis else term)
    return rows


def dot3(left, right):
    high = left.astype(jnp.bfloat16)
    low = (left - high.astype(f32)).astype(jnp.bfloat16)
    dot = functools.partial(jnp.dot, preferred_element_type=f32)
    return dot(high, right[0]) + (dot(low, right[0]) + dot(high, right[1]))


def acoustic_rate(state, mean, halos, deriv, along_z):
    shape = state[0].shape
    table = derivative_matrix()
    flux = wave_flux(state, mean, 0)
    if halos is None:
        halos = [([jnp.zeros((8, 128), f32)] * 4,) * 2] + [([None] * 4,) * 2] * 2
    before, after = halos[0]
    low_mean, high_mean = [m[0] for m in mean], [m[7] for m in mean]
    low_jump = [b - s[0] for b, s in zip(before, state)]
    high_jump = [a - s[7] for a, s in zip(after, state)]
    low_flux = wave_flux(low_jump, low_mean, 0)
    high_flux = wave_flux(high_jump, high_mean, 0)
    half, lift = 0.5 * face_lift, 0.5 * face_lift * upwind_speed
    total = []
    for c in range(4):
        planes = []
        for i in range(8):
            plane = -float(table[i, 0]) * flux[c][0]
            for a in range(1, 8):
                if abs(table[i, a]) > 1e-12:
                    plane = plane - float(table[i, a]) * flux[c][a]
            if i == 0:
                plane = plane + (half * low_flux[c] + lift * low_jump[c])
            if i == 7:
                plane = plane - (half * high_flux[c] - lift * high_jump[c])
            planes.append(plane)
        total.append(jnp.stack(planes, axis=0))
    flux = wave_flux(state, mean, 1)
    before, after = halos[1]
    row = sublane(shape)
    sign = jnp.where(row == 0, half, jnp.where(row == 7, -half, 0.0))
    jump = []
    for s, b, a in zip(state, before, after):
        planes = []
        for x in range(8):
            low = 0.0 if b is None else rolled(b, -x, 0)
            high = 0.0 if a is None else rolled(a, 7 - x, 0)
            planes.append(jnp.where(row[x] == 0, low, jnp.where(row[x] == 7, high, s[x])) - s[x])
        jump.append(jnp.stack(planes, axis=0))
    jump_flux = wave_flux(jump, mean, 1)
    for c in range(4):
        change = lift * jump[c] + sign * jump_flux[c]
        for b in range(8):
            change = change - deriv[:, b : b + 1][None] * flux[c][:, b : b + 1, :]
        total[c] = total[c] + change
    flux = wave_flux(state, mean, 2)
    before, after = halos[2]
    column = lane(shape)
    place = lax.rem(column, 8)
    sign = jnp.where(place == 0, half, jnp.where(place == 7, -half, 0.0))
    jump = [
        jnp.where(
            place == 0,
            shifted(s, 2, -1, b),
            jnp.where(place == 7, shifted(s, 2, 1, a), s),
        )
        - s
        for s, b, a in zip(state, before, after)
    ]
    jump_flux = wave_flux(jump, mean, 2)
    for c in range(4):
        slope = dot3(flux[c].reshape(64, 128), along_z).reshape(shape)
        total[c] = total[c] + (lift * jump[c] + sign * jump_flux[c] - slope)
    return total


def mean_layers(mean):
    return [
        [m[0] for m in mean],
        [m[7] for m in mean],
        [m[:, 0, :] for m in mean],
        [m[:, 7, :] for m in mean],
        [z_layer(m, jnp.int32(0)) for m in mean],
        [z_layer(m, jnp.int32(127)) for m in mean],
    ]


def acoustic_outer(mean_faces, halos):
    half, lift = 0.5 * face_lift, 0.5 * face_lift * upwind_speed
    layers = []
    for axis, halo in enumerate(halos):
        if halo is None:
            layers.append(None)
            continue
        before, after = halo
        low_flux = wave_flux(before, mean_faces[2 * axis], axis)
        high_flux = wave_flux(after, mean_faces[2 * axis + 1], axis)
        layers.append(
            (
                [half * f + lift * b for f, b in zip(low_flux, before)],
                [lift * a - half * f for f, a in zip(high_flux, after)],
            )
        )
    return layers


def tile_rows(matrix):
    spread = (lax.rem(lane((8, 128)), 8) == sublane((8, 128))).astype(f32)
    return jnp.dot(
        matrix, spread, precision=lax.Precision.HIGHEST, preferred_element_type=f32
    )


def pairings(count):
    sets = []
    for first in (0, 1):
        pairs = [(i, i + 1) for i in range(first, count - 1, 2)]
        if pairs:
            sets.append(pairs)
    return sets


def slots(counts):
    found = [(axis, n) for axis in range(3) for n in range(len(pairings(counts[axis])))]
    lower = ((2, 1), (2, 0), (0, 1), (1, 0), (1, 1), (0, 0))
    upper = ((2, 1), (0, 1), (2, 0), (0, 0), (1, 1), (1, 0))
    lower = [swap for swap in lower if swap in found]
    upper = [swap for swap in upper if swap in found] if counts[1] == 4 else lower
    return list(zip(lower, upper))


def in_upper_half(counts):
    return lax.axis_index("gy") >= counts[1] // 2


def routes(counts):
    places = [(x, y, z) for x in range(counts[0]) for y in range(counts[1]) for z in range(counts[2])]
    number = {place: n for n, place in enumerate(places)}

    def partner(place, axis, n):
        pairs = pairings(counts[axis])[n]
        swap = dict(pairs + [(j, i) for i, j in pairs])
        alone = [i for i in range(counts[axis]) if i not in swap]
        spare = 0 if axis else 2
        other = list(place)
        if place[axis] in swap:
            other[axis] = swap[place[axis]]
        elif axis == 0 and len(alone) == 2:
            other[axis] = sum(alone) - place[axis]
        elif counts[spare] % 2 == 0:
            other[spare] = place[spare] ^ 1
        return number[tuple(other)]

    return [
        [
            (number[place], partner(place, *(upper if place[1] >= counts[1] // 2 else lower)))
            for place in places
        ]
        for lower, upper in slots(counts)
    ]


def z_layer(field, at):
    packed = jnp.zeros((8, 128), f32)
    column = lane((8, 128))
    for x in range(8):
        turned = pltpu.roll(field[x], lax.rem(2 * x - at + 128, 128), 1)
        packed = jnp.where(column == 2 * x, turned, packed)
    return packed


def store_faces(fields, out_refs, counts, rows_ref=None):
    high_half = in_upper_half(counts)
    for c, field in enumerate(fields):
        faces = {}
        for axis in range(3):
            even = lax.rem(lax.axis_index(axes[axis]), 2) == 0
            if axis == 0:
                low, high = field[0], field[7]
            elif axis == 1:
                low, high = (
                (field[:, 0, :], field[:, 7, :])
                if rows_ref is None
                else [rows_ref[c, pl.ds(at, 8, stride=8), :] for at in (0, 7)]
            )
            for n in range(len(pairings(counts[axis]))):
                last = even == (n == 0)
                if axis == 2:
                    faces[axis, n] = z_layer(field, jnp.where(last, 127, 0))
                else:
                    faces[axis, n] = jnp.where(last, high, low)
        for ref, (lower, upper) in zip(out_refs, slots(counts)):
            if lower == upper:
                ref[c] = faces[lower]
            else:
                ref[c] = jnp.where(high_half, faces[upper], faces[lower])


def load_faces(in_refs, counts, first, last, chosen=(0, 1, 2)):
    high_half = in_upper_half(counts)
    lower, upper = zip(*slots(counts))
    halos = []
    for axis in range(3):
        if axis not in chosen:
            halos.append(None)
            continue
        place = lax.axis_index(axes[axis])
        even = lax.rem(place, 2) == 0
        got = []
        for n in range(len(pairings(counts[axis]))):
            a, b = in_refs[lower.index((axis, n))], in_refs[upper.index((axis, n))]
            got.append(
                [a[c] if a is b else jnp.where(high_half, b[c], a[c]) for c in range(first, last)]
            )
        while len(got) < 2:
            got.append([jnp.zeros((8, 128), f32)] * (last - first))
        before = [jnp.where(place == 0, 0.0, jnp.where(even, b, a)) for a, b in zip(*got)]
        after = [
            jnp.where(place == counts[axis] - 1, 0.0, jnp.where(even, a, b))
            for a, b in zip(*got)
        ]
        halos.append((before, after))
    return halos


def face_shapes(counts, width):
    total = sum(len(pairings(count)) for count in counts)
    return [jax.ShapeDtypeStruct((width, 8, 128), f32)] * total


def exchange(faces, counts):
    return [lax.ppermute(face, axes, way) for face, way in zip(faces, routes(counts))]


def read_all(ref):
    return [ref[c] for c in range(ref.shape[0])]


def load_kernel(counts, *refs):
    sources, targets, out_refs, sems = refs[:5], refs[5:10], refs[10:-1], refs[-1]
    copies = [
        pltpu.make_async_copy(source, target, sems.at[n])
        for n, (source, target) in enumerate(zip(sources, targets))
    ]
    for copy in copies:
        copy.start()
    for copy, target, first in zip(copies, targets, (0, 5)):
        copy.wait()
        count = target.shape[0]
        fields = [field.reshape(8, 8, 128) for field in read_all(target)]
        faces = [ref.at[first : first + count] for ref in out_refs]
        store_faces(fields, faces, counts, target)
    for copy in copies[2:]:
        copy.wait()


def partners(count):
    if count == window:
        return [[(i, i ^ mask) for i in range(count)] for mask in range(count)]
    turns = sorted({d % count for d in range(1 - window, window)})
    return [[(i, (i + turn) % count) for i in range(count)] for turn in turns]


def sending_sets(count):
    return [3, 2, 1, 0] if count == window else list(range(count))


def plan_kernel(
    counts, owner_ref, slot_ref, proj_ref, order_ref, marks_ref, along_x_ref, along_y_ref, tile_ref
):
    count = counts[0]
    n_sets = len(partners(count))
    own = lax.axis_index("gx")
    n_blocks = owner_ref.shape[-1]
    square = (n_blocks, n_blocks)
    block, other = sublane(square), lane(square)

    def spread(ref):
        by_lane = jnp.broadcast_to(ref[0], square)
        here = jnp.where(block == other, by_lane, 0).astype(f32)
        return by_lane, jnp.sum(here, axis=1, keepdims=True).astype(jnp.int32)

    def group_of(owner):
        if count == window:
            return lax.bitwise_xor(owner, own)
        turn = lax.rem(owner - own + count, count)
        if n_sets == count:
            return turn
        return jnp.where(turn < window, turn, turn - (count - n_sets))

    owner_by_lane, owner = spread(owner_ref)
    slot = spread(slot_ref)[1]
    group = group_of(owner)
    before = (group_of(owner_by_lane) == group) & (other < block)
    taken = jnp.sum(before.astype(f32), axis=1, keepdims=True).astype(jnp.int32)
    wide = (n_blocks, 128)
    place = jnp.broadcast_to(group * window + taken, wide)
    column = lane((8, 128))
    quarter = column // 32
    for s in range((n_sets + 3) // 4):
        here = place - 16 * s == lane(wide) // 8
        label = jnp.sum(jnp.where(here, (slot + 1).astype(f32), 0.0), axis=0, keepdims=True) - 1.0
        source = jnp.sum(
            jnp.where(here, (8 * sublane(wide)).astype(f32), 0.0), axis=0, keepdims=True
        )
        labels = jnp.broadcast_to(label, (8, 128))
        order = jnp.broadcast_to(source, (8, 128)).astype(jnp.int32) + lax.rem(column, 8)
        for t in range(4):
            order_ref[4 * s + t] = rolled(order, 32 * t, 1)
        for r in range(min(4, n_sets - 4 * s)):
            marks = labels
            for t in range(1, 4):
                marks = jnp.where(quarter == (r + t) % 4, rolled(labels, 32 * t, 1), marks)
            marks_ref[4 * s + r] = marks
    proj = proj_ref[...]
    for a in range(8):
        along_y = jnp.broadcast_to(proj[:, a : a + 1], (8, 128))
        along_y_ref[a] = along_y
        for i in range(8):
            along_x_ref[8 * i + a] = jnp.broadcast_to(along_y[i : i + 1], (8, 128))
    tile = tile_rows(proj)
    high = tile.astype(jnp.bfloat16).astype(f32)
    tile_ref[0] = high
    tile_ref[1] = tile - high


def speeds(state):
    inverse = 1.0 / (state[0] + 1.0)
    return [state[c] * inverse for c in (1, 2, 3)]


def vorticity_kernel(les_ref, velocity_ref, vort_ref):
    velocity = speeds([les_ref[c] for c in range(4)])

    def slope(c, axis):
        return shifted(velocity[c], axis, 1) - shifted(velocity[c], axis, -1)

    vort = [slope(2, 1) - slope(1, 2), slope(0, 2) - slope(2, 0), slope(1, 0) - slope(0, 1)]
    for c in range(3):
        velocity_ref[c] = velocity[c]
        vort_ref[c] = vort[c]


def vorticity_z_kernel(counts, present, vort_ref, *refs):
    refs = list(refs)
    face_refs = [refs.pop(0) if here else None for here in present]
    (out_ref,) = refs
    before, after = [speeds(layer) for layer in load_faces(face_refs, counts, 0, 4, (2,))[2]]
    for c, layer in ((0, (before[1], -after[1])), (1, (-before[0], after[0]))):
        for x, plane in enumerate(with_layers(vort_ref[c], (None, None, layer))):
            out_ref[c, x] = plane
    out_ref[2] = vort_ref[2]


def lamb_kernel(
    counts, n_faces, order_ref, marks_ref, along_x_ref, along_y_ref, velocity_ref, vort_ref, *refs
):
    face_refs, out_refs = refs[:n_faces], refs[n_faces:]
    outer = [
        halo and (speeds(halo[0]), speeds(halo[1]))
        for halo in load_faces(face_refs, counts, 0, 4, (0, 1))
    ]

    def rise(c, axis):
        return -outer[axis][0][c], outer[axis][1][c]

    def fall(c, axis):
        return outer[axis][0][c], -outer[axis][1][c]

    layers = [
        (None, rise(2, 1), None),
        (fall(2, 0), None, None),
        (rise(1, 0), fall(0, 1), None),
    ]
    vort = [0.5 * jnp.stack(with_layers(vort_ref[c], layers[c]), axis=0) for c in range(3)]
    velocity = read_all(velocity_ref)
    lamb = [
        vort[1] * velocity[2] - vort[2] * velocity[1],
        vort[2] * velocity[0] - vort[0] * velocity[2],
        vort[0] * velocity[1] - vort[1] * velocity[0],
    ]
    blocks = []
    for field in lamb:
        along_y = along_y_ref[0][None] * field[:, 0:1, :]
        for b in range(1, 8):
            along_y = along_y + along_y_ref[b][None] * field[:, b : b + 1, :]
        for i in range(8):
            plane = along_x_ref[8 * i] * along_y[0]
            for a in range(1, 8):
                plane = plane + along_x_ref[8 * i + a] * along_y[a]
            blocks.append(plane)

    quarter = lane((8, 128)) // 32
    for s in range((len(out_refs) + 3) // 4):
        ordered = [
            jnp.take_along_axis(block, order_ref[4 * s + k % 4], axis=1)
            for k, block in enumerate(blocks)
        ]
        for r in range(min(4, len(out_refs) - 4 * s)):
            out = out_refs[4 * s + r]
            for q in range(6):
                packed = ordered[4 * q]
                for t in range(1, 4):
                    packed = jnp.where(quarter == (r + t) % 4, ordered[4 * q + t], packed)
                out[q] = packed
            out[6] = marks_ref[4 * s + r]


def first_kernel(
    counts, n_faces, deriv_ref, high_ref, low_ref, les_ref, wave_ref, mean_ref, *refs
):
    face_refs, (section_ref, rate_ref, mean_faces_ref), out_refs = (
        refs[:n_faces], refs[n_faces : n_faces + 3], refs[n_faces + 3 :],
    )
    for n, face in enumerate(mean_layers(read_all(mean_ref))):
        for c in range(3):
            mean_faces_ref[n, c] = face[c]
    state = read_all(les_ref)
    rate = les_rate(state, load_faces(face_refs, counts, 0, 5))
    section = [s + r for s, r in zip(state, rate)]
    for c in range(5):
        section_ref[c] = section[c]
    rate = acoustic_rate(
        read_all(wave_ref), read_all(mean_ref), load_faces(face_refs, counts, 5, 9),
        deriv_ref[...], (high_ref[...], low_ref[...]),
    )
    for c in range(4):
        rate_ref[c] = rate[c]
    store_faces(section + [wave_ref[0] + acoustic_step * rate[0]], out_refs, counts)


def source_kernel(counts, n_faces, tile_ref, wave_ref, rate_ref, *refs):
    n_pieces = len(partners(counts[0]))
    pieces = [None] * n_pieces
    for ref, k in zip(refs, sending_sets(n_pieces)):
        pieces[k] = ref
    refs = refs[n_pieces:]
    ready_faces, source_ref, face_refs, rows_ref = (
        refs[:n_faces], refs[n_faces], refs[n_faces + 1 : -1], refs[-1],
    )
    quarter = lane((8, 128)) // 32
    tile_high, tile_low = tile_ref[0], tile_ref[1]
    total = None
    for s in range((n_pieces + 3) // 4):
        count = min(4, n_pieces - 4 * s)

        def gathered(q, t):
            value = jnp.full((8, 128), -1.0 if q == 6 else 0.0, f32)
            for r in range(count):
                value = jnp.where(quarter == (r + t) % 4, pieces[4 * s + r][q], value)
            return value

        here = [gathered(6, 0).astype(jnp.int32) == slot for slot in range(16)]
        chosen_high, chosen_low = [
            jnp.concatenate([jnp.where(h, part, 0.0) for h in here], axis=0).astype(jnp.bfloat16)
            for part in (tile_high, tile_low)
        ]
        data = []
        for k in range(24):
            piece = gathered(k // 4, k % 4)
            data.append(pltpu.roll(piece, 128 - 32 * (k % 4), 1) if k % 4 else piece)
        data = jnp.concatenate(data, axis=0)
        high = data.astype(jnp.bfloat16)
        low = (data - high.astype(f32)).astype(jnp.bfloat16)
        dot = functools.partial(
            lax.dot_general,
            dimension_numbers=(((1,), (1,)), ((), ())),
            preferred_element_type=f32,
        )
        moved = dot(high, chosen_high) + (dot(low, chosen_high) + dot(high, chosen_low))
        total = moved if total is None else total + moved
    source = [total[64 * c : 64 * c + 64].reshape(8, 8, 128) for c in range(3)]
    middle = []
    for c in range(3):
        source_ref[c] = source[c]
        middle.append(wave_ref[1 + c] + acoustic_step * (rate_ref[1 + c] + source[c]))
        rows_ref[c] = middle[c].reshape(64, 128)
    for ready, face in zip(ready_faces, face_refs):
        face[0:6] = ready[...]
    store_faces(middle, [face.at[6:9] for face in face_refs], counts, rows_ref)


def inner_kernel(
    deriv_ref, high_ref, low_ref, les_ref, section_ref, wave_ref, rate_ref, mean_ref, source_ref,
    les_base_ref, wave_base_ref, source_out, sem,
):
    copy = pltpu.make_async_copy(source_ref, source_out, sem)
    copy.start()
    section = read_all(section_ref)
    rate = les_rate(section, None)
    for c in range(5):
        les_base_ref[c] = 0.5 * ((les_ref[c] + section[c]) + rate[c])
    first = read_all(rate_ref)
    middle = [wave_ref[0] + acoustic_step * first[0]]
    for c in range(1, 4):
        middle.append(wave_ref[c] + acoustic_step * (first[c] + source_ref[c - 1]))
    rate = acoustic_rate(
        middle, read_all(mean_ref), None, deriv_ref[...], (high_ref[...], low_ref[...])
    )
    for c in range(4):
        total = rate[c] + source_ref[c - 1] if c else rate[c]
        wave_base_ref[c] = 0.5 * (wave_ref[c] + middle[c] + acoustic_step * total)
    copy.wait()


def add_layers(counts, chosen, face_refs, mean_faces_ref, les_base_ref, wave_base_ref, put):
    layers = les_outer(load_faces(face_refs, counts, 0, 5, chosen))
    for c in range(5):
        part = [layer and (0.5 * layer[0][c], 0.5 * layer[1][c]) for layer in layers]
        put(c, with_layers(les_base_ref[c], part))
    mean_faces = [[mean_faces_ref[n, c] for c in range(3)] for n in range(6)]
    layers = acoustic_outer(mean_faces, load_faces(face_refs, counts, 5, 9, chosen))
    step = 0.5 * acoustic_step
    for c in range(4):
        part = [layer and (step * layer[0][c], step * layer[1][c]) for layer in layers]
        put(5 + c, with_layers(wave_base_ref[c], part))


def z_faces(faces, counts):
    holds = [any(axis == 2 for axis, _ in pair) for pair in slots(counts)]
    return [face if hold else None for face, hold in zip(faces, holds)]


def z_kernel(counts, present, les_base_ref, wave_base_ref, mean_faces_ref, *refs):
    refs = list(refs)
    face_refs = [refs.pop(0) if here else None for here in present]
    les_ref, wave_ref = refs

    def put(c, planes):
        for x, plane in enumerate(planes):
            if c < 5:
                les_ref[c, x] = plane
            else:
                wave_ref[c - 5, x] = plane

    add_layers(counts, (2,), face_refs, mean_faces_ref, les_base_ref, wave_base_ref, put)


def last_kernel(counts, n_faces, les_base_ref, wave_base_ref, mean_faces_ref, *refs):
    face_refs, (les_out, wave_out, les_ref, wave_ref, sems) = (
        refs[:n_faces], refs[n_faces:],
    )
    copies = []

    def put(c, planes):
        kept, target = (les_ref.at[c], les_out.at[c]) if c < 5 else (
            wave_ref.at[c - 5], wave_out.at[c - 5]
        )
        for x, plane in enumerate(planes):
            kept[x] = plane
        copies.append(pltpu.make_async_copy(kept, target, sems.at[c]))
        copies[-1].start()

    add_layers(counts, (0, 1), face_refs, mean_faces_ref, les_base_ref, wave_base_ref, put)
    for copy in copies:
        copy.wait()


VMEM = pl.BlockSpec(memory_space=pltpu.VMEM)


HBM = pl.BlockSpec(memory_space=pltpu.HBM)


def call(kernel, in_specs, out_shapes, name, cost, scratch=(), out_spec=None):
    return pl.pallas_call(
        kernel,
        in_specs=in_specs,
        out_specs=out_spec or [VMEM] * len(out_shapes),
        out_shape=out_shapes,
        scratch_shapes=list(scratch),
        name=name,
        cost_estimate=pl.CostEstimate(flops=cost, bytes_accessed=800000, transcendentals=0),
        compiler_params=pltpu.CompilerParams(vmem_limit_bytes=24 * 1024 * 1024),
    )


def local(counts, les, wave, mean, projection, owner, slot):
    shape = les.shape[1:]
    faces = face_shapes(counts, 9)
    n_faces = len(faces)
    like = lambda n: jax.ShapeDtypeStruct((n,) + shape, f32)

    table = derivative_matrix()
    deriv = jnp.asarray(table, f32)
    along_z = np.kron(np.eye(16), table.T).astype(np.float32)
    high = along_z.astype(jnp.bfloat16)
    low = (along_z - high.astype(np.float32)).astype(jnp.bfloat16)
    tables = (deriv, jnp.asarray(high), jnp.asarray(low))

    arguments = (les.reshape(5, 64, 128), wave.reshape(4, 64, 128), owner, slot, projection)
    les, wave, owner, slot, projection, *sent = call(
        functools.partial(load_kernel, counts),
        [HBM] * 5,
        [jax.ShapeDtypeStruct(a.shape, a.dtype) for a in arguments] + faces,
        "load_and_faces",
        100000,
        [pltpu.SemaphoreType.DMA((5,))],
    )(*(pltpu.with_memory_space_constraint(a, pltpu.HBM) for a in arguments))
    les, wave = les.reshape((5,) + shape), wave.reshape((4,) + shape)
    got = exchange(sent, counts)

    sets = partners(counts[0])
    n_plans = 4 * ((len(sets) + 3) // 4)
    order, marks, along_x, along_y, tile = call(
        functools.partial(plan_kernel, counts),
        [VMEM] * 3,
        [
            jax.ShapeDtypeStruct((n_plans, 8, 128), jnp.int32),
            jax.ShapeDtypeStruct((len(sets), 8, 128), f32),
            jax.ShapeDtypeStruct((64, 8, 128), f32),
            jax.ShapeDtypeStruct((8, 8, 128), f32),
            jax.ShapeDtypeStruct((2, 8, 128), f32),
        ],
        "plan",
        1000000,
    )(owner, slot, projection)
    turning = list(call(vorticity_kernel, [VMEM], [like(3)] * 2, "vorticity", 1000000)(les))
    z_got = z_faces(got, counts)
    present = [face is not None for face in z_got]
    turning[1] = call(
        functools.partial(vorticity_z_kernel, counts, present),
        [VMEM] * (1 + sum(present)),
        [like(3)],
        "vorticity_z",
        1000000,
    )(turning[1], *(face for face in z_got if face is not None))[0]
    pieces = call(
        functools.partial(lamb_kernel, counts, n_faces),
        [VMEM] * (6 + n_faces),
        [jax.ShapeDtypeStruct((7, 8, 128), f32)] * len(sets),
        "lamb_blocks",
        10000000,
    )(order, marks, along_x, along_y, *turning, *got)
    moved = []
    for k in sending_sets(len(sets)):
        still = all(i == j for i, j in sets[k])
        moved.append(pieces[k] if still else lax.ppermute(pieces[k], "gx", sets[k]))
    section, rate, mean_faces, *ready_faces = call(
        functools.partial(first_kernel, counts, n_faces),
        [VMEM] * (6 + n_faces),
        [like(5), like(4), jax.ShapeDtypeStruct((6, 3, 8, 128), f32)] + face_shapes(counts, 6),
        "first_rates",
        40000000,
    )(*tables, les, wave, mean, *got)

    source, *sent = call(
        functools.partial(source_kernel, counts, n_faces),
        [VMEM] * (3 + len(moved) + n_faces),
        [like(3)] + faces,
        "source_and_faces",
        10000000,
        [pltpu.VMEM((3, 64, 128), f32)],
    )(tile, wave, rate, *moved, *ready_faces)
    got = exchange(sent, counts)
    les_base, wave_base, source_out = call(
        inner_kernel,
        [VMEM] * 9,
        [like(5), like(4), like(3)],
        "second_rates_inner",
        40000000,
        [pltpu.SemaphoreType.DMA],
        out_spec=[VMEM, VMEM, HBM],
    )(*tables, les, section, wave, rate, mean, source)
    z_got = z_faces(got, counts)
    present = [face is not None for face in z_got]
    les_base, wave_base = call(
        functools.partial(z_kernel, counts, present),
        [VMEM] * (3 + sum(present)),
        [like(5), like(4)],
        "second_rates_z",
        1000000,
    )(les_base, wave_base, mean_faces, *(face for face in z_got if face is not None))
    les_next, wave_next = call(
        functools.partial(last_kernel, counts, n_faces),
        [VMEM] * (3 + n_faces),
        [like(5), like(4)],
        "second_rates_outer",
        4000000,
        [
            pltpu.VMEM(les.shape, f32),
            pltpu.VMEM(wave.shape, f32),
            pltpu.SemaphoreType.DMA((9,)),
        ],
        out_spec=[HBM, HBM],
    )(les_base, wave_base, mean_faces, *got)
    return les_next, source_out, wave_next


def solution(mesh):
    counts = tuple(mesh.shape[axis] for axis in axes)
    field = P(None, *axes)
    return jax.shard_map(
        functools.partial(local, counts),
        mesh=mesh,
        in_specs=(field, field, field, P(), P(*axes), P(*axes)),
        out_specs=(field, field, field),
        check_vma=False,
    )
```

```python
import functools

import jax
import jax.numpy as jnp
import numpy as np
from jax import lax
from jax.experimental import pallas as pl
from jax.experimental.pallas import tpu as pltpu
from jax.sharding import PartitionSpec as P

lobatto_points = np.array(
    [
        -1.0,
        -0.8717401485096066,
        -0.5917001814331423,
        -0.2092992179024789,
        0.2092992179024789,
        0.5917001814331423,
        0.8717401485096066,
        1.0,
    ]
)
flux_half = 0.08
gamma_less = 0.4
acoustic_step = 0.01
upwind_speed = 1.5
face_lift = 28.0
free_stream = (1.0, 0.0, 0.0, 0.0, 2.5)
axes = ("gx", "gy", "gz")
window = 4
f32 = jnp.float32


def derivative_matrix():
    points = lobatto_points
    products = [np.prod([points[i] - points[j] for j in range(8) if j != i]) for i in range(8)]
    matrix = np.zeros((8, 8))
    for i in range(8):
        for j in range(8):
            if j != i:
                matrix[i, j] = products[i] / (products[j] * (points[i] - points[j]))
        matrix[i, i] = -np.sum(matrix[i])
    return matrix


def sublane(shape):
    return lax.broadcasted_iota(jnp.int32, shape, len(shape) - 2)


def lane(shape):
    return lax.broadcasted_iota(jnp.int32, shape, len(shape) - 1)


def rolled(tile, amount, axis):
    amount = amount % tile.shape[axis]
    return pltpu.roll(tile, amount, axis) if amount else tile


def shifted(field, axis, step, outer=None):
    if axis == 0:
        outer = jnp.zeros((8, 128), f32) if outer is None else outer
        if step == 1:
            return jnp.concatenate([field[1:], outer[None]], axis=0)
        return jnp.concatenate([outer[None], field[:-1]], axis=0)
    count = (8, 128)[axis - 1]
    edge = count - 1 if step == 1 else 0
    at_edge = (sublane if axis == 1 else lane)((8, 128)) == edge
    planes = []
    for x in range(8):
        layer = 0.0 if outer is None else rolled(outer, edge - axis * x, axis - 1)
        planes.append(jnp.where(at_edge, layer, rolled(field[x], -step, axis - 1)))
    return jnp.stack(planes, axis=0)


def fluid(state):
    density, mx, my, mz, energy = [s + r for s, r in zip(state, free_stream)]
    inverse = 1.0 / density
    momentum = (mx, my, mz)
    velocity = [m * inverse for m in momentum]
    pressure = gamma_less * (
        energy - 0.5 * (mx * velocity[0] + my * velocity[1] + mz * velocity[2])
    )
    return momentum, velocity, pressure, energy + pressure


def split_flux(state, parts, axis, sign):
    momentum, velocity, pressure, enthalpy = parts
    speed = velocity[axis]
    flux = [momentum[axis]]
    for c in range(3):
        term = momentum[c] * speed
        flux.append(term + pressure if c == axis else term)
    flux.append(enthalpy * speed)
    if sign > 0:
        return [flux_half * (s + f) for s, f in zip(state, flux)]
    return [flux_half * (s - f) for s, f in zip(state, flux)]


def les_rate(state, halos):
    parts = fluid(state)
    total = [-6.0 * flux_half * s for s in state]
    for axis in range(3):
        ahead = split_flux(state, parts, axis, -1)
        behind = split_flux(state, parts, axis, 1)
        ahead_outer = behind_outer = [None] * 5
        if halos is not None:
            before, after = halos[axis]
            ahead_outer = split_flux(after, fluid(after), axis, -1)
            behind_outer = split_flux(before, fluid(before), axis, 1)
        for c in range(5):
            total[c] = total[c] + (
                shifted(ahead[c], axis, 1, ahead_outer[c])
                + shifted(behind[c], axis, -1, behind_outer[c])
            )
    return total


def les_outer(halos):
    return [
        halo
        and (
            split_flux(halo[0], fluid(halo[0]), axis, 1),
            split_flux(halo[1], fluid(halo[1]), axis, -1),
        )
        for axis, halo in enumerate(halos)
    ]


def with_layers(field, layers):
    row, column = sublane((8, 128)), lane((8, 128))
    along_z = layers[2]
    if along_z is not None:
        along_z = jnp.where(lax.rem(column, 2) == 0, along_z[0], rolled(along_z[1], -1, 1))
    planes = []
    for x in range(8):
        plane = field[x]
        if layers[0] is not None and x in (0, 7):
            plane = plane + layers[0][x // 7]
        if layers[1] is not None:
            low, high = layers[1]
            plane = plane + jnp.where(
                row == 0, rolled(low, -x, 0), jnp.where(row == 7, rolled(high, 7 - x, 0), 0.0)
            )
        if along_z is not None:
            ends = (column == 0) | (column == 127)
            plane = plane + jnp.where(ends, rolled(along_z, -2 * x, 1), 0.0)
        planes.append(plane)
    return planes


def wave_flux(state, mean, axis):
    speed = mean[axis]
    pressure = state[0]
    rows = [speed * pressure + state[1 + axis]]
    for c in range(3):
        term = speed * state[1 + c]
        rows.append(term + pressure if c == axis else term)
    return rows


def dot3(left, right):
    high = left.astype(jnp.bfloat16)
    low = (left - high.astype(f32)).astype(jnp.bfloat16)
    dot = functools.partial(jnp.dot, preferred_element_type=f32)
    return dot(high, right[0]) + (dot(low, right[0]) + dot(high, right[1]))


def acoustic_rate(state, mean, halos, deriv, along_z):
    shape = state[0].shape
    table = derivative_matrix()
    flux = wave_flux(state, mean, 0)
    if halos is None:
        halos = [([jnp.zeros((8, 128), f32)] * 4,) * 2] + [([None] * 4,) * 2] * 2
    before, after = halos[0]
    low_mean, high_mean = [m[0] for m in mean], [m[7] for m in mean]
    low_jump = [b - s[0] for b, s in zip(before, state)]
    high_jump = [a - s[7] for a, s in zip(after, state)]
    low_flux = wave_flux(low_jump, low_mean, 0)
    high_flux = wave_flux(high_jump, high_mean, 0)
    half, lift = 0.5 * face_lift, 0.5 * face_lift * upwind_speed
    total = []
    for c in range(4):
        planes = []
        for i in range(8):
            plane = -float(table[i, 0]) * flux[c][0]
            for a in range(1, 8):
                if abs(table[i, a]) > 1e-12:
                    plane = plane - float(table[i, a]) * flux[c][a]
            if i == 0:
                plane = plane + (half * low_flux[c] + lift * low_jump[c])
            if i == 7:
                plane = plane - (half * high_flux[c] - lift * high_jump[c])
            planes.append(plane)
        total.append(jnp.stack(planes, axis=0))
    flux = wave_flux(state, mean, 1)
    before, after = halos[1]
    row = sublane(shape)
    sign = jnp.where(row == 0, half, jnp.where(row == 7, -half, 0.0))
    jump = []
    for s, b, a in zip(state, before, after):
        planes = []
        for x in range(8):
            low = 0.0 if b is None else rolled(b, -x, 0)
            high = 0.0 if a is None else rolled(a, 7 - x, 0)
            planes.append(jnp.where(row[x] == 0, low, jnp.where(row[x] == 7, high, s[x])) - s[x])
        jump.append(jnp.stack(planes, axis=0))
    jump_flux = wave_flux(jump, mean, 1)
    for c in range(4):
        change = lift * jump[c] + sign * jump_flux[c]
        for b in range(8):
            change = change - deriv[:, b : b + 1][None] * flux[c][:, b : b + 1, :]
        total[c] = total[c] + change
    flux = wave_flux(state, mean, 2)
    before, after = halos[2]
    column = lane(shape)
    place = lax.rem(column, 8)
    sign = jnp.where(place == 0, half, jnp.where(place == 7, -half, 0.0))
    jump = [
        jnp.where(
            place == 0,
            shifted(s, 2, -1, b),
            jnp.where(place == 7, shifted(s, 2, 1, a), s),
        )
        - s
        for s, b, a in zip(state, before, after)
    ]
    jump_flux = wave_flux(jump, mean, 2)
    for c in range(4):
        slope = dot3(flux[c].reshape(64, 128), along_z).reshape(shape)
        total[c] = total[c] + (lift * jump[c] + sign * jump_flux[c] - slope)
    return total


def mean_layers(mean):
    return [
        [m[0] for m in mean],
        [m[7] for m in mean],
        [m[:, 0, :] for m in mean],
        [m[:, 7, :] for m in mean],
        [z_layer(m, jnp.int32(0)) for m in mean],
        [z_layer(m, jnp.int32(127)) for m in mean],
    ]


def acoustic_outer(mean_faces, halos):
    half, lift = 0.5 * face_lift, 0.5 * face_lift * upwind_speed
    layers = []
    for axis, halo in enumerate(halos):
        if halo is None:
            layers.append(None)
            continue
        before, after = halo
        low_flux = wave_flux(before, mean_faces[2 * axis], axis)
        high_flux = wave_flux(after, mean_faces[2 * axis + 1], axis)
        layers.append(
            (
                [half * f + lift * b for f, b in zip(low_flux, before)],
                [lift * a - half * f for f, a in zip(high_flux, after)],
            )
        )
    return layers


def tile_rows(matrix):
    spread = (lax.rem(lane((8, 128)), 8) == sublane((8, 128))).astype(f32)
    return jnp.dot(
        matrix, spread, precision=lax.Precision.HIGHEST, preferred_element_type=f32
    )


def pairings(count):
    sets = []
    for first in (0, 1):
        pairs = [(i, i + 1) for i in range(first, count - 1, 2)]
        if pairs:
            sets.append(pairs)
    return sets


def slots(counts):
    found = [(axis, n) for axis in range(3) for n in range(len(pairings(counts[axis])))]
    lower = ((2, 1), (2, 0), (0, 1), (1, 0), (1, 1), (0, 0))
    upper = ((2, 1), (0, 1), (2, 0), (0, 0), (1, 1), (1, 0))
    lower = [swap for swap in lower if swap in found]
    upper = [swap for swap in upper if swap in found] if counts[1] == 4 else lower
    return list(zip(lower, upper))


def in_upper_half(counts):
    return lax.axis_index("gy") >= counts[1] // 2


def routes(counts):
    places = [(x, y, z) for x in range(counts[0]) for y in range(counts[1]) for z in range(counts[2])]
    number = {place: n for n, place in enumerate(places)}

    def partner(place, axis, n):
        pairs = pairings(counts[axis])[n]
        swap = dict(pairs + [(j, i) for i, j in pairs])
        alone = [i for i in range(counts[axis]) if i not in swap]
        spare = 0 if axis else 2
        other = list(place)
        if place[axis] in swap:
            other[axis] = swap[place[axis]]
        elif axis == 0 and len(alone) == 2:
            other[axis] = sum(alone) - place[axis]
        elif counts[spare] % 2 == 0:
            other[spare] = place[spare] ^ 1
        return number[tuple(other)]

    return [
        [
            (number[place], partner(place, *(upper if place[1] >= counts[1] // 2 else lower)))
            for place in places
        ]
        for lower, upper in slots(counts)
    ]


def z_layer(field, at):
    packed = jnp.zeros((8, 128), f32)
    column = lane((8, 128))
    for x in range(8):
        turned = pltpu.roll(field[x], lax.rem(2 * x - at + 128, 128), 1)
        packed = jnp.where(column == 2 * x, turned, packed)
    return packed


def store_faces(fields, out_refs, counts):
    high_half = in_upper_half(counts)
    for c, field in enumerate(fields):
        faces = {}
        for axis in range(3):
            even = lax.rem(lax.axis_index(axes[axis]), 2) == 0
            if axis == 0:
                low, high = field[0], field[7]
            elif axis == 1:
                low, high = field[:, 0, :], field[:, 7, :]
            for n in range(len(pairings(counts[axis]))):
                last = even == (n == 0)
                if axis == 2:
                    faces[axis, n] = z_layer(field, jnp.where(last, 127, 0))
                else:
                    faces[axis, n] = jnp.where(last, high, low)
        for ref, (lower, upper) in zip(out_refs, slots(counts)):
            if lower == upper:
                ref[c] = faces[lower]
            else:
                ref[c] = jnp.where(high_half, faces[upper], faces[lower])


def load_faces(in_refs, counts, first, last, chosen=(0, 1, 2)):
    high_half = in_upper_half(counts)
    lower, upper = zip(*slots(counts))
    halos = []
    for axis in range(3):
        if axis not in chosen:
            halos.append(None)
            continue
        place = lax.axis_index(axes[axis])
        even = lax.rem(place, 2) == 0
        got = []
        for n in range(len(pairings(counts[axis]))):
            a, b = in_refs[lower.index((axis, n))], in_refs[upper.index((axis, n))]
            got.append(
                [a[c] if a is b else jnp.where(high_half, b[c], a[c]) for c in range(first, last)]
            )
        while len(got) < 2:
            got.append([jnp.zeros((8, 128), f32)] * (last - first))
        before = [jnp.where(place == 0, 0.0, jnp.where(even, b, a)) for a, b in zip(*got)]
        after = [
            jnp.where(place == counts[axis] - 1, 0.0, jnp.where(even, a, b))
            for a, b in zip(*got)
        ]
        halos.append((before, after))
    return halos


def face_shapes(counts, width):
    total = sum(len(pairings(count)) for count in counts)
    return [jax.ShapeDtypeStruct((width, 8, 128), f32)] * total


def exchange(faces, counts):
    return [lax.ppermute(face, axes, way) for face, way in zip(faces, routes(counts))]


def read_all(ref):
    return [ref[c] for c in range(ref.shape[0])]


def load_kernel(counts, les_hbm, wave_hbm, les_ref, wave_ref, *refs):
    out_refs, sems = refs[:-1], refs[-1]
    parts = [
        (source.at[low:high], target.at[low:high], first + low, high - low)
        for source, target, low, high, first in (
            (les_hbm, les_ref, 0, 3, 0),
            (les_hbm, les_ref, 3, 5, 0),
            (wave_hbm, wave_ref, 0, 2, 5),
            (wave_hbm, wave_ref, 2, 4, 5),
        )
    ]
    copies = [
        pltpu.make_async_copy(source, target, sems.at[n])
        for n, (source, target, _, _) in enumerate(parts)
    ]
    for copy in copies:
        copy.start()
    for copy, (_, target, first, count) in zip(copies, parts):
        copy.wait()
        fields = [target[c] for c in range(count)]
        store_faces(fields, [ref.at[first : first + count] for ref in out_refs], counts)


def partners(count):
    if count == window:
        return [[(i, i ^ mask) for i in range(count)] for mask in range(count)]
    turns = sorted({d % count for d in range(1 - window, window)})
    return [[(i, (i + turn) % count) for i in range(count)] for turn in turns]


def speeds(state):
    inverse = 1.0 / (state[0] + 1.0)
    return [state[c] * inverse for c in (1, 2, 3)]


def vorticity(les_ref, velocity_ref, vort_ref):
    velocity = speeds([les_ref[c] for c in range(4)])

    def slope(c, axis):
        return shifted(velocity[c], axis, 1) - shifted(velocity[c], axis, -1)

    vort = [slope(2, 1) - slope(1, 2), slope(0, 2) - slope(2, 0), slope(1, 0) - slope(0, 1)]
    for c in range(3):
        velocity_ref[c] = velocity[c]
        vort_ref[c] = vort[c]


def sending_sets(count):
    return [3, 2, 1, 0] if count == window else list(range(count))


def plan_kernel(
    counts, owner_hbm, slot_hbm, proj_hbm, les_ref, order_ref, marks_ref, along_x_ref, along_y_ref,
    tile_ref, velocity_ref, vort_ref, owner_ref, slot_ref, proj_ref, sems,
):
    copies = [
        pltpu.make_async_copy(source, target, sems.at[n])
        for n, (source, target) in enumerate(
            ((owner_hbm, owner_ref), (slot_hbm, slot_ref), (proj_hbm, proj_ref))
        )
    ]
    for copy in copies:
        copy.start()
    vorticity(les_ref, velocity_ref, vort_ref)
    for copy in copies:
        copy.wait()
    count = counts[0]
    n_sets = len(partners(count))
    own = lax.axis_index("gx")
    n_blocks = owner_ref.shape[-1]
    square = (n_blocks, n_blocks)
    block, other = sublane(square), lane(square)

    def spread(ref):
        by_lane = jnp.broadcast_to(ref[0], square)
        here = jnp.where(block == other, by_lane, 0).astype(f32)
        return by_lane, jnp.sum(here, axis=1, keepdims=True).astype(jnp.int32)

    def group_of(owner):
        if count == window:
            return lax.bitwise_xor(owner, own)
        turn = lax.rem(owner - own + count, count)
        if n_sets == count:
            return turn
        return jnp.where(turn < window, turn, turn - (count - n_sets))

    owner_by_lane, owner = spread(owner_ref)
    slot = spread(slot_ref)[1]
    group = group_of(owner)
    before = (group_of(owner_by_lane) == group) & (other < block)
    taken = jnp.sum(before.astype(f32), axis=1, keepdims=True).astype(jnp.int32)
    wide = (n_blocks, 128)
    place = jnp.broadcast_to(group * window + taken, wide)
    column = lane((8, 128))
    quarter = column // 32
    for s in range((n_sets + 3) // 4):
        here = place - 16 * s == lane(wide) // 8
        label = jnp.sum(jnp.where(here, (slot + 1).astype(f32), 0.0), axis=0, keepdims=True) - 1.0
        source = jnp.sum(
            jnp.where(here, (8 * sublane(wide)).astype(f32), 0.0), axis=0, keepdims=True
        )
        labels = jnp.broadcast_to(label, (8, 128))
        order = jnp.broadcast_to(source, (8, 128)).astype(jnp.int32) + lax.rem(column, 8)
        for t in range(4):
            order_ref[4 * s + t] = rolled(order, 32 * t, 1)
        for r in range(min(4, n_sets - 4 * s)):
            marks = labels
            for t in range(1, 4):
                marks = jnp.where(quarter == (r + t) % 4, rolled(labels, 32 * t, 1), marks)
            marks_ref[4 * s + r] = marks
    proj = proj_ref[...]
    for a in range(8):
        along_y = jnp.broadcast_to(proj[:, a : a + 1], (8, 128))
        along_y_ref[a] = along_y
        for i in range(8):
            along_x_ref[8 * i + a] = jnp.broadcast_to(along_y[i : i + 1], (8, 128))
    tile = tile_rows(proj)
    high = tile.astype(jnp.bfloat16).astype(f32)
    tile_ref[0] = high
    tile_ref[1] = tile - high


def vorticity_z_kernel(counts, present, vort_ref, *refs):
    refs = list(refs)
    face_refs = [refs.pop(0) if here else None for here in present]
    (out_ref,) = refs
    before, after = [speeds(layer) for layer in load_faces(face_refs, counts, 0, 4, (2,))[2]]
    for c, layer in ((0, (before[1], -after[1])), (1, (-before[0], after[0]))):
        for x, plane in enumerate(with_layers(vort_ref[c], (None, None, layer))):
            out_ref[c, x] = plane
    out_ref[2] = vort_ref[2]


def lamb_kernel(
    counts, n_faces, order_ref, marks_ref, along_x_ref, along_y_ref, velocity_ref, vort_ref, *refs
):
    face_refs, out_refs = refs[:n_faces], refs[n_faces:]
    outer = [
        halo and (speeds(halo[0]), speeds(halo[1]))
        for halo in load_faces(face_refs, counts, 0, 4, (0, 1))
    ]

    def rise(c, axis):
        return -outer[axis][0][c], outer[axis][1][c]

    def fall(c, axis):
        return outer[axis][0][c], -outer[axis][1][c]

    layers = [
        (None, rise(2, 1), None),
        (fall(2, 0), None, None),
        (rise(1, 0), fall(0, 1), None),
    ]
    vort = [0.5 * jnp.stack(with_layers(vort_ref[c], layers[c]), axis=0) for c in range(3)]
    velocity = read_all(velocity_ref)
    lamb = [
        vort[1] * velocity[2] - vort[2] * velocity[1],
        vort[2] * velocity[0] - vort[0] * velocity[2],
        vort[0] * velocity[1] - vort[1] * velocity[0],
    ]
    blocks = []
    for field in lamb:
        along_y = along_y_ref[0][None] * field[:, 0:1, :]
        for b in range(1, 8):
            along_y = along_y + along_y_ref[b][None] * field[:, b : b + 1, :]
        for i in range(8):
            plane = along_x_ref[8 * i] * along_y[0]
            for a in range(1, 8):
                plane = plane + along_x_ref[8 * i + a] * along_y[a]
            blocks.append(plane)

    quarter = lane((8, 128)) // 32
    for s in range((len(out_refs) + 3) // 4):
        ordered = [
            jnp.take_along_axis(block, order_ref[4 * s + k % 4], axis=1)
            for k, block in enumerate(blocks)
        ]
        for r in range(min(4, len(out_refs) - 4 * s)):
            out = out_refs[4 * s + r]
            for q in range(6):
                packed = ordered[4 * q]
                for t in range(1, 4):
                    packed = jnp.where(quarter == (r + t) % 4, ordered[4 * q + t], packed)
                out[q] = packed
            out[6] = marks_ref[4 * s + r]


def first_kernel(
    counts, n_faces, deriv_ref, high_ref, low_ref, les_ref, wave_ref, mean_ref, *refs
):
    face_refs, (section_ref, rate_ref, mean_faces_ref), out_refs = (
        refs[:n_faces], refs[n_faces : n_faces + 3], refs[n_faces + 3 :],
    )
    for n, face in enumerate(mean_layers(read_all(mean_ref))):
        for c in range(3):
            mean_faces_ref[n, c] = face[c]
    state = read_all(les_ref)
    rate = les_rate(state, load_faces(face_refs, counts, 0, 5))
    section = [s + r for s, r in zip(state, rate)]
    for c in range(5):
        section_ref[c] = section[c]
    rate = acoustic_rate(
        read_all(wave_ref), read_all(mean_ref), load_faces(face_refs, counts, 5, 9),
        deriv_ref[...], (high_ref[...], low_ref[...]),
    )
    for c in range(4):
        rate_ref[c] = rate[c]
    store_faces(section + [wave_ref[0] + acoustic_step * rate[0]], out_refs, counts)


def source_kernel(counts, n_faces, tile_ref, wave_ref, rate_ref, *refs):
    n_pieces = len(partners(counts[0]))
    pieces = [None] * n_pieces
    for ref, k in zip(refs, sending_sets(n_pieces)):
        pieces[k] = ref
    refs = refs[n_pieces:]
    ready_faces, source_ref, face_refs = refs[:n_faces], refs[n_faces], refs[n_faces + 1 :]
    quarter = lane((8, 128)) // 32
    tile_high, tile_low = tile_ref[0], tile_ref[1]
    total = None
    for s in range((n_pieces + 3) // 4):
        count = min(4, n_pieces - 4 * s)

        def gathered(q, t):
            value = jnp.full((8, 128), -1.0 if q == 6 else 0.0, f32)
            for r in range(count):
                value = jnp.where(quarter == (r + t) % 4, pieces[4 * s + r][q], value)
            return value

        here = [gathered(6, 0).astype(jnp.int32) == slot for slot in range(16)]
        chosen_high, chosen_low = [
            jnp.concatenate([jnp.where(h, part, 0.0) for h in here], axis=0).astype(jnp.bfloat16)
            for part in (tile_high, tile_low)
        ]
        data = []
        for k in range(24):
            piece = gathered(k // 4, k % 4)
            data.append(pltpu.roll(piece, 128 - 32 * (k % 4), 1) if k % 4 else piece)
        data = jnp.concatenate(data, axis=0)
        high = data.astype(jnp.bfloat16)
        low = (data - high.astype(f32)).astype(jnp.bfloat16)
        dot = functools.partial(
            lax.dot_general,
            dimension_numbers=(((1,), (1,)), ((), ())),
            preferred_element_type=f32,
        )
        moved = dot(high, chosen_high) + (dot(low, chosen_high) + dot(high, chosen_low))
        total = moved if total is None else total + moved
    source = [total[64 * c : 64 * c + 64].reshape(8, 8, 128) for c in range(3)]
    middle = []
    for c in range(3):
        source_ref[c] = source[c]
        middle.append(wave_ref[1 + c] + acoustic_step * (rate_ref[1 + c] + source[c]))
    for ready, face in zip(ready_faces, face_refs):
        face[0:6] = ready[...]
    store_faces(middle, [face.at[6:9] for face in face_refs], counts)


def inner_kernel(
    deriv_ref, high_ref, low_ref, les_ref, section_ref, wave_ref, rate_ref, mean_ref, source_ref,
    les_base_ref, wave_base_ref, source_out, sem,
):
    copy = pltpu.make_async_copy(source_ref, source_out, sem)
    copy.start()
    section = read_all(section_ref)
    rate = les_rate(section, None)
    for c in range(5):
        les_base_ref[c] = 0.5 * ((les_ref[c] + section[c]) + rate[c])
    first = read_all(rate_ref)
    middle = [wave_ref[0] + acoustic_step * first[0]]
    for c in range(1, 4):
        middle.append(wave_ref[c] + acoustic_step * (first[c] + source_ref[c - 1]))
    rate = acoustic_rate(
        middle, read_all(mean_ref), None, deriv_ref[...], (high_ref[...], low_ref[...])
    )
    for c in range(4):
        total = rate[c] + source_ref[c - 1] if c else rate[c]
        wave_base_ref[c] = 0.5 * (wave_ref[c] + middle[c] + acoustic_step * total)
    copy.wait()


def add_layers(counts, chosen, face_refs, mean_faces_ref, les_base_ref, wave_base_ref, put):
    layers = les_outer(load_faces(face_refs, counts, 0, 5, chosen))
    for c in range(5):
        part = [layer and (0.5 * layer[0][c], 0.5 * layer[1][c]) for layer in layers]
        put(c, with_layers(les_base_ref[c], part))
    mean_faces = [[mean_faces_ref[n, c] for c in range(3)] for n in range(6)]
    layers = acoustic_outer(mean_faces, load_faces(face_refs, counts, 5, 9, chosen))
    step = 0.5 * acoustic_step
    for c in range(4):
        part = [layer and (step * layer[0][c], step * layer[1][c]) for layer in layers]
        put(5 + c, with_layers(wave_base_ref[c], part))


def z_faces(faces, counts):
    holds = [any(axis == 2 for axis, _ in pair) for pair in slots(counts)]
    return [face if hold else None for face, hold in zip(faces, holds)]


def z_kernel(counts, present, les_base_ref, wave_base_ref, mean_faces_ref, *refs):
    refs = list(refs)
    face_refs = [refs.pop(0) if here else None for here in present]
    les_ref, wave_ref = refs

    def put(c, planes):
        for x, plane in enumerate(planes):
            if c < 5:
                les_ref[c, x] = plane
            else:
                wave_ref[c - 5, x] = plane

    add_layers(counts, (2,), face_refs, mean_faces_ref, les_base_ref, wave_base_ref, put)


def last_kernel(counts, n_faces, les_base_ref, wave_base_ref, mean_faces_ref, *refs):
    face_refs, (les_out, wave_out, les_ref, wave_ref, sems) = (
        refs[:n_faces], refs[n_faces:],
    )
    copies = []

    def put(c, planes):
        kept, target = (les_ref.at[c], les_out.at[c]) if c < 5 else (
            wave_ref.at[c - 5], wave_out.at[c - 5]
        )
        for x, plane in enumerate(planes):
            kept[x] = plane
        copies.append(pltpu.make_async_copy(kept, target, sems.at[c]))
        copies[-1].start()

    add_layers(counts, (0, 1), face_refs, mean_faces_ref, les_base_ref, wave_base_ref, put)
    for copy in copies:
        copy.wait()


VMEM = pl.BlockSpec(memory_space=pltpu.VMEM)


HBM = pl.BlockSpec(memory_space=pltpu.HBM)


def call(kernel, in_specs, out_shapes, name, cost, scratch=(), out_spec=None):
    return pl.pallas_call(
        kernel,
        in_specs=in_specs,
        out_specs=out_spec or [VMEM] * len(out_shapes),
        out_shape=out_shapes,
        scratch_shapes=list(scratch),
        name=name,
        cost_estimate=pl.CostEstimate(flops=cost, bytes_accessed=800000, transcendentals=0),
        compiler_params=pltpu.CompilerParams(vmem_limit_bytes=24 * 1024 * 1024),
    )


def local(counts, les, wave, mean, projection, owner, slot):
    shape = les.shape[1:]
    faces = face_shapes(counts, 9)
    n_faces = len(faces)
    like = lambda n: jax.ShapeDtypeStruct((n,) + shape, f32)

    table = derivative_matrix()
    deriv = jnp.asarray(table, f32)
    along_z = np.kron(np.eye(16), table.T).astype(np.float32)
    high = along_z.astype(jnp.bfloat16)
    low = (along_z - high.astype(np.float32)).astype(jnp.bfloat16)
    tables = (deriv, jnp.asarray(high), jnp.asarray(low))

    in_hbm = lambda *arrays: [pltpu.with_memory_space_constraint(a, pltpu.HBM) for a in arrays]
    les, wave, *sent = call(
        functools.partial(load_kernel, counts),
        [HBM] * 2,
        [like(5), like(4)] + faces,
        "load_and_faces",
        100000,
        [pltpu.SemaphoreType.DMA((4,))],
    )(*in_hbm(les, wave))
    got = exchange(sent, counts)

    sets = partners(counts[0])
    n_plans = 4 * ((len(sets) + 3) // 4)
    small = (owner, slot, projection)
    order, marks, along_x, along_y, tile, *turning = call(
        functools.partial(plan_kernel, counts),
        [HBM] * 3 + [VMEM],
        [
            jax.ShapeDtypeStruct((n_plans, 8, 128), jnp.int32),
            jax.ShapeDtypeStruct((len(sets), 8, 128), f32),
            jax.ShapeDtypeStruct((64, 8, 128), f32),
            jax.ShapeDtypeStruct((8, 8, 128), f32),
            jax.ShapeDtypeStruct((2, 8, 128), f32),
            like(3),
            like(3),
        ],
        "plan_and_vorticity",
        1000000,
        [pltpu.VMEM(a.shape, a.dtype) for a in small] + [pltpu.SemaphoreType.DMA((3,))],
    )(*in_hbm(*small), les)
    z_got = z_faces(got, counts)
    present = [face is not None for face in z_got]
    turning[1] = call(
        functools.partial(vorticity_z_kernel, counts, present),
        [VMEM] * (1 + sum(present)),
        [like(3)],
        "vorticity_z",
        1000000,
    )(turning[1], *(face for face in z_got if face is not None))[0]
    pieces = call(
        functools.partial(lamb_kernel, counts, n_faces),
        [VMEM] * (6 + n_faces),
        [jax.ShapeDtypeStruct((7, 8, 128), f32)] * len(sets),
        "lamb_blocks",
        10000000,
    )(order, marks, along_x, along_y, *turning, *got)
    moved = []
    for k in sending_sets(len(sets)):
        still = all(i == j for i, j in sets[k])
        moved.append(pieces[k] if still else lax.ppermute(pieces[k], "gx", sets[k]))
    section, rate, mean_faces, *ready_faces = call(
        functools.partial(first_kernel, counts, n_faces),
        [VMEM] * (6 + n_faces),
        [like(5), like(4), jax.ShapeDtypeStruct((6, 3, 8, 128), f32)] + face_shapes(counts, 6),
        "first_rates",
        40000000,
    )(*tables, les, wave, mean, *got)

    source, *sent = call(
        functools.partial(source_kernel, counts, n_faces),
        [VMEM] * (3 + len(moved) + n_faces),
        [like(3)] + faces,
        "source_and_faces",
        10000000,
    )(tile, wave, rate, *moved, *ready_faces)
    got = exchange(sent, counts)
    les_base, wave_base, source_out = call(
        inner_kernel,
        [VMEM] * 9,
        [like(5), like(4), like(3)],
        "second_rates_inner",
        40000000,
        [pltpu.SemaphoreType.DMA],
        out_spec=[VMEM, VMEM, HBM],
    )(*tables, les, section, wave, rate, mean, source)
    z_got = z_faces(got, counts)
    present = [face is not None for face in z_got]
    les_base, wave_base = call(
        functools.partial(z_kernel, counts, present),
        [VMEM] * (3 + sum(present)),
        [like(5), like(4)],
        "second_rates_z",
        1000000,
    )(les_base, wave_base, mean_faces, *(face for face in z_got if face is not None))
    les_next, wave_next = call(
        functools.partial(last_kernel, counts, n_faces),
        [VMEM] * (3 + n_faces),
        [like(5), like(4)],
        "second_rates_outer",
        4000000,
        [
            pltpu.VMEM(les.shape, f32),
            pltpu.VMEM(wave.shape, f32),
            pltpu.SemaphoreType.DMA((9,)),
        ],
        out_spec=[HBM, HBM],
    )(les_base, wave_base, mean_faces, *got)
    return les_next, source_out, wave_next


def solution(mesh):
    counts = tuple(mesh.shape[axis] for axis in axes)
    field = P(None, *axes)
    return jax.shard_map(
        functools.partial(local, counts),
        mesh=mesh,
        in_specs=(field, field, field, P(), P(*axes), P(*axes)),
        out_specs=(field, field, field),
        check_vma=False,
    )
```

```python
import functools

import jax
import jax.numpy as jnp
import numpy as np
from jax import lax
from jax.experimental import pallas as pl
from jax.experimental.pallas import tpu as pltpu
from jax.sharding import PartitionSpec as P

lobatto_points = np.array(
    [
        -1.0,
        -0.8717401485096066,
        -0.5917001814331423,
        -0.2092992179024789,
        0.2092992179024789,
        0.5917001814331423,
        0.8717401485096066,
        1.0,
    ]
)
flux_half = 0.08
gamma_less = 0.4
acoustic_step = 0.01
upwind_speed = 1.5
face_lift = 28.0
free_stream = (1.0, 0.0, 0.0, 0.0, 2.5)
axes = ("gx", "gy", "gz")
window = 4
f32 = jnp.float32


def derivative_matrix():
    points = lobatto_points
    products = [np.prod([points[i] - points[j] for j in range(8) if j != i]) for i in range(8)]
    matrix = np.zeros((8, 8))
    for i in range(8):
        for j in range(8):
            if j != i:
                matrix[i, j] = products[i] / (products[j] * (points[i] - points[j]))
        matrix[i, i] = -np.sum(matrix[i])
    return matrix


def sublane(shape):
    return lax.broadcasted_iota(jnp.int32, shape, len(shape) - 2)


def lane(shape):
    return lax.broadcasted_iota(jnp.int32, shape, len(shape) - 1)


def rolled(tile, amount, axis):
    amount = amount % tile.shape[axis]
    return pltpu.roll(tile, amount, axis) if amount else tile


def shifted(field, axis, step, outer=None):
    if axis == 0:
        outer = jnp.zeros((8, 128), f32) if outer is None else outer
        if step == 1:
            return jnp.concatenate([field[1:], outer[None]], axis=0)
        return jnp.concatenate([outer[None], field[:-1]], axis=0)
    count = (8, 128)[axis - 1]
    edge = count - 1 if step == 1 else 0
    at_edge = (sublane if axis == 1 else lane)((8, 128)) == edge
    planes = []
    for x in range(8):
        layer = 0.0 if outer is None else rolled(outer, edge - axis * x, axis - 1)
        planes.append(jnp.where(at_edge, layer, rolled(field[x], -step, axis - 1)))
    return jnp.stack(planes, axis=0)


def fluid(state):
    density, mx, my, mz, energy = [s + r for s, r in zip(state, free_stream)]
    inverse = 1.0 / density
    momentum = (mx, my, mz)
    velocity = [m * inverse for m in momentum]
    pressure = gamma_less * (
        energy - 0.5 * (mx * velocity[0] + my * velocity[1] + mz * velocity[2])
    )
    return momentum, velocity, pressure, energy + pressure


def split_flux(state, parts, axis, sign):
    momentum, velocity, pressure, enthalpy = parts
    speed = velocity[axis]
    flux = [momentum[axis]]
    for c in range(3):
        term = momentum[c] * speed
        flux.append(term + pressure if c == axis else term)
    flux.append(enthalpy * speed)
    if sign > 0:
        return [flux_half * (s + f) for s, f in zip(state, flux)]
    return [flux_half * (s - f) for s, f in zip(state, flux)]


def les_rate(state, halos):
    parts = fluid(state)
    total = [-6.0 * flux_half * s for s in state]
    for axis in range(3):
        ahead = split_flux(state, parts, axis, -1)
        behind = split_flux(state, parts, axis, 1)
        ahead_outer = behind_outer = [None] * 5
        if halos is not None:
            before, after = halos[axis]
            ahead_outer = split_flux(after, fluid(after), axis, -1)
            behind_outer = split_flux(before, fluid(before), axis, 1)
        for c in range(5):
            total[c] = total[c] + (
                shifted(ahead[c], axis, 1, ahead_outer[c])
                + shifted(behind[c], axis, -1, behind_outer[c])
            )
    return total


def les_outer(halos):
    return [
        halo
        and (
            split_flux(halo[0], fluid(halo[0]), axis, 1),
            split_flux(halo[1], fluid(halo[1]), axis, -1),
        )
        for axis, halo in enumerate(halos)
    ]


def with_layers(field, layers):
    row, column = sublane((8, 128)), lane((8, 128))
    along_z = layers[2]
    if along_z is not None:
        along_z = jnp.where(lax.rem(column, 2) == 0, along_z[0], rolled(along_z[1], -1, 1))
    planes = []
    for x in range(8):
        plane = field[x]
        if layers[0] is not None and x in (0, 7):
            plane = plane + layers[0][x // 7]
        if layers[1] is not None:
            low, high = layers[1]
            plane = plane + jnp.where(
                row == 0, rolled(low, -x, 0), jnp.where(row == 7, rolled(high, 7 - x, 0), 0.0)
            )
        if along_z is not None:
            ends = (column == 0) | (column == 127)
            plane = plane + jnp.where(ends, rolled(along_z, -2 * x, 1), 0.0)
        planes.append(plane)
    return planes


def wave_flux(state, mean, axis):
    speed = mean[axis]
    pressure = state[0]
    rows = [speed * pressure + state[1 + axis]]
    for c in range(3):
        term = speed * state[1 + c]
        rows.append(term + pressure if c == axis else term)
    return rows


def dot3(left, right):
    high = left.astype(jnp.bfloat16)
    low = (left - high.astype(f32)).astype(jnp.bfloat16)
    dot = functools.partial(jnp.dot, preferred_element_type=f32)
    return dot(high, right[0]) + (dot(low, right[0]) + dot(high, right[1]))


def acoustic_rate(state, mean, halos, deriv, along_z):
    shape = state[0].shape
    table = derivative_matrix()
    flux = wave_flux(state, mean, 0)
    if halos is None:
        halos = [([jnp.zeros((8, 128), f32)] * 4,) * 2] + [([None] * 4,) * 2] * 2
    before, after = halos[0]
    low_mean, high_mean = [m[0] for m in mean], [m[7] for m in mean]
    low_jump = [b - s[0] for b, s in zip(before, state)]
    high_jump = [a - s[7] for a, s in zip(after, state)]
    low_flux = wave_flux(low_jump, low_mean, 0)
    high_flux = wave_flux(high_jump, high_mean, 0)
    half, lift = 0.5 * face_lift, 0.5 * face_lift * upwind_speed
    total = []
    for c in range(4):
        planes = []
        for i in range(8):
            plane = -float(table[i, 0]) * flux[c][0]
            for a in range(1, 8):
                if abs(table[i, a]) > 1e-12:
                    plane = plane - float(table[i, a]) * flux[c][a]
            if i == 0:
                plane = plane + (half * low_flux[c] + lift * low_jump[c])
            if i == 7:
                plane = plane - (half * high_flux[c] - lift * high_jump[c])
            planes.append(plane)
        total.append(jnp.stack(planes, axis=0))
    flux = wave_flux(state, mean, 1)
    before, after = halos[1]
    row = sublane(shape)
    sign = jnp.where(row == 0, half, jnp.where(row == 7, -half, 0.0))
    jump = []
    for s, b, a in zip(state, before, after):
        planes = []
        for x in range(8):
            low = 0.0 if b is None else rolled(b, -x, 0)
            high = 0.0 if a is None else rolled(a, 7 - x, 0)
            planes.append(jnp.where(row[x] == 0, low, jnp.where(row[x] == 7, high, s[x])) - s[x])
        jump.append(jnp.stack(planes, axis=0))
    jump_flux = wave_flux(jump, mean, 1)
    for c in range(4):
        change = lift * jump[c] + sign * jump_flux[c]
        for b in range(8):
            change = change - deriv[:, b : b + 1][None] * flux[c][:, b : b + 1, :]
        total[c] = total[c] + change
    flux = wave_flux(state, mean, 2)
    before, after = halos[2]
    column = lane(shape)
    place = lax.rem(column, 8)
    sign = jnp.where(place == 0, half, jnp.where(place == 7, -half, 0.0))
    jump = [
        jnp.where(
            place == 0,
            shifted(s, 2, -1, b),
            jnp.where(place == 7, shifted(s, 2, 1, a), s),
        )
        - s
        for s, b, a in zip(state, before, after)
    ]
    jump_flux = wave_flux(jump, mean, 2)
    for c in range(4):
        slope = dot3(flux[c].reshape(64, 128), along_z).reshape(shape)
        total[c] = total[c] + (lift * jump[c] + sign * jump_flux[c] - slope)
    return total


def mean_layers(mean):
    return [
        [m[0] for m in mean],
        [m[7] for m in mean],
        [m[:, 0, :] for m in mean],
        [m[:, 7, :] for m in mean],
        [z_layer(m, jnp.int32(0)) for m in mean],
        [z_layer(m, jnp.int32(127)) for m in mean],
    ]


def acoustic_outer(mean_faces, halos):
    half, lift = 0.5 * face_lift, 0.5 * face_lift * upwind_speed
    layers = []
    for axis, halo in enumerate(halos):
        if halo is None:
            layers.append(None)
            continue
        before, after = halo
        low_flux = wave_flux(before, mean_faces[2 * axis], axis)
        high_flux = wave_flux(after, mean_faces[2 * axis + 1], axis)
        layers.append(
            (
                [half * f + lift * b for f, b in zip(low_flux, before)],
                [lift * a - half * f for f, a in zip(high_flux, after)],
            )
        )
    return layers


def tile_rows(matrix):
    spread = (lax.rem(lane((8, 128)), 8) == sublane((8, 128))).astype(f32)
    return jnp.dot(
        matrix, spread, precision=lax.Precision.HIGHEST, preferred_element_type=f32
    )


def pairings(count):
    sets = []
    for first in (0, 1):
        pairs = [(i, i + 1) for i in range(first, count - 1, 2)]
        if pairs:
            sets.append(pairs)
    return sets


def slots(counts):
    found = [(axis, n) for axis in range(3) for n in range(len(pairings(counts[axis])))]
    lower = ((2, 1), (2, 0), (0, 1), (1, 0), (1, 1), (0, 0))
    upper = ((2, 1), (0, 1), (2, 0), (0, 0), (1, 1), (1, 0))
    lower = [swap for swap in lower if swap in found]
    upper = [swap for swap in upper if swap in found] if counts[1] == 4 else lower
    return list(zip(lower, upper))


def in_upper_half(counts):
    return lax.axis_index("gy") >= counts[1] // 2


def routes(counts):
    places = [(x, y, z) for x in range(counts[0]) for y in range(counts[1]) for z in range(counts[2])]
    number = {place: n for n, place in enumerate(places)}

    def partner(place, axis, n):
        pairs = pairings(counts[axis])[n]
        swap = dict(pairs + [(j, i) for i, j in pairs])
        alone = [i for i in range(counts[axis]) if i not in swap]
        spare = 0 if axis else 2
        other = list(place)
        if place[axis] in swap:
            other[axis] = swap[place[axis]]
        elif axis == 0 and len(alone) == 2:
            other[axis] = sum(alone) - place[axis]
        elif counts[spare] % 2 == 0:
            other[spare] = place[spare] ^ 1
        return number[tuple(other)]

    return [
        [
            (number[place], partner(place, *(upper if place[1] >= counts[1] // 2 else lower)))
            for place in places
        ]
        for lower, upper in slots(counts)
    ]


def z_layer(field, at):
    packed = jnp.zeros((8, 128), f32)
    column = lane((8, 128))
    for x in range(8):
        turned = pltpu.roll(field[x], lax.rem(2 * x - at + 128, 128), 1)
        packed = jnp.where(column == 2 * x, turned, packed)
    return packed


def store_faces(fields, out_refs, counts):
    high_half = in_upper_half(counts)
    for c, field in enumerate(fields):
        faces = {}
        for axis in range(3):
            even = lax.rem(lax.axis_index(axes[axis]), 2) == 0
            if axis == 0:
                low, high = field[0], field[7]
            elif axis == 1:
                low, high = field[:, 0, :], field[:, 7, :]
            for n in range(len(pairings(counts[axis]))):
                last = even == (n == 0)
                if axis == 2:
                    faces[axis, n] = z_layer(field, jnp.where(last, 127, 0))
                else:
                    faces[axis, n] = jnp.where(last, high, low)
        for ref, (lower, upper) in zip(out_refs, slots(counts)):
            if lower == upper:
                ref[c] = faces[lower]
            else:
                ref[c] = jnp.where(high_half, faces[upper], faces[lower])


def load_faces(in_refs, counts, first, last, chosen=(0, 1, 2)):
    high_half = in_upper_half(counts)
    lower, upper = zip(*slots(counts))
    halos = []
    for axis in range(3):
        if axis not in chosen:
            halos.append(None)
            continue
        place = lax.axis_index(axes[axis])
        even = lax.rem(place, 2) == 0
        got = []
        for n in range(len(pairings(counts[axis]))):
            a, b = in_refs[lower.index((axis, n))], in_refs[upper.index((axis, n))]
            got.append(
                [a[c] if a is b else jnp.where(high_half, b[c], a[c]) for c in range(first, last)]
            )
        while len(got) < 2:
            got.append([jnp.zeros((8, 128), f32)] * (last - first))
        before = [jnp.where(place == 0, 0.0, jnp.where(even, b, a)) for a, b in zip(*got)]
        after = [
            jnp.where(place == counts[axis] - 1, 0.0, jnp.where(even, a, b))
            for a, b in zip(*got)
        ]
        halos.append((before, after))
    return halos


def face_shapes(counts, width):
    total = sum(len(pairings(count)) for count in counts)
    return [jax.ShapeDtypeStruct((width, 8, 128), f32)] * total


def exchange(faces, counts):
    return [lax.ppermute(face, axes, way) for face, way in zip(faces, routes(counts))]


def read_all(ref):
    return [ref[c] for c in range(ref.shape[0])]


def load_kernel(counts, *refs):
    sources, targets, out_refs, sems = refs[:5], refs[5:10], refs[10:-1], refs[-1]
    copies = [
        pltpu.make_async_copy(source, target, sems.at[n])
        for n, (source, target) in enumerate(zip(sources, targets))
    ]
    for copy in copies:
        copy.start()
    for copy in copies:
        copy.wait()
    store_faces(read_all(targets[0]) + read_all(targets[1]), out_refs, counts)


def partners(count):
    if count == window:
        return [[(i, i ^ mask) for i in range(count)] for mask in range(count)]
    turns = sorted({d % count for d in range(1 - window, window)})
    return [[(i, (i + turn) % count) for i in range(count)] for turn in turns]


def sending_sets(count):
    return [3, 2, 1, 0] if count == window else list(range(count))


def plan_kernel(
    counts, owner_ref, slot_ref, proj_ref, order_ref, marks_ref, along_x_ref, along_y_ref, tile_ref
):
    count = counts[0]
    n_sets = len(partners(count))
    own = lax.axis_index("gx")
    n_blocks = owner_ref.shape[-1]
    square = (n_blocks, n_blocks)
    block, other = sublane(square), lane(square)

    def spread(ref):
        by_lane = jnp.broadcast_to(ref[0], square)
        here = jnp.where(block == other, by_lane, 0).astype(f32)
        return by_lane, jnp.sum(here, axis=1, keepdims=True).astype(jnp.int32)

    def group_of(owner):
        if count == window:
            return lax.bitwise_xor(owner, own)
        turn = lax.rem(owner - own + count, count)
        if n_sets == count:
            return turn
        return jnp.where(turn < window, turn, turn - (count - n_sets))

    owner_by_lane, owner = spread(owner_ref)
    slot = spread(slot_ref)[1]
    group = group_of(owner)
    before = (group_of(owner_by_lane) == group) & (other < block)
    taken = jnp.sum(before.astype(f32), axis=1, keepdims=True).astype(jnp.int32)
    wide = (n_blocks, 128)
    place = jnp.broadcast_to(group * window + taken, wide)
    column = lane((8, 128))
    quarter = column // 32
    for s in range((n_sets + 3) // 4):
        here = place - 16 * s == lane(wide) // 8
        label = jnp.sum(jnp.where(here, (slot + 1).astype(f32), 0.0), axis=0, keepdims=True) - 1.0
        source = jnp.sum(
            jnp.where(here, (8 * sublane(wide)).astype(f32), 0.0), axis=0, keepdims=True
        )
        labels = jnp.broadcast_to(label, (8, 128))
        order = jnp.broadcast_to(source, (8, 128)).astype(jnp.int32) + lax.rem(column, 8)
        for t in range(4):
            order_ref[4 * s + t] = rolled(order, 32 * t, 1)
        for r in range(min(4, n_sets - 4 * s)):
            marks = labels
            for t in range(1, 4):
                marks = jnp.where(quarter == (r + t) % 4, rolled(labels, 32 * t, 1), marks)
            marks_ref[4 * s + r] = marks
    proj = proj_ref[...]
    for a in range(8):
        along_y = jnp.broadcast_to(proj[:, a : a + 1], (8, 128))
        along_y_ref[a] = along_y
        for i in range(8):
            along_x_ref[8 * i + a] = jnp.broadcast_to(along_y[i : i + 1], (8, 128))
    tile = tile_rows(proj)
    high = tile.astype(jnp.bfloat16).astype(f32)
    tile_ref[0] = high
    tile_ref[1] = tile - high


def speeds(state):
    inverse = 1.0 / (state[0] + 1.0)
    return [state[c] * inverse for c in (1, 2, 3)]


def vorticity_kernel(les_ref, velocity_ref, vort_ref):
    velocity = speeds([les_ref[c] for c in range(4)])

    def slope(c, axis):
        return shifted(velocity[c], axis, 1) - shifted(velocity[c], axis, -1)

    vort = [slope(2, 1) - slope(1, 2), slope(0, 2) - slope(2, 0), slope(1, 0) - slope(0, 1)]
    for c in range(3):
        velocity_ref[c] = velocity[c]
        vort_ref[c] = vort[c]


def vorticity_z_kernel(counts, present, vort_ref, *refs):
    refs = list(refs)
    face_refs = [refs.pop(0) if here else None for here in present]
    (out_ref,) = refs
    before, after = [speeds(layer) for layer in load_faces(face_refs, counts, 0, 4, (2,))[2]]
    for c, layer in ((0, (before[1], -after[1])), (1, (-before[0], after[0]))):
        for x, plane in enumerate(with_layers(vort_ref[c], (None, None, layer))):
            out_ref[c, x] = plane
    out_ref[2] = vort_ref[2]


def lamb_kernel(
    counts, n_faces, order_ref, marks_ref, along_x_ref, along_y_ref, velocity_ref, vort_ref, *refs
):
    face_refs, out_refs = refs[:n_faces], refs[n_faces:]
    outer = [
        halo and (speeds(halo[0]), speeds(halo[1]))
        for halo in load_faces(face_refs, counts, 0, 4, (0, 1))
    ]

    def rise(c, axis):
        return -outer[axis][0][c], outer[axis][1][c]

    def fall(c, axis):
        return outer[axis][0][c], -outer[axis][1][c]

    layers = [
        (None, rise(2, 1), None),
        (fall(2, 0), None, None),
        (rise(1, 0), fall(0, 1), None),
    ]
    vort = [0.5 * jnp.stack(with_layers(vort_ref[c], layers[c]), axis=0) for c in range(3)]
    velocity = read_all(velocity_ref)
    lamb = [
        vort[1] * velocity[2] - vort[2] * velocity[1],
        vort[2] * velocity[0] - vort[0] * velocity[2],
        vort[0] * velocity[1] - vort[1] * velocity[0],
    ]
    blocks = []
    for field in lamb:
        along_y = along_y_ref[0][None] * field[:, 0:1, :]
        for b in range(1, 8):
            along_y = along_y + along_y_ref[b][None] * field[:, b : b + 1, :]
        for i in range(8):
            plane = along_x_ref[8 * i] * along_y[0]
            for a in range(1, 8):
                plane = plane + along_x_ref[8 * i + a] * along_y[a]
            blocks.append(plane)

    quarter = lane((8, 128)) // 32
    for s in range((len(out_refs) + 3) // 4):
        ordered = [
            jnp.take_along_axis(block, order_ref[4 * s + k % 4], axis=1)
            for k, block in enumerate(blocks)
        ]
        for r in range(min(4, len(out_refs) - 4 * s)):
            out = out_refs[4 * s + r]
            for q in range(6):
                packed = ordered[4 * q]
                for t in range(1, 4):
                    packed = jnp.where(quarter == (r + t) % 4, ordered[4 * q + t], packed)
                out[q] = packed
            out[6] = marks_ref[4 * s + r]


def first_kernel(
    counts, n_faces, deriv_ref, high_ref, low_ref, les_ref, wave_ref, mean_ref, *refs
):
    face_refs, (section_ref, rate_ref, mean_faces_ref), out_refs = (
        refs[:n_faces], refs[n_faces : n_faces + 3], refs[n_faces + 3 :],
    )
    for n, face in enumerate(mean_layers(read_all(mean_ref))):
        for c in range(3):
            mean_faces_ref[n, c] = face[c]
    state = read_all(les_ref)
    rate = les_rate(state, load_faces(face_refs, counts, 0, 5))
    section = [s + r for s, r in zip(state, rate)]
    for c in range(5):
        section_ref[c] = section[c]
    rate = acoustic_rate(
        read_all(wave_ref), read_all(mean_ref), load_faces(face_refs, counts, 5, 9),
        deriv_ref[...], (high_ref[...], low_ref[...]),
    )
    for c in range(4):
        rate_ref[c] = rate[c]
    store_faces(section + [wave_ref[0] + acoustic_step * rate[0]], out_refs, counts)


def source_kernel(counts, n_faces, tile_ref, wave_ref, rate_ref, *refs):
    n_pieces = len(partners(counts[0]))
    pieces = [None] * n_pieces
    for ref, k in zip(refs, sending_sets(n_pieces)):
        pieces[k] = ref
    refs = refs[n_pieces:]
    ready_faces, source_ref, face_refs = refs[:n_faces], refs[n_faces], refs[n_faces + 1 :]
    quarter = lane((8, 128)) // 32
    tile_high, tile_low = tile_ref[0], tile_ref[1]
    total = None
    for s in range((n_pieces + 3) // 4):
        count = min(4, n_pieces - 4 * s)

        def gathered(q, t):
            value = jnp.full((8, 128), -1.0 if q == 6 else 0.0, f32)
            for r in range(count):
                value = jnp.where(quarter == (r + t) % 4, pieces[4 * s + r][q], value)
            return value

        here = [gathered(6, 0).astype(jnp.int32) == slot for slot in range(16)]
        chosen_high, chosen_low = [
            jnp.concatenate([jnp.where(h, part, 0.0) for h in here], axis=0).astype(jnp.bfloat16)
            for part in (tile_high, tile_low)
        ]
        data = []
        for k in range(24):
            piece = gathered(k // 4, k % 4)
            data.append(pltpu.roll(piece, 128 - 32 * (k % 4), 1) if k % 4 else piece)
        data = jnp.concatenate(data, axis=0)
        high = data.astype(jnp.bfloat16)
        low = (data - high.astype(f32)).astype(jnp.bfloat16)
        dot = functools.partial(
            lax.dot_general,
            dimension_numbers=(((1,), (1,)), ((), ())),
            preferred_element_type=f32,
        )
        moved = dot(high, chosen_high) + (dot(low, chosen_high) + dot(high, chosen_low))
        total = moved if total is None else total + moved
    source = [total[64 * c : 64 * c + 64].reshape(8, 8, 128) for c in range(3)]
    middle = []
    for c in range(3):
        source_ref[c] = source[c]
        middle.append(wave_ref[1 + c] + acoustic_step * (rate_ref[1 + c] + source[c]))
    for ready, face in zip(ready_faces, face_refs):
        face[0:6] = ready[...]
    store_faces(middle, [face.at[6:9] for face in face_refs], counts)


def inner_kernel(
    deriv_ref, high_ref, low_ref, les_ref, section_ref, wave_ref, rate_ref, mean_ref, source_ref,
    les_base_ref, wave_base_ref, source_out, sem,
):
    copy = pltpu.make_async_copy(source_ref, source_out, sem)
    copy.start()
    section = read_all(section_ref)
    rate = les_rate(section, None)
    for c in range(5):
        les_base_ref[c] = 0.5 * ((les_ref[c] + section[c]) + rate[c])
    first = read_all(rate_ref)
    middle = [wave_ref[0] + acoustic_step * first[0]]
    for c in range(1, 4):
        middle.append(wave_ref[c] + acoustic_step * (first[c] + source_ref[c - 1]))
    rate = acoustic_rate(
        middle, read_all(mean_ref), None, deriv_ref[...], (high_ref[...], low_ref[...])
    )
    for c in range(4):
        total = rate[c] + source_ref[c - 1] if c else rate[c]
        wave_base_ref[c] = 0.5 * (wave_ref[c] + middle[c] + acoustic_step * total)
    copy.wait()


def add_layers(counts, chosen, face_refs, mean_faces_ref, les_base_ref, wave_base_ref, put):
    layers = les_outer(load_faces(face_refs, counts, 0, 5, chosen))
    for c in range(5):
        part = [layer and (0.5 * layer[0][c], 0.5 * layer[1][c]) for layer in layers]
        put(c, with_layers(les_base_ref[c], part))
    mean_faces = [[mean_faces_ref[n, c] for c in range(3)] for n in range(6)]
    layers = acoustic_outer(mean_faces, load_faces(face_refs, counts, 5, 9, chosen))
    step = 0.5 * acoustic_step
    for c in range(4):
        part = [layer and (step * layer[0][c], step * layer[1][c]) for layer in layers]
        put(5 + c, with_layers(wave_base_ref[c], part))


def z_faces(faces, counts):
    holds = [any(axis == 2 for axis, _ in pair) for pair in slots(counts)]
    return [face if hold else None for face, hold in zip(faces, holds)]


def z_kernel(counts, present, les_base_ref, wave_base_ref, mean_faces_ref, *refs):
    refs = list(refs)
    face_refs = [refs.pop(0) if here else None for here in present]
    les_ref, wave_ref = refs

    def put(c, planes):
        for x, plane in enumerate(planes):
            if c < 5:
                les_ref[c, x] = plane
            else:
                wave_ref[c - 5, x] = plane

    add_layers(counts, (2,), face_refs, mean_faces_ref, les_base_ref, wave_base_ref, put)


def last_kernel(counts, n_faces, les_base_ref, wave_base_ref, mean_faces_ref, *refs):
    face_refs, (les_out, wave_out, les_ref, wave_ref, sems) = (
        refs[:n_faces], refs[n_faces:],
    )
    copies = [
        pltpu.make_async_copy(les_ref, les_out, sems.at[0]),
        pltpu.make_async_copy(wave_ref, wave_out, sems.at[1]),
    ]

    def put(c, planes):
        for x, plane in enumerate(planes):
            if c < 5:
                les_ref[c, x] = plane
            else:
                wave_ref[c - 5, x] = plane
        if c in (4, 8):
            copies[c // 8].start()

    add_layers(counts, (0, 1), face_refs, mean_faces_ref, les_base_ref, wave_base_ref, put)
    for copy in copies:
        copy.wait()


VMEM = pl.BlockSpec(memory_space=pltpu.VMEM)


HBM = pl.BlockSpec(memory_space=pltpu.HBM)


def call(kernel, in_specs, out_shapes, name, cost, scratch=(), out_spec=None):
    return pl.pallas_call(
        kernel,
        in_specs=in_specs,
        out_specs=out_spec or [VMEM] * len(out_shapes),
        out_shape=out_shapes,
        scratch_shapes=list(scratch),
        name=name,
        cost_estimate=pl.CostEstimate(flops=cost, bytes_accessed=800000, transcendentals=0),
        compiler_params=pltpu.CompilerParams(vmem_limit_bytes=24 * 1024 * 1024),
    )


def local(counts, les, wave, mean, projection, owner, slot):
    shape = les.shape[1:]
    faces = face_shapes(counts, 9)
    n_faces = len(faces)
    like = lambda n: jax.ShapeDtypeStruct((n,) + shape, f32)

    table = derivative_matrix()
    deriv = jnp.asarray(table, f32)
    along_z = np.kron(np.eye(16), table.T).astype(np.float32)
    high = along_z.astype(jnp.bfloat16)
    low = (along_z - high.astype(np.float32)).astype(jnp.bfloat16)
    tables = (deriv, jnp.asarray(high), jnp.asarray(low))

    arguments = (les, wave, owner, slot, projection)
    les, wave, owner, slot, projection, *sent = call(
        functools.partial(load_kernel, counts),
        [HBM] * 5,
        [jax.ShapeDtypeStruct(a.shape, a.dtype) for a in arguments] + faces,
        "load_and_faces",
        100000,
        [pltpu.SemaphoreType.DMA((5,))],
    )(*(pltpu.with_memory_space_constraint(a, pltpu.HBM) for a in arguments))
    got = exchange(sent, counts)

    sets = partners(counts[0])
    n_plans = 4 * ((len(sets) + 3) // 4)
    order, marks, along_x, along_y, tile = call(
        functools.partial(plan_kernel, counts),
        [VMEM] * 3,
        [
            jax.ShapeDtypeStruct((n_plans, 8, 128), jnp.int32),
            jax.ShapeDtypeStruct((len(sets), 8, 128), f32),
            jax.ShapeDtypeStruct((64, 8, 128), f32),
            jax.ShapeDtypeStruct((8, 8, 128), f32),
            jax.ShapeDtypeStruct((2, 8, 128), f32),
        ],
        "plan",
        1000000,
    )(owner, slot, projection)
    turning = list(call(vorticity_kernel, [VMEM], [like(3)] * 2, "vorticity", 1000000)(les))
    z_got = z_faces(got, counts)
    present = [face is not None for face in z_got]
    turning[1] = call(
        functools.partial(vorticity_z_kernel, counts, present),
        [VMEM] * (1 + sum(present)),
        [like(3)],
        "vorticity_z",
        1000000,
    )(turning[1], *(face for face in z_got if face is not None))[0]
    pieces = call(
        functools.partial(lamb_kernel, counts, n_faces),
        [VMEM] * (6 + n_faces),
        [jax.ShapeDtypeStruct((7, 8, 128), f32)] * len(sets),
        "lamb_blocks",
        10000000,
    )(order, marks, along_x, along_y, *turning, *got)
    moved = []
    for k in sending_sets(len(sets)):
        still = all(i == j for i, j in sets[k])
        moved.append(pieces[k] if still else lax.ppermute(pieces[k], "gx", sets[k]))
    section, rate, mean_faces, *ready_faces = call(
        functools.partial(first_kernel, counts, n_faces),
        [VMEM] * (6 + n_faces),
        [like(5), like(4), jax.ShapeDtypeStruct((6, 3, 8, 128), f32)] + face_shapes(counts, 6),
        "first_rates",
        40000000,
    )(*tables, les, wave, mean, *got)

    source, *sent = call(
        functools.partial(source_kernel, counts, n_faces),
        [VMEM] * (3 + len(moved) + n_faces),
        [like(3)] + faces,
        "source_and_faces",
        10000000,
    )(tile, wave, rate, *moved, *ready_faces)
    got = exchange(sent, counts)
    les_base, wave_base, source_out = call(
        inner_kernel,
        [VMEM] * 9,
        [like(5), like(4), like(3)],
        "second_rates_inner",
        40000000,
        [pltpu.SemaphoreType.DMA],
        out_spec=[VMEM, VMEM, HBM],
    )(*tables, les, section, wave, rate, mean, source)
    z_got = z_faces(got, counts)
    present = [face is not None for face in z_got]
    les_base, wave_base = call(
        functools.partial(z_kernel, counts, present),
        [VMEM] * (3 + sum(present)),
        [like(5), like(4)],
        "second_rates_z",
        1000000,
    )(les_base, wave_base, mean_faces, *(face for face in z_got if face is not None))
    les_next, wave_next = call(
        functools.partial(last_kernel, counts, n_faces),
        [VMEM] * (3 + n_faces),
        [like(5), like(4)],
        "second_rates_outer",
        4000000,
        [
            pltpu.VMEM(les.shape, f32),
            pltpu.VMEM(wave.shape, f32),
            pltpu.SemaphoreType.DMA((2,)),
        ],
        out_spec=[HBM, HBM],
    )(les_base, wave_base, mean_faces, *got)
    return les_next, source_out, wave_next


def solution(mesh):
    counts = tuple(mesh.shape[axis] for axis in axes)
    field = P(None, *axes)
    return jax.shard_map(
        functools.partial(local, counts),
        mesh=mesh,
        in_specs=(field, field, field, P(), P(*axes), P(*axes)),
        out_specs=(field, field, field),
        check_vma=False,
    )
```

```python
import functools

import jax
import jax.numpy as jnp
import numpy as np
from jax import lax
from jax.experimental import pallas as pl
from jax.experimental.pallas import tpu as pltpu
from jax.sharding import PartitionSpec as P

lobatto_points = np.array(
    [
        -1.0,
        -0.8717401485096066,
        -0.5917001814331423,
        -0.2092992179024789,
        0.2092992179024789,
        0.5917001814331423,
        0.8717401485096066,
        1.0,
    ]
)
flux_half = 0.08
gamma_less = 0.4
acoustic_step = 0.01
upwind_speed = 1.5
face_lift = 28.0
free_stream = (1.0, 0.0, 0.0, 0.0, 2.5)
axes = ("gx", "gy", "gz")
window = 4
f32 = jnp.float32


def derivative_matrix():
    points = lobatto_points
    products = [np.prod([points[i] - points[j] for j in range(8) if j != i]) for i in range(8)]
    matrix = np.zeros((8, 8))
    for i in range(8):
        for j in range(8):
            if j != i:
                matrix[i, j] = products[i] / (products[j] * (points[i] - points[j]))
        matrix[i, i] = -np.sum(matrix[i])
    return matrix


def sublane(shape):
    return lax.broadcasted_iota(jnp.int32, shape, len(shape) - 2)


def lane(shape):
    return lax.broadcasted_iota(jnp.int32, shape, len(shape) - 1)


def rolled(tile, amount, axis):
    amount = amount % tile.shape[axis]
    return pltpu.roll(tile, amount, axis) if amount else tile


def shifted(field, axis, step, outer=None):
    if axis == 0:
        outer = jnp.zeros((8, 128), f32) if outer is None else outer
        if step == 1:
            return jnp.concatenate([field[1:], outer[None]], axis=0)
        return jnp.concatenate([outer[None], field[:-1]], axis=0)
    count = (8, 128)[axis - 1]
    edge = count - 1 if step == 1 else 0
    at_edge = (sublane if axis == 1 else lane)((8, 128)) == edge
    planes = []
    for x in range(8):
        layer = 0.0 if outer is None else rolled(outer, edge - axis * x, axis - 1)
        planes.append(jnp.where(at_edge, layer, rolled(field[x], -step, axis - 1)))
    return jnp.stack(planes, axis=0)


def fluid(state):
    density, mx, my, mz, energy = [s + r for s, r in zip(state, free_stream)]
    inverse = 1.0 / density
    momentum = (mx, my, mz)
    velocity = [m * inverse for m in momentum]
    pressure = gamma_less * (
        energy - 0.5 * (mx * velocity[0] + my * velocity[1] + mz * velocity[2])
    )
    return momentum, velocity, pressure, energy + pressure


def split_flux(state, parts, axis, sign):
    momentum, velocity, pressure, enthalpy = parts
    speed = velocity[axis]
    flux = [momentum[axis]]
    for c in range(3):
        term = momentum[c] * speed
        flux.append(term + pressure if c == axis else term)
    flux.append(enthalpy * speed)
    if sign > 0:
        return [flux_half * (s + f) for s, f in zip(state, flux)]
    return [flux_half * (s - f) for s, f in zip(state, flux)]


def les_rate(state, halos):
    parts = fluid(state)
    total = [-6.0 * flux_half * s for s in state]
    for axis in range(3):
        ahead = split_flux(state, parts, axis, -1)
        behind = split_flux(state, parts, axis, 1)
        ahead_outer = behind_outer = [None] * 5
        if halos is not None:
            before, after = halos[axis]
            ahead_outer = split_flux(after, fluid(after), axis, -1)
            behind_outer = split_flux(before, fluid(before), axis, 1)
        for c in range(5):
            total[c] = total[c] + (
                shifted(ahead[c], axis, 1, ahead_outer[c])
                + shifted(behind[c], axis, -1, behind_outer[c])
            )
    return total


def les_outer(halos):
    return [
        halo
        and (
            split_flux(halo[0], fluid(halo[0]), axis, 1),
            split_flux(halo[1], fluid(halo[1]), axis, -1),
        )
        for axis, halo in enumerate(halos)
    ]


def with_layers(field, layers):
    row, column = sublane((8, 128)), lane((8, 128))
    along_z = layers[2]
    if along_z is not None:
        along_z = jnp.where(lax.rem(column, 2) == 0, along_z[0], rolled(along_z[1], -1, 1))
    planes = []
    for x in range(8):
        plane = field[x]
        if layers[0] is not None and x in (0, 7):
            plane = plane + layers[0][x // 7]
        if layers[1] is not None:
            low, high = layers[1]
            plane = plane + jnp.where(
                row == 0, rolled(low, -x, 0), jnp.where(row == 7, rolled(high, 7 - x, 0), 0.0)
            )
        if along_z is not None:
            ends = (column == 0) | (column == 127)
            plane = plane + jnp.where(ends, rolled(along_z, -2 * x, 1), 0.0)
        planes.append(plane)
    return planes


def wave_flux(state, mean, axis):
    speed = mean[axis]
    pressure = state[0]
    rows = [speed * pressure + state[1 + axis]]
    for c in range(3):
        term = speed * state[1 + c]
        rows.append(term + pressure if c == axis else term)
    return rows


def dot3(left, right):
    high = left.astype(jnp.bfloat16)
    low = (left - high.astype(f32)).astype(jnp.bfloat16)
    dot = functools.partial(jnp.dot, preferred_element_type=f32)
    return dot(high, right[0]) + (dot(low, right[0]) + dot(high, right[1]))


def acoustic_rate(state, mean, halos, deriv, along_z):
    shape = state[0].shape
    table = derivative_matrix()
    flux = wave_flux(state, mean, 0)
    if halos is None:
        halos = [([jnp.zeros((8, 128), f32)] * 4,) * 2] + [([None] * 4,) * 2] * 2
    before, after = halos[0]
    low_mean, high_mean = [m[0] for m in mean], [m[7] for m in mean]
    low_jump = [b - s[0] for b, s in zip(before, state)]
    high_jump = [a - s[7] for a, s in zip(after, state)]
    low_flux = wave_flux(low_jump, low_mean, 0)
    high_flux = wave_flux(high_jump, high_mean, 0)
    half, lift = 0.5 * face_lift, 0.5 * face_lift * upwind_speed
    total = []
    for c in range(4):
        planes = []
        for i in range(8):
            plane = -float(table[i, 0]) * flux[c][0]
            for a in range(1, 8):
                if abs(table[i, a]) > 1e-12:
                    plane = plane - float(table[i, a]) * flux[c][a]
            if i == 0:
                plane = plane + (half * low_flux[c] + lift * low_jump[c])
            if i == 7:
                plane = plane - (half * high_flux[c] - lift * high_jump[c])
            planes.append(plane)
        total.append(jnp.stack(planes, axis=0))
    flux = wave_flux(state, mean, 1)
    before, after = halos[1]
    row = sublane(shape)
    sign = jnp.where(row == 0, half, jnp.where(row == 7, -half, 0.0))
    jump = []
    for s, b, a in zip(state, before, after):
        planes = []
        for x in range(8):
            low = 0.0 if b is None else rolled(b, -x, 0)
            high = 0.0 if a is None else rolled(a, 7 - x, 0)
            planes.append(jnp.where(row[x] == 0, low, jnp.where(row[x] == 7, high, s[x])) - s[x])
        jump.append(jnp.stack(planes, axis=0))
    jump_flux = wave_flux(jump, mean, 1)
    for c in range(4):
        change = lift * jump[c] + sign * jump_flux[c]
        for b in range(8):
            change = change - deriv[:, b : b + 1][None] * flux[c][:, b : b + 1, :]
        total[c] = total[c] + change
    flux = wave_flux(state, mean, 2)
    before, after = halos[2]
    column = lane(shape)
    place = lax.rem(column, 8)
    sign = jnp.where(place == 0, half, jnp.where(place == 7, -half, 0.0))
    jump = [
        jnp.where(
            place == 0,
            shifted(s, 2, -1, b),
            jnp.where(place == 7, shifted(s, 2, 1, a), s),
        )
        - s
        for s, b, a in zip(state, before, after)
    ]
    jump_flux = wave_flux(jump, mean, 2)
    for c in range(4):
        slope = dot3(flux[c].reshape(64, 128), along_z).reshape(shape)
        total[c] = total[c] + (lift * jump[c] + sign * jump_flux[c] - slope)
    return total


def mean_layers(mean):
    return [
        [m[0] for m in mean],
        [m[7] for m in mean],
        [m[:, 0, :] for m in mean],
        [m[:, 7, :] for m in mean],
        [z_layer(m, jnp.int32(0)) for m in mean],
        [z_layer(m, jnp.int32(127)) for m in mean],
    ]


def acoustic_outer(mean_faces, halos):
    half, lift = 0.5 * face_lift, 0.5 * face_lift * upwind_speed
    layers = []
    for axis, halo in enumerate(halos):
        if halo is None:
            layers.append(None)
            continue
        before, after = halo
        low_flux = wave_flux(before, mean_faces[2 * axis], axis)
        high_flux = wave_flux(after, mean_faces[2 * axis + 1], axis)
        layers.append(
            (
                [half * f + lift * b for f, b in zip(low_flux, before)],
                [lift * a - half * f for f, a in zip(high_flux, after)],
            )
        )
    return layers


def tile_rows(matrix):
    spread = (lax.rem(lane((8, 128)), 8) == sublane((8, 128))).astype(f32)
    return jnp.dot(
        matrix, spread, precision=lax.Precision.HIGHEST, preferred_element_type=f32
    )


def pairings(count):
    sets = []
    for first in (0, 1):
        pairs = [(i, i + 1) for i in range(first, count - 1, 2)]
        if pairs:
            sets.append(pairs)
    return sets


def slots(counts):
    found = [(axis, n) for axis in range(3) for n in range(len(pairings(counts[axis])))]
    lower = ((2, 1), (2, 0), (0, 1), (1, 0), (1, 1), (0, 0))
    upper = ((2, 1), (0, 1), (2, 0), (0, 0), (1, 1), (1, 0))
    lower = [swap for swap in lower if swap in found]
    upper = [swap for swap in upper if swap in found] if counts[1] == 4 else lower
    return list(zip(lower, upper))


def in_upper_half(counts):
    return lax.axis_index("gy") >= counts[1] // 2


def routes(counts):
    places = [(x, y, z) for x in range(counts[0]) for y in range(counts[1]) for z in range(counts[2])]
    number = {place: n for n, place in enumerate(places)}

    def partner(place, axis, n):
        pairs = pairings(counts[axis])[n]
        swap = dict(pairs + [(j, i) for i, j in pairs])
        alone = [i for i in range(counts[axis]) if i not in swap]
        spare = 0 if axis else 2
        other = list(place)
        if place[axis] in swap:
            other[axis] = swap[place[axis]]
        elif axis == 0 and len(alone) == 2:
            other[axis] = sum(alone) - place[axis]
        elif counts[spare] % 2 == 0:
            other[spare] = place[spare] ^ 1
        return number[tuple(other)]

    return [
        [
            (number[place], partner(place, *(upper if place[1] >= counts[1] // 2 else lower)))
            for place in places
        ]
        for lower, upper in slots(counts)
    ]


def z_layer(field, at):
    packed = jnp.zeros((8, 128), f32)
    column = lane((8, 128))
    for x in range(8):
        turned = pltpu.roll(field[x], lax.rem(2 * x - at + 128, 128), 1)
        packed = jnp.where(column == 2 * x, turned, packed)
    return packed


def store_faces(fields, out_refs, counts):
    high_half = in_upper_half(counts)
    for c, field in enumerate(fields):
        faces = {}
        for axis in range(3):
            even = lax.rem(lax.axis_index(axes[axis]), 2) == 0
            if axis == 0:
                low, high = field[0], field[7]
            elif axis == 1:
                low, high = field[:, 0, :], field[:, 7, :]
            for n in range(len(pairings(counts[axis]))):
                last = even == (n == 0)
                if axis == 2:
                    faces[axis, n] = z_layer(field, jnp.where(last, 127, 0))
                else:
                    faces[axis, n] = jnp.where(last, high, low)
        for ref, (lower, upper) in zip(out_refs, slots(counts)):
            if lower == upper:
                ref[c] = faces[lower]
            else:
                ref[c] = jnp.where(high_half, faces[upper], faces[lower])


def load_faces(in_refs, counts, first, last, chosen=(0, 1, 2)):
    high_half = in_upper_half(counts)
    lower, upper = zip(*slots(counts))
    halos = []
    for axis in range(3):
        if axis not in chosen:
            halos.append(None)
            continue
        place = lax.axis_index(axes[axis])
        even = lax.rem(place, 2) == 0
        got = []
        for n in range(len(pairings(counts[axis]))):
            a, b = in_refs[lower.index((axis, n))], in_refs[upper.index((axis, n))]
            got.append(
                [a[c] if a is b else jnp.where(high_half, b[c], a[c]) for c in range(first, last)]
            )
        while len(got) < 2:
            got.append([jnp.zeros((8, 128), f32)] * (last - first))
        before = [jnp.where(place == 0, 0.0, jnp.where(even, b, a)) for a, b in zip(*got)]
        after = [
            jnp.where(place == counts[axis] - 1, 0.0, jnp.where(even, a, b))
            for a, b in zip(*got)
        ]
        halos.append((before, after))
    return halos


def face_shapes(counts, width):
    total = sum(len(pairings(count)) for count in counts)
    return [jax.ShapeDtypeStruct((width, 8, 128), f32)] * total


def exchange(faces, counts):
    return [lax.ppermute(face, axes, way) for face, way in zip(faces, routes(counts))]


def read_all(ref):
    return [ref[c] for c in range(ref.shape[0])]


def load_kernel(counts, *refs):
    sources, targets, out_refs, sems = refs[:5], refs[5:10], refs[10:-1], refs[-1]
    copies = [
        pltpu.make_async_copy(source, target, sems.at[n])
        for n, (source, target) in enumerate(zip(sources, targets))
    ]
    for copy in copies:
        copy.start()
    for copy, target, first in zip(copies, targets, (0, 5)):
        copy.wait()
        count = target.shape[0]
        store_faces(read_all(target), [ref.at[first : first + count] for ref in out_refs], counts)
    for copy in copies[2:]:
        copy.wait()


def partners(count):
    if count == window:
        return [[(i, i ^ mask) for i in range(count)] for mask in range(count)]
    turns = sorted({d % count for d in range(1 - window, window)})
    return [[(i, (i + turn) % count) for i in range(count)] for turn in turns]


def sending_sets(count):
    return [3, 2, 1, 0] if count == window else list(range(count))


def plan_kernel(
    counts, owner_ref, slot_ref, proj_ref, order_ref, marks_ref, along_x_ref, along_y_ref, tile_ref
):
    count = counts[0]
    n_sets = len(partners(count))
    own = lax.axis_index("gx")
    n_blocks = owner_ref.shape[-1]
    square = (n_blocks, n_blocks)
    block, other = sublane(square), lane(square)

    def spread(ref):
        by_lane = jnp.broadcast_to(ref[0], square)
        here = jnp.where(block == other, by_lane, 0).astype(f32)
        return by_lane, jnp.sum(here, axis=1, keepdims=True).astype(jnp.int32)

    def group_of(owner):
        if count == window:
            return lax.bitwise_xor(owner, own)
        turn = lax.rem(owner - own + count, count)
        if n_sets == count:
            return turn
        return jnp.where(turn < window, turn, turn - (count - n_sets))

    owner_by_lane, owner = spread(owner_ref)
    slot = spread(slot_ref)[1]
    group = group_of(owner)
    before = (group_of(owner_by_lane) == group) & (other < block)
    taken = jnp.sum(before.astype(f32), axis=1, keepdims=True).astype(jnp.int32)
    wide = (n_blocks, 128)
    place = jnp.broadcast_to(group * window + taken, wide)
    column = lane((8, 128))
    quarter = column // 32
    for s in range((n_sets + 3) // 4):
        here = place - 16 * s == lane(wide) // 8
        label = jnp.sum(jnp.where(here, (slot + 1).astype(f32), 0.0), axis=0, keepdims=True) - 1.0
        source = jnp.sum(
            jnp.where(here, (8 * sublane(wide)).astype(f32), 0.0), axis=0, keepdims=True
        )
        labels = jnp.broadcast_to(label, (8, 128))
        order = jnp.broadcast_to(source, (8, 128)).astype(jnp.int32) + lax.rem(column, 8)
        for t in range(4):
            order_ref[4 * s + t] = rolled(order, 32 * t, 1)
        for r in range(min(4, n_sets - 4 * s)):
            marks = labels
            for t in range(1, 4):
                marks = jnp.where(quarter == (r + t) % 4, rolled(labels, 32 * t, 1), marks)
            marks_ref[4 * s + r] = marks
    proj = proj_ref[...]
    for a in range(8):
        along_y = jnp.broadcast_to(proj[:, a : a + 1], (8, 128))
        along_y_ref[a] = along_y
        for i in range(8):
            along_x_ref[8 * i + a] = jnp.broadcast_to(along_y[i : i + 1], (8, 128))
    tile = tile_rows(proj)
    high = tile.astype(jnp.bfloat16).astype(f32)
    tile_ref[0] = high
    tile_ref[1] = tile - high


def speeds(state):
    inverse = 1.0 / (state[0] + 1.0)
    return [state[c] * inverse for c in (1, 2, 3)]


def vorticity_kernel(les_ref, velocity_ref, vort_ref):
    velocity = speeds([les_ref[c] for c in range(4)])

    def slope(c, axis):
        return shifted(velocity[c], axis, 1) - shifted(velocity[c], axis, -1)

    vort = [slope(2, 1) - slope(1, 2), slope(0, 2) - slope(2, 0), slope(1, 0) - slope(0, 1)]
    for c in range(3):
        velocity_ref[c] = velocity[c]
        vort_ref[c] = vort[c]


def vorticity_z_kernel(counts, present, vort_ref, *refs):
    refs = list(refs)
    face_refs = [refs.pop(0) if here else None for here in present]
    (out_ref,) = refs
    before, after = [speeds(layer) for layer in load_faces(face_refs, counts, 0, 4, (2,))[2]]
    for c, layer in ((0, (before[1], -after[1])), (1, (-before[0], after[0]))):
        for x, plane in enumerate(with_layers(vort_ref[c], (None, None, layer))):
            out_ref[c, x] = plane
    out_ref[2] = vort_ref[2]


def lamb_kernel(
    counts, n_faces, order_ref, marks_ref, along_x_ref, along_y_ref, velocity_ref, vort_ref, *refs
):
    face_refs, out_refs = refs[:n_faces], refs[n_faces:]
    outer = [
        halo and (speeds(halo[0]), speeds(halo[1]))
        for halo in load_faces(face_refs, counts, 0, 4, (0, 1))
    ]

    def rise(c, axis):
        return -outer[axis][0][c], outer[axis][1][c]

    def fall(c, axis):
        return outer[axis][0][c], -outer[axis][1][c]

    layers = [
        (None, rise(2, 1), None),
        (fall(2, 0), None, None),
        (rise(1, 0), fall(0, 1), None),
    ]
    vort = [0.5 * jnp.stack(with_layers(vort_ref[c], layers[c]), axis=0) for c in range(3)]
    velocity = read_all(velocity_ref)
    lamb = [
        vort[1] * velocity[2] - vort[2] * velocity[1],
        vort[2] * velocity[0] - vort[0] * velocity[2],
        vort[0] * velocity[1] - vort[1] * velocity[0],
    ]
    blocks = []
    for field in lamb:
        along_y = along_y_ref[0][None] * field[:, 0:1, :]
        for b in range(1, 8):
            along_y = along_y + along_y_ref[b][None] * field[:, b : b + 1, :]
        for i in range(8):
            plane = along_x_ref[8 * i] * along_y[0]
            for a in range(1, 8):
                plane = plane + along_x_ref[8 * i + a] * along_y[a]
            blocks.append(plane)

    quarter = lane((8, 128)) // 32
    for s in range((len(out_refs) + 3) // 4):
        ordered = [
            jnp.take_along_axis(block, order_ref[4 * s + k % 4], axis=1)
            for k, block in enumerate(blocks)
        ]
        for r in range(min(4, len(out_refs) - 4 * s)):
            out = out_refs[4 * s + r]
            for q in range(6):
                packed = ordered[4 * q]
                for t in range(1, 4):
                    packed = jnp.where(quarter == (r + t) % 4, ordered[4 * q + t], packed)
                out[q] = packed
            out[6] = marks_ref[4 * s + r]


def first_kernel(
    counts, n_faces, deriv_ref, high_ref, low_ref, les_ref, wave_ref, mean_ref, *refs
):
    face_refs, (section_ref, rate_ref, mean_faces_ref), out_refs = (
        refs[:n_faces], refs[n_faces : n_faces + 3], refs[n_faces + 3 :],
    )
    for n, face in enumerate(mean_layers(read_all(mean_ref))):
        for c in range(3):
            mean_faces_ref[n, c] = face[c]
    state = read_all(les_ref)
    rate = les_rate(state, load_faces(face_refs, counts, 0, 5))
    section = [s + r for s, r in zip(state, rate)]
    for c in range(5):
        section_ref[c] = section[c]
    rate = acoustic_rate(
        read_all(wave_ref), read_all(mean_ref), load_faces(face_refs, counts, 5, 9),
        deriv_ref[...], (high_ref[...], low_ref[...]),
    )
    for c in range(4):
        rate_ref[c] = rate[c]
    store_faces(section + [wave_ref[0] + acoustic_step * rate[0]], out_refs, counts)


def source_kernel(counts, n_faces, tile_ref, wave_ref, rate_ref, *refs):
    n_pieces = len(partners(counts[0]))
    pieces = [None] * n_pieces
    for ref, k in zip(refs, sending_sets(n_pieces)):
        pieces[k] = ref
    refs = refs[n_pieces:]
    ready_faces, source_ref, face_refs = refs[:n_faces], refs[n_faces], refs[n_faces + 1 :]
    quarter = lane((8, 128)) // 32
    tile_high, tile_low = tile_ref[0], tile_ref[1]
    total = None
    for s in range((n_pieces + 3) // 4):
        count = min(4, n_pieces - 4 * s)

        def gathered(q, t):
            value = jnp.full((8, 128), -1.0 if q == 6 else 0.0, f32)
            for r in range(count):
                value = jnp.where(quarter == (r + t) % 4, pieces[4 * s + r][q], value)
            return value

        here = [gathered(6, 0).astype(jnp.int32) == slot for slot in range(16)]
        chosen_high, chosen_low = [
            jnp.concatenate([jnp.where(h, part, 0.0) for h in here], axis=0).astype(jnp.bfloat16)
            for part in (tile_high, tile_low)
        ]
        data = []
        for k in range(24):
            piece = gathered(k // 4, k % 4)
            data.append(pltpu.roll(piece, 128 - 32 * (k % 4), 1) if k % 4 else piece)
        data = jnp.concatenate(data, axis=0)
        high = data.astype(jnp.bfloat16)
        low = (data - high.astype(f32)).astype(jnp.bfloat16)
        dot = functools.partial(
            lax.dot_general,
            dimension_numbers=(((1,), (1,)), ((), ())),
            preferred_element_type=f32,
        )
        moved = dot(high, chosen_high) + (dot(low, chosen_high) + dot(high, chosen_low))
        total = moved if total is None else total + moved
    source = [total[64 * c : 64 * c + 64].reshape(8, 8, 128) for c in range(3)]
    middle = []
    for c in range(3):
        source_ref[c] = source[c]
        middle.append(wave_ref[1 + c] + acoustic_step * (rate_ref[1 + c] + source[c]))
    for ready, face in zip(ready_faces, face_refs):
        face[0:6] = ready[...]
    store_faces(middle, [face.at[6:9] for face in face_refs], counts)


def inner_kernel(
    deriv_ref, high_ref, low_ref, les_ref, section_ref, wave_ref, rate_ref, mean_ref, source_ref,
    les_base_ref, wave_base_ref, source_out, sem,
):
    copy = pltpu.make_async_copy(source_ref, source_out, sem)
    copy.start()
    section = read_all(section_ref)
    rate = les_rate(section, None)
    for c in range(5):
        les_base_ref[c] = 0.5 * ((les_ref[c] + section[c]) + rate[c])
    first = read_all(rate_ref)
    middle = [wave_ref[0] + acoustic_step * first[0]]
    for c in range(1, 4):
        middle.append(wave_ref[c] + acoustic_step * (first[c] + source_ref[c - 1]))
    rate = acoustic_rate(
        middle, read_all(mean_ref), None, deriv_ref[...], (high_ref[...], low_ref[...])
    )
    for c in range(4):
        total = rate[c] + source_ref[c - 1] if c else rate[c]
        wave_base_ref[c] = 0.5 * (wave_ref[c] + middle[c] + acoustic_step * total)
    copy.wait()


def add_layers(counts, chosen, face_refs, mean_faces_ref, les_base_ref, wave_base_ref, put):
    layers = les_outer(load_faces(face_refs, counts, 0, 5, chosen))
    for c in range(5):
        part = [layer and (0.5 * layer[0][c], 0.5 * layer[1][c]) for layer in layers]
        put(c, with_layers(les_base_ref[c], part))
    mean_faces = [[mean_faces_ref[n, c] for c in range(3)] for n in range(6)]
    layers = acoustic_outer(mean_faces, load_faces(face_refs, counts, 5, 9, chosen))
    step = 0.5 * acoustic_step
    for c in range(4):
        part = [layer and (step * layer[0][c], step * layer[1][c]) for layer in layers]
        put(5 + c, with_layers(wave_base_ref[c], part))


def z_faces(faces, counts):
    holds = [any(axis == 2 for axis, _ in pair) for pair in slots(counts)]
    return [face if hold else None for face, hold in zip(faces, holds)]


def z_kernel(counts, present, les_base_ref, wave_base_ref, mean_faces_ref, *refs):
    refs = list(refs)
    face_refs = [refs.pop(0) if here else None for here in present]
    les_ref, wave_ref = refs

    def put(c, planes):
        for x, plane in enumerate(planes):
            if c < 5:
                les_ref[c, x] = plane
            else:
                wave_ref[c - 5, x] = plane

    add_layers(counts, (2,), face_refs, mean_faces_ref, les_base_ref, wave_base_ref, put)


def last_kernel(counts, n_faces, les_base_ref, wave_base_ref, mean_faces_ref, *refs):
    face_refs, (les_out, wave_out, les_ref, wave_ref, sems) = (
        refs[:n_faces], refs[n_faces:],
    )
    copies = [
        pltpu.make_async_copy(les_ref, les_out, sems.at[0]),
        pltpu.make_async_copy(wave_ref, wave_out, sems.at[1]),
    ]

    def put(c, planes):
        for x, plane in enumerate(planes):
            if c < 5:
                les_ref[c, x] = plane
            else:
                wave_ref[c - 5, x] = plane
        if c in (4, 8):
            copies[c // 8].start()

    add_layers(counts, (0, 1), face_refs, mean_faces_ref, les_base_ref, wave_base_ref, put)
    for copy in copies:
        copy.wait()


VMEM = pl.BlockSpec(memory_space=pltpu.VMEM)


HBM = pl.BlockSpec(memory_space=pltpu.HBM)


def call(kernel, in_specs, out_shapes, name, cost, scratch=(), out_spec=None):
    return pl.pallas_call(
        kernel,
        in_specs=in_specs,
        out_specs=out_spec or [VMEM] * len(out_shapes),
        out_shape=out_shapes,
        scratch_shapes=list(scratch),
        name=name,
        cost_estimate=pl.CostEstimate(flops=cost, bytes_accessed=800000, transcendentals=0),
        compiler_params=pltpu.CompilerParams(vmem_limit_bytes=24 * 1024 * 1024),
    )


def local(counts, les, wave, mean, projection, owner, slot):
    shape = les.shape[1:]
    faces = face_shapes(counts, 9)
    n_faces = len(faces)
    like = lambda n: jax.ShapeDtypeStruct((n,) + shape, f32)

    table = derivative_matrix()
    deriv = jnp.asarray(table, f32)
    along_z = np.kron(np.eye(16), table.T).astype(np.float32)
    high = along_z.astype(jnp.bfloat16)
    low = (along_z - high.astype(np.float32)).astype(jnp.bfloat16)
    tables = (deriv, jnp.asarray(high), jnp.asarray(low))

    arguments = (les, wave, owner, slot, projection)
    les, wave, owner, slot, projection, *sent = call(
        functools.partial(load_kernel, counts),
        [HBM] * 5,
        [jax.ShapeDtypeStruct(a.shape, a.dtype) for a in arguments] + faces,
        "load_and_faces",
        100000,
        [pltpu.SemaphoreType.DMA((5,))],
    )(*(pltpu.with_memory_space_constraint(a, pltpu.HBM) for a in arguments))
    got = exchange(sent, counts)

    sets = partners(counts[0])
    n_plans = 4 * ((len(sets) + 3) // 4)
    order, marks, along_x, along_y, tile = call(
        functools.partial(plan_kernel, counts),
        [VMEM] * 3,
        [
            jax.ShapeDtypeStruct((n_plans, 8, 128), jnp.int32),
            jax.ShapeDtypeStruct((len(sets), 8, 128), f32),
            jax.ShapeDtypeStruct((64, 8, 128), f32),
            jax.ShapeDtypeStruct((8, 8, 128), f32),
            jax.ShapeDtypeStruct((2, 8, 128), f32),
        ],
        "plan",
        1000000,
    )(owner, slot, projection)
    turning = list(call(vorticity_kernel, [VMEM], [like(3)] * 2, "vorticity", 1000000)(les))
    z_got = z_faces(got, counts)
    present = [face is not None for face in z_got]
    turning[1] = call(
        functools.partial(vorticity_z_kernel, counts, present),
        [VMEM] * (1 + sum(present)),
        [like(3)],
        "vorticity_z",
        1000000,
    )(turning[1], *(face for face in z_got if face is not None))[0]
    pieces = call(
        functools.partial(lamb_kernel, counts, n_faces),
        [VMEM] * (6 + n_faces),
        [jax.ShapeDtypeStruct((7, 8, 128), f32)] * len(sets),
        "lamb_blocks",
        10000000,
    )(order, marks, along_x, along_y, *turning, *got)
    moved = []
    for k in sending_sets(len(sets)):
        still = all(i == j for i, j in sets[k])
        moved.append(pieces[k] if still else lax.ppermute(pieces[k], "gx", sets[k]))
    section, rate, mean_faces, *ready_faces = call(
        functools.partial(first_kernel, counts, n_faces),
        [VMEM] * (6 + n_faces),
        [like(5), like(4), jax.ShapeDtypeStruct((6, 3, 8, 128), f32)] + face_shapes(counts, 6),
        "first_rates",
        40000000,
    )(*tables, les, wave, mean, *got)

    source, *sent = call(
        functools.partial(source_kernel, counts, n_faces),
        [VMEM] * (3 + len(moved) + n_faces),
        [like(3)] + faces,
        "source_and_faces",
        10000000,
    )(tile, wave, rate, *moved, *ready_faces)
    got = exchange(sent, counts)
    les_base, wave_base, source_out = call(
        inner_kernel,
        [VMEM] * 9,
        [like(5), like(4), like(3)],
        "second_rates_inner",
        40000000,
        [pltpu.SemaphoreType.DMA],
        out_spec=[VMEM, VMEM, HBM],
    )(*tables, les, section, wave, rate, mean, source)
    z_got = z_faces(got, counts)
    present = [face is not None for face in z_got]
    les_base, wave_base = call(
        functools.partial(z_kernel, counts, present),
        [VMEM] * (3 + sum(present)),
        [like(5), like(4)],
        "second_rates_z",
        1000000,
    )(les_base, wave_base, mean_faces, *(face for face in z_got if face is not None))
    les_next, wave_next = call(
        functools.partial(last_kernel, counts, n_faces),
        [VMEM] * (3 + n_faces),
        [like(5), like(4)],
        "second_rates_outer",
        4000000,
        [
            pltpu.VMEM(les.shape, f32),
            pltpu.VMEM(wave.shape, f32),
            pltpu.SemaphoreType.DMA((2,)),
        ],
        out_spec=[HBM, HBM],
    )(les_base, wave_base, mean_faces, *got)
    return les_next, source_out, wave_next


def solution(mesh):
    counts = tuple(mesh.shape[axis] for axis in axes)
    field = P(None, *axes)
    return jax.shard_map(
        functools.partial(local, counts),
        mesh=mesh,
        in_specs=(field, field, field, P(), P(*axes), P(*axes)),
        out_specs=(field, field, field),
        check_vma=False,
    )
```

```python
import functools

import jax
import jax.numpy as jnp
import numpy as np
from jax import lax
from jax.experimental import pallas as pl
from jax.experimental.pallas import tpu as pltpu
from jax.sharding import PartitionSpec as P

lobatto_points = np.array(
    [
        -1.0,
        -0.8717401485096066,
        -0.5917001814331423,
        -0.2092992179024789,
        0.2092992179024789,
        0.5917001814331423,
        0.8717401485096066,
        1.0,
    ]
)
flux_half = 0.08
gamma_less = 0.4
acoustic_step = 0.01
upwind_speed = 1.5
face_lift = 28.0
free_stream = (1.0, 0.0, 0.0, 0.0, 2.5)
axes = ("gx", "gy", "gz")
window = 4
f32 = jnp.float32


def derivative_matrix():
    points = lobatto_points
    products = [np.prod([points[i] - points[j] for j in range(8) if j != i]) for i in range(8)]
    matrix = np.zeros((8, 8))
    for i in range(8):
        for j in range(8):
            if j != i:
                matrix[i, j] = products[i] / (products[j] * (points[i] - points[j]))
        matrix[i, i] = -np.sum(matrix[i])
    return matrix


def sublane(shape):
    return lax.broadcasted_iota(jnp.int32, shape, len(shape) - 2)


def lane(shape):
    return lax.broadcasted_iota(jnp.int32, shape, len(shape) - 1)


def rolled(tile, amount, axis):
    amount = amount % tile.shape[axis]
    return pltpu.roll(tile, amount, axis) if amount else tile


def shifted(field, axis, step, outer=None):
    if axis == 0:
        outer = jnp.zeros((8, 128), f32) if outer is None else outer
        if step == 1:
            return jnp.concatenate([field[1:], outer[None]], axis=0)
        return jnp.concatenate([outer[None], field[:-1]], axis=0)
    count = (8, 128)[axis - 1]
    edge = count - 1 if step == 1 else 0
    at_edge = (sublane if axis == 1 else lane)((8, 128)) == edge
    planes = []
    for x in range(8):
        layer = 0.0 if outer is None else rolled(outer, edge - axis * x, axis - 1)
        planes.append(jnp.where(at_edge, layer, rolled(field[x], -step, axis - 1)))
    return jnp.stack(planes, axis=0)


def fluid(state):
    density, mx, my, mz, energy = [s + r for s, r in zip(state, free_stream)]
    inverse = 1.0 / density
    momentum = (mx, my, mz)
    velocity = [m * inverse for m in momentum]
    pressure = gamma_less * (
        energy - 0.5 * (mx * velocity[0] + my * velocity[1] + mz * velocity[2])
    )
    return momentum, velocity, pressure, energy + pressure


def split_flux(state, parts, axis, sign):
    momentum, velocity, pressure, enthalpy = parts
    speed = velocity[axis]
    flux = [momentum[axis]]
    for c in range(3):
        term = momentum[c] * speed
        flux.append(term + pressure if c == axis else term)
    flux.append(enthalpy * speed)
    if sign > 0:
        return [flux_half * (s + f) for s, f in zip(state, flux)]
    return [flux_half * (s - f) for s, f in zip(state, flux)]


def les_rate(state, halos):
    parts = fluid(state)
    total = [-6.0 * flux_half * s for s in state]
    for axis in range(3):
        ahead = split_flux(state, parts, axis, -1)
        behind = split_flux(state, parts, axis, 1)
        ahead_outer = behind_outer = [None] * 5
        if halos is not None:
            before, after = halos[axis]
            ahead_outer = split_flux(after, fluid(after), axis, -1)
            behind_outer = split_flux(before, fluid(before), axis, 1)
        for c in range(5):
            total[c] = total[c] + (
                shifted(ahead[c], axis, 1, ahead_outer[c])
                + shifted(behind[c], axis, -1, behind_outer[c])
            )
    return total


def les_outer(halos):
    return [
        halo
        and (
            split_flux(halo[0], fluid(halo[0]), axis, 1),
            split_flux(halo[1], fluid(halo[1]), axis, -1),
        )
        for axis, halo in enumerate(halos)
    ]


def with_layers(field, layers):
    row, column = sublane((8, 128)), lane((8, 128))
    along_z = layers[2]
    if along_z is not None:
        along_z = jnp.where(lax.rem(column, 2) == 0, along_z[0], rolled(along_z[1], -1, 1))
    planes = []
    for x in range(8):
        plane = field[x]
        if layers[0] is not None and x in (0, 7):
            plane = plane + layers[0][x // 7]
        if layers[1] is not None:
            low, high = layers[1]
            plane = plane + jnp.where(
                row == 0, rolled(low, -x, 0), jnp.where(row == 7, rolled(high, 7 - x, 0), 0.0)
            )
        if along_z is not None:
            ends = (column == 0) | (column == 127)
            plane = plane + jnp.where(ends, rolled(along_z, -2 * x, 1), 0.0)
        planes.append(plane)
    return planes


def wave_flux(state, mean, axis):
    speed = mean[axis]
    pressure = state[0]
    rows = [speed * pressure + state[1 + axis]]
    for c in range(3):
        term = speed * state[1 + c]
        rows.append(term + pressure if c == axis else term)
    return rows


def dot3(left, right):
    high = left.astype(jnp.bfloat16)
    low = (left - high.astype(f32)).astype(jnp.bfloat16)
    dot = functools.partial(jnp.dot, preferred_element_type=f32)
    return dot(high, right[0]) + (dot(low, right[0]) + dot(high, right[1]))


def acoustic_rate(state, mean, halos, deriv, along_z):
    shape = state[0].shape
    table = derivative_matrix()
    flux = wave_flux(state, mean, 0)
    if halos is None:
        halos = [([jnp.zeros((8, 128), f32)] * 4,) * 2] + [([None] * 4,) * 2] * 2
    before, after = halos[0]
    low_mean, high_mean = [m[0] for m in mean], [m[7] for m in mean]
    low_jump = [b - s[0] for b, s in zip(before, state)]
    high_jump = [a - s[7] for a, s in zip(after, state)]
    low_flux = wave_flux(low_jump, low_mean, 0)
    high_flux = wave_flux(high_jump, high_mean, 0)
    half, lift = 0.5 * face_lift, 0.5 * face_lift * upwind_speed
    total = []
    for c in range(4):
        planes = []
        for i in range(8):
            plane = -float(table[i, 0]) * flux[c][0]
            for a in range(1, 8):
                if abs(table[i, a]) > 1e-12:
                    plane = plane - float(table[i, a]) * flux[c][a]
            if i == 0:
                plane = plane + (half * low_flux[c] + lift * low_jump[c])
            if i == 7:
                plane = plane - (half * high_flux[c] - lift * high_jump[c])
            planes.append(plane)
        total.append(jnp.stack(planes, axis=0))
    flux = wave_flux(state, mean, 1)
    before, after = halos[1]
    row = sublane(shape)
    sign = jnp.where(row == 0, half, jnp.where(row == 7, -half, 0.0))
    jump = []
    for s, b, a in zip(state, before, after):
        planes = []
        for x in range(8):
            low = 0.0 if b is None else rolled(b, -x, 0)
            high = 0.0 if a is None else rolled(a, 7 - x, 0)
            planes.append(jnp.where(row[x] == 0, low, jnp.where(row[x] == 7, high, s[x])) - s[x])
        jump.append(jnp.stack(planes, axis=0))
    jump_flux = wave_flux(jump, mean, 1)
    for c in range(4):
        change = lift * jump[c] + sign * jump_flux[c]
        for b in range(8):
            change = change - deriv[:, b : b + 1][None] * flux[c][:, b : b + 1, :]
        total[c] = total[c] + change
    flux = wave_flux(state, mean, 2)
    before, after = halos[2]
    column = lane(shape)
    place = lax.rem(column, 8)
    sign = jnp.where(place == 0, half, jnp.where(place == 7, -half, 0.0))
    jump = [
        jnp.where(
            place == 0,
            shifted(s, 2, -1, b),
            jnp.where(place == 7, shifted(s, 2, 1, a), s),
        )
        - s
        for s, b, a in zip(state, before, after)
    ]
    jump_flux = wave_flux(jump, mean, 2)
    for c in range(4):
        slope = dot3(flux[c].reshape(64, 128), along_z).reshape(shape)
        total[c] = total[c] + (lift * jump[c] + sign * jump_flux[c] - slope)
    return total


def mean_layers(mean):
    return [
        [m[0] for m in mean],
        [m[7] for m in mean],
        [m[:, 0, :] for m in mean],
        [m[:, 7, :] for m in mean],
        [z_layer(m, jnp.int32(0)) for m in mean],
        [z_layer(m, jnp.int32(127)) for m in mean],
    ]


def acoustic_outer(mean_faces, halos):
    half, lift = 0.5 * face_lift, 0.5 * face_lift * upwind_speed
    layers = []
    for axis, halo in enumerate(halos):
        if halo is None:
            layers.append(None)
            continue
        before, after = halo
        low_flux = wave_flux(before, mean_faces[2 * axis], axis)
        high_flux = wave_flux(after, mean_faces[2 * axis + 1], axis)
        layers.append(
            (
                [half * f + lift * b for f, b in zip(low_flux, before)],
                [lift * a - half * f for f, a in zip(high_flux, after)],
            )
        )
    return layers


def tile_rows(matrix):
    spread = (lax.rem(lane((8, 128)), 8) == sublane((8, 128))).astype(f32)
    return jnp.dot(
        matrix, spread, precision=lax.Precision.HIGHEST, preferred_element_type=f32
    )


def pairings(count):
    sets = []
    for first in (0, 1):
        pairs = [(i, i + 1) for i in range(first, count - 1, 2)]
        if pairs:
            sets.append(pairs)
    return sets


def slots(counts):
    found = [(axis, n) for axis in range(3) for n in range(len(pairings(counts[axis])))]
    lower = ((2, 1), (2, 0), (0, 1), (1, 0), (1, 1), (0, 0))
    upper = ((2, 1), (0, 1), (2, 0), (0, 0), (1, 1), (1, 0))
    lower = [swap for swap in lower if swap in found]
    upper = [swap for swap in upper if swap in found] if counts[1] == 4 else lower
    return list(zip(lower, upper))


def in_upper_half(counts):
    return lax.axis_index("gy") >= counts[1] // 2


def routes(counts):
    places = [(x, y, z) for x in range(counts[0]) for y in range(counts[1]) for z in range(counts[2])]
    number = {place: n for n, place in enumerate(places)}

    def partner(place, axis, n):
        pairs = pairings(counts[axis])[n]
        swap = dict(pairs + [(j, i) for i, j in pairs])
        alone = [i for i in range(counts[axis]) if i not in swap]
        spare = 0 if axis else 2
        other = list(place)
        if place[axis] in swap:
            other[axis] = swap[place[axis]]
        elif axis == 0 and len(alone) == 2:
            other[axis] = sum(alone) - place[axis]
        elif counts[spare] % 2 == 0:
            other[spare] = place[spare] ^ 1
        return number[tuple(other)]

    return [
        [
            (number[place], partner(place, *(upper if place[1] >= counts[1] // 2 else lower)))
            for place in places
        ]
        for lower, upper in slots(counts)
    ]


def z_layer(field, at):
    packed = jnp.zeros((8, 128), f32)
    column = lane((8, 128))
    for x in range(8):
        turned = pltpu.roll(field[x], lax.rem(2 * x - at + 128, 128), 1)
        packed = jnp.where(column == 2 * x, turned, packed)
    return packed


def store_faces(fields, out_refs, counts):
    high_half = in_upper_half(counts)
    for c, field in enumerate(fields):
        faces = {}
        for axis in range(3):
            even = lax.rem(lax.axis_index(axes[axis]), 2) == 0
            if axis == 0:
                low, high = field[0], field[7]
            elif axis == 1:
                low, high = field[:, 0, :], field[:, 7, :]
            for n in range(len(pairings(counts[axis]))):
                last = even == (n == 0)
                if axis == 2:
                    faces[axis, n] = z_layer(field, jnp.where(last, 127, 0))
                else:
                    faces[axis, n] = jnp.where(last, high, low)
        for ref, (lower, upper) in zip(out_refs, slots(counts)):
            if lower == upper:
                ref[c] = faces[lower]
            else:
                ref[c] = jnp.where(high_half, faces[upper], faces[lower])


def load_faces(in_refs, counts, first, last, chosen=(0, 1, 2)):
    high_half = in_upper_half(counts)
    lower, upper = zip(*slots(counts))
    halos = []
    for axis in range(3):
        if axis not in chosen:
            halos.append(None)
            continue
        place = lax.axis_index(axes[axis])
        even = lax.rem(place, 2) == 0
        got = []
        for n in range(len(pairings(counts[axis]))):
            a, b = in_refs[lower.index((axis, n))], in_refs[upper.index((axis, n))]
            got.append(
                [a[c] if a is b else jnp.where(high_half, b[c], a[c]) for c in range(first, last)]
            )
        while len(got) < 2:
            got.append([jnp.zeros((8, 128), f32)] * (last - first))
        before = [jnp.where(place == 0, 0.0, jnp.where(even, b, a)) for a, b in zip(*got)]
        after = [
            jnp.where(place == counts[axis] - 1, 0.0, jnp.where(even, a, b))
            for a, b in zip(*got)
        ]
        halos.append((before, after))
    return halos


def face_shapes(counts, width):
    total = sum(len(pairings(count)) for count in counts)
    return [jax.ShapeDtypeStruct((width, 8, 128), f32)] * total


def exchange(faces, counts):
    return [lax.ppermute(face, axes, way) for face, way in zip(faces, routes(counts))]


def read_all(ref):
    return [ref[c] for c in range(ref.shape[0])]


def load_kernel(counts, les_hbm, wave_hbm, les_ref, wave_ref, *refs):
    out_refs, sems = refs[:-1], refs[-1]
    parts = [
        (source.at[low:high], target.at[low:high], first + low, high - low)
        for source, target, low, high, first in (
            (les_hbm, les_ref, 0, 5, 0),
            (wave_hbm, wave_ref, 0, 4, 5),
        )
    ]
    copies = [
        pltpu.make_async_copy(source, target, sems.at[n])
        for n, (source, target, _, _) in enumerate(parts)
    ]
    for copy in copies:
        copy.start()
    for copy, (_, target, first, count) in zip(copies, parts):
        copy.wait()
        fields = [target[c] for c in range(count)]
        store_faces(fields, [ref.at[first : first + count] for ref in out_refs], counts)


def partners(count):
    if count == window:
        return [[(i, i ^ mask) for i in range(count)] for mask in range(count)]
    turns = sorted({d % count for d in range(1 - window, window)})
    return [[(i, (i + turn) % count) for i in range(count)] for turn in turns]


def speeds(state):
    inverse = 1.0 / (state[0] + 1.0)
    return [state[c] * inverse for c in (1, 2, 3)]


def vorticity(les_ref, velocity_ref, vort_ref):
    velocity = speeds([les_ref[c] for c in range(4)])

    def slope(c, axis):
        return shifted(velocity[c], axis, 1) - shifted(velocity[c], axis, -1)

    vort = [slope(2, 1) - slope(1, 2), slope(0, 2) - slope(2, 0), slope(1, 0) - slope(0, 1)]
    for c in range(3):
        velocity_ref[c] = velocity[c]
        vort_ref[c] = vort[c]


def sending_sets(count):
    return [3, 2, 1, 0] if count == window else list(range(count))


def plan_kernel(
    counts, owner_hbm, slot_hbm, proj_hbm, les_ref, order_ref, marks_ref, along_x_ref, along_y_ref,
    tile_ref, velocity_ref, vort_ref, owner_ref, slot_ref, proj_ref, sems,
):
    copies = [
        pltpu.make_async_copy(source, target, sems.at[n])
        for n, (source, target) in enumerate(
            ((owner_hbm, owner_ref), (slot_hbm, slot_ref), (proj_hbm, proj_ref))
        )
    ]
    for copy in copies:
        copy.start()
    vorticity(les_ref, velocity_ref, vort_ref)
    for copy in copies:
        copy.wait()
    count = counts[0]
    n_sets = len(partners(count))
    own = lax.axis_index("gx")
    n_blocks = owner_ref.shape[-1]
    square = (n_blocks, n_blocks)
    block, other = sublane(square), lane(square)

    def spread(ref):
        by_lane = jnp.broadcast_to(ref[0], square)
        here = jnp.where(block == other, by_lane, 0).astype(f32)
        return by_lane, jnp.sum(here, axis=1, keepdims=True).astype(jnp.int32)

    def group_of(owner):
        if count == window:
            return lax.bitwise_xor(owner, own)
        turn = lax.rem(owner - own + count, count)
        if n_sets == count:
            return turn
        return jnp.where(turn < window, turn, turn - (count - n_sets))

    owner_by_lane, owner = spread(owner_ref)
    slot = spread(slot_ref)[1]
    group = group_of(owner)
    before = (group_of(owner_by_lane) == group) & (other < block)
    taken = jnp.sum(before.astype(f32), axis=1, keepdims=True).astype(jnp.int32)
    wide = (n_blocks, 128)
    place = jnp.broadcast_to(group * window + taken, wide)
    column = lane((8, 128))
    quarter = column // 32
    for s in range((n_sets + 3) // 4):
        here = place - 16 * s == lane(wide) // 8
        label = jnp.sum(jnp.where(here, (slot + 1).astype(f32), 0.0), axis=0, keepdims=True) - 1.0
        source = jnp.sum(
            jnp.where(here, (8 * sublane(wide)).astype(f32), 0.0), axis=0, keepdims=True
        )
        labels = jnp.broadcast_to(label, (8, 128))
        order = jnp.broadcast_to(source, (8, 128)).astype(jnp.int32) + lax.rem(column, 8)
        for t in range(4):
            order_ref[4 * s + t] = rolled(order, 32 * t, 1)
        for r in range(min(4, n_sets - 4 * s)):
            marks = labels
            for t in range(1, 4):
                marks = jnp.where(quarter == (r + t) % 4, rolled(labels, 32 * t, 1), marks)
            marks_ref[4 * s + r] = marks
    proj = proj_ref[...]
    for a in range(8):
        along_y = jnp.broadcast_to(proj[:, a : a + 1], (8, 128))
        along_y_ref[a] = along_y
        for i in range(8):
            along_x_ref[8 * i + a] = jnp.broadcast_to(along_y[i : i + 1], (8, 128))
    tile = tile_rows(proj)
    high = tile.astype(jnp.bfloat16).astype(f32)
    tile_ref[0] = high
    tile_ref[1] = tile - high


def vorticity_z_kernel(counts, present, vort_ref, *refs):
    refs = list(refs)
    face_refs = [refs.pop(0) if here else None for here in present]
    (out_ref,) = refs
    before, after = [speeds(layer) for layer in load_faces(face_refs, counts, 0, 4, (2,))[2]]
    for c, layer in ((0, (before[1], -after[1])), (1, (-before[0], after[0]))):
        for x, plane in enumerate(with_layers(vort_ref[c], (None, None, layer))):
            out_ref[c, x] = plane
    out_ref[2] = vort_ref[2]


def lamb_kernel(
    counts, n_faces, order_ref, marks_ref, along_x_ref, along_y_ref, velocity_ref, vort_ref, *refs
):
    face_refs, out_refs = refs[:n_faces], refs[n_faces:]
    outer = [
        halo and (speeds(halo[0]), speeds(halo[1]))
        for halo in load_faces(face_refs, counts, 0, 4, (0, 1))
    ]

    def rise(c, axis):
        return -outer[axis][0][c], outer[axis][1][c]

    def fall(c, axis):
        return outer[axis][0][c], -outer[axis][1][c]

    layers = [
        (None, rise(2, 1), None),
        (fall(2, 0), None, None),
        (rise(1, 0), fall(0, 1), None),
    ]
    vort = [0.5 * jnp.stack(with_layers(vort_ref[c], layers[c]), axis=0) for c in range(3)]
    velocity = read_all(velocity_ref)
    lamb = [
        vort[1] * velocity[2] - vort[2] * velocity[1],
        vort[2] * velocity[0] - vort[0] * velocity[2],
        vort[0] * velocity[1] - vort[1] * velocity[0],
    ]
    blocks = []
    for field in lamb:
        along_y = along_y_ref[0][None] * field[:, 0:1, :]
        for b in range(1, 8):
            along_y = along_y + along_y_ref[b][None] * field[:, b : b + 1, :]
        for i in range(8):
            plane = along_x_ref[8 * i] * along_y[0]
            for a in range(1, 8):
                plane = plane + along_x_ref[8 * i + a] * along_y[a]
            blocks.append(plane)

    quarter = lane((8, 128)) // 32
    for s in range((len(out_refs) + 3) // 4):
        ordered = [
            jnp.take_along_axis(block, order_ref[4 * s + k % 4], axis=1)
            for k, block in enumerate(blocks)
        ]
        for r in range(min(4, len(out_refs) - 4 * s)):
            out = out_refs[4 * s + r]
            for q in range(6):
                packed = ordered[4 * q]
                for t in range(1, 4):
                    packed = jnp.where(quarter == (r + t) % 4, ordered[4 * q + t], packed)
                out[q] = packed
            out[6] = marks_ref[4 * s + r]


def first_kernel(
    counts, n_faces, deriv_ref, high_ref, low_ref, les_ref, wave_ref, mean_ref, *refs
):
    face_refs, (section_ref, rate_ref, mean_faces_ref), out_refs = (
        refs[:n_faces], refs[n_faces : n_faces + 3], refs[n_faces + 3 :],
    )
    for n, face in enumerate(mean_layers(read_all(mean_ref))):
        for c in range(3):
            mean_faces_ref[n, c] = face[c]
    state = read_all(les_ref)
    rate = les_rate(state, load_faces(face_refs, counts, 0, 5))
    section = [s + r for s, r in zip(state, rate)]
    for c in range(5):
        section_ref[c] = section[c]
    rate = acoustic_rate(
        read_all(wave_ref), read_all(mean_ref), load_faces(face_refs, counts, 5, 9),
        deriv_ref[...], (high_ref[...], low_ref[...]),
    )
    for c in range(4):
        rate_ref[c] = rate[c]
    store_faces(section + [wave_ref[0] + acoustic_step * rate[0]], out_refs, counts)


def source_kernel(counts, n_faces, tile_ref, wave_ref, rate_ref, *refs):
    n_pieces = len(partners(counts[0]))
    pieces = [None] * n_pieces
    for ref, k in zip(refs, sending_sets(n_pieces)):
        pieces[k] = ref
    refs = refs[n_pieces:]
    ready_faces, source_ref, face_refs = refs[:n_faces], refs[n_faces], refs[n_faces + 1 :]
    quarter = lane((8, 128)) // 32
    tile_high, tile_low = tile_ref[0], tile_ref[1]
    total = None
    for s in range((n_pieces + 3) // 4):
        count = min(4, n_pieces - 4 * s)

        def gathered(q, t):
            value = jnp.full((8, 128), -1.0 if q == 6 else 0.0, f32)
            for r in range(count):
                value = jnp.where(quarter == (r + t) % 4, pieces[4 * s + r][q], value)
            return value

        here = [gathered(6, 0).astype(jnp.int32) == slot for slot in range(16)]
        chosen_high, chosen_low = [
            jnp.concatenate([jnp.where(h, part, 0.0) for h in here], axis=0).astype(jnp.bfloat16)
            for part in (tile_high, tile_low)
        ]
        data = []
        for k in range(24):
            piece = gathered(k // 4, k % 4)
            data.append(pltpu.roll(piece, 128 - 32 * (k % 4), 1) if k % 4 else piece)
        data = jnp.concatenate(data, axis=0)
        high = data.astype(jnp.bfloat16)
        low = (data - high.astype(f32)).astype(jnp.bfloat16)
        dot = functools.partial(
            lax.dot_general,
            dimension_numbers=(((1,), (1,)), ((), ())),
            preferred_element_type=f32,
        )
        moved = dot(high, chosen_high) + (dot(low, chosen_high) + dot(high, chosen_low))
        total = moved if total is None else total + moved
    source = [total[64 * c : 64 * c + 64].reshape(8, 8, 128) for c in range(3)]
    middle = []
    for c in range(3):
        source_ref[c] = source[c]
        middle.append(wave_ref[1 + c] + acoustic_step * (rate_ref[1 + c] + source[c]))
    for ready, face in zip(ready_faces, face_refs):
        face[0:6] = ready[...]
    store_faces(middle, [face.at[6:9] for face in face_refs], counts)


def inner_kernel(
    deriv_ref, high_ref, low_ref, les_ref, section_ref, wave_ref, rate_ref, mean_ref, source_ref,
    les_base_ref, wave_base_ref, source_out, sem,
):
    copy = pltpu.make_async_copy(source_ref, source_out, sem)
    copy.start()
    section = read_all(section_ref)
    rate = les_rate(section, None)
    for c in range(5):
        les_base_ref[c] = 0.5 * ((les_ref[c] + section[c]) + rate[c])
    first = read_all(rate_ref)
    middle = [wave_ref[0] + acoustic_step * first[0]]
    for c in range(1, 4):
        middle.append(wave_ref[c] + acoustic_step * (first[c] + source_ref[c - 1]))
    rate = acoustic_rate(
        middle, read_all(mean_ref), None, deriv_ref[...], (high_ref[...], low_ref[...])
    )
    for c in range(4):
        total = rate[c] + source_ref[c - 1] if c else rate[c]
        wave_base_ref[c] = 0.5 * (wave_ref[c] + middle[c] + acoustic_step * total)
    copy.wait()


def add_layers(counts, chosen, face_refs, mean_faces_ref, les_base_ref, wave_base_ref, put):
    layers = les_outer(load_faces(face_refs, counts, 0, 5, chosen))
    for c in range(5):
        part = [layer and (0.5 * layer[0][c], 0.5 * layer[1][c]) for layer in layers]
        put(c, with_layers(les_base_ref[c], part))
    mean_faces = [[mean_faces_ref[n, c] for c in range(3)] for n in range(6)]
    layers = acoustic_outer(mean_faces, load_faces(face_refs, counts, 5, 9, chosen))
    step = 0.5 * acoustic_step
    for c in range(4):
        part = [layer and (step * layer[0][c], step * layer[1][c]) for layer in layers]
        put(5 + c, with_layers(wave_base_ref[c], part))


def z_faces(faces, counts):
    holds = [any(axis == 2 for axis, _ in pair) for pair in slots(counts)]
    return [face if hold else None for face, hold in zip(faces, holds)]


def z_kernel(counts, present, les_base_ref, wave_base_ref, mean_faces_ref, *refs):
    refs = list(refs)
    face_refs = [refs.pop(0) if here else None for here in present]
    les_ref, wave_ref = refs

    def put(c, planes):
        for x, plane in enumerate(planes):
            if c < 5:
                les_ref[c, x] = plane
            else:
                wave_ref[c - 5, x] = plane

    add_layers(counts, (2,), face_refs, mean_faces_ref, les_base_ref, wave_base_ref, put)


def last_kernel(counts, n_faces, les_base_ref, wave_base_ref, mean_faces_ref, *refs):
    face_refs, (les_out, wave_out, les_ref, wave_ref, sems) = (
        refs[:n_faces], refs[n_faces:],
    )
    copies = [
        pltpu.make_async_copy(les_ref, les_out, sems.at[0]),
        pltpu.make_async_copy(wave_ref, wave_out, sems.at[1]),
    ]

    def put(c, planes):
        for x, plane in enumerate(planes):
            if c < 5:
                les_ref[c, x] = plane
            else:
                wave_ref[c - 5, x] = plane
        if c in (4, 8):
            copies[c // 8].start()

    add_layers(counts, (0, 1), face_refs, mean_faces_ref, les_base_ref, wave_base_ref, put)
    for copy in copies:
        copy.wait()


VMEM = pl.BlockSpec(memory_space=pltpu.VMEM)


HBM = pl.BlockSpec(memory_space=pltpu.HBM)


def call(kernel, in_specs, out_shapes, name, cost, scratch=(), out_spec=None):
    return pl.pallas_call(
        kernel,
        in_specs=in_specs,
        out_specs=out_spec or [VMEM] * len(out_shapes),
        out_shape=out_shapes,
        scratch_shapes=list(scratch),
        name=name,
        cost_estimate=pl.CostEstimate(flops=cost, bytes_accessed=800000, transcendentals=0),
        compiler_params=pltpu.CompilerParams(vmem_limit_bytes=24 * 1024 * 1024),
    )


def local(counts, les, wave, mean, projection, owner, slot):
    shape = les.shape[1:]
    faces = face_shapes(counts, 9)
    n_faces = len(faces)
    like = lambda n: jax.ShapeDtypeStruct((n,) + shape, f32)

    table = derivative_matrix()
    deriv = jnp.asarray(table, f32)
    along_z = np.kron(np.eye(16), table.T).astype(np.float32)
    high = along_z.astype(jnp.bfloat16)
    low = (along_z - high.astype(np.float32)).astype(jnp.bfloat16)
    tables = (deriv, jnp.asarray(high), jnp.asarray(low))

    in_hbm = lambda *arrays: [pltpu.with_memory_space_constraint(a, pltpu.HBM) for a in arrays]
    les, wave, *sent = call(
        functools.partial(load_kernel, counts),
        [HBM] * 2,
        [like(5), like(4)] + faces,
        "load_and_faces",
        100000,
        [pltpu.SemaphoreType.DMA((2,))],
    )(*in_hbm(les, wave))
    got = exchange(sent, counts)

    sets = partners(counts[0])
    n_plans = 4 * ((len(sets) + 3) // 4)
    small = (owner, slot, projection)
    order, marks, along_x, along_y, tile, *turning = call(
        functools.partial(plan_kernel, counts),
        [HBM] * 3 + [VMEM],
        [
            jax.ShapeDtypeStruct((n_plans, 8, 128), jnp.int32),
            jax.ShapeDtypeStruct((len(sets), 8, 128), f32),
            jax.ShapeDtypeStruct((64, 8, 128), f32),
            jax.ShapeDtypeStruct((8, 8, 128), f32),
            jax.ShapeDtypeStruct((2, 8, 128), f32),
            like(3),
            like(3),
        ],
        "plan_and_vorticity",
        1000000,
        [pltpu.VMEM(a.shape, a.dtype) for a in small] + [pltpu.SemaphoreType.DMA((3,))],
    )(*in_hbm(*small), les)
    z_got = z_faces(got, counts)
    present = [face is not None for face in z_got]
    turning[1] = call(
        functools.partial(vorticity_z_kernel, counts, present),
        [VMEM] * (1 + sum(present)),
        [like(3)],
        "vorticity_z",
        1000000,
    )(turning[1], *(face for face in z_got if face is not None))[0]
    pieces = call(
        functools.partial(lamb_kernel, counts, n_faces),
        [VMEM] * (6 + n_faces),
        [jax.ShapeDtypeStruct((7, 8, 128), f32)] * len(sets),
        "lamb_blocks",
        10000000,
    )(order, marks, along_x, along_y, *turning, *got)
    moved = []
    for k in sending_sets(len(sets)):
        still = all(i == j for i, j in sets[k])
        moved.append(pieces[k] if still else lax.ppermute(pieces[k], "gx", sets[k]))
    section, rate, mean_faces, *ready_faces = call(
        functools.partial(first_kernel, counts, n_faces),
        [VMEM] * (6 + n_faces),
        [like(5), like(4), jax.ShapeDtypeStruct((6, 3, 8, 128), f32)] + face_shapes(counts, 6),
        "first_rates",
        40000000,
    )(*tables, les, wave, mean, *got)

    source, *sent = call(
        functools.partial(source_kernel, counts, n_faces),
        [VMEM] * (3 + len(moved) + n_faces),
        [like(3)] + faces,
        "source_and_faces",
        10000000,
    )(tile, wave, rate, *moved, *ready_faces)
    got = exchange(sent, counts)
    les_base, wave_base, source_out = call(
        inner_kernel,
        [VMEM] * 9,
        [like(5), like(4), like(3)],
        "second_rates_inner",
        40000000,
        [pltpu.SemaphoreType.DMA],
        out_spec=[VMEM, VMEM, HBM],
    )(*tables, les, section, wave, rate, mean, source)
    z_got = z_faces(got, counts)
    present = [face is not None for face in z_got]
    les_base, wave_base = call(
        functools.partial(z_kernel, counts, present),
        [VMEM] * (3 + sum(present)),
        [like(5), like(4)],
        "second_rates_z",
        1000000,
    )(les_base, wave_base, mean_faces, *(face for face in z_got if face is not None))
    les_next, wave_next = call(
        functools.partial(last_kernel, counts, n_faces),
        [VMEM] * (3 + n_faces),
        [like(5), like(4)],
        "second_rates_outer",
        4000000,
        [
            pltpu.VMEM(les.shape, f32),
            pltpu.VMEM(wave.shape, f32),
            pltpu.SemaphoreType.DMA((2,)),
        ],
        out_spec=[HBM, HBM],
    )(les_base, wave_base, mean_faces, *got)
    return les_next, source_out, wave_next


def solution(mesh):
    counts = tuple(mesh.shape[axis] for axis in axes)
    field = P(None, *axes)
    return jax.shard_map(
        functools.partial(local, counts),
        mesh=mesh,
        in_specs=(field, field, field, P(), P(*axes), P(*axes)),
        out_specs=(field, field, field),
        check_vma=False,
    )
```
